32 devices in a mesh: wide: 16 (over z, y, x), tp: 2 (over core).
Axes of the slice: x: 2, y: 2, z: 4, core: 2. Of those that a mesh axis runs over, the one named last changes fastest.
Arguments:
- tokens: bfloat16 [32, 256, 1152], P('wide', 'tp'), may hold values from -6 to 6
- cotangent: bfloat16 [32, 256, 1152], P('wide', 'tp'), may hold values from -6 to 6
- caption: bfloat16 [240, 4096], P('wide'), may hold values from -6 to 6
- caption_len: int32 [2], replicated, may hold values from 5 to 120, as said below
- clip_id: int32 [32], replicated, may hold values from 0 to 1, never falling along the last dimension, each value on 1 to 31 neighbouring positions
- timestep: int32 [2], replicated, may hold values from 0 to 999
- w_mod: bfloat16 [1152, 6912], P(None, 'tp'), may hold values from -0.1875 to 0.1875
- b_mod: bfloat16 [6912], P('tp'), may hold values from 0.5 to 1.5
- w_text: bfloat16 [4096, 1152], P(None, 'tp'), may hold values from -0.09375 to 0.09375
- w_sqkv: bfloat16 [1152, 3, 1152], P(None, None, 'tp'), may hold values from -0.1875 to 0.1875
- w_so: bfloat16 [1152, 1152], P('tp'), may hold values from -0.75 to 0.75
- w_tqkv: bfloat16 [1152, 3, 1152], P(None, None, 'tp'), may hold values from -0.1875 to 0.1875
- w_to: bfloat16 [1152, 1152], P('tp'), may hold values from -0.375 to 0.375
- w_cq: bfloat16 [1152, 1152], P(None, 'tp'), may hold values from -0.1875 to 0.1875
- w_ckv: bfloat16 [1152, 2, 1152], P(None, None, 'tp'), may hold values from -0.1875 to 0.1875
- w_co: bfloat16 [1152, 1152], P('tp'), may hold values from -0.5 to 0.5
- w_fc1: bfloat16 [1152, 4608], P(None, 'tp'), may hold values from -0.1875 to 0.1875
- w_fc2: bfloat16 [4608, 1152], P('tp'), may hold values from -0.09375 to 0.09375
Outputs:
- block_out: bfloat16 [32, 256, 1152], P('wide', 'tp')
- grad_tokens: bfloat16 [32, 256, 1152], P('wide', 'tp')
- grad_w_mod: float32 [1152, 6912], P(None, ('tp', 'wide'))
- grad_b_mod: float32 [6912], P(('tp', 'wide'))
- grad_w_text: float32 [4096, 1152], P('wide', 'tp')
- grad_w_sqkv: float32 [1152, 3, 1152], P('wide', None, 'tp')
- grad_w_so: float32 [1152, 1152], P('tp', 'wide')
- grad_w_tqkv: float32 [1152, 3, 1152], P('wide', None, 'tp')
- grad_w_to: float32 [1152, 1152], P('tp', 'wide')
- grad_w_cq: float32 [1152, 1152], P('wide', 'tp')
- grad_w_ckv: float32 [1152, 2, 1152], P('wide', None, 'tp')
- grad_w_co: float32 [1152, 1152], P('tp', 'wide')
- grad_w_fc1: float32 [1152, 4608], P('wide', 'tp')
- grad_w_fc2: float32 [4608, 1152], P('tp', 'wide')
The draws below stay inside these ranges and needn't reach their ends.
Inputs may be any that keep to these rules, and one draw needn't show every extreme that they name: `clip_id`: frame ids never fall; every clip has 1 to 31 frames. A clip's real caption tokens are the first caption_len rows of its 120; some clip fills all 120.
All inputs are finite; a program needn't handle non-finite values.
Results may differ from the reference program's by a relative error of at most 0.03.
Values may be sent and summed in bfloat16 or wider, within the bound.
A program may use at most 256 MiB of HBM per device.

```python
import math
import jax
import jax.numpy as jnp
import numpy as np
from jax import lax

D = 1152
HEADS = 16
HD = 72
FF = 4608
TXT = 4096
LTXT = 120
P_SIZE = 256
F_DEV = 2
FRAMES = 32
CLIPS = 2
CLIP_MOST = 31


def draw_caption_len(key, part):
    shortest = min(5, LTXT)
    lengths = jax.random.randint(jax.random.fold_in(key, 11), (CLIPS,), shortest, LTXT + 1)
    full_at = jax.random.randint(jax.random.fold_in(key, 12), (), 0, CLIPS)
    return jnp.where(jnp.arange(CLIPS) == full_at, LTXT, lengths).astype(jnp.int32)


def strengthened(array, own_key, source, target, shards_of, factor):
    owner, partner = [(jnp.arange(array.shape[position]) // (array.shape[position] // shards_of)).reshape([-1 if axis == position else 1 for axis in range(array.ndim)]) for position in (source, target)]
    chosen = jax.random.permutation(own_key, shards_of)[partner]
    strong = (owner == chosen) | (owner == (partner + shards_of // 2) % shards_of)
    return jnp.where(strong, factor * array, array)


def steps_of(own_key, dims, cuts, low, largest):
    factor_of = 1.0
    for position, shards_of in cuts:
        steps = jax.random.uniform(jax.random.fold_in(jax.random.fold_in(own_key, 6), position), (shards_of,), jnp.float32, low / len(cuts), largest / len(cuts))
        factor_of = factor_of * jnp.repeat(jnp.exp(steps), dims[position] // shards_of).reshape((-1,) + (1,) * (len(dims) - 1 - position))
    return factor_of


def length_profile(count, total, limit, lean):
    loads = [(1 << 20) // math.isqrt(grade ** lean) + 1 for grade in range(2, count + 1)]
    surplus, holding = total - limit - (count - 1), [1] * (count - 1)
    while surplus > 0:
        candidates = [i for i in range(count - 1) if holding[i] < limit]
        whole, remaining = sum([loads[i] for i in candidates]), surplus
        for i in candidates:
            extra = min(limit - holding[i], max(1, remaining * loads[i] // whole), surplus)
            holding[i] = holding[i] + extra
            surplus = surplus - extra
    return np.array([limit] + holding)


def uneven(key, count, total, reach, skew):
    if count == 2:
        one = jax.random.randint(key, (), max(1, total - reach), min(reach, total - 1) + 1)
        return jnp.stack([one, total - one])
    sizes = jnp.asarray(length_profile(count, total, reach, skew), jnp.int32)
    twos = (count - 1) // 2
    donor, receiver = sizes[1:1 + 2 * twos:2], sizes[2:2 + 2 * twos:2]
    slack = jnp.minimum(donor - 1, reach - receiver)
    passed = jax.random.randint(jax.random.fold_in(key, 1), (twos,), 0, 1 << 20) % (slack + 1)
    sizes = sizes.at[1:1 + 2 * twos:2].set(donor - passed).at[2:2 + 2 * twos:2].set(receiver + passed)
    return sizes[jax.random.permutation(jax.random.fold_in(key, 2), count)]


def bell_draw(rng, extent, scale, most, cuts=(), dtype=jnp.bfloat16):
    level = steps_of(rng, extent, cuts, -0.22, 0.18) if cuts else 1.0
    entries = jax.random.normal(rng, extent, jnp.float32) * scale * level
    return jnp.minimum(jnp.maximum(entries, -most), most).astype(dtype)


def gaussian_with(key, extent, scale, bound, split, heavy, held_as=jnp.bfloat16):
    array = scale * jax.random.normal(key, extent, jnp.float32)
    if split:
        array = array * steps_of(key, extent, split, -0.22, 0.18)
    return jnp.clip(strengthened(array, jax.random.fold_in(key, 3), *heavy), -bound, bound).astype(held_as)


def setup_inputs(seed: int = 0) -> dict:
    key_of = jax.random.split(jax.random.key(seed), 19)
    return {
        "tokens": bell_draw(key_of[0], (FRAMES, P_SIZE, D), 1.0, 6.0, ((0, 16), (1, 2))),
        "cotangent": gaussian_with(key_of[1], (FRAMES, P_SIZE, D), 1.0, 6.0, ((0, 16), (1, 2)), (0, 2, 16, 2.0)),
        "caption": bell_draw(key_of[2], (CLIPS * LTXT, TXT), 1.0, 6.0, ((0, 16),)),
        "caption_len": draw_caption_len(jax.random.fold_in(key_of[18], 71), 0),
        "clip_id": jnp.searchsorted(jnp.cumsum(uneven(key_of[4], CLIPS, FRAMES, CLIP_MOST, 2)), jnp.arange(FRAMES), side="right").astype(jnp.int32),
        "timestep": jax.random.randint(key_of[5], (CLIPS,), 0, 1000).astype(jnp.int32),
        "w_mod": bell_draw(key_of[6], (D, 6 * D), D ** -0.5, 0.1875, ((1, 2),)),
        "b_mod": jnp.clip(0.5 + 1.0 * jax.random.uniform(key_of[7], (6 * D,), jnp.float32) ** steps_of(key_of[7], (6 * D,), ((0, 2),), -0.2, 0.2), 0.5, 1.5).astype(jnp.bfloat16),
        "w_text": bell_draw(key_of[8], (TXT, D), TXT ** -0.5, 0.09375, ((1, 2),)),
        "w_sqkv": bell_draw(key_of[9], (D, 3, D), D ** -0.5, 0.1875, ((2, 2),)),
        "w_so": bell_draw(key_of[10], (D, D), (D // 16) ** -0.5, 0.75, ((0, 2),)),
        "w_tqkv": bell_draw(key_of[11], (D, 3, D), D ** -0.5, 0.1875, ((2, 2),)),
        "w_to": bell_draw(key_of[12], (D, D), (D // 4) ** -0.5, 0.375, ((0, 2),)),
        "w_cq": bell_draw(key_of[13], (D, D), D ** -0.5, 0.1875, ((1, 2),)),
        "w_ckv": bell_draw(key_of[14], (D, 2, D), D ** -0.5, 0.1875, ((2, 2),)),
        "w_co": bell_draw(key_of[15], (D, D), (D // 8) ** -0.5, 0.5, ((0, 2),)),
        "w_fc1": bell_draw(key_of[16], (D, FF), D ** -0.5, 0.1875, ((1, 2),)),
        "w_fc2": bell_draw(key_of[17], (FF, D), FF ** -0.5, 0.09375, ((0, 2),)),
    }


@jax.custom_vjp
def low(v):
    return lax.optimization_barrier(v.astype(jnp.bfloat16)).astype(jnp.float32)

@jax.custom_vjp
def low_back(v):
    return v

def low_keep(v):
    return (low(v), None)

def low_pass(kept, grad):
    return (grad,)

def back_keep(v):
    return (v, None)

def back_low(kept, grad):
    return (low(grad),)
low.defvjp(low_keep, low_pass)
low_back.defvjp(back_keep, back_low)
EPS = 1e-06
HIGH = lax.Precision.HIGHEST

def product(left, right):
    return jnp.dot(left, right, precision=HIGH, preferred_element_type=jnp.float32)

def layer_norm(operand):
    average = lax.optimization_barrier(jnp.mean(operand, axis=-1, keepdims=True))
    centred = operand - average
    spread = lax.optimization_barrier(jnp.mean(centred * centred, axis=-1, keepdims=True))
    return centred * lax.rsqrt(spread + EPS)

def attend(queries, key_rows, value_rows, allowed):
    scores = jnp.einsum('...qd,...kd->...qk', queries, key_rows, precision=HIGH) * HD ** (-0.5)
    scores = low_back(scores)
    scores = jnp.where(allowed, scores, -1e+30)
    attn_probs = jax.nn.softmax(scores, axis=-1)
    return jnp.einsum('...qk,...kd->...qd', low(attn_probs), value_rows, precision=HIGH)

def reference(tokens, cotangent, caption, caption_len, clip_id, timestep, w_mod, b_mod, w_text, w_sqkv, w_so, w_tqkv, w_to, w_cq, w_ckv, w_co, w_fc1, w_fc2):
    half_width = D // 2
    frequencies = jnp.exp(-math.log(10000.0) * jnp.arange(half_width).astype(jnp.float32) / half_width)
    angles = timestep.astype(jnp.float32)[:, None] * frequencies[None, :]
    embedding = jnp.concatenate([jnp.cos(angles), jnp.sin(angles)], axis=1)
    caption_full = caption.astype(jnp.float32)
    key_valid = jnp.arange(LTXT)[None, :] < caption_len[:, None]
    same_clip = clip_id[:, None] == clip_id[None, :]
    blocks = FRAMES // F_DEV
    clip_blocks = clip_id.reshape(blocks, F_DEV)

    def forward(stream, params):
        mod_weight, mod_bias, text_weight, sqkv_weight, so_weight, tqkv_weight, to_weight, cq_weight, ckv_weight, co_weight, fc1_weight, fc2_weight = params
        silu_embed = low(jax.nn.silu(embedding))
        modulation = low(product(silu_embed, mod_weight) + mod_bias)
        frame_mod = modulation[clip_id]
        pieces = [frame_mod[:, None, slot_index * D:(slot_index + 1) * D] for slot_index in range(6)]
        shift_one, scale_one, gate_one, shift_two, scale_two, gate_two = pieces
        h_one = low(layer_norm(stream) * (1.0 + scale_one) + shift_one)
        qkv_one = low(low_back(product(h_one.reshape(-1, D), sqkv_weight.reshape(D, 3 * D))))
        qkv_one = qkv_one.reshape(FRAMES, P_SIZE, 3, HEADS, HD).transpose(2, 0, 3, 1, 4)
        qkv_one = qkv_one.reshape(3, blocks, F_DEV, HEADS, P_SIZE, HD).transpose(1, 0, 2, 3, 4, 5)

        def spatial_block(block_parts):
            return attend(block_parts[0], block_parts[1], block_parts[2], True)
        spatial = lax.map(jax.checkpoint(spatial_block), qkv_one)
        spatial = spatial.reshape(FRAMES, HEADS, P_SIZE, HD).transpose(0, 2, 1, 3).reshape(-1, D)
        attn_one = low(low_back(spatial))
        y_one = low_back(product(attn_one, so_weight)).reshape(FRAMES, P_SIZE, D)
        stream_one = stream + gate_one * y_one
        h_two = low(layer_norm(stream_one))
        qkv_two = low(low_back(product(h_two.reshape(-1, D), tqkv_weight.reshape(D, 3 * D))))
        qkv_two = qkv_two.reshape(FRAMES, P_SIZE // 8, 8, 3, HEADS, HD).transpose(1, 3, 2, 4, 0, 5)

        def temporal_block(block_parts):
            return attend(block_parts[0], block_parts[1], block_parts[2], same_clip)
        temporal = lax.map(jax.checkpoint(temporal_block), qkv_two)
        temporal = temporal.reshape(P_SIZE, HEADS, FRAMES, HD).transpose(2, 0, 1, 3).reshape(-1, D)
        attn_two = low(low_back(temporal))
        y_two = low_back(product(attn_two, to_weight)).reshape(FRAMES, P_SIZE, D)
        stream_two = stream_one + y_two
        h_three = low(layer_norm(stream_two))
        queries = low(low_back(product(h_three.reshape(-1, D), cq_weight)))
        queries = queries.reshape(FRAMES, P_SIZE, HEADS, HD).transpose(0, 2, 1, 3).reshape(blocks, F_DEV, HEADS, P_SIZE, HD)
        context = low(low_back(product(caption_full, text_weight)))
        keyval = low(low_back(product(context, ckv_weight.reshape(D, 2 * D))))
        keyval = keyval.reshape(CLIPS, LTXT, 2, HEADS, HD).transpose(2, 0, 3, 1, 4)

        def cross_block(block_parts):
            block_queries, block_clips = block_parts
            key_rows = keyval[0][block_clips]
            value_rows = keyval[1][block_clips]
            allowed = key_valid[block_clips][:, None, None, :]
            return attend(block_queries, key_rows, value_rows, allowed)
        cross = lax.map(jax.checkpoint(cross_block), (queries, clip_blocks))
        cross = cross.reshape(FRAMES, HEADS, P_SIZE, HD).transpose(0, 2, 1, 3).reshape(-1, D)
        attn_three = low(low_back(cross))
        y_three = low_back(product(attn_three, co_weight)).reshape(FRAMES, P_SIZE, D)
        stream_three = stream_two + y_three
        h_four = low(layer_norm(stream_three) * (1.0 + scale_two) + shift_two)
        upper = low_back(product(h_four.reshape(-1, D), fc1_weight))
        active = low(jax.nn.gelu(upper, approximate=True))
        y_four = low_back(product(active, fc2_weight)).reshape(FRAMES, P_SIZE, D)
        return stream_three + gate_two * y_four
    params = (w_mod, b_mod, w_text, w_sqkv, w_so, w_tqkv, w_to, w_cq, w_ckv, w_co, w_fc1, w_fc2)
    params = jax.tree.map(lambda weight: weight.astype(jnp.float32), params)
    block_out, pullback = jax.vjp(forward, tokens.astype(jnp.float32), params)
    grad_stream, grad_params = pullback(cotangent.astype(jnp.float32))
    return (block_out.astype(jnp.bfloat16), grad_stream.astype(jnp.bfloat16), grad_params[0], grad_params[1], grad_params[2], grad_params[3], grad_params[4], grad_params[5], grad_params[6], grad_params[7], grad_params[8], grad_params[9], grad_params[10], grad_params[11])
```

```python
import math

import jax
import jax.numpy as jnp
from jax import lax
from jax.sharding import PartitionSpec as P

HD = 72
LTXT = 120
EPS = 1e-06
NEGATIVE = -1e30
HIGH = lax.Precision.HIGHEST
BF = jnp.bfloat16
F32 = jnp.float32


def dot32(left, right):
    return jnp.dot(left, right, preferred_element_type=F32)


def dot_nt(left, right):
    return lax.dot_general(left, right, (((1,), (1,)), ((), ())), preferred_element_type=F32)


def dot_tn(left, right):
    return lax.dot_general(left, right, (((0,), (0,)), ((), ())), preferred_element_type=F32)


def layer_norm(operand):
    average = jnp.mean(operand, axis=-1, keepdims=True)
    centred = operand - average
    spread = jnp.mean(centred * centred, axis=-1, keepdims=True)
    inverse = lax.rsqrt(spread + EPS)
    return (centred * inverse, inverse)


def norm_back(grad_normed, normed, inverse):
    grad_mean = jnp.mean(grad_normed, axis=-1, keepdims=True)
    grad_cross = jnp.mean(grad_normed * normed, axis=-1, keepdims=True)
    return inverse * (grad_normed - grad_mean - normed * grad_cross)


def gelu_tanh(operand):
    return jax.nn.gelu(operand, approximate=True)


def attend_forward(queries, key_rows, value_rows, allowed):
    scores = jnp.einsum("...qd,...kd->...qk", queries, key_rows, preferred_element_type=F32)
    scores = scores * HD ** (-0.5)
    if allowed is not None:
        scores = jnp.where(allowed, scores, NEGATIVE)
    largest = jnp.max(scores, axis=-1, keepdims=True)
    log_total = largest + jnp.log(jnp.sum(jnp.exp(scores - largest), axis=-1, keepdims=True))
    attn_probs = jnp.exp(scores - log_total).astype(BF)
    output = jnp.einsum("...qk,...kd->...qd", attn_probs, value_rows, preferred_element_type=F32)
    return (output.astype(BF), log_total)


def attend_backward(queries, key_rows, value_rows, log_total, grad_out, allowed):
    factor = HD ** (-0.5)
    scores = jnp.einsum("...qd,...kd->...qk", queries, key_rows, preferred_element_type=F32)
    scores = scores * factor
    if allowed is not None:
        scores = jnp.where(allowed, scores, NEGATIVE)
    attn_probs = jnp.exp(scores - log_total)
    grad_probs = jnp.einsum("...qd,...kd->...qk", grad_out, value_rows, preferred_element_type=F32)
    row_dot = jnp.sum(attn_probs * grad_probs, axis=-1, keepdims=True)
    grad_scores = (attn_probs * (grad_probs - row_dot)).astype(BF)
    grad_queries = (
        jnp.einsum("...qk,...kd->...qd", grad_scores, key_rows, preferred_element_type=F32) * factor
    )
    grad_keys = (
        jnp.einsum("...qk,...qd->...kd", grad_scores, queries, preferred_element_type=F32) * factor
    )
    grad_values = jnp.einsum(
        "...qk,...qd->...kd", attn_probs.astype(BF), grad_out, preferred_element_type=F32
    )
    return (grad_queries, grad_keys, grad_values)


def tp_from(operand, shift):
    size = lax.axis_size("tp")
    return lax.ppermute(operand, "tp", [(s, (s - shift) % size) for s in range(size)])


def tp_to(operand, shift):
    size = lax.axis_size("tp")
    return lax.ppermute(operand, "tp", [(s, (s + shift) % size) for s in range(size)])


def tp_gather(operand):
    return [operand] + [tp_from(operand, k) for k in range(1, lax.axis_size("tp"))]


def tp_sum(parts):
    total = parts[0].astype(F32)
    for k in range(1, lax.axis_size("tp")):
        total = total + tp_to(parts[k].astype(BF), k).astype(F32)
    return total


def tp_ordered(relative):
    size = lax.axis_size("tp")
    start = (size - lax.axis_index("tp")) % size
    return lax.dynamic_slice_in_dim(jnp.stack(relative + relative), start, size, axis=0)


def flip(operand, mask):
    size = lax.axis_size("wide")
    return lax.ppermute(operand, "wide", [(s, s ^ mask) for s in range(size)])


def pick(operand, index, axis):
    return lax.dynamic_index_in_dim(operand, index, axis, keepdims=False)


def exchange_halves(sides, bit):
    mine = (lax.axis_index("wide") >> bit) & 1
    keep = [pick(side, mine, -2) for side in sides]
    give = [pick(side, 1 - mine, -2) for side in sides]
    return keep, [flip(side, 1 << bit) for side in give]


def weight_grad(pairs, first):
    wide = lax.axis_index("wide")
    second = 1 - first
    depth = lax.axis_size("wide") // 4
    total = None
    for model_side, head_side in pairs:
        term = dot_tn(model_side, head_side)
        total = term if total is None else total + term
    columns = total.shape[1]
    total = total.astype(BF).reshape(depth, 2, 2, total.shape[0] // (4 * depth), columns)
    axis = 1 if second == 1 else 2
    mine = (wide >> second) & 1
    half = pick(total, mine, axis).astype(F32) + flip(
        pick(total, 1 - mine, axis), 1 << second
    ).astype(F32)
    at = wide >> 2
    block = pick(half, at, 0)
    narrow = half.astype(BF)
    for k in range(1, depth):
        block = block + flip(pick(narrow, at ^ k, 0), 4 * k).astype(F32)
    mine = (wide >> first) & 1
    keep = pick(block, mine, 0)
    got = flip(pick(block, 1 - mine, 0).astype(BF), 1 << first).astype(F32)
    return jnp.where(mine == 0, jnp.stack([keep, got], axis=1), jnp.stack([got, keep], axis=1))


def paired_tokens(model_side, head_sides, first):
    stack = jnp.stack(head_sides)
    (keep,), (got,) = exchange_halves([stack], first)
    keep = keep.reshape(keep.shape[0], keep.shape[1], -1)
    got = got.reshape(keep.shape)
    model_got = flip(model_side, 1 << first)
    pairs = [(model_side, keep[0]), (model_got, got[0])]
    for k in range(1, lax.axis_size("tp")):
        pairs.append((tp_to(model_side, k), tp_to(keep[k], k)))
        pairs.append((tp_to(model_got, k), tp_to(got[k], k)))
    return pairs


def on_device(
    tokens,
    cotangent,
    caption,
    caption_len,
    clip_id,
    timestep,
    w_mod,
    b_mod,
    w_text,
    w_sqkv,
    w_so,
    w_tqkv,
    w_to,
    w_cq,
    w_ckv,
    w_co,
    w_fc1,
    w_fc2,
):
    n_tp = lax.axis_size("tp")
    n_wide = lax.axis_size("wide")
    frames_here, patch_part, width = tokens.shape
    local_cols = w_so.shape[0]
    heads_here = local_cols // HD
    hidden = w_fc1.shape[1]
    clip_count = timestep.shape[0]
    frames = clip_id.shape[0]
    patch_here = patch_part // n_wide
    rows = frames_here * patch_part
    wide_at = lax.axis_index("wide")

    def qkv_rows(weight):
        return weight.transpose(1, 2, 0)

    tqkv_all = tp_gather(qkv_rows(w_tqkv))
    to_all = tp_gather(w_to)
    cq_all = tp_gather(w_cq.T)
    co_all = tp_gather(w_co)
    fc1_all = tp_gather(w_fc1)
    fc2_all = tp_gather(w_fc2)

    half_width = width // 2
    frequencies = jnp.exp(-math.log(10000.0) * jnp.arange(half_width).astype(F32) / half_width)
    angles = timestep.astype(F32)[:, None] * frequencies[None, :]
    embedding = jnp.concatenate([jnp.cos(angles), jnp.sin(angles)], axis=1)
    silu_embed = jax.nn.silu(embedding).astype(BF)
    mod_part = (dot32(silu_embed, w_mod) + b_mod.astype(F32)).astype(BF)
    modulation = tp_ordered(tp_gather(mod_part)).transpose(1, 0, 2).reshape(clip_count, -1)
    my_clips = lax.dynamic_slice_in_dim(clip_id, wide_at * frames_here, frames_here)
    clip_hot = (clip_id[:, None] == jnp.arange(clip_count)[None, :]).astype(BF)
    mod_frames = dot32(clip_hot, modulation)
    mod_here = lax.dynamic_slice_in_dim(mod_frames, wide_at * frames_here, frames_here)
    here = [mod_here[:, None, i * width : (i + 1) * width] for i in range(3)]
    every = [mod_frames[:, None, i * width : (i + 1) * width] for i in range(3, 6)]
    shift_one, scale_one, gate_one = here
    shift_two, scale_two, gate_two = every

    context_part = dot32(caption, w_text).astype(BF)
    context = tp_ordered(tp_gather(context_part)).transpose(1, 0, 2).reshape(caption.shape[0], -1)
    ckv_rows = w_ckv.transpose(1, 2, 0).reshape(2 * local_cols, width)
    keyval_part = dot_nt(context, ckv_rows).astype(BF)
    keyval = lax.all_gather(keyval_part, "wide", axis=0, tiled=True)
    keyval_all = tp_gather(keyval)
    text_cols = caption.shape[1] // n_wide
    context_cols = width // n_wide
    for_owner = jnp.concatenate(
        [
            caption.reshape(-1, n_wide, text_cols),
            context.reshape(-1, n_wide, context_cols),
        ],
        axis=2,
    ).transpose(1, 0, 2)
    for_owner = lax.all_to_all(for_owner, "wide", split_axis=0, concat_axis=0, tiled=True)
    for_owner = for_owner.reshape(-1, text_cols + context_cols)
    caption_cols, context_cols = for_owner[:, :text_cols], for_owner[:, text_cols:]

    def to_patches(operand):
        operand = operand.reshape(frames_here, n_wide, patch_here, width).transpose(1, 0, 2, 3)
        operand = lax.all_to_all(operand, "wide", split_axis=0, concat_axis=0, tiled=True)
        return operand.reshape(frames, patch_here, width)

    def to_frames(operand):
        operand = operand.reshape(n_wide, frames_here, patch_here, width)
        operand = lax.all_to_all(operand, "wide", split_axis=0, concat_axis=0, tiled=True)
        return operand.transpose(1, 0, 2, 3).reshape(frames_here, patch_part, width)

    grad_out = to_patches(cotangent).astype(F32)

    tokens_all = jnp.stack(tp_gather(tokens)).astype(F32)
    normed_one, inverse_one = layer_norm(tokens_all)
    h_one = (normed_one * (1.0 + scale_one) + shift_one).astype(BF)
    normed_one, inverse_one = normed_one[0], inverse_one[0]
    h_one_rows = h_one.reshape(n_tp * rows, width)
    sqkv_rows = qkv_rows(w_sqkv)

    def spatial_heads(operand):
        return (
            operand.reshape(n_tp, frames_here, patch_part, heads_here, HD)
            .transpose(1, 3, 0, 2, 4)
            .reshape(frames_here, heads_here, n_tp * patch_part, HD)
        )

    def spatial_rows(operand):
        return (
            operand.reshape(frames_here, heads_here, n_tp, patch_part, HD)
            .transpose(2, 0, 3, 1, 4)
            .reshape(n_tp * rows, local_cols)
        )

    heads_one = [spatial_heads(dot_nt(h_one_rows, sqkv_rows[i]).astype(BF)) for i in range(3)]
    out_one, total_one = attend_forward(*heads_one, None)
    attn_one = spatial_rows(out_one)
    y_one = tp_sum(dot32(attn_one, w_so).reshape(n_tp, frames_here, patch_part, width))
    stream_one = (tokens.astype(F32) + gate_one * y_one).astype(BF)

    count = frames * patch_here
    stream = to_patches(stream_one).astype(F32)
    clip_rows = jnp.repeat(clip_id, patch_here)
    patch_rows = jnp.tile(jnp.arange(patch_here), frames)
    allowed_two = (clip_rows[:, None] == clip_rows[None, :]) & (
        patch_rows[:, None] == patch_rows[None, :]
    )
    key_clip = jnp.repeat(jnp.arange(clip_count), LTXT)
    key_at = jnp.tile(jnp.arange(LTXT), clip_count)
    allowed_three = (clip_rows[:, None] == key_clip[None, :]) & (
        key_at < jnp.repeat(caption_len, LTXT)
    )[None, :]

    def heads(operand):
        return operand.reshape(-1, heads_here, HD).transpose(1, 0, 2)

    def unheads(operand):
        return operand.transpose(1, 0, 2).reshape(-1, local_cols)

    stream = stream.reshape(count, width)
    normed_two, inverse_two = layer_norm(stream)
    h_two = normed_two.astype(BF)
    heads_two = [
        [heads(dot_nt(h_two, weight[i]).astype(BF)) for i in range(3)] for weight in tqkv_all
    ]
    kept_two = [attend_forward(*part, allowed_two) for part in heads_two]
    attn_two = [unheads(part[0]) for part in kept_two]
    stream = stream + sum(dot32(part, weight) for part, weight in zip(attn_two, to_all))

    normed_three, inverse_three = layer_norm(stream)
    h_three = normed_three.astype(BF)
    heads_three = []
    for r in range(n_tp):
        query = heads(dot_nt(h_three, cq_all[r]).astype(BF))
        key_rows = heads(keyval_all[r][:, :local_cols])
        value_rows = heads(keyval_all[r][:, local_cols:])
        heads_three.append((query, key_rows, value_rows))
    kept_three = [attend_forward(*part, allowed_three) for part in heads_three]
    attn_three = [unheads(part[0]) for part in kept_three]
    stream = stream + sum(dot32(part, weight) for part, weight in zip(attn_three, co_all))

    def by_frame(operand):
        return operand.reshape(frames, patch_here, -1)

    def by_row(operand):
        return operand.reshape(count, -1)

    normed_four, inverse_four = layer_norm(stream)
    h_four = by_row((by_frame(normed_four) * (1.0 + scale_two) + shift_two)).astype(BF)
    upper = [dot32(h_four, weight) for weight in fc1_all]
    active = [gelu_tanh(part).astype(BF) for part in upper]
    y_four = sum(dot32(part, weight) for part, weight in zip(active, fc2_all))
    block_out = (by_frame(stream) + gate_two * by_frame(y_four)).astype(BF)
    block_out = to_frames(block_out)

    def clip_sums(operand, hot):
        return lax.dot_general(
            hot, jnp.sum(operand, axis=1), (((0,), (0,)), ((), ())), precision=HIGH
        )

    hot_all = clip_hot.astype(F32)
    hot_here = lax.dynamic_slice_in_dim(hot_all, wide_at * frames_here, frames_here)

    grad_gate_two = clip_sums(grad_out * by_frame(y_four), hot_all)
    grad_y4 = by_row(gate_two * grad_out).astype(BF)
    grad_upper = []
    for r in range(n_tp):
        unused, gelu_back = jax.vjp(gelu_tanh, upper[r])
        grad_upper.append(gelu_back(dot_nt(grad_y4, fc2_all[r]))[0].astype(BF))
    grad_h4 = sum(dot_nt(part, weight) for part, weight in zip(grad_upper, fc1_all))
    grad_shift_two = clip_sums(by_frame(grad_h4), hot_all)
    grad_scale_two = clip_sums(by_frame(grad_h4 * normed_four), hot_all)
    grad_normed = by_row(by_frame(grad_h4) * (1.0 + scale_two))
    grad = by_row(grad_out) + norm_back(grad_normed, normed_four, inverse_four)

    def halves(parts, groups):
        return [part.reshape(part.shape[0], groups, 2, -1) for part in parts]

    grad_fc2 = weight_grad(paired_tokens(grad_y4, halves(active, 1), 1), 1)
    grad_fc1 = weight_grad(paired_tokens(h_four, halves(grad_upper, 1), 0), 0)

    grad_y3 = grad.astype(BF)
    grad_co = weight_grad(paired_tokens(grad_y3, halves(attn_three, 1), 1), 1)
    grad_q3, grad_kv = [], []
    for r in range(n_tp):
        grad_attn = heads(dot_nt(grad_y3, co_all[r]).astype(BF))
        grads = attend_backward(*heads_three[r], kept_three[r][1], grad_attn, allowed_three)
        grad_q3.append(unheads(grads[0]).astype(BF))
        grad_kv.append(jnp.concatenate([unheads(grads[1]), unheads(grads[2])], axis=1))
    grad_cq = weight_grad(paired_tokens(h_three, halves(grad_q3, 1), 0), 0)
    grad_h3 = sum(dot32(part, weight) for part, weight in zip(grad_q3, cq_all))
    grad = grad + norm_back(grad_h3, normed_three, inverse_three)
    grad_kv = lax.psum(tp_sum(grad_kv), "wide").astype(BF)
    grad_ckv = dot_tn(context_cols, grad_kv).reshape(-1, 2, local_cols)
    grad_context = dot32(grad_kv, ckv_rows)
    relative = [
        pick(
            grad_context.reshape(-1, n_tp, width // n_tp),
            (lax.axis_index("tp") + k) % n_tp,
            1,
        )
        for k in range(n_tp)
    ]
    grad_context = tp_sum(relative).astype(BF)
    grad_text = dot_tn(caption_cols, grad_context)

    grad_y2 = grad.astype(BF)
    grad_to = weight_grad(paired_tokens(grad_y2, halves(attn_two, 1), 1), 1)
    grad_qkv2 = []
    for r in range(n_tp):
        grad_attn = heads(dot_nt(grad_y2, to_all[r]).astype(BF))
        grads = attend_backward(*heads_two[r], kept_two[r][1], grad_attn, allowed_two)
        grad_qkv2.append(jnp.stack([unheads(part).astype(BF) for part in grads], axis=1))
    grad_tqkv = weight_grad(
        paired_tokens(h_two, [part.reshape(count, 3, 2, -1) for part in grad_qkv2], 0), 0
    )
    grad_h2 = sum(
        dot32(part[:, i], weight[i])
        for part, weight in zip(grad_qkv2, tqkv_all)
        for i in range(3)
    )
    grad = grad + norm_back(grad_h2, normed_two, inverse_two)
    grad = to_frames(by_frame(grad.astype(BF))).astype(F32)

    grad_gate_one = clip_sums(grad * y_one, hot_here)
    grad_y1 = (gate_one * grad).astype(BF)
    grad_y1_rows = jnp.stack(tp_gather(grad_y1)).reshape(n_tp * rows, width)
    grad_attn1 = spatial_heads(dot_nt(grad_y1_rows, w_so).astype(BF))
    grads_one = attend_backward(*heads_one, total_one, grad_attn1, None)
    grad_qkv1 = jnp.stack([spatial_rows(part).astype(BF) for part in grads_one], axis=1)
    grad_h1 = sum(dot32(grad_qkv1[:, i], sqkv_rows[i]) for i in range(3))
    grad_h1 = tp_sum(grad_h1.reshape(n_tp, frames_here, patch_part, width))
    grad_shift_one = clip_sums(grad_h1, hot_here)
    grad_scale_one = clip_sums(grad_h1 * normed_one, hot_here)
    grad = grad + norm_back(grad_h1 * (1.0 + scale_one), normed_one, inverse_one)
    grad_tokens = grad.astype(BF)

    def spatial_pairs(model_rows, own_rows, head_side, first):
        (keep,), (got,) = exchange_halves([head_side], first)
        keep, got = (side.reshape(side.shape[0], -1) for side in (keep, got))
        model_got = jnp.concatenate(tp_gather(flip(own_rows, 1 << first)))
        return [(model_rows, keep), (model_got, got)]

    grad_so = weight_grad(
        spatial_pairs(
            grad_y1_rows, grad_y1.reshape(rows, width), halves([attn_one], 1)[0], 1
        ),
        1,
    )
    grad_sqkv = weight_grad(
        spatial_pairs(
            h_one_rows,
            h_one[0].reshape(rows, width),
            grad_qkv1.reshape(n_tp * rows, 3, 2, -1),
            0,
        ),
        0,
    )

    grad_mod = jnp.concatenate(
        [
            grad_shift_one,
            grad_scale_one,
            grad_gate_one,
            grad_shift_two,
            grad_scale_two,
            grad_gate_two,
        ],
        axis=1,
    )
    grad_mod = lax.psum_scatter(grad_mod, ("tp", "wide"), scatter_dimension=1, tiled=True)
    grad_w_mod = lax.dot_general(
        silu_embed.astype(F32), grad_mod, (((0,), (0,)), ((), ())), precision=HIGH
    )

    def plain(block):
        return block.reshape(block.shape[0], -1)

    def triple(block):
        return block.reshape(block.shape[0], 2, 3, -1).transpose(0, 2, 1, 3).reshape(
            block.shape[0], 3, local_cols
        )

    return (
        block_out,
        grad_tokens,
        grad_w_mod,
        jnp.sum(grad_mod, axis=0),
        grad_text,
        triple(grad_sqkv),
        plain(grad_so).T,
        triple(grad_tqkv),
        plain(grad_to).T,
        plain(grad_cq),
        grad_ckv,
        plain(grad_co).T,
        plain(grad_fc1),
        plain(grad_fc2).T,
    )


def solution(mesh):
    placed = (
        P("wide", "tp", None),
        P("wide", "tp", None),
        P("wide", None),
        P(),
        P(),
        P(),
        P(None, "tp"),
        P("tp"),
        P(None, "tp"),
        P(None, None, "tp"),
        P("tp", None),
        P(None, None, "tp"),
        P("tp", None),
        P(None, "tp"),
        P(None, None, "tp"),
        P("tp", None),
        P(None, "tp"),
        P("tp", None),
    )
    return jax.shard_map(
        on_device,
        mesh=mesh,
        in_specs=placed,
        out_specs=(
            P("wide", "tp", None),
            P("wide", "tp", None),
            P(None, ("tp", "wide")),
            P(("tp", "wide")),
            P("wide", "tp"),
            P("wide", None, "tp"),
            P("tp", "wide"),
            P("wide", None, "tp"),
            P("tp", "wide"),
            P("wide", "tp"),
            P("wide", None, "tp"),
            P("tp", "wide"),
            P("wide", "tp"),
            P("tp", "wide"),
        ),
        check_vma=False,
    )
```

```python
import functools
import math

import jax
import jax.numpy as jnp
from jax import lax
from jax.experimental import pallas as pl
from jax.experimental.pallas import tpu as pltpu
from jax.sharding import PartitionSpec as P

HD = 72
LTXT = 120
EPS = 1e-06
NEGATIVE = -1e30
HIGH = lax.Precision.HIGHEST
BF = jnp.bfloat16
F32 = jnp.float32
LANES = 128
FACTOR = HD ** (-0.5)
VMEM = pltpu.VMEM
MB = 1 << 20


def dot_nn(left, right):
    return lax.dot_general(left, right, (((1,), (0,)), ((), ())), preferred_element_type=F32)


def dot_nt(left, right):
    return lax.dot_general(left, right, (((1,), (1,)), ((), ())), preferred_element_type=F32)


def dot_tn(left, right):
    return lax.dot_general(left, right, (((0,), (0,)), ((), ())), preferred_element_type=F32)


def norm_of(rows):
    average = jnp.mean(rows, axis=-1, keepdims=True)
    centred = rows - average
    inverse = lax.rsqrt(jnp.mean(centred * centred, axis=-1, keepdims=True) + EPS)
    return centred * inverse, inverse


def norm_back(grad_normed, normed, inverse):
    grad_mean = jnp.mean(grad_normed, axis=-1, keepdims=True)
    grad_cross = jnp.mean(grad_normed * normed, axis=-1, keepdims=True)
    return inverse * (grad_normed - grad_mean - normed * grad_cross)


def window(head, columns):
    low = HD * head
    start = low // LANES * LANES
    stop = min(-(-(low + HD) // LANES) * LANES, columns)
    at = lax.broadcasted_iota(jnp.int32, (1, stop - start), 1) + start
    own = jnp.where((at >= low) & (at < low + HD), 1.0, 0.0).astype(BF)
    return start, stop, own


class Tiles:
    def __init__(self, write, columns, scale=None):
        self.write, self.columns, self.scale, self.open = write, columns, scale, {}

    def add(self, start, stop, value):
        for low in range(start, stop, LANES):
            part = value[:, low - start : min(low + LANES, stop) - start]
            self.open[low] = self.open[low] + part if low in self.open else part

    def flush(self, below):
        for low in sorted(self.open):
            if low + LANES <= below or below >= self.columns:
                part = self.open.pop(low)
                if self.scale is not None:
                    part = part * self.scale
                self.write(low, min(low + LANES, self.columns), part)


def attend(query, key, value, bias, heads, columns, keep_probs, write):
    out = Tiles(write, columns)
    for head in range(heads):
        start, stop, own = window(head, columns)
        scores = dot_nt(query(start, stop) * own, key(start, stop)) * FACTOR
        if bias is not None:
            scores = scores + bias
        scores = jnp.exp(scores - jnp.max(scores, axis=-1, keepdims=True))
        probs = (scores * (1.0 / jnp.sum(scores, axis=-1, keepdims=True))).astype(BF)
        keep_probs(head, probs)
        out.add(start, stop, dot_nn(probs, value(start, stop) * own))
        out.flush(HD * (head + 1))


def attend_back(query, key, value, grad_out, probs_of, heads, columns, write_q, write_k, write_v):
    grad_q = Tiles(write_q, columns, FACTOR)
    grad_k = Tiles(write_k, columns, FACTOR)
    grad_v = Tiles(write_v, columns)
    for head in range(heads):
        start, stop, own = window(head, columns)
        probs = probs_of(head)
        grad_own = grad_out(start, stop) * own
        grad_probs = dot_nt(grad_own, value(start, stop))
        wide_probs = probs.astype(F32)
        grad_scores = wide_probs * grad_probs
        row = jnp.sum(grad_scores, axis=-1, keepdims=True)
        grad_scores = (grad_scores - wide_probs * row).astype(BF)
        grad_q.add(start, stop, dot_nn(grad_scores, key(start, stop) * own))
        grad_k.add(start, stop, dot_tn(grad_scores, query(start, stop) * own))
        grad_v.add(start, stop, dot_tn(probs, grad_own))
        for tiles in (grad_q, grad_k, grad_v):
            tiles.flush(HD * (head + 1))


class Moves:
    def __init__(self, sems):
        self.sems, self.used = sems, 0

    def start(self, source, target):
        copy = pltpu.make_async_copy(source, target, self.sems.at[self.used])
        self.used += 1
        copy.start()
        return copy


def any_spec():
    return pl.BlockSpec(memory_space=pl.ANY)


def vmem_spec():
    return pl.BlockSpec(memory_space=VMEM)


def call(kernel, outs, ins, in_any, out_any, scratch, flops, limit=56, **params):
    moved = sum(math.prod(a.shape) * a.dtype.itemsize for a in list(ins) + list(outs))
    return pl.pallas_call(
        kernel,
        out_shape=tuple(outs),
        in_specs=[any_spec() if flag else vmem_spec() for flag in in_any],
        out_specs=tuple(any_spec() if flag else vmem_spec() for flag in out_any),
        scratch_shapes=scratch,
        compiler_params=pltpu.CompilerParams(vmem_limit_bytes=limit * MB, **params),
        cost_estimate=pl.CostEstimate(flops=flops, bytes_accessed=moved, transcendentals=0),
    )(*ins)


def like(shape, dtype=BF):
    return jax.ShapeDtypeStruct(shape, dtype)


def spatial_forward(tokens_list, mod_here, sqkv_rows, w_so, frames_here):
    n_tp = len(tokens_list)
    rows, width = tokens_list[0].shape
    columns = w_so.shape[0]
    patch_part = rows // frames_here
    per_frame = n_tp * patch_part
    count = n_tp * rows
    heads = columns // HD

    def kernel(*refs):
        token_refs = refs[:n_tp]
        mod_ref, qkv_hbm, so_hbm = refs[n_tp : n_tp + 3]
        h_ref, h_own, qkv_out, probs_out, a_keep, a_give, y_ref = refs[n_tp + 3 : n_tp + 10]
        y_others = refs[n_tp + 10 : 2 * n_tp + 9]
        weight_qkv, weight_o, qkv_ref, probs_ref, attn_ref, sems = refs[2 * n_tp + 9 :]
        moves = Moves(sems)
        weights = [moves.start(qkv_hbm.at[i], weight_qkv.at[i]) for i in range(3)]
        weight_out = moves.start(so_hbm, weight_o)
        for frame in range(frames_here):
            shift = mod_ref[frame : frame + 1, 0:width]
            scale = 1.0 + mod_ref[frame : frame + 1, width : 2 * width]
            for r in range(n_tp):
                part = token_refs[r][frame * patch_part : (frame + 1) * patch_part, :]
                normed, unused = norm_of(part.astype(F32))
                at = frame * per_frame + r * patch_part
                value = (normed * scale + shift).astype(BF)
                h_ref[at : at + patch_part, :] = value
                if r == 0:
                    h_own[frame * patch_part : (frame + 1) * patch_part, :] = value
        outgoing = []
        for i in range(3):
            weights[i].wait()
            qkv_ref[i] = dot_nt(h_ref[...], weight_qkv[i]).astype(BF)
        outgoing.append(moves.start(qkv_ref, qkv_out))
        for frame in range(frames_here):
            at = slice(frame * per_frame, (frame + 1) * per_frame)

            def keep_probs(head, probs, frame=frame):
                probs_ref[frame * heads + head] = probs

            def write(low, high, part, at=at):
                attn_ref[at, low:high] = part.astype(BF)

            attend(
                lambda low, high, at=at: qkv_ref[0, at, low:high],
                lambda low, high, at=at: qkv_ref[1, at, low:high],
                lambda low, high, at=at: qkv_ref[2, at, low:high],
                None,
                heads,
                columns,
                keep_probs,
                write,
            )
        outgoing.append(moves.start(probs_ref, probs_out))
        mine = lax.rem(lax.div(lax.axis_index("wide"), 2), 2)
        first, second = attn_ref[:, : columns // 2], attn_ref[:, columns // 2 :]
        a_keep[...] = jnp.where(mine == 0, first, second)
        a_give[...] = jnp.where(mine == 0, second, first)
        weight_out.wait()
        for frame in range(frames_here):
            at = frame * per_frame
            branch = dot_nn(attn_ref[at : at + per_frame, :], weight_o[...])
            here = slice(frame * patch_part, (frame + 1) * patch_part)
            y_ref[here, :] = branch[:patch_part]
            for r in range(1, n_tp):
                y_others[r - 1][here, :] = branch[r * patch_part : (r + 1) * patch_part].astype(BF)
        for copy in outgoing:
            copy.wait()

    outs = [
        like((count, width)),
        like((rows, width)),
        like((3, count, columns)),
        like((frames_here * heads, per_frame, per_frame)),
        like((count, columns // 2)),
        like((count, columns // 2)),
        like((rows, width), F32),
    ] + [like((rows, width))] * (n_tp - 1)
    ins = list(tokens_list) + [mod_here, sqkv_rows, w_so]
    return call(
        kernel,
        outs,
        ins,
        [False] * (n_tp + 1) + [True, True],
        [False, False, True, True] + [False] * (n_tp + 2),
        [
            VMEM((3, columns, width), BF),
            VMEM((columns, width), BF),
            VMEM((3, count, columns), BF),
            VMEM((frames_here * heads, per_frame, per_frame), BF),
            VMEM((count, columns), BF),
            pltpu.SemaphoreType.DMA((6,)),
        ],
        2 * count * width * columns * 4 + 4 * frames_here * heads * per_frame * per_frame * 256,
    )


def greet(others):
    barrier = pltpu.get_barrier_semaphore()
    size = lax.axis_size("wide")
    me = lax.axis_index("wide")

    def signal(k, carry):
        pl.semaphore_signal(
            barrier, inc=1, device_id={"wide": lax.rem(me + k, size)}, device_id_type=pl.DeviceIdType.MESH
        )
        return carry

    lax.fori_loop(1, size, signal, 0)
    pl.semaphore_wait(barrier, others)


def swap_blocks(send, recv, send_sem, recv_sem):
    size = lax.axis_size("wide")
    me = lax.axis_index("wide")

    def copy(k, source, target, peer):
        return pltpu.make_async_remote_copy(
            src_ref=send.at[source],
            dst_ref=recv.at[target],
            send_sem=send_sem.at[k],
            recv_sem=recv_sem.at[k],
            device_id={"wide": peer},
            device_id_type=pl.DeviceIdType.MESH,
        )

    def start(k, carry):
        peer = lax.rem(me + k, size)
        copy(k, peer, me, peer).start()
        return carry

    def finish(k, carry):
        peer = lax.rem(me + size - k, size)
        copy(k, peer, peer, peer).wait_recv()
        return carry

    def drain(k, carry):
        peer = lax.rem(me + k, size)
        copy(k, peer, me, peer).wait_send()
        return carry

    lax.fori_loop(1, size, start, 0)
    recv[me] = send[me]
    lax.fori_loop(1, size, finish, 0)
    lax.fori_loop(1, size, drain, 0)


def swap_scratch(size, block, width):
    return [
        VMEM((size, block, width), BF),
        VMEM((size, block, width), BF),
        pltpu.SemaphoreType.DMA((size,)),
        pltpu.SemaphoreType.DMA((size,)),
    ]


def stream_to_patches(tokens_rows, y_own, y_others, mod_here, frames_here):
    size = lax.axis_size("wide")
    rows, width = tokens_rows.shape
    patch_part = rows // frames_here
    patch_here = patch_part // size
    block = frames_here * patch_here
    others = len(y_others)

    def kernel(*refs):
        token_ref, y_ref, mod_ref = refs[0], refs[1], refs[2 + others]
        out_ref, total_ref = refs[3 + others : 5 + others]
        send, recv, send_sem, recv_sem = refs[5 + others :]
        for frame in range(frames_here):
            at = slice(frame * patch_part, (frame + 1) * patch_part)
            branch = y_ref[at, :]
            for other in refs[2 : 2 + others]:
                branch = branch + other[at, :].astype(F32)
            total_ref[at, :] = branch
            gate = mod_ref[frame : frame + 1, 2 * width : 3 * width]
            stream = token_ref[at, :].astype(F32) + gate * branch
            for owner in range(size):
                send[owner, frame * patch_here : (frame + 1) * patch_here, :] = stream[
                    owner * patch_here : (owner + 1) * patch_here
                ].astype(BF)
        greet(size - 1)
        swap_blocks(send, recv, send_sem, recv_sem)
        out_ref[...] = recv[...]

    ins = [tokens_rows, y_own] + list(y_others) + [mod_here]
    return call(
        kernel,
        [like((size, block, width)), like((rows, width), F32)],
        ins,
        [False] * len(ins),
        [False, False],
        swap_scratch(size, block, width),
        10 * rows * width,
        collective_id=1,
        has_side_effects=True,
    )


def grads_to_frames(grad_blocks, y_one, mod_here, frames_here):
    size, block, width = grad_blocks.shape
    rows = y_one.shape[0]
    patch_part = rows // frames_here
    patch_here = patch_part // size

    def kernel(grad_ref, y_ref, mod_ref, stream_ref, branch_ref, gate_ref, recv, send_sem, recv_sem):
        greet(size - 1)
        swap_blocks(grad_ref, recv, send_sem, recv_sem)
        for owner in range(size):
            part = recv[owner].astype(F32)
            for frame in range(frames_here):
                at = frame * patch_part + owner * patch_here
                stream_ref[at : at + patch_here, :] = part[
                    frame * patch_here : (frame + 1) * patch_here
                ]
        for frame in range(frames_here):
            at = slice(frame * patch_part, (frame + 1) * patch_part)
            stream = stream_ref[at, :]
            gate_ref[frame : frame + 1, :] = jnp.sum(stream * y_ref[at, :], axis=0, keepdims=True)
            branch_ref[at, :] = (stream * mod_ref[frame : frame + 1, 2 * width : 3 * width]).astype(BF)

    ins = [grad_blocks, y_one, mod_here]
    return call(
        kernel,
        [like((rows, width), F32), like((rows, width)), like((frames_here, width), F32)],
        ins,
        [False] * 3,
        [False] * 3,
        swap_scratch(size, block, width)[1:],
        10 * rows * width,
        collective_id=2,
        has_side_effects=True,
    )


def fill_rows(moves, sources, target):
    step = sources[0].shape[0]
    return [moves.start(ref, target.at[pl.ds(r * step, step), :]) for r, ref in enumerate(sources)]


def middle_forward(stream, bias_two, bias_three, keyval_list, tqkv_list, to_list, cq_list, co_list):
    n_tp = len(tqkv_list)
    count, width = stream.shape
    keys = bias_three.shape[1]
    columns = to_list[0].shape[0]
    heads = width // HD

    def kernel(*refs):
        stream_ref, bias_two_ref, bias_three_ref = refs[:3]
        at = 3
        groups = []
        for unused in range(5):
            groups.append(refs[at : at + n_tp])
            at += n_tp
        keyvals, tqkvs, tos, cqs, cos = groups
        h2_out, qkv_out, p2_out, a2_out, inv2_ref, h3_out, q3_out, p3_out, a3_out, inv3_ref, x_ref, kv_ref = refs[at : at + 12]
        w_qkv, w_o, w_q, w_c, h2, qkv, p2, a2, h3, q3, p3, a3, sems = refs[at + 12 :]
        moves = Moves(sems)
        qkv_in = [
            [
                moves.start(tqkvs[r].at[i], w_qkv.at[i, pl.ds(r * columns, columns), :])
                for r in range(n_tp)
            ]
            for i in range(3)
        ]
        o_in = fill_rows(moves, tos, w_o)
        q_in = fill_rows(moves, cqs, w_q)
        c_in = fill_rows(moves, cos, w_c)
        outgoing = []
        for i in range(2):
            for r in range(n_tp):
                kv_ref[i, :, r * columns : (r + 1) * columns] = keyvals[r][i]
        stream_one = stream_ref[...].astype(F32)
        normed, inverse = norm_of(stream_one)
        inv2_ref[...] = jnp.broadcast_to(inverse, inv2_ref.shape)
        h2[...] = normed.astype(BF)
        outgoing.append(moves.start(h2, h2_out))
        for i in range(3):
            for copy in qkv_in[i]:
                copy.wait()
            qkv[i] = dot_nt(h2[...], w_qkv[i]).astype(BF)
        outgoing.append(moves.start(qkv, qkv_out))

        def keep_two(head, probs):
            p2[head] = probs

        def write_two(low, high, part):
            a2[:, low:high] = part.astype(BF)

        attend(
            lambda low, high: qkv[0, :, low:high],
            lambda low, high: qkv[1, :, low:high],
            lambda low, high: qkv[2, :, low:high],
            bias_two_ref[...],
            heads,
            width,
            keep_two,
            write_two,
        )
        outgoing.append(moves.start(p2, p2_out))
        outgoing.append(moves.start(a2, a2_out))
        for copy in o_in:
            copy.wait()
        x_ref[...] = stream_one + dot_nn(a2[...], w_o[...])
        normed, inverse = norm_of(x_ref[...])
        inv3_ref[...] = jnp.broadcast_to(inverse, inv3_ref.shape)
        h3[...] = normed.astype(BF)
        outgoing.append(moves.start(h3, h3_out))
        for copy in q_in:
            copy.wait()
        q3[...] = dot_nt(h3[...], w_q[...]).astype(BF)
        outgoing.append(moves.start(q3, q3_out))

        def keep_three(head, probs):
            p3[head] = probs

        def write_three(low, high, part):
            a3[:, low:high] = part.astype(BF)

        attend(
            lambda low, high: q3[:, low:high],
            lambda low, high: kv_ref[0, :, low:high],
            lambda low, high: kv_ref[1, :, low:high],
            bias_three_ref[...],
            heads,
            width,
            keep_three,
            write_three,
        )
        outgoing.append(moves.start(p3, p3_out))
        outgoing.append(moves.start(a3, a3_out))
        for copy in c_in:
            copy.wait()
        x_ref[...] = x_ref[...] + dot_nn(a3[...], w_c[...])
        for copy in outgoing:
            copy.wait()

    square = (count, width)
    outs = [
        like(square),
        like((3,) + square),
        like((heads, count, count)),
        like(square),
        like((count, LANES), F32),
        like(square),
        like(square),
        like((heads, count, keys)),
        like(square),
        like((count, LANES), F32),
        like(square, F32),
        like((2, keys, width)),
    ]
    kept = [square, (3,) + square, (heads, count, count), square, square, square, (heads, count, keys), square]
    ins = [stream, bias_two, bias_three, *keyval_list, *tqkv_list, *to_list, *cq_list, *co_list]
    full = n_tp * columns
    return call(
        kernel,
        outs,
        ins,
        [False] * (3 + n_tp) + [True] * (4 * n_tp),
        [True, True, True, True, False, True, True, True, True, False, False, False],
        [VMEM((3, full, width), BF)]
        + [VMEM((full, width), BF)] * 3
        + [VMEM(shape, BF) for shape in kept]
        + [pltpu.SemaphoreType.DMA((6 * n_tp + 8,))],
        2 * count * width * width * 6 + 4 * heads * count * (count + keys) * 256,
    )


def feed_forward(stream, grad_out, mod_rows, hot_rows, fc1_list, fc2_list):
    n_tp = len(fc1_list)
    count, width = stream.shape
    hidden = fc1_list[0].shape[1]
    half = hidden // 2
    clips = hot_rows.shape[1]

    def kernel(*refs):
        stream_ref, grad_ref, mod_ref, hot_ref = refs[:4]
        fc1s, fc2s = refs[4 : 4 + n_tp], refs[4 + n_tp : 4 + 2 * n_tp]
        at = 4 + 2 * n_tp
        out_ref, up_keep, up_give, down_keep, down_give, g_ref, mod_sum = refs[at : at + 7]
        w1, w2, normed_ref, total_y, total_h, sems = refs[at + 7 :]
        moves = Moves(sems)
        loads = []
        pieces = 2 if half % LANES == 0 else 1
        for r in range(n_tp):
            for piece in range(pieces):
                cols = pl.ds(piece * (hidden // pieces), hidden // pieces)
                loads.append(
                    (
                        moves.start(fc1s[r].at[:, cols], w1.at[r, :, cols]),
                        moves.start(fc2s[r].at[cols, :], w2.at[r, cols, :]),
                    )
                )
        wide = lax.axis_index("wide")
        bit = [lax.rem(wide, 2), lax.rem(lax.div(wide, 2), 2)]
        shift = mod_ref[:, 0:width].astype(F32)
        scale = 1.0 + mod_ref[:, width : 2 * width].astype(F32)
        gate = mod_ref[:, 2 * width :].astype(F32)
        normed, inverse = norm_of(stream_ref[...])
        normed_ref[...] = normed
        h_four = (normed * scale + shift).astype(BF)
        grad_y = (gate * grad_ref[...].astype(F32)).astype(BF)
        for pack in (up_keep, up_give):
            pack[:, 0:width] = h_four
        for pack in (down_keep, down_give):
            pack[:, 0:width] = grad_y
        for r in range(n_tp):
            for part in range(2):
                at_chunk = 2 * r + part
                if at_chunk % (2 // pieces) == 0:
                    for copy in loads[at_chunk // (2 // pieces)]:
                        copy.wait()
                hid = slice(part * half, (part + 1) * half)
                upper = dot_nn(up_keep[:, 0:width], w1[r, :, hid])
                square = upper * upper
                tanh = jnp.tanh(upper * (0.7978845608028654 + 0.035677408136300125 * square))
                rise = 0.5 + 0.5 * tanh
                active = (upper * rise).astype(BF)
                slope = rise + (0.5 * upper) * (1.0 - tanh * tanh) * (
                    0.7978845608028654 + 0.10703222440890037 * square
                )
                grad_upper = (dot_nt(down_keep[:, 0:width], w2[r, hid, :]) * slope).astype(BF)
                cols = slice(width + r * half, width + (r + 1) * half)
                for keep, give, mine, value in (
                    (up_keep, up_give, bit[0], grad_upper),
                    (down_keep, down_give, bit[1], active),
                ):

                    @pl.when(mine == part)
                    def _():
                        keep[:, cols] = value

                    @pl.when(mine != part)
                    def _():
                        give[:, cols] = value

                y_term = dot_nn(active, w2[r, hid, :])
                h_term = dot_nt(grad_upper, w1[r, :, hid])
                if at_chunk == 0:
                    total_y[...] = y_term
                    total_h[...] = h_term
                else:
                    total_y[...] += y_term
                    total_h[...] += h_term
        gate = mod_ref[:, 2 * width :].astype(F32)
        out_ref[...] = (stream_ref[...] + gate * total_y[...]).astype(BF)
        grad = grad_ref[...].astype(F32)
        hot = hot_ref[...]
        mod_sum[:, 2 * width :] = dot_tn(hot, (grad * total_y[...]).astype(BF))
        grad_h = total_h[...]
        mod_sum[:, 0:width] = dot_tn(hot, grad_h.astype(BF))
        normed = normed_ref[...]
        mod_sum[:, width : 2 * width] = dot_tn(hot, (grad_h * normed).astype(BF))
        scale = 1.0 + mod_ref[:, width : 2 * width].astype(F32)
        unused, inverse = norm_of(stream_ref[...])
        g_ref[...] = grad + norm_back(grad_h * scale, normed, inverse)

    pack = like((count, width + n_tp * half))
    ins = [stream, grad_out, mod_rows, hot_rows, *fc1_list, *fc2_list]
    return call(
        kernel,
        [like((count, width)), pack, pack, pack, pack, like((count, width), F32), like((clips, 3 * width), F32)],
        ins,
        [False] * 4 + [True] * (2 * n_tp),
        [False] * 7,
        [
            VMEM((n_tp, width, hidden), BF),
            VMEM((n_tp, hidden, width), BF),
            VMEM((count, width), F32),
            VMEM((count, width), F32),
            VMEM((count, width), F32),
            pltpu.SemaphoreType.DMA((4 * n_tp,)),
        ],
        2 * count * width * hidden * n_tp * 4,
    )


def middle_backward(grad, kept, keyval, tqkv_list, to_list, cq_list, co_list):
    n_tp = len(tqkv_list)
    h2, qkv, p2, a2, inv2, h3, q3, p3, a3, inv3 = kept
    count, width = grad.shape
    keys = keyval.shape[1]
    columns = to_list[0].shape[0]
    part = columns // 2
    heads = width // HD
    full = n_tp * columns

    def kernel(*refs):
        grad_ref, inv2_ref, inv3_ref, h2_ref, h3_ref = refs[:5]
        qkv_hbm, p2_hbm, a2_hbm, q3_hbm, p3_hbm, a3_hbm, kv_hbm = refs[5:12]
        at = 12
        groups = []
        for unused in range(4):
            groups.append(refs[at : at + n_tp])
            at += n_tp
        tqkvs, tos, cqs, cos = groups
        in_keep, in_give, out_keep, out_give, stream_ref = refs[at : at + 5]
        kv_outs = refs[at + 5 : at + 5 + n_tp]
        (
            w_qkv, w_o, w_q, w_c, qkv_ref, p2_ref, a2_ref, q3_ref, p3_ref, a3_ref, kv_ref,
            grad_attn, d_q, d_k, d_v, total, sems,
        ) = refs[at + 5 + n_tp :]
        moves = Moves(sems)
        c_in = fill_rows(moves, cos, w_c)
        kv_in = moves.start(kv_hbm, kv_ref)
        p3_in = moves.start(p3_hbm, p3_ref)
        q3_in = moves.start(q3_hbm, q3_ref)
        q_in = fill_rows(moves, cqs, w_q)
        o_in = fill_rows(moves, tos, w_o)
        qkv_load = moves.start(qkv_hbm, qkv_ref)
        p2_in = moves.start(p2_hbm, p2_ref)
        a3_in = moves.start(a3_hbm, a3_ref)
        a2_in = moves.start(a2_hbm, a2_ref)
        qkv_in = [
            [
                moves.start(tqkvs[r].at[i], w_qkv.at[i, pl.ds(r * columns, columns), :])
                for r in range(n_tp)
            ]
            for i in range(3)
        ]
        wide = lax.axis_index("wide")
        bit = [lax.rem(wide, 2), lax.rem(lax.div(wide, 2), 2)]

        def split(value, r, mine, keep, give, low):
            first = value[:, r * columns : r * columns + part]
            second = value[:, r * columns + part : (r + 1) * columns]
            keep[:, low : low + part] = jnp.where(mine == 0, first, second)
            give[:, low : low + part] = jnp.where(mine == 0, second, first)

        def into(ref, upto):
            def write(low, high, value):
                ref[0:upto, low:high] = value.astype(BF)

            return write

        grad_y = grad_ref[...].astype(BF)
        for pack in (out_keep, out_give):
            pack[:, width : 2 * width] = grad_y
        for pack in (in_keep, in_give):
            pack[:, 0:width] = h2_ref[...]
            pack[:, width : 2 * width] = h3_ref[...]
        for copy in c_in:
            copy.wait()
        grad_attn[...] = dot_nt(grad_y, w_c[...]).astype(BF)
        for copy in (kv_in, p3_in, q3_in):
            copy.wait()
        attend_back(
            lambda low, high: q3_ref[:, low:high],
            lambda low, high: kv_ref[0, :, low:high],
            lambda low, high: kv_ref[1, :, low:high],
            lambda low, high: grad_attn[:, low:high],
            lambda head: p3_ref[head],
            heads,
            width,
            into(d_q, count),
            into(d_k, keys),
            into(d_v, keys),
        )
        for r in range(n_tp):
            kv_outs[r][0] = d_k[0:keys, r * columns : (r + 1) * columns]
            kv_outs[r][1] = d_v[0:keys, r * columns : (r + 1) * columns]
            split(d_q[...], r, bit[0], in_keep, in_give, 2 * width + r * 4 * part + 3 * part)
        for copy in q_in:
            copy.wait()
        grad_h = dot_nn(d_q[...], w_q[...])
        total[...] = grad_ref[...] + norm_back(grad_h, h3_ref[...].astype(F32), inv3_ref[:, 0:1])

        grad_y = total[...].astype(BF)
        for pack in (out_keep, out_give):
            pack[:, 0:width] = grad_y
        for copy in o_in:
            copy.wait()
        grad_attn[...] = dot_nt(grad_y, w_o[...]).astype(BF)
        for copy in (qkv_load, p2_in):
            copy.wait()
        attend_back(
            lambda low, high: qkv_ref[0, :, low:high],
            lambda low, high: qkv_ref[1, :, low:high],
            lambda low, high: qkv_ref[2, :, low:high],
            lambda low, high: grad_attn[:, low:high],
            lambda head: p2_ref[head],
            heads,
            width,
            into(d_q, count),
            into(d_k, count),
            into(d_v, count),
        )
        for i, ref in enumerate((d_q, d_k, d_v)):
            for r in range(n_tp):
                split(ref[0:count, :], r, bit[0], in_keep, in_give, 2 * width + r * 4 * part + i * part)
            for copy in qkv_in[i]:
                copy.wait()
            term = dot_nn(ref[0:count, :], w_qkv[i])
            grad_h = term if i == 0 else grad_h + term
        stream_ref[...] = (
            total[...] + norm_back(grad_h, h2_ref[...].astype(F32), inv2_ref[:, 0:1])
        ).astype(BF)
        a2_in.wait()
        a3_in.wait()
        for r in range(n_tp):
            split(a2_ref[...], r, bit[1], out_keep, out_give, 2 * width + r * 2 * part)
            split(a3_ref[...], r, bit[1], out_keep, out_give, 2 * width + r * 2 * part + part)

    square = (count, width)
    in_pack = like((count, 2 * width + n_tp * 4 * part))
    out_pack = like((count, 2 * width + n_tp * 2 * part))
    ins = [grad, inv2, inv3, h2, h3, qkv, p2, a2, q3, p3, a3, keyval]
    ins = ins + [*tqkv_list, *to_list, *cq_list, *co_list]
    square_keys = (keys, width)
    return call(
        kernel,
        [in_pack, in_pack, out_pack, out_pack, like(square)] + [like((2, keys, columns))] * n_tp,
        ins,
        [False] * 5 + [True] * (7 + 4 * n_tp),
        [False] * (5 + n_tp),
        [VMEM((3, full, width), BF)]
        + [VMEM((full, width), BF)] * 3
        + [
            VMEM((3,) + square, BF),
            VMEM((heads, count, count), BF),
            VMEM(square, BF),
            VMEM(square, BF),
            VMEM((heads, count, keys), BF),
            VMEM(square, BF),
            VMEM((2,) + square_keys, BF),
            VMEM(square, BF),
            VMEM(square, BF),
            VMEM((max(count, keys), width), BF),
            VMEM((max(count, keys), width), BF),
            VMEM(square, F32),
            pltpu.SemaphoreType.DMA((6 * n_tp + 7,)),
        ],
        2 * count * width * width * 6 + 6 * heads * count * (count + keys) * 256,
    )


def spatial_backward(grad_y_list, probs, qkv, sqkv_rows, w_so, frames_here):
    n_tp = len(grad_y_list)
    rows, width = grad_y_list[0].shape
    columns = w_so.shape[0]
    part = columns // 2
    patch_part = rows // frames_here
    per_frame = n_tp * patch_part
    count = n_tp * rows
    heads = columns // HD

    def kernel(*refs):
        grads = refs[:n_tp]
        probs_hbm, qkv_hbm, wqkv_hbm, so_hbm = refs[n_tp : n_tp + 4]
        keep, give, own_ref = refs[n_tp + 4 : n_tp + 7]
        others = refs[n_tp + 7 : 2 * n_tp + 6]
        w_qkv, w_o, qkv_ref, probs_ref, grad_y, grad_attn, d_all, sems = refs[2 * n_tp + 6 :]
        moves = Moves(sems)
        o_in = moves.start(so_hbm, w_o)
        qkv_in = moves.start(qkv_hbm, qkv_ref)
        probs_in = moves.start(probs_hbm, probs_ref)
        weight_in = moves.start(wqkv_hbm, w_qkv)
        for frame in range(frames_here):
            for r in range(n_tp):
                at = frame * per_frame + r * patch_part
                grad_y[at : at + patch_part, :] = grads[r][
                    frame * patch_part : (frame + 1) * patch_part, :
                ]
        o_in.wait()
        grad_attn[...] = dot_nt(grad_y[...], w_o[...]).astype(BF)
        qkv_in.wait()
        probs_in.wait()
        for frame in range(frames_here):
            at = slice(frame * per_frame, (frame + 1) * per_frame)

            def into(i, at=at):
                def write(low, high, value):
                    d_all[i, at, low:high] = value.astype(BF)

                return write

            attend_back(
                lambda low, high, at=at: qkv_ref[0, at, low:high],
                lambda low, high, at=at: qkv_ref[1, at, low:high],
                lambda low, high, at=at: qkv_ref[2, at, low:high],
                lambda low, high, at=at: grad_attn[at, low:high],
                lambda head, frame=frame: probs_ref[frame * heads + head],
                heads,
                columns,
                into(0),
                into(1),
                into(2),
            )
        mine = lax.rem(lax.axis_index("wide"), 2)
        weight_in.wait()
        for i in range(3):
            value = d_all[i]
            first, second = value[:, :part], value[:, part:]
            keep[:, i * part : (i + 1) * part] = jnp.where(mine == 0, first, second)
            give[:, i * part : (i + 1) * part] = jnp.where(mine == 0, second, first)
        for frame in range(frames_here):
            at = slice(frame * per_frame, (frame + 1) * per_frame)
            grad_h = dot_nn(d_all[0, at, :], w_qkv[0])
            for i in (1, 2):
                grad_h = grad_h + dot_nn(d_all[i, at, :], w_qkv[i])
            here = slice(frame * patch_part, (frame + 1) * patch_part)
            own_ref[here, :] = grad_h[:patch_part]
            for r in range(1, n_tp):
                others[r - 1][here, :] = grad_h[r * patch_part : (r + 1) * patch_part].astype(BF)

    ins = [*grad_y_list, probs, qkv, sqkv_rows, w_so]
    return call(
        kernel,
        [like((count, 3 * part))] * 2 + [like((rows, width), F32)] + [like((rows, width))] * (n_tp - 1),
        ins,
        [False] * n_tp + [True] * 4,
        [False] * (n_tp + 2),
        [
            VMEM((3, columns, width), BF),
            VMEM((columns, width), BF),
            VMEM((3, count, columns), BF),
            VMEM(probs.shape, BF),
            VMEM((count, width), BF),
            VMEM((count, columns), BF),
            VMEM((3, count, columns), BF),
            pltpu.SemaphoreType.DMA((4,)),
        ],
        2 * count * width * columns * 4 + 8 * frames_here * heads * per_frame * per_frame * 256,
    )


def tokens_gradient(tokens_rows, grad, grad_h_own, grad_h_others, mod_here, frames_here):
    rows, width = tokens_rows.shape
    patch_part = rows // frames_here
    others = len(grad_h_others)

    def kernel(*refs):
        token_ref, grad_ref, own_ref = refs[:3]
        mod_ref, out_ref, sum_ref = refs[3 + others :]
        for frame in range(frames_here):
            at = slice(frame * patch_part, (frame + 1) * patch_part)
            grad_h = own_ref[at, :]
            for other in refs[3 : 3 + others]:
                grad_h = grad_h + other[at, :].astype(F32)
            normed, inverse = norm_of(token_ref[at, :].astype(F32))
            sum_ref[frame : frame + 1, 0:width] = jnp.sum(grad_h, axis=0, keepdims=True)
            sum_ref[frame : frame + 1, width:] = jnp.sum(grad_h * normed, axis=0, keepdims=True)
            scale = 1.0 + mod_ref[frame : frame + 1, width : 2 * width]
            out_ref[at, :] = (grad_ref[at, :] + norm_back(grad_h * scale, normed, inverse)).astype(BF)

    ins = [tokens_rows, grad, grad_h_own, *grad_h_others, mod_here]
    return call(
        kernel,
        [like((rows, width)), like((frames_here, 2 * width), F32)],
        ins,
        [False] * len(ins),
        [False] * 2,
        [],
        20 * rows * width,
    )


def flip(operand, mask):
    size = lax.axis_size("wide")
    return lax.ppermute(operand, "wide", [(s, s ^ mask) for s in range(size)])


def tp_from(operand, shift):
    size = lax.axis_size("tp")
    return lax.ppermute(operand, "tp", [(s, (s - shift) % size) for s in range(size)])


def tp_to(operand, shift):
    size = lax.axis_size("tp")
    return lax.ppermute(operand, "tp", [(s, (s + shift) % size) for s in range(size)])


def tp_gather(operand):
    return [operand] + [tp_from(operand, k) for k in range(1, lax.axis_size("tp"))]


def scatter_rows(total, keep, give, second, size):
    block = total.shape[0] // size
    mine = lax.rem(lax.div(lax.axis_index("wide"), 1 << second), 2)
    for deep in range(size // 4):
        for other in range(2):
            parts = []
            for value in range(2):
                y, x = (value, other) if second == 1 else (other, value)
                at = (4 * deep + 2 * y + x) * block
                parts.append(total[at : at + block, :].astype(BF))
            keep[deep, other] = jnp.where(mine == 0, parts[0], parts[1])
            give[deep, other] = jnp.where(mine == 0, parts[1], parts[0])


def pack_products(packs, weights, width, second, size):
    across = sum(cols for unused, unused2, cols in weights)

    def kernel(*refs):
        keep, give, total = refs[len(packs) :]
        low = 0
        for model, slot, cols in weights:
            for i, (unused, k) in enumerate(packs):
                at = slot(k)
                term = dot_tn(refs[i][:, model : model + width], refs[i][:, at : at + cols])
                if i == 0:
                    total[:, low : low + cols] = term
                else:
                    total[:, low : low + cols] += term
            low += cols
        scatter_rows(total, keep, give, second, size)

    block = width // size
    shape = like((size // 4, 2, block, across))
    ins = [array for array, unused in packs]
    return call(
        kernel,
        [shape, shape],
        ins,
        [False] * len(ins),
        [False] * 2,
        [VMEM((width, across), F32)],
        2 * ins[0].shape[0] * len(ins) * width * across,
    )


def spatial_products(model_all, model_got, keep_side, got_side, second, size, frames_here):
    own_list = isinstance(model_all, list)
    own = model_all if own_list else [model_all]
    rows, width = model_got[0].shape
    n_tp = len(model_got)
    count = n_tp * rows
    across = keep_side.shape[1]
    patch_part = rows // frames_here

    def kernel(*refs):
        own_refs, got_refs = refs[: len(own)], refs[len(own) : len(own) + n_tp]
        keep_ref, got_ref, keep, give, model, total = refs[len(own) + n_tp :]

        def gather(parts):
            for frame in range(frames_here):
                for r in range(n_tp):
                    at = (frame * n_tp + r) * patch_part
                    model[at : at + patch_part, :] = parts[r][
                        frame * patch_part : (frame + 1) * patch_part, :
                    ]

        if own_list:
            gather(own_refs)
            total[...] = dot_tn(model[...], keep_ref[...])
        else:
            total[...] = dot_tn(own_refs[0][...], keep_ref[...])
        gather(got_refs)
        total[...] += dot_tn(model[...], got_ref[...])
        scatter_rows(total, keep, give, second, size)

    shape = like((size // 4, 2, width // size, across))
    ins = [*own, *model_got, keep_side, got_side]
    return call(
        kernel,
        [shape, shape],
        ins,
        [False] * len(ins),
        [False] * 2,
        [VMEM((count, width), BF), VMEM((width, across), F32)],
        4 * count * width * across,
    )


def reduce_rest(keep, give, first, layout):
    size = lax.axis_size("wide")
    depth = size // 4
    got = flip(give, 1 << (1 - first))
    unused, pair, block, across = keep.shape

    def split(*refs):
        keep_ref, got_ref, own = refs[:3]
        at = lax.div(lax.axis_index("wide"), 4)
        for k in range(depth):
            place = at ^ k
            value = keep_ref[place].astype(F32) + got_ref[place].astype(F32)
            if k == 0:
                own[...] = value
            else:
                refs[2 + k][...] = value.astype(BF)

    shape = (pair, block, across)
    ins = [keep, got]
    own, *sends = call(
        split, [like(shape, F32)] + [like(shape)] * (depth - 1), ins, [False] * 2, [False] * depth, [], 1000
    )
    parts = [flip(send, 4 * (k + 1)) for k, send in enumerate(sends)]

    def gather(*refs):
        keep_ref, give_ref = refs[depth:]
        mine = lax.rem(lax.div(lax.axis_index("wide"), 1 << first), 2)
        total = refs[0][...]
        for ref in refs[1:depth]:
            total = total + ref[...].astype(F32)
        keep_ref[...] = jnp.where(mine == 0, total[0], total[1])
        give_ref[...] = jnp.where(mine == 0, total[1], total[0]).astype(BF)

    ins = [own, *parts]
    shape = (block, across)
    keep, give = call(gather, [like(shape, F32), like(shape)], ins, [False] * depth, [False] * 2, [], 1000)
    got = flip(give, 1 << first)

    def place(*refs):
        keep_ref, got_ref = refs[:2]
        mine = lax.rem(lax.div(lax.axis_index("wide"), 1 << first), 2)
        own, other = keep_ref[...], got_ref[...].astype(F32)
        sides = [jnp.where(mine == 0, own, other), jnp.where(mine == 0, other, own)]
        low = 0
        for out, (groups, cols) in zip(refs[2:], layout):
            for g in range(groups):
                for side in range(2):
                    value = sides[side][:, low + g * cols : low + (g + 1) * cols]
                    if groups == 1:
                        out[:, side * cols : (side + 1) * cols] = value
                    else:
                        out[g, :, side * cols : (side + 1) * cols] = value
            low += groups * cols

    outs = [
        like((block, 2 * cols) if groups == 1 else (groups, block, 2 * cols), F32)
        for groups, cols in layout
    ]
    ins = [keep, got]
    return call(place, outs, ins, [False] * 2, [False] * len(outs), [], 1000)


def pack_gradients(keep, give, weights, width, first, layout):
    got = flip(give, 1 << first)
    packs = [(keep, 0), (got, 0)]
    for k in range(1, lax.axis_size("tp")):
        packs += [(tp_to(keep, k), k), (tp_to(got, k), k)]
    kept, given = pack_products(packs, weights, width, 1 - first, lax.axis_size("wide"))
    return reduce_rest(kept, given, first, layout)


def tp_sum(parts, dtype=BF):
    total = parts[0].astype(F32)
    for k in range(1, lax.axis_size("tp")):
        total = total + tp_to(parts[k].astype(dtype), k).astype(F32)
    return total


def tp_ordered(relative):
    size = lax.axis_size("tp")
    start = (size - lax.axis_index("tp")) % size
    return lax.dynamic_slice_in_dim(jnp.stack(relative + relative), start, size, axis=0)


def swap_wide(blocks):
    return lax.all_to_all(blocks, "wide", split_axis=0, concat_axis=0, tiled=True)


def on_device(
    tokens,
    cotangent,
    caption,
    caption_len,
    clip_id,
    timestep,
    w_mod,
    b_mod,
    w_text,
    w_sqkv,
    w_so,
    w_tqkv,
    w_to,
    w_cq,
    w_ckv,
    w_co,
    w_fc1,
    w_fc2,
):
    n_tp = lax.axis_size("tp")
    n_wide = lax.axis_size("wide")
    frames_here, patch_part, width = tokens.shape
    columns = w_so.shape[0]
    part = columns // 2
    half = w_fc1.shape[1] // 2
    clip_count = timestep.shape[0]
    frames = clip_id.shape[0]
    patch_here = patch_part // n_wide
    rows = frames_here * patch_part
    block = frames_here * patch_here
    count = frames * patch_here
    wide_at = lax.axis_index("wide")
    tp_at = lax.axis_index("tp")

    tokens_rows = tokens.reshape(rows, width)
    tokens_list = tp_gather(tokens_rows)
    sqkv_rows = w_sqkv.transpose(1, 2, 0)
    tqkv_list = tp_gather(w_tqkv.transpose(1, 2, 0))
    to_list = tp_gather(w_to)
    cq_list = tp_gather(w_cq.T)
    co_list = tp_gather(w_co)
    fc1_list = tp_gather(w_fc1)
    fc2_list = tp_gather(w_fc2)

    half_width = width // 2
    frequencies = jnp.exp(-math.log(10000.0) * jnp.arange(half_width).astype(F32) / half_width)
    angles = timestep.astype(F32)[:, None] * frequencies[None, :]
    embedding = jnp.concatenate([jnp.cos(angles), jnp.sin(angles)], axis=1)
    silu_embed = jax.nn.silu(embedding).astype(BF)
    mod_part = (dot_nn(silu_embed, w_mod) + b_mod.astype(F32)).astype(BF)
    modulation = tp_ordered(tp_gather(mod_part)).transpose(1, 0, 2).reshape(clip_count, -1)
    clip_hot = clip_id[:, None] == jnp.arange(clip_count)[None, :]
    hot_here = lax.dynamic_slice_in_dim(
        clip_hot.astype(F32), wide_at * frames_here, frames_here
    )
    mod_here = dot_nn(hot_here.astype(BF), modulation[:, : 3 * width])
    clip_rows = jnp.repeat(clip_id, patch_here, total_repeat_length=count)
    hot_rows = (clip_rows[:, None] == jnp.arange(clip_count)[None, :]).astype(BF)
    mod_rows = dot_nn(hot_rows, modulation[:, 3 * width :]).astype(BF)

    caption_rows = caption.shape[0]
    block_rows = -(-caption_rows // 16) * 16
    keys = n_wide * block_rows
    padded = jnp.pad(caption, ((0, block_rows - caption_rows), (0, 0)))
    context_part = dot_nt(padded, w_text.T).astype(BF)
    context = tp_ordered(tp_gather(context_part)).transpose(1, 0, 2).reshape(block_rows, width)
    ckv_rows = w_ckv.transpose(1, 2, 0).reshape(2 * columns, width)
    keyval_part = dot_nt(context, ckv_rows).astype(BF)
    keyval = swap_wide(jnp.broadcast_to(keyval_part[None], (n_wide, block_rows, 2 * columns)))
    keyval = keyval.reshape(keys, 2, columns).transpose(1, 0, 2)
    keyval_list = tp_gather(keyval)
    text_cols = caption.shape[1] // n_wide
    context_cols = width // n_wide
    for_owner = jnp.concatenate(
        [
            padded.reshape(block_rows, n_wide, text_cols),
            context.reshape(block_rows, n_wide, context_cols),
        ],
        axis=2,
    ).transpose(1, 0, 2)
    for_owner = swap_wide(for_owner).reshape(keys, text_cols + context_cols)
    caption_cols, context_cols = for_owner[:, :text_cols], for_owner[:, text_cols:]

    patch_rows = jnp.arange(count) % patch_here
    allowed = (clip_rows[:, None] == clip_rows[None, :]) & (patch_rows[:, None] == patch_rows[None, :])
    bias_two = jnp.where(allowed, 0.0, NEGATIVE).astype(F32)
    key_in = jnp.arange(keys) % block_rows
    key_row = (jnp.arange(keys) // block_rows) * caption_rows + key_in
    key_ok = (key_in < caption_rows)[None, :] & (
        (key_row % LTXT)[None, :]
        < jnp.sum(jnp.where(clip_hot, caption_len[None, :], 0), axis=1)[:, None]
    )
    key_ok = key_ok & ((key_row // LTXT)[None, :] == clip_id[:, None])
    bias_three = jnp.where(key_ok, 0.0, NEGATIVE).astype(F32)
    bias_three = jnp.broadcast_to(bias_three[:, None, :], (frames, patch_here, keys)).reshape(count, keys)

    def to_blocks(operand):
        operand = operand.reshape(frames_here, n_wide, patch_here, width)
        return operand.transpose(1, 0, 2, 3).reshape(n_wide, block, width)

    grad_out = swap_wide(to_blocks(cotangent)).reshape(count, width)

    h_all, h_own, qkv_one, probs_one, a_keep, a_give, y_own, *y_others = spatial_forward(
        tokens_list, mod_here, sqkv_rows, w_so, frames_here
    )
    y_others = [tp_to(other, k + 1) for k, other in enumerate(y_others)]
    h_got = tp_gather(flip(h_own, 1))
    a_got = flip(a_give, 2)
    stream, y_one = stream_to_patches(tokens_rows, y_own, y_others, mod_here, frames_here)
    *kept, stream, keyval_full = middle_forward(
        stream.reshape(count, width), bias_two, bias_three, keyval_list, tqkv_list, to_list, cq_list, co_list
    )
    block_out, up_keep, up_give, down_keep, down_give, grad, mod_sum = feed_forward(
        stream, grad_out, mod_rows, hot_rows, fc1_list, fc2_list
    )
    block_out = swap_wide(block_out.reshape(n_wide, block, width))
    block_out = block_out.reshape(n_wide, frames_here, patch_here, width).transpose(1, 0, 2, 3)
    block_out = block_out.reshape(frames_here, patch_part, width)

    fc_slots = [(0, lambda k: width + k * half, half)]
    (grad_fc1,) = pack_gradients(up_keep, up_give, fc_slots, width, 0, [(1, half)])
    (grad_fc2,) = pack_gradients(down_keep, down_give, fc_slots, width, 1, [(1, half)])

    in_keep, in_give, out_keep, out_give, grad, *grad_kv = middle_backward(
        grad, kept, keyval_full, tqkv_list, to_list, cq_list, co_list
    )
    grad_stream, grad_y1, grad_gate = grads_to_frames(
        grad.reshape(n_wide, block, width), y_one, mod_here, frames_here
    )
    grad_y1_list = tp_gather(grad_y1)
    q_keep, q_give, grad_h_own, *grad_h_others = spatial_backward(
        grad_y1_list, probs_one, qkv_one, sqkv_rows, w_so, frames_here
    )
    grad_h_others = [tp_to(other, k + 1) for k, other in enumerate(grad_h_others)]
    grad_tokens, frame_sums = tokens_gradient(
        tokens_rows, grad_stream, grad_h_own, grad_h_others, mod_here, frames_here
    )

    grad_tqkv, grad_cq = pack_gradients(
        in_keep,
        in_give,
        [
            (0, lambda k: 2 * width + k * 4 * part, 3 * part),
            (width, lambda k: 2 * width + k * 4 * part + 3 * part, part),
        ],
        width,
        0,
        [(3, part), (1, part)],
    )
    grad_to, grad_co = pack_gradients(
        out_keep,
        out_give,
        [
            (0, lambda k: 2 * width + k * 2 * part, part),
            (width, lambda k: 2 * width + k * 2 * part + part, part),
        ],
        width,
        1,
        [(1, part), (1, part)],
    )
    kept_so, given_so = spatial_products(
        grad_y1_list, tp_gather(flip(grad_y1, 2)), a_keep, a_got, 0, n_wide, frames_here
    )
    (grad_so,) = reduce_rest(kept_so, given_so, 1, [(1, part)])
    kept_q, given_q = spatial_products(h_all, h_got, q_keep, flip(q_give, 1), 1, n_wide, frames_here)
    (grad_sqkv,) = reduce_rest(kept_q, given_q, 0, [(3, part)])

    grad_kv = tp_sum(grad_kv).astype(BF)
    grad_kv = grad_kv.reshape(2, n_wide, block_rows, columns).transpose(1, 2, 0, 3)
    grad_kv = swap_wide(grad_kv.reshape(n_wide, block_rows, 2 * columns))
    grad_kv = jnp.sum(grad_kv.astype(F32), axis=0).astype(BF)
    grad_kv = swap_wide(jnp.broadcast_to(grad_kv[None], (n_wide, block_rows, 2 * columns)))
    grad_kv = grad_kv.reshape(keys, 2 * columns)
    grad_ckv = dot_tn(context_cols, grad_kv).reshape(-1, 2, columns)
    grad_context = dot_nn(grad_kv, ckv_rows)
    sides = grad_context.reshape(keys, n_tp, width // n_tp)
    relative = [
        lax.dynamic_index_in_dim(sides, (tp_at + k) % n_tp, 1, keepdims=False) for k in range(n_tp)
    ]
    grad_context = tp_sum(relative).astype(BF)
    grad_text = dot_tn(caption_cols, grad_context)

    frame_sums = jnp.concatenate([frame_sums, grad_gate], axis=1)
    here_sum = lax.dot_general(hot_here, frame_sums, (((0,), (0,)), ((), ())), precision=HIGH)
    grad_mod = jnp.concatenate([here_sum, mod_sum], axis=1).reshape(clip_count, n_tp, -1)
    relative = [
        lax.dynamic_index_in_dim(grad_mod, (tp_at + k) % n_tp, 1, keepdims=False) for k in range(n_tp)
    ]
    grad_mod = tp_sum(relative, F32).reshape(clip_count, n_wide, -1).transpose(1, 0, 2)
    grad_mod = jnp.sum(swap_wide(grad_mod), axis=0)
    grad_w_mod = lax.dot_general(
        silu_embed.astype(F32), grad_mod, (((0,), (0,)), ((), ())), precision=HIGH
    )

    return (
        block_out,
        grad_tokens.reshape(tokens.shape),
        grad_w_mod,
        jnp.sum(grad_mod, axis=0),
        grad_text,
        grad_sqkv.transpose(1, 0, 2),
        grad_so.T,
        grad_tqkv.transpose(1, 0, 2),
        grad_to.T,
        grad_cq,
        grad_ckv,
        grad_co.T,
        grad_fc1,
        grad_fc2.T,
    )


def solution(mesh):
    placed = (
        P("wide", "tp", None),
        P("wide", "tp", None),
        P("wide", None),
        P(),
        P(),
        P(),
        P(None, "tp"),
        P("tp"),
        P(None, "tp"),
        P(None, None, "tp"),
        P("tp", None),
        P(None, None, "tp"),
        P("tp", None),
        P(None, "tp"),
        P(None, None, "tp"),
        P("tp", None),
        P(None, "tp"),
        P("tp", None),
    )
    return jax.shard_map(
        on_device,
        mesh=mesh,
        in_specs=placed,
        out_specs=(
            P("wide", "tp", None),
            P("wide", "tp", None),
            P(None, ("tp", "wide")),
            P(("tp", "wide")),
            P("wide", "tp"),
            P("wide", None, "tp"),
            P("tp", "wide"),
            P("wide", None, "tp"),
            P("tp", "wide"),
            P("wide", "tp"),
            P("wide", None, "tp"),
            P("tp", "wide"),
            P("wide", "tp"),
            P("tp", "wide"),
        ),
        check_vma=False,
    )
```

```python
import functools
import math

import jax
import jax.numpy as jnp
import numpy as np
from jax import lax
from jax.experimental import pallas as pl
from jax.experimental.pallas import tpu as pltpu
from jax.sharding import PartitionSpec as P

HD = 72
LTXT = 120
EPS = 1e-06
NEGATIVE = -1e30
HIGH = lax.Precision.HIGHEST
BF = jnp.bfloat16
F32 = jnp.float32
LANES = 128
FACTOR = HD ** (-0.5)
VMEM = pltpu.VMEM
MB = 1 << 20


def dot_nn(left, right):
    return lax.dot_general(left, right, (((1,), (0,)), ((), ())), preferred_element_type=F32)


def dot_nt(left, right):
    return lax.dot_general(left, right, (((1,), (1,)), ((), ())), preferred_element_type=F32)


def dot_tn(left, right):
    return lax.dot_general(left, right, (((0,), (0,)), ((), ())), preferred_element_type=F32)


def norm_of(rows):
    average = jnp.mean(rows, axis=-1, keepdims=True)
    centred = rows - average
    inverse = lax.rsqrt(jnp.mean(centred * centred, axis=-1, keepdims=True) + EPS)
    return centred * inverse, inverse


def norm_back(grad_normed, normed, inverse):
    grad_mean = jnp.mean(grad_normed, axis=-1, keepdims=True)
    grad_cross = jnp.mean(grad_normed * normed, axis=-1, keepdims=True)
    return inverse * (grad_normed - grad_mean - normed * grad_cross)


def window(head, columns):
    low = HD * head
    start = low // LANES * LANES
    stop = min(-(-(low + HD) // LANES) * LANES, columns)
    at = lax.broadcasted_iota(jnp.int32, (1, stop - start), 1) + start
    own = jnp.where((at >= low) & (at < low + HD), 1.0, 0.0).astype(BF)
    return start, stop, own


class Tiles:
    def __init__(self, write, columns, scale=None):
        self.write, self.columns, self.scale, self.open = write, columns, scale, {}

    def add(self, start, stop, value):
        for low in range(start, stop, LANES):
            part = value[:, low - start : min(low + LANES, stop) - start]
            self.open[low] = self.open[low] + part if low in self.open else part

    def flush(self, below):
        for low in sorted(self.open):
            if low + LANES <= below or below >= self.columns:
                part = self.open.pop(low)
                if self.scale is not None:
                    part = part * self.scale
                self.write(low, min(low + LANES, self.columns), part)


def attend(query, key, value, bias, heads, columns, keep_probs, write):
    out = Tiles(write, columns)
    for head in range(heads):
        start, stop, own = window(head, columns)
        scores = dot_nt(query(start, stop) * own, key(start, stop)) * FACTOR
        if bias is not None:
            scores = scores + bias
        scores = jnp.exp(scores - jnp.max(scores, axis=-1, keepdims=True))
        probs = (scores * (1.0 / jnp.sum(scores, axis=-1, keepdims=True))).astype(BF)
        keep_probs(head, probs)
        out.add(start, stop, dot_nn(probs, value(start, stop) * own))
        out.flush(HD * (head + 1))


def attend_back(query, key, value, grad_out, probs_of, heads, columns, write_q, write_k, write_v):
    grad_q = Tiles(write_q, columns, FACTOR)
    grad_k = Tiles(write_k, columns, FACTOR)
    grad_v = Tiles(write_v, columns)
    for head in range(heads):
        start, stop, own = window(head, columns)
        probs = probs_of(head)
        grad_own = grad_out(start, stop) * own
        grad_probs = dot_nt(grad_own, value(start, stop))
        wide_probs = probs.astype(F32)
        grad_scores = wide_probs * grad_probs
        row = jnp.sum(grad_scores, axis=-1, keepdims=True)
        grad_scores = (grad_scores - wide_probs * row).astype(BF)
        grad_q.add(start, stop, dot_nn(grad_scores, key(start, stop) * own))
        grad_k.add(start, stop, dot_tn(grad_scores, query(start, stop) * own))
        grad_v.add(start, stop, dot_tn(probs, grad_own))
        for tiles in (grad_q, grad_k, grad_v):
            tiles.flush(HD * (head + 1))


class Moves:
    def __init__(self, sems):
        self.sems, self.used = sems, 0

    def start(self, source, target):
        copy = pltpu.make_async_copy(source, target, self.sems.at[self.used])
        self.used += 1
        copy.start()
        return copy


def any_spec():
    return pl.BlockSpec(memory_space=pl.ANY)


def vmem_spec():
    return pl.BlockSpec(memory_space=VMEM)


def call(kernel, outs, ins, in_any, out_any, scratch, after=(), limit=56, **params):
    given, extra = len(ins), len(after)

    def ordered(*refs):
        kernel(*refs[:given], *refs[given + extra :])

    return pl.pallas_call(
        ordered,
        out_shape=tuple(outs),
        in_specs=[any_spec() if flag else vmem_spec() for flag in in_any] + [any_spec()] * extra,
        out_specs=tuple(any_spec() if flag else vmem_spec() for flag in out_any),
        scratch_shapes=scratch,
        compiler_params=pltpu.CompilerParams(vmem_limit_bytes=limit * MB, **params),
        cost_estimate=pl.CostEstimate(flops=1, bytes_accessed=1, transcendentals=0),
    )(*ins, *after)


def whole_tiles(columns):
    return -(-columns // LANES) * LANES


def like(shape, dtype=BF):
    return jax.ShapeDtypeStruct(shape, dtype)


def greet():
    barrier = pltpu.get_barrier_semaphore()
    size = lax.axis_size("wide")
    me = lax.axis_index("wide")

    def signal(k, carry):
        pl.semaphore_signal(
            barrier,
            inc=1,
            device_id={"wide": lax.rem(me + k, size)},
            device_id_type=pl.DeviceIdType.MESH,
        )
        return carry

    lax.fori_loop(1, size, signal, 0)
    pl.semaphore_wait(barrier, size - 1)


class Swap:
    def __init__(self, send, recv, send_sem, recv_sem, shared=False):
        self.send, self.recv, self.shared = send, recv, shared
        self.send_sem, self.recv_sem = send_sem, recv_sem

    def source(self, at):
        return self.send if self.shared else self.send.at[at]

    def copy(self, k, source, target, peer):
        return pltpu.make_async_remote_copy(
            src_ref=self.source(source),
            dst_ref=self.recv.at[target],
            send_sem=self.send_sem.at[k],
            recv_sem=self.recv_sem.at[k],
            device_id={"wide": peer},
            device_id_type=pl.DeviceIdType.MESH,
        )

    def start(self):
        size, me = lax.axis_size("wide"), lax.axis_index("wide")

        def step(k, carry):
            peer = lax.rem(me + k, size)
            self.copy(k, peer, me, peer).start()
            return carry

        lax.fori_loop(1, size, step, 0)
        self.recv[me] = self.send[...] if self.shared else self.send[me]

    def finish(self):
        size, me = lax.axis_size("wide"), lax.axis_index("wide")

        def arrive(k, carry):
            peer = lax.rem(me + size - k, size)
            self.copy(k, peer, peer, peer).wait_recv()
            return carry

        def leave(k, carry):
            peer = lax.rem(me + k, size)
            self.copy(k, peer, me, peer).wait_send()
            return carry

        lax.fori_loop(1, size, arrive, 0)
        lax.fori_loop(1, size, leave, 0)


def wide_bits():
    return lax.axis_size("wide").bit_length() - 1


def mirrored(at):
    bits = wide_bits()
    return sum(((at >> bit) & 1) << (bits - 1 - bit) for bit in range(bits))


def bit_of(bit):
    return lax.rem(lax.div(lax.axis_index("wide"), 1 << bit), 2)


def partner(bit):
    return lax.axis_index("wide") + (1 - 2 * bit_of(bit)) * (1 << bit)


def greet_devices(places):
    barrier = pltpu.get_barrier_semaphore()
    for place in places:
        pl.semaphore_signal(barrier, inc=1, device_id=place, device_id_type=pl.DeviceIdType.MESH)
    pl.semaphore_wait(barrier, len(places))


def pair_places():
    return [{"wide": partner(bit)} for bit in range(wide_bits())]


def core_places():
    size, me = lax.axis_size("tp"), lax.axis_index("tp")
    return [{"tp": lax.rem(me + k, size)} for k in range(1, size)]


class Doubling:
    def __init__(self, levels, send_sem, recv_sem):
        self.levels, self.send_sem, self.recv_sem = levels, send_sem, recv_sem
        self.bit = wide_bits()
        self.copy = None

    def start(self):
        self.send()

    def send(self):
        bit = self.bit - 1
        have = self.levels[self.bit]
        half = have.shape[0]
        mine = bit_of(bit)
        there = self.levels[bit].at[pl.ds(mine * half, half)]
        self.copy = pltpu.make_async_remote_copy(
            src_ref=have,
            dst_ref=there,
            send_sem=self.send_sem.at[bit],
            recv_sem=self.recv_sem.at[bit],
            device_id={"wide": partner(bit)},
            device_id_type=pl.DeviceIdType.MESH,
        )
        self.copy.start()
        self.levels[bit][pl.ds(mine * half, half)] = have[...]

    def advance(self):
        if self.bit == 0:
            return
        self.copy.wait()
        self.bit -= 1
        if self.bit:
            self.send()

    def finish(self, out):
        while self.bit:
            self.advance()
        for at in range(self.levels[0].shape[0]):
            out[at] = self.levels[0][mirrored(at)]


class Halving:
    def __init__(self, levels, landing, send_sem, recv_sem):
        self.levels, self.landing = levels, landing
        self.send_sem, self.recv_sem = send_sem, recv_sem
        self.bit = 0

    def start(self):
        self.send()

    def send(self):
        bit = self.bit
        half = self.landing[bit].shape[0]
        other = 1 - bit_of(bit)
        self.copy = pltpu.make_async_remote_copy(
            src_ref=self.levels[bit].at[pl.ds(other * half, half)],
            dst_ref=self.landing[bit],
            send_sem=self.send_sem.at[bit],
            recv_sem=self.recv_sem.at[bit],
            device_id={"wide": partner(bit)},
            device_id_type=pl.DeviceIdType.MESH,
        )
        self.copy.start()

    def advance(self):
        bit = self.bit
        if bit == wide_bits():
            return
        half = self.landing[bit].shape[0]
        self.copy.wait()
        own = self.levels[bit][pl.ds(bit_of(bit) * half, half)]
        self.levels[bit + 1][...] = (own.astype(F32) + self.landing[bit][...].astype(F32)).astype(BF)
        self.bit += 1
        if self.bit < wide_bits():
            self.send()

    def finish(self, out):
        while self.bit < wide_bits():
            self.advance()
        out[...] = self.levels[-1][0]


def level_scratch(size, block):
    bits = size.bit_length() - 1
    return [VMEM((size >> s,) + block, BF) for s in range(bits + 1)]


def swap_sems(size, count):
    return [pltpu.SemaphoreType.DMA((size,))] * (2 * count)


def spatial_forward(tokens_list, mod_here, sqkv_rows, w_so, frames_here, grad_blocks, keyval_part, texts):
    n_tp = len(tokens_list)
    rows, width = tokens_list[0].shape
    columns = w_so.shape[0]
    patch_part = rows // frames_here
    per_frame = n_tp * patch_part
    count = n_tp * rows
    heads = columns // HD
    size = grad_blocks.shape[0]
    bits = size.bit_length() - 1

    def kernel(*refs):
        token_refs = refs[:n_tp]
        mod_ref, qkv_hbm, so_hbm, grad_ref, kv_ref, text_ref = refs[n_tp : n_tp + 6]
        at = n_tp + 6
        h_ref, h_own, qkv_out, probs_out, a_keep, a_give, y_ref = refs[at : at + 7]
        y_others = refs[at + 7 : at + 6 + n_tp]
        at += 6 + n_tp
        grad_out, kv_out, text_out = refs[at : at + 3]
        weight_qkv, weight_o, qkv_ref, probs_ref, attn_ref, sems, *swap = refs[at + 3 :]
        grad_got, text_got, *swap = swap
        levels, swap = swap[: bits + 1], swap[bits + 1 :]
        greet()
        swaps = [
            Swap(grad_ref, grad_got, swap[0], swap[1]),
            Swap(text_ref, text_got, swap[2], swap[3]),
        ]
        share = Doubling(levels, swap[4], swap[5])
        levels[bits][0] = kv_ref[...]
        share.start()
        for exchange in swaps:
            exchange.start()
        moves = Moves(sems)
        weights = [moves.start(qkv_hbm.at[i], weight_qkv.at[i]) for i in range(3)]
        weight_out = moves.start(so_hbm, weight_o)
        for frame in range(frames_here):
            shift = mod_ref[frame : frame + 1, 0:width]
            scale = 1.0 + mod_ref[frame : frame + 1, width : 2 * width]
            for r in range(n_tp):
                part = token_refs[r][frame * patch_part : (frame + 1) * patch_part, :]
                normed, unused = norm_of(part.astype(F32))
                at = frame * per_frame + r * patch_part
                value = (normed * scale + shift).astype(BF)
                h_ref[at : at + patch_part, :] = value
                if r == 0:
                    h_own[frame * patch_part : (frame + 1) * patch_part, :] = value
        outgoing = []
        for i in range(3):
            weights[i].wait()
            qkv_ref[i] = dot_nt(h_ref[...], weight_qkv[i]).astype(BF)
        share.advance()
        outgoing.append(moves.start(qkv_ref, qkv_out))
        for frame in range(frames_here):
            at = slice(frame * per_frame, (frame + 1) * per_frame)

            def keep_probs(head, probs, frame=frame):
                probs_ref[frame * heads + head] = probs

            def write(low, high, part, at=at):
                attn_ref[at, low:high] = part.astype(BF)

            attend(
                lambda low, high, at=at: qkv_ref[0, at, low:high],
                lambda low, high, at=at: qkv_ref[1, at, low:high],
                lambda low, high, at=at: qkv_ref[2, at, low:high],
                None,
                heads,
                columns,
                keep_probs,
                write,
            )
            share.advance()
        outgoing.append(moves.start(probs_ref, probs_out))
        mine = lax.rem(lax.div(lax.axis_index("wide"), 2), 2)
        first, second = attn_ref[:, : columns // 2], attn_ref[:, columns // 2 :]
        a_keep[...] = jnp.where(mine == 0, first, second)
        a_give[...] = jnp.where(mine == 0, second, first)
        weight_out.wait()
        for frame in range(frames_here):
            at = frame * per_frame
            branch = dot_nn(attn_ref[at : at + per_frame, :], weight_o[...])
            here = slice(frame * patch_part, (frame + 1) * patch_part)
            y_ref[here, :] = branch[:patch_part]
            for r in range(1, n_tp):
                y_others[r - 1][here, :] = branch[r * patch_part : (r + 1) * patch_part].astype(BF)
        for copy in outgoing:
            copy.wait()
        share.finish(kv_out)
        for exchange, out in zip(swaps, (grad_out, text_out)):
            exchange.finish()
            out[...] = exchange.recv[...]

    outs = [
        like((count, width)),
        like((rows, width)),
        like((3, count, columns)),
        like((frames_here * heads, per_frame, per_frame)),
        like((count, columns // 2)),
        like((count, columns // 2)),
        like((rows, width), F32),
    ] + [like((rows, width))] * (n_tp - 1)
    landed = [grad_blocks.shape, (size,) + keyval_part.shape, texts.shape]
    outs += [like(shape) for shape in landed]
    ins = list(tokens_list) + [mod_here, sqkv_rows, w_so, grad_blocks, keyval_part, texts]
    return call(
        kernel,
        outs,
        ins,
        [False] * (n_tp + 1) + [True, True] + [False] * 3,
        [False, False, True, True] + [False] * (n_tp + 5),
        [
            VMEM((3, columns, width), BF),
            VMEM((columns, width), BF),
            VMEM((3, count, columns), BF),
            VMEM((frames_here * heads, per_frame, per_frame), BF),
            VMEM((count, columns), BF),
            pltpu.SemaphoreType.DMA((6,)),
        ]
        + [VMEM(grad_blocks.shape, BF), VMEM(texts.shape, BF)]
        + level_scratch(size, keyval_part.shape)
        + swap_sems(size, 3),
        collective_id=1,
        has_side_effects=True,
    )


def stream_to_patches(tokens_rows, y_own, y_others, mod_here, frames_here):
    size = lax.axis_size("wide")
    rows, width = tokens_rows.shape
    patch_part = rows // frames_here
    patch_here = patch_part // size
    block = frames_here * patch_here
    others = len(y_others)

    def kernel(*refs):
        token_ref, y_ref, mod_ref = refs[0], refs[1], refs[2 + others]
        out_ref, total_ref = refs[3 + others : 5 + others]
        send, recv, send_sem, recv_sem = refs[5 + others :]
        greet()
        for frame in range(frames_here):
            at = slice(frame * patch_part, (frame + 1) * patch_part)
            branch = y_ref[at, :]
            for other in refs[2 : 2 + others]:
                branch = branch + other[at, :].astype(F32)
            total_ref[at, :] = branch
            gate = mod_ref[frame : frame + 1, 2 * width : 3 * width]
            stream = token_ref[at, :].astype(F32) + gate * branch
            for owner in range(size):
                send[owner, frame * patch_here : (frame + 1) * patch_here, :] = stream[
                    owner * patch_here : (owner + 1) * patch_here
                ].astype(BF)
        exchange = Swap(send, recv, send_sem, recv_sem)
        exchange.start()
        exchange.finish()
        out_ref[...] = recv[...]

    ins = [tokens_rows, y_own] + list(y_others) + [mod_here]
    return call(
        kernel,
        [like((size, block, width)), like((rows, width), F32)],
        ins,
        [False] * len(ins),
        [False, False],
        [VMEM((size, block, width), BF)] * 2 + swap_sems(size, 1),
        collective_id=2,
        has_side_effects=True,
    )


def grads_to_frames(grad_blocks, y_one, mod_here, frames_here, after):
    size, block, width = grad_blocks.shape
    rows = y_one.shape[0]
    patch_part = rows // frames_here
    patch_here = patch_part // size

    def kernel(grad_ref, y_ref, mod_ref, stream_ref, branch_ref, gate_ref, recv, send_sem, recv_sem):
        greet()
        exchange = Swap(grad_ref, recv, send_sem, recv_sem)
        exchange.start()
        exchange.finish()
        for owner in range(size):
            part = recv[owner].astype(F32)
            for frame in range(frames_here):
                at = frame * patch_part + owner * patch_here
                stream_ref[at : at + patch_here, :] = part[
                    frame * patch_here : (frame + 1) * patch_here
                ]
        for frame in range(frames_here):
            at = slice(frame * patch_part, (frame + 1) * patch_part)
            stream = stream_ref[at, :]
            gate_ref[frame : frame + 1, :] = jnp.sum(stream * y_ref[at, :], axis=0, keepdims=True)
            branch_ref[at, :] = (stream * mod_ref[frame : frame + 1, 2 * width : 3 * width]).astype(BF)

    ins = [grad_blocks, y_one, mod_here]
    return call(
        kernel,
        [like((rows, width), F32), like((rows, width)), like((frames_here, width), F32)],
        ins,
        [False] * 3,
        [False] * 3,
        [VMEM((size, block, width), BF)] + swap_sems(size, 1),
        after,
        collective_id=3,
        has_side_effects=True,
    )


def fill_rows(moves, sources, target):
    step = sources[0].shape[0]
    return [moves.start(ref, target.at[pl.ds(r * step, step), :]) for r, ref in enumerate(sources)]


def middle_forward(stream, row_codes, key_codes, keyval_list, tqkv_list, to_list, cq_list, co_list):
    n_tp = len(tqkv_list)
    count, width = stream.shape
    keys = keyval_list[0].shape[0]
    columns = to_list[0].shape[0]
    heads = width // HD

    def kernel(*refs):
        stream_ref, row_ref, key_ref = refs[:3]
        at = 3
        groups = []
        for unused in range(5):
            groups.append(refs[at : at + n_tp])
            at += n_tp
        keyvals, tqkvs, tos, cqs, cos = groups
        h2_out, qkv_out, p2_out, a2_out, inv2_ref, h3_out, q3_out, p3_out, a3_out, inv3_ref, x_ref, kv_ref = refs[at : at + 12]
        w_qkv, w_o, w_q, w_c, h2, qkv, p2, a2, h3, q3, p3, a3, sems = refs[at + 12 :]
        moves = Moves(sems)
        qkv_in = [
            [
                moves.start(tqkvs[r].at[i], w_qkv.at[i, pl.ds(r * columns, columns), :])
                for r in range(n_tp)
            ]
            for i in range(3)
        ]
        o_in = fill_rows(moves, tos, w_o)
        q_in = fill_rows(moves, cqs, w_q)
        c_in = fill_rows(moves, cos, w_c)
        outgoing = []
        for i in range(2):
            for r in range(n_tp):
                kv_ref[i, :, r * columns : (r + 1) * columns] = keyvals[r][
                    :, i * columns : (i + 1) * columns
                ]
        stream_one = stream_ref[...].astype(F32)
        normed, inverse = norm_of(stream_one)
        inv2_ref[...] = jnp.broadcast_to(inverse, inv2_ref.shape)
        h2[...] = normed.astype(BF)
        outgoing.append(moves.start(h2, h2_out))
        for i in range(3):
            for copy in qkv_in[i]:
                copy.wait()
            qkv[i] = dot_nt(h2[...], w_qkv[i]).astype(BF)
        outgoing.append(moves.start(qkv, qkv_out))

        def keep_two(head, probs):
            p2[head] = probs

        def write_two(low, high, part):
            a2[:, low:high] = part.astype(BF)

        attend(
            lambda low, high: qkv[0, :, low:high],
            lambda low, high: qkv[1, :, low:high],
            lambda low, high: qkv[2, :, low:high],
            jnp.where(row_ref[:, 0:1] == key_ref[0:1, 0:count], 0.0, NEGATIVE),
            heads,
            width,
            keep_two,
            write_two,
        )
        outgoing.append(moves.start(p2, p2_out))
        outgoing.append(moves.start(a2, a2_out))
        for copy in o_in:
            copy.wait()
        x_ref[...] = stream_one + dot_nn(a2[...], w_o[...])
        normed, inverse = norm_of(x_ref[...])
        inv3_ref[...] = jnp.broadcast_to(inverse, inv3_ref.shape)
        h3[...] = normed.astype(BF)
        outgoing.append(moves.start(h3, h3_out))
        for copy in q_in:
            copy.wait()
        q3[...] = dot_nt(h3[...], w_q[...]).astype(BF)
        outgoing.append(moves.start(q3, q3_out))

        def keep_three(head, probs):
            p3[head] = probs

        def write_three(low, high, part):
            a3[:, low:high] = part.astype(BF)

        attend(
            lambda low, high: q3[:, low:high],
            lambda low, high: kv_ref[0, :, low:high],
            lambda low, high: kv_ref[1, :, low:high],
            jnp.where(row_ref[:, 1:2] == key_ref[1:2, 0:keys], 0.0, NEGATIVE),
            heads,
            width,
            keep_three,
            write_three,
        )
        outgoing.append(moves.start(p3, p3_out))
        outgoing.append(moves.start(a3, a3_out))
        for copy in c_in:
            copy.wait()
        x_ref[...] = x_ref[...] + dot_nn(a3[...], w_c[...])
        for copy in outgoing:
            copy.wait()

    square = (count, width)
    outs = [
        like(square),
        like((3,) + square),
        like((heads, count, count)),
        like(square),
        like((count, LANES), F32),
        like(square),
        like(square),
        like((heads, count, keys)),
        like(square),
        like((count, LANES), F32),
        like(square, F32),
        like((2, keys, width)),
    ]
    kept = [square, (3,) + square, (heads, count, count), square, square, square, (heads, count, keys), square]
    ins = [stream, row_codes, key_codes, *keyval_list, *tqkv_list, *to_list, *cq_list, *co_list]
    full = n_tp * columns
    return call(
        kernel,
        outs,
        ins,
        [False] * (3 + n_tp) + [True] * (4 * n_tp),
        [True, True, True, True, False, True, True, True, True, False, False, False],
        [VMEM((3, full, width), BF)]
        + [VMEM((full, width), BF)] * 3
        + [VMEM(shape, BF) for shape in kept]
        + [pltpu.SemaphoreType.DMA((6 * n_tp + 8,))],
    )


def feed_forward(stream, grad_out, mod_rows, hot_rows, fc1_list, fc2_list, firsts):
    n_tp = len(fc1_list)
    count, width = stream.shape
    hidden = fc1_list[0].shape[1]
    half = hidden // 2
    slot = whole_tiles(half)
    clips = hot_rows.shape[1]

    def kernel(*refs):
        stream_ref, grad_ref, mod_ref, hot_ref = refs[:4]
        fc1s, fc2s = refs[4 : 4 + n_tp], refs[4 + n_tp : 4 + 2 * n_tp]
        at = 4 + 2 * n_tp
        out_ref, up_keep, up_give, down_keep, down_give, g_ref, mod_sum = refs[at : at + 7]
        w1, w2, normed_ref, total_y, total_h, sems = refs[at + 7 :]
        moves = Moves(sems)
        loads = []
        pieces = 2 if half % LANES == 0 else 1
        for r in range(n_tp):
            for piece in range(pieces):
                cols = pl.ds(piece * (hidden // pieces), hidden // pieces)
                loads.append(
                    (
                        moves.start(fc1s[r].at[:, cols], w1.at[r, :, cols]),
                        moves.start(fc2s[r].at[cols, :], w2.at[r, cols, :]),
                    )
                )
        bit = [bit_of(first) for first in firsts]
        shift = mod_ref[:, 0:width].astype(F32)
        scale = 1.0 + mod_ref[:, width : 2 * width].astype(F32)
        gate = mod_ref[:, 2 * width :].astype(F32)
        normed, inverse = norm_of(stream_ref[...])
        normed_ref[...] = normed
        h_four = (normed * scale + shift).astype(BF)
        grad_y = (gate * grad_ref[...].astype(F32)).astype(BF)
        for pack in (up_keep, up_give):
            pack[:, 0:width] = h_four
        for pack in (down_keep, down_give):
            pack[:, 0:width] = grad_y
        for pack in (up_keep, up_give, down_keep, down_give):
            for r in range(n_tp if slot > half else 0):
                at = width + r * slot
                pack[:, at + half : at + slot] = jnp.zeros((count, slot - half), BF)
        for r in range(n_tp):
            for part in range(2):
                at_chunk = 2 * r + part
                if at_chunk % (2 // pieces) == 0:
                    for copy in loads[at_chunk // (2 // pieces)]:
                        copy.wait()
                hid = slice(part * half, (part + 1) * half)
                upper = dot_nn(up_keep[:, 0:width], w1[r, :, hid])
                square = upper * upper
                tanh = jnp.tanh(upper * (0.7978845608028654 + 0.035677408136300125 * square))
                rise = 0.5 + 0.5 * tanh
                active = (upper * rise).astype(BF)
                slope = rise + (0.5 * upper) * (1.0 - tanh * tanh) * (
                    0.7978845608028654 + 0.10703222440890037 * square
                )
                grad_upper = (dot_nt(down_keep[:, 0:width], w2[r, hid, :]) * slope).astype(BF)
                cols = slice(width + r * slot, width + r * slot + half)
                for keep, give, mine, value in (
                    (up_keep, up_give, bit[0], grad_upper),
                    (down_keep, down_give, bit[1], active),
                ):

                    @pl.when(mine == part)
                    def _():
                        keep[:, cols] = value

                    @pl.when(mine != part)
                    def _():
                        give[:, cols] = value

                y_term = dot_nn(active, w2[r, hid, :])
                h_term = dot_nt(grad_upper, w1[r, :, hid])
                if at_chunk == 0:
                    total_y[...] = y_term
                    total_h[...] = h_term
                else:
                    total_y[...] += y_term
                    total_h[...] += h_term
        gate = mod_ref[:, 2 * width :].astype(F32)
        out_ref[...] = (stream_ref[...] + gate * total_y[...]).astype(BF)
        grad = grad_ref[...].astype(F32)
        hot = hot_ref[...]
        mod_sum[:, 2 * width :] = dot_tn(hot, (grad * total_y[...]).astype(BF))
        grad_h = total_h[...]
        mod_sum[:, 0:width] = dot_tn(hot, grad_h.astype(BF))
        normed = normed_ref[...]
        mod_sum[:, width : 2 * width] = dot_tn(hot, (grad_h * normed).astype(BF))
        scale = 1.0 + mod_ref[:, width : 2 * width].astype(F32)
        unused, inverse = norm_of(stream_ref[...])
        g_ref[...] = grad + norm_back(grad_h * scale, normed, inverse)

    pack = like((count, width + n_tp * slot))
    ins = [stream, grad_out, mod_rows, hot_rows, *fc1_list, *fc2_list]
    return call(
        kernel,
        [like((count, width)), pack, pack, pack, pack, like((count, width), F32), like((clips, 3 * width), F32)],
        ins,
        [False] * 4 + [True] * (2 * n_tp),
        [False] * 7,
        [
            VMEM((n_tp, width, hidden), BF),
            VMEM((n_tp, hidden, width), BF),
            VMEM((count, width), F32),
            VMEM((count, width), F32),
            VMEM((count, width), F32),
            pltpu.SemaphoreType.DMA((4 * n_tp,)),
        ],
    )


def middle_backward(grad, kept, keyval, tqkv_list, to_list, cq_list, co_list, firsts):
    n_tp = len(tqkv_list)
    h2, qkv, p2, a2, inv2, h3, q3, p3, a3, inv3 = kept
    count, width = grad.shape
    keys = keyval.shape[1]
    columns = to_list[0].shape[0]
    part = columns // 2
    heads = width // HD
    full = n_tp * columns
    in_slot, out_slot = whole_tiles(4 * part), whole_tiles(2 * part)

    def kernel(*refs):
        grad_ref, inv2_ref, inv3_ref, h2_ref, h3_ref = refs[:5]
        qkv_hbm, p2_hbm, a2_hbm, q3_hbm, p3_hbm, a3_hbm, kv_hbm = refs[5:12]
        at = 12
        groups = []
        for unused in range(4):
            groups.append(refs[at : at + n_tp])
            at += n_tp
        tqkvs, tos, cqs, cos = groups
        in_keep, in_give, out_keep, out_give, stream_ref = refs[at : at + 5]
        kv_outs = refs[at + 5 : at + 5 + n_tp]
        (
            w_qkv, w_o, w_q, w_c, qkv_ref, p2_ref, a2_ref, q3_ref, p3_ref, a3_ref, kv_ref,
            grad_attn, d_q, d_k, d_v, total, sems,
        ) = refs[at + 5 + n_tp :]
        moves = Moves(sems)
        c_in = fill_rows(moves, cos, w_c)
        kv_in = moves.start(kv_hbm, kv_ref)
        p3_in = moves.start(p3_hbm, p3_ref)
        q3_in = moves.start(q3_hbm, q3_ref)
        q_in = fill_rows(moves, cqs, w_q)
        o_in = fill_rows(moves, tos, w_o)
        qkv_load = moves.start(qkv_hbm, qkv_ref)
        p2_in = moves.start(p2_hbm, p2_ref)
        a3_in = moves.start(a3_hbm, a3_ref)
        a2_in = moves.start(a2_hbm, a2_ref)
        qkv_in = [
            [
                moves.start(tqkvs[r].at[i], w_qkv.at[i, pl.ds(r * columns, columns), :])
                for r in range(n_tp)
            ]
            for i in range(3)
        ]
        bit = [bit_of(first) for first in firsts]

        def split(value, r, mine, keep, give, low):
            first = value[:, r * columns : r * columns + part]
            second = value[:, r * columns + part : (r + 1) * columns]
            keep[:, low : low + part] = jnp.where(mine == 0, first, second)
            give[:, low : low + part] = jnp.where(mine == 0, second, first)

        def into(ref, upto):
            def write(low, high, value):
                ref[0:upto, low:high] = value.astype(BF)

            return write

        for packs, used, slot in (((in_keep, in_give), 4 * part, in_slot), ((out_keep, out_give), 2 * part, out_slot)):
            for pack in packs:
                for r in range(n_tp if slot > used else 0):
                    at = 2 * width + r * slot
                    pack[:, at + used : at + slot] = jnp.zeros((count, slot - used), BF)
        grad_y = grad_ref[...].astype(BF)
        for pack in (out_keep, out_give):
            pack[:, width : 2 * width] = grad_y
        for pack in (in_keep, in_give):
            pack[:, 0:width] = h2_ref[...]
            pack[:, width : 2 * width] = h3_ref[...]
        for copy in c_in:
            copy.wait()
        grad_attn[...] = dot_nt(grad_y, w_c[...]).astype(BF)
        for copy in (kv_in, p3_in, q3_in):
            copy.wait()
        attend_back(
            lambda low, high: q3_ref[:, low:high],
            lambda low, high: kv_ref[0, :, low:high],
            lambda low, high: kv_ref[1, :, low:high],
            lambda low, high: grad_attn[:, low:high],
            lambda head: p3_ref[head],
            heads,
            width,
            into(d_q, count),
            into(d_k, keys),
            into(d_v, keys),
        )
        for r in range(n_tp):
            kv_outs[r][:, 0:columns] = d_k[0:keys, r * columns : (r + 1) * columns]
            kv_outs[r][:, columns:] = d_v[0:keys, r * columns : (r + 1) * columns]
            split(d_q[...], r, bit[0], in_keep, in_give, 2 * width + r * in_slot + 3 * part)
        for copy in q_in:
            copy.wait()
        grad_h = dot_nn(d_q[...], w_q[...])
        total[...] = grad_ref[...] + norm_back(grad_h, h3_ref[...].astype(F32), inv3_ref[:, 0:1])

        grad_y = total[...].astype(BF)
        for pack in (out_keep, out_give):
            pack[:, 0:width] = grad_y
        for copy in o_in:
            copy.wait()
        grad_attn[...] = dot_nt(grad_y, w_o[...]).astype(BF)
        for copy in (qkv_load, p2_in):
            copy.wait()
        attend_back(
            lambda low, high: qkv_ref[0, :, low:high],
            lambda low, high: qkv_ref[1, :, low:high],
            lambda low, high: qkv_ref[2, :, low:high],
            lambda low, high: grad_attn[:, low:high],
            lambda head: p2_ref[head],
            heads,
            width,
            into(d_q, count),
            into(d_k, count),
            into(d_v, count),
        )
        for i, ref in enumerate((d_q, d_k, d_v)):
            for r in range(n_tp):
                split(ref[0:count, :], r, bit[0], in_keep, in_give, 2 * width + r * in_slot + i * part)
            for copy in qkv_in[i]:
                copy.wait()
            term = dot_nn(ref[0:count, :], w_qkv[i])
            grad_h = term if i == 0 else grad_h + term
        stream_ref[...] = (
            total[...] + norm_back(grad_h, h2_ref[...].astype(F32), inv2_ref[:, 0:1])
        ).astype(BF)
        a2_in.wait()
        a3_in.wait()
        for r in range(n_tp):
            split(a2_ref[...], r, bit[1], out_keep, out_give, 2 * width + r * out_slot)
            split(a3_ref[...], r, bit[1], out_keep, out_give, 2 * width + r * out_slot + part)

    square = (count, width)
    in_pack = like((count, 2 * width + n_tp * in_slot))
    out_pack = like((count, 2 * width + n_tp * out_slot))
    ins = [grad, inv2, inv3, h2, h3, qkv, p2, a2, q3, p3, a3, keyval]
    ins = ins + [*tqkv_list, *to_list, *cq_list, *co_list]
    square_keys = (keys, width)
    return call(
        kernel,
        [in_pack, in_pack, out_pack, out_pack, like(square)] + [like((keys, 2 * columns))] * n_tp,
        ins,
        [False] * 5 + [True] * (7 + 4 * n_tp),
        [False] * (5 + n_tp),
        [VMEM((3, full, width), BF)]
        + [VMEM((full, width), BF)] * 3
        + [
            VMEM((3,) + square, BF),
            VMEM((heads, count, count), BF),
            VMEM(square, BF),
            VMEM(square, BF),
            VMEM((heads, count, keys), BF),
            VMEM(square, BF),
            VMEM((2,) + square_keys, BF),
            VMEM(square, BF),
            VMEM(square, BF),
            VMEM((max(count, keys), width), BF),
            VMEM((max(count, keys), width), BF),
            VMEM(square, F32),
            pltpu.SemaphoreType.DMA((6 * n_tp + 7,)),
        ],
    )


def spatial_backward(grad_y_list, probs, qkv, sqkv_rows, w_so, frames_here, after):
    n_tp = len(grad_y_list)
    rows, width = grad_y_list[0].shape
    columns = w_so.shape[0]
    part = columns // 2
    patch_part = rows // frames_here
    per_frame = n_tp * patch_part
    count = n_tp * rows
    heads = columns // HD

    def kernel(*refs):
        grads = refs[:n_tp]
        probs_hbm, qkv_hbm, wqkv_hbm, so_hbm = refs[n_tp : n_tp + 4]
        keep, give, own_ref = refs[n_tp + 4 : n_tp + 7]
        others = refs[n_tp + 7 : 2 * n_tp + 6]
        w_qkv, w_o, qkv_ref, probs_ref, grad_y, grad_attn, d_all, sems = refs[2 * n_tp + 6 :]
        moves = Moves(sems)
        o_in = moves.start(so_hbm, w_o)
        qkv_in = moves.start(qkv_hbm, qkv_ref)
        probs_in = moves.start(probs_hbm, probs_ref)
        weight_in = moves.start(wqkv_hbm, w_qkv)
        for frame in range(frames_here):
            for r in range(n_tp):
                at = frame * per_frame + r * patch_part
                grad_y[at : at + patch_part, :] = grads[r][
                    frame * patch_part : (frame + 1) * patch_part, :
                ]
        o_in.wait()
        grad_attn[...] = dot_nt(grad_y[...], w_o[...]).astype(BF)
        qkv_in.wait()
        probs_in.wait()
        for frame in range(frames_here):
            at = slice(frame * per_frame, (frame + 1) * per_frame)

            def into(i, at=at):
                def write(low, high, value):
                    d_all[i, at, low:high] = value.astype(BF)

                return write

            attend_back(
                lambda low, high, at=at: qkv_ref[0, at, low:high],
                lambda low, high, at=at: qkv_ref[1, at, low:high],
                lambda low, high, at=at: qkv_ref[2, at, low:high],
                lambda low, high, at=at: grad_attn[at, low:high],
                lambda head, frame=frame: probs_ref[frame * heads + head],
                heads,
                columns,
                into(0),
                into(1),
                into(2),
            )
        mine = lax.rem(lax.axis_index("wide"), 2)
        weight_in.wait()
        for i in range(3):
            value = d_all[i]
            first, second = value[:, :part], value[:, part:]
            keep[:, i * part : (i + 1) * part] = jnp.where(mine == 0, first, second)
            give[:, i * part : (i + 1) * part] = jnp.where(mine == 0, second, first)
        for frame in range(frames_here):
            at = slice(frame * per_frame, (frame + 1) * per_frame)
            grad_h = dot_nn(d_all[0, at, :], w_qkv[0])
            for i in (1, 2):
                grad_h = grad_h + dot_nn(d_all[i, at, :], w_qkv[i])
            here = slice(frame * patch_part, (frame + 1) * patch_part)
            own_ref[here, :] = grad_h[:patch_part]
            for r in range(1, n_tp):
                others[r - 1][here, :] = grad_h[r * patch_part : (r + 1) * patch_part].astype(BF)

    ins = [*grad_y_list, probs, qkv, sqkv_rows, w_so]
    return call(
        kernel,
        [like((count, 3 * part))] * 2 + [like((rows, width), F32)] + [like((rows, width))] * (n_tp - 1),
        ins,
        [False] * n_tp + [True] * 4,
        [False] * (n_tp + 2),
        [
            VMEM((3, columns, width), BF),
            VMEM((columns, width), BF),
            VMEM((3, count, columns), BF),
            VMEM(probs.shape, BF),
            VMEM((count, width), BF),
            VMEM((count, columns), BF),
            VMEM((3, count, columns), BF),
            pltpu.SemaphoreType.DMA((4,)),
        ],
        after,
    )


def tokens_gradient(tokens_rows, grad, grad_h_own, grad_h_others, mod_here, frames_here):
    rows, width = tokens_rows.shape
    patch_part = rows // frames_here
    others = len(grad_h_others)

    def kernel(*refs):
        token_ref, grad_ref, own_ref = refs[:3]
        mod_ref, out_ref, sum_ref = refs[3 + others :]
        for frame in range(frames_here):
            at = slice(frame * patch_part, (frame + 1) * patch_part)
            grad_h = own_ref[at, :]
            for other in refs[3 : 3 + others]:
                grad_h = grad_h + other[at, :].astype(F32)
            normed, inverse = norm_of(token_ref[at, :].astype(F32))
            sum_ref[frame : frame + 1, 0:width] = jnp.sum(grad_h, axis=0, keepdims=True)
            sum_ref[frame : frame + 1, width:] = jnp.sum(grad_h * normed, axis=0, keepdims=True)
            scale = 1.0 + mod_ref[frame : frame + 1, width : 2 * width]
            out_ref[at, :] = (grad_ref[at, :] + norm_back(grad_h * scale, normed, inverse)).astype(BF)

    ins = [tokens_rows, grad, grad_h_own, *grad_h_others, mod_here]
    return call(
        kernel,
        [like((rows, width)), like((frames_here, 2 * width), F32)],
        ins,
        [False] * len(ins),
        [False] * 2,
        [],
    )


def flip(operand, mask):
    size = lax.axis_size("wide")
    return lax.ppermute(operand, "wide", [(s, s ^ mask) for s in range(size)])


def tp_from(operand, shift):
    size = lax.axis_size("tp")
    return lax.ppermute(operand, "tp", [(s, (s - shift) % size) for s in range(size)])


def tp_to(operand, shift):
    size = lax.axis_size("tp")
    return lax.ppermute(operand, "tp", [(s, (s + shift) % size) for s in range(size)])


def tp_gather(operand):
    return [operand] + [tp_from(operand, k) for k in range(1, lax.axis_size("tp"))]


class Pack:
    def __init__(self, first, order, layout):
        bits = lax.axis_size("wide").bit_length() - 1
        self.first, self.layout = first, layout
        self.order = order + [bit for bit in range(bits) if bit != first and bit not in order]
        self.across = sum(groups * cols for groups, cols in layout)


def scatter_rows(total, keep, give, pack, size, low=0):
    block = total.shape[0] // size
    mine = bit_of(pack.order[0])
    inner = pack.order[1:] + [pack.first]
    for at in range(size // 2):
        parts = []
        for value in range(2):
            place = value << pack.order[0]
            for depth, bit in enumerate(inner):
                place |= ((at >> (len(inner) - 1 - depth)) & 1) << bit
            parts.append(total[place * block : (place + 1) * block, :].astype(BF))
        keep[at] = jnp.where(mine == 0, parts[0], parts[1])
        give[at] = jnp.where(mine == 0, parts[1], parts[0])


def half_shape(pack, width, size):
    return like((size // 2, width // size, pack.across))


class CoreCopies:
    def __init__(self, send_sem, recv_sem):
        self.send_sem, self.recv_sem, self.used = send_sem, recv_sem, 0

    def start(self, source, target, place):
        copy = pltpu.make_async_remote_copy(
            src_ref=source,
            dst_ref=target,
            send_sem=self.send_sem.at[self.used],
            recv_sem=self.recv_sem.at[self.used],
            device_id=place,
            device_id_type=pl.DeviceIdType.MESH,
        )
        copy.start()
        self.used += 1
        return copy


def pack_products(members, width, size, after, collective_id, chore=None):
    n_tp = lax.axis_size("tp")
    count = len(members)
    sources = [array for unused, keep, got, *unused2 in members for array in (keep, got)]
    chore_ins, chore_outs, chore_scratch, chore_make = chore or ([], [], [], None)
    copies = 4 * (n_tp - 1) * count

    def kernel(*refs):
        refs = list(refs)

        def take(number):
            taken = refs[:number]
            del refs[:number]
            return taken

        source_refs = take(2 * count)
        extra_ins = take(len(chore_ins))
        outs = take(2 * count)
        extra_outs = take(len(chore_outs))
        totals = take(count)
        landing = take(2 * count * (n_tp - 1))
        send_sem, recv_sem = take(2)
        greet_devices(core_places() + (pair_places() if chore else []))
        steps = iter(chore_make(extra_ins, extra_outs, refs)) if chore else iter(())
        next(steps, None)
        core = CoreCopies(send_sem, recv_sem)
        flights = {}
        for m, (pack, unused, unused2, models, slot, weights) in enumerate(members):
            for k, place in enumerate(core_places()):
                for side in range(2):
                    ref, to = source_refs[2 * m + side], landing[(2 * m + side) * (n_tp - 1) + k]
                    front = pl.ds(0, models * width)
                    cols = pl.ds(models * width + (k + 1) * slot, slot)
                    flights[m, k, side] = [
                        core.start(ref.at[:, front], to.at[:, front], place),
                        core.start(ref.at[:, cols], to.at[:, cols], place),
                    ]

        def add(m, arrays, first):
            pack, unused, unused2, models, slot, weights = members[m]
            low = 0
            for model, column, cols in weights:
                terms = None
                for ref, k in arrays:
                    at = models * width + k * slot + column
                    term = dot_tn(ref[:, model : model + width], ref[:, at : at + cols])
                    terms = term if terms is None else terms + term
                if first:
                    totals[m][:, low : low + cols] = terms
                else:
                    totals[m][:, low : low + cols] += terms
                low += cols

        for m in range(count):
            add(m, [(source_refs[2 * m], 0), (source_refs[2 * m + 1], 0)], True)
            next(steps, None)
        for m in range(count):
            for k in range(n_tp - 1):
                for side in range(2):
                    for copy in flights[m, k, side]:
                        copy.wait()
                add(m, [(landing[(2 * m + side) * (n_tp - 1) + k], k + 1) for side in range(2)], False)
            scatter_rows(totals[m], outs[2 * m], outs[2 * m + 1], members[m][0], size)
            next(steps, None)
        for unused in steps:
            pass

    outs = [half_shape(member[0], width, size) for member in members for unused in range(2)]
    ins = sources + list(chore_ins)
    outs += list(chore_outs)
    out = call(
        kernel,
        outs,
        ins,
        [False] * len(ins),
        [False] * len(outs),
        [VMEM((width, member[0].across), F32) for member in members]
        + [VMEM(array.shape, BF) for array in sources for unused in range(n_tp - 1)]
        + [pltpu.SemaphoreType.DMA((copies,))] * 2
        + list(chore_scratch),
        after,
        collective_id=collective_id,
        has_side_effects=True,
    )
    return [(out[2 * m], out[2 * m + 1]) for m in range(count)], out[2 * count :]


def sum_chore(parts):
    size, block, across = parts[0].shape
    bits = size.bit_length() - 1
    count = len(parts)

    def make(ins, outs, scratch):
        levels, landing, sems = scratch[: bits + 1], scratch[bits + 1 : 2 * bits + 1], scratch[2 * bits + 1 :]
        for at in range(size):
            total = ins[0][at].astype(F32)
            for ref in ins[1:]:
                total = total + ref[at].astype(F32)
            levels[0][mirrored(at)] = total.astype(BF)
        halving = Halving(levels, landing, *sems)
        halving.start()
        yield
        for unused in range(bits):
            halving.advance()
            yield
        halving.finish(outs[0])

    scratch = level_scratch(size, (block, across)) + level_scratch(size, (block, across))[1:]
    return parts, [like((block, across))], scratch + swap_sems(bits, 1), make


def share_chore(part, size):
    bits = size.bit_length() - 1

    def make(ins, outs, scratch):
        levels, sems = scratch[: bits + 1], scratch[bits + 1 :]
        levels[bits][0] = ins[0][...]
        doubling = Doubling(levels, *sems)
        doubling.start()
        yield
        for unused in range(bits):
            doubling.advance()
            yield
        doubling.finish(outs[0])

    return [part], [like((size,) + part.shape)], level_scratch(size, part.shape) + swap_sems(bits, 1), make


def spatial_products(q_pack, o_pack, h_all, h_got, q_keep, q_got, dy_list, dy_got, a_keep, a_got, frames_here, size, after, collective_id):
    rows, width = h_got.shape
    n_tp = len(dy_list)
    count = n_tp * rows
    patch_part = rows // frames_here

    def kernel(*refs):
        h_ref, q_keep_ref, q_got_ref, a_keep_ref, a_got_ref, h_part, dy_part = refs[:7]
        dy_parts = refs[7 : 7 + n_tp]
        q_keep_out, q_give_out, o_keep_out, o_give_out, model, total_q, total_o = refs[7 + n_tp : 14 + n_tp]
        h_land, dy_land, send_sem, recv_sem = refs[14 + n_tp :]
        greet_devices(core_places())
        core = CoreCopies(send_sem, recv_sem)
        flights = []
        for k, place in enumerate(core_places()):
            back = n_tp - 2 - k
            flights.append(core.start(h_part, h_land.at[back], place))
            flights.append(core.start(dy_part, dy_land.at[back], place))

        def gather(parts):
            for frame in range(frames_here):
                for r in range(n_tp):
                    at = (frame * n_tp + r) * patch_part
                    model[at : at + patch_part, :] = parts[r][
                        frame * patch_part : (frame + 1) * patch_part, :
                    ]

        total_q[...] = dot_tn(h_ref[...], q_keep_ref[...])
        gather(dy_parts)
        total_o[...] = dot_tn(model[...], a_keep_ref[...])
        for copy in flights:
            copy.wait()
        gather([h_part] + [h_land.at[k] for k in range(n_tp - 1)])
        total_q[...] += dot_tn(model[...], q_got_ref[...])
        scatter_rows(total_q, q_keep_out, q_give_out, q_pack, size)
        gather([dy_part] + [dy_land.at[k] for k in range(n_tp - 1)])
        total_o[...] += dot_tn(model[...], a_got_ref[...])
        scatter_rows(total_o, o_keep_out, o_give_out, o_pack, size)

    ins = [h_all, q_keep, q_got, a_keep, a_got, h_got, dy_got, *dy_list]
    outs = [half_shape(q_pack, width, size)] * 2 + [half_shape(o_pack, width, size)] * 2
    out = call(
        kernel,
        outs,
        ins,
        [False] * len(ins),
        [False] * 4,
        [VMEM((count, width), BF), VMEM((width, q_pack.across), F32), VMEM((width, o_pack.across), F32)]
        + [VMEM((n_tp - 1, rows, width), BF)] * 2
        + [pltpu.SemaphoreType.DMA((2 * (n_tp - 1),))] * 2,
        after,
        collective_id=collective_id,
        has_side_effects=True,
    )
    return [(out[0], out[1]), (out[2], out[3])]


def by_bit(bits):
    return [(bit, [i for i, other in enumerate(bits) if other == bit]) for bit in sorted(set(bits))]


def halve(keeps, gots, bits_now, bits_next, after):
    now, later = by_bit(bits_now), by_bit(bits_next)
    count = len(keeps)
    widths = [keep.shape[-1] for keep in keeps]
    rest = keeps[0].shape[0] // 2
    block = keeps[0].shape[1]

    def kernel(*refs):
        keep_refs, got_refs = refs[:count], refs[count : count + len(now)]
        outs, gives = refs[count + len(now) :][:count], refs[count + len(now) + count :]
        sources = {}
        for ref, (unused, members) in zip(got_refs, now):
            low = 0
            for i in members:
                sources[i] = (ref, low)
                low += widths[i]
        for ref, (bit, members) in zip(gives, later):
            mine = bit_of(bit)
            low = 0
            for i in members:
                got, at = sources[i]
                keep = keep_refs[i]
                here = pl.ds(mine * rest, rest)
                there = pl.ds((1 - mine) * rest, rest)
                outs[i][...] = (
                    keep[here].astype(F32) + got[here, :, at : at + widths[i]].astype(F32)
                ).astype(BF)
                ref[:, :, low : low + widths[i]] = (
                    keep[there].astype(F32) + got[there, :, at : at + widths[i]].astype(F32)
                ).astype(BF)
                low += widths[i]

    outs = [like((rest, block, cols)) for cols in widths]
    outs += [like((rest, block, sum(widths[i] for i in members))) for unused, members in later]
    ins = [*keeps, *gots]
    out = call(kernel, outs, ins, [False] * len(ins), [False] * len(outs), [], after)
    return out[:count], out[count:]


def flip_all(gives, bits):
    return [flip(give, 1 << bit) for give, (bit, unused) in zip(gives, by_bit(bits))]


def place(packs, keeps, gots):
    now = by_bit([pack.first for pack in packs])
    count = len(packs)

    def kernel(*refs):
        keep_refs, got_refs, outs = refs[:count], refs[count : count + len(now)], list(refs[count + len(now) :])
        sources = {}
        for ref, (unused, members) in zip(got_refs, now):
            low = 0
            for i in members:
                sources[i] = (ref, low)
                low += packs[i].across
        for i, pack in enumerate(packs):
            mine = bit_of(pack.first)
            got, at = sources[i]
            own = keep_refs[i][0].astype(F32)
            other = got[0, :, at : at + pack.across].astype(F32)
            sides = [jnp.where(mine == 0, own, other), jnp.where(mine == 0, other, own)]
            low = 0
            for groups, cols in pack.layout:
                out = outs.pop(0)
                for g in range(groups):
                    for side in range(2):
                        value = sides[side][:, low + g * cols : low + (g + 1) * cols]
                        if groups == 1:
                            out[:, side * cols : (side + 1) * cols] = value
                        else:
                            out[g, :, side * cols : (side + 1) * cols] = value
                low += groups * cols

    block = keeps[0].shape[1]
    outs = [
        like((block, 2 * cols) if groups == 1 else (groups, block, 2 * cols), F32)
        for pack in packs
        for groups, cols in pack.layout
    ]
    ins = [*keeps, *gots]
    return call(kernel, outs, ins, [False] * len(ins), [False] * len(outs), [])


class Reduction:
    def __init__(self, packs, products):
        self.packs = packs
        self.bits = [pack.order[0] for pack in packs]
        self.keeps = [keep for keep, unused in products]
        self.gots = None
        gives = [give for unused, give in products]
        groups = by_bit(self.bits)
        self.gots = [
            flip(gives[members[0]] if len(members) == 1 else jnp.concatenate([gives[i] for i in members], axis=-1), 1 << bit)
            for bit, members in groups
        ]
        self.done = 0

    def step(self, after=()):
        self.done += 1
        later = [
            pack.order[self.done] if self.done < len(pack.order) else pack.first for pack in self.packs
        ]
        self.keeps, gives = halve(self.keeps, self.gots, self.bits, later, after)
        self.gots = flip_all(gives, later)
        self.bits = later
        return self.keeps[0]

    def finish(self):
        return place(self.packs, self.keeps, self.gots)


def tp_sum(parts, dtype=BF):
    total = parts[0].astype(F32)
    for k in range(1, lax.axis_size("tp")):
        total = total + tp_to(parts[k].astype(dtype), k).astype(F32)
    return total


def tp_ordered(relative):
    size = lax.axis_size("tp")
    start = (size - lax.axis_index("tp")) % size
    return lax.dynamic_slice_in_dim(jnp.stack(relative + relative), start, size, axis=0)


def swap_wide(blocks):
    return lax.all_to_all(blocks, "wide", split_axis=0, concat_axis=0, tiled=True)


def on_device(
    tokens,
    cotangent,
    caption,
    caption_len,
    clip_id,
    timestep,
    w_mod,
    b_mod,
    w_text,
    w_sqkv,
    w_so,
    w_tqkv,
    w_to,
    w_cq,
    w_ckv,
    w_co,
    w_fc1,
    w_fc2,
):
    n_tp = lax.axis_size("tp")
    n_wide = lax.axis_size("wide")
    frames_here, patch_part, width = tokens.shape
    columns = w_so.shape[0]
    part = columns // 2
    half = w_fc1.shape[1] // 2
    clip_count = timestep.shape[0]
    frames = clip_id.shape[0]
    patch_here = patch_part // n_wide
    rows = frames_here * patch_part
    block = frames_here * patch_here
    count = frames * patch_here
    wide_at = lax.axis_index("wide")
    tp_at = lax.axis_index("tp")

    tokens_rows = tokens.reshape(rows, width)
    tokens_list = tp_gather(tokens_rows)
    sqkv_rows = w_sqkv.transpose(1, 2, 0)
    tqkv_list = tp_gather(w_tqkv.transpose(1, 2, 0))
    to_list = tp_gather(w_to)
    cq_list = tp_gather(w_cq.T)
    co_list = tp_gather(w_co)
    fc1_list = tp_gather(w_fc1)
    fc2_list = tp_gather(w_fc2)

    half_width = width // 2
    frequencies = jnp.exp(-math.log(10000.0) * jnp.arange(half_width).astype(F32) / half_width)
    angles = timestep.astype(F32)[:, None] * frequencies[None, :]
    embedding = jnp.concatenate([jnp.cos(angles), jnp.sin(angles)], axis=1)
    silu_embed = jax.nn.silu(embedding).astype(BF)
    mod_part = (dot_nn(silu_embed, w_mod) + b_mod.astype(F32)).astype(BF)
    modulation = tp_ordered(tp_gather(mod_part)).transpose(1, 0, 2).reshape(clip_count, -1)
    clip_hot = clip_id[:, None] == jnp.arange(clip_count)[None, :]
    hot_here = lax.dynamic_slice_in_dim(
        clip_hot.astype(F32), wide_at * frames_here, frames_here
    )
    mod_here = dot_nn(hot_here.astype(BF), modulation[:, : 3 * width])
    clip_rows = jnp.broadcast_to(clip_id[:, None], (frames, patch_here)).reshape(count)
    hot_rows = (clip_rows[:, None] == jnp.arange(clip_count)[None, :]).astype(BF)
    mod_rows = dot_nn(hot_rows, modulation[:, 3 * width :]).astype(BF)

    caption_rows = caption.shape[0]
    block_rows = -(-caption_rows // 16) * 16
    keys = n_wide * block_rows
    padded = jnp.pad(caption, ((0, block_rows - caption_rows), (0, 0)))
    context_part = dot_nt(padded, w_text.T).astype(BF)
    context = tp_ordered(tp_gather(context_part)).transpose(1, 0, 2).reshape(block_rows, width)
    ckv_rows = w_ckv.transpose(1, 2, 0).reshape(2 * columns, width)
    keyval_part = dot_nt(context, ckv_rows).astype(BF)
    text_cols = caption.shape[1] // n_wide
    context_cols = width // n_wide
    spare = -(text_cols + context_cols) % LANES
    texts = jnp.concatenate(
        [
            padded.reshape(block_rows, n_wide, text_cols),
            context.reshape(block_rows, n_wide, context_cols),
            jnp.zeros((block_rows, n_wide, spare), BF),
        ],
        axis=2,
    ).transpose(1, 0, 2)

    row_two = clip_rows * patch_here + np.arange(count, dtype=np.int32) % patch_here
    key_at = np.arange(keys)
    key_row = key_at // block_rows * caption_rows + key_at % block_rows
    key_real = jnp.asarray(key_at % block_rows < caption_rows)[None, :]
    key_clip = (key_row // LTXT).astype(np.int32)[None, :]
    key_in = (key_row % LTXT).astype(np.int32)[None, :]
    key_three = jnp.full((1, keys), -1, jnp.int32)
    for clip in range(clip_count):
        seen = key_real & (key_clip == clip) & (key_in < caption_len[clip])
        key_three = jnp.where(seen, clip, key_three)
    row_codes = jnp.stack([row_two, clip_rows], axis=1)
    longest = max(count, keys)
    key_codes = jnp.concatenate(
        [jnp.pad(row_two[None, :], ((0, 0), (0, longest - count))), jnp.pad(key_three, ((0, 0), (0, longest - keys)))]
    )

    grad_blocks = cotangent.reshape(frames_here, n_wide, patch_here, width).transpose(1, 0, 2, 3)
    grad_blocks = grad_blocks.reshape(n_wide, block, width)

    h_all, h_own, qkv_one, probs_one, a_keep, a_give, y_own, *others = spatial_forward(
        tokens_list, mod_here, sqkv_rows, w_so, frames_here, grad_blocks, keyval_part, texts
    )
    y_others, (grad_out, keyval, texts) = others[: n_tp - 1], others[n_tp - 1 :]
    grad_out = grad_out.reshape(count, width)
    keyval_list = tp_gather(keyval.reshape(keys, 2 * columns))
    texts = texts.reshape(keys, -1)
    caption_cols, context_cols = texts[:, :text_cols], texts[:, text_cols : text_cols + context_cols]
    y_others = [tp_to(other, k + 1) for k, other in enumerate(y_others)]
    h_flip = flip(h_own, 1)
    a_got = flip(a_give, 2)
    stream, y_one = stream_to_patches(tokens_rows, y_own, y_others, mod_here, frames_here)
    *kept, stream, keyval_full = middle_forward(
        stream.reshape(count, width), row_codes, key_codes, keyval_list, tqkv_list, to_list, cq_list, co_list
    )
    block_out, up_keep, up_give, down_keep, down_give, grad, mod_sum = feed_forward(
        stream, grad_out, mod_rows, hot_rows, fc1_list, fc2_list, [0, 2]
    )

    up = Pack(0, [1, 2, 3], [(1, half)])
    down = Pack(2, [0, 1, 3], [(1, half)])
    inner = Pack(1, [0, 2, 3], [(3, part), (1, part)])
    outer = Pack(0, [1, 2, 3], [(1, part), (1, part)])
    q_pack = Pack(0, [1, 2, 3], [(3, part)])
    o_pack = Pack(1, [2, 0, 3], [(1, part)])
    up_got = flip(up_give, 1 << up.first)
    down_got = flip(down_give, 1 << down.first)

    in_keep, in_give, out_keep, out_give, grad, *grad_kv = middle_backward(
        grad, kept, keyval_full, tqkv_list, to_list, cq_list, co_list, [1, 0]
    )
    in_got = flip(in_give, 1 << inner.first)
    out_got = flip(out_give, 1 << outer.first)
    block_out = swap_wide(block_out.reshape(n_wide, block, width))
    block_out = block_out.reshape(n_wide, frames_here, patch_here, width).transpose(1, 0, 2, 3)
    block_out = block_out.reshape(frames_here, patch_part, width)
    grad_stream, grad_y1, grad_gate = grads_to_frames(
        grad.reshape(n_wide, block, width), y_one, mod_here, frames_here, []
    )
    grad_y1_list = tp_gather(grad_y1)
    dy_flip = flip(grad_y1, 1 << o_pack.first)
    q_keep, q_give, grad_h_own, *grad_h_others = spatial_backward(
        grad_y1_list, probs_one, qkv_one, sqkv_rows, w_so, frames_here, [up_got, down_got]
    )
    q_got = flip(q_give, 1 << q_pack.first)
    grad_h_others = [tp_to(other, k + 1) for k, other in enumerate(grad_h_others)]
    grad_tokens, frame_sums = tokens_gradient(
        tokens_rows, grad_stream, grad_h_own, grad_h_others, mod_here, frames_here
    )
    fc_slot, in_slot, out_slot = whole_tiles(half), whole_tiles(4 * part), whole_tiles(2 * part)
    kv_parts = [grad_kv[0].reshape(n_wide, block_rows, -1)]
    kv_parts += [tp_to(grad_kv[k], k).reshape(n_wide, block_rows, -1) for k in range(1, n_tp)]
    products, (grad_kv,) = pack_products(
        [
            (up, up_keep, up_got, 1, fc_slot, [(0, 0, half)]),
            (down, down_keep, down_got, 1, fc_slot, [(0, 0, half)]),
        ],
        width,
        n_wide,
        [grad_tokens],
        4,
        sum_chore(kv_parts),
    )
    feed = Reduction([up, down], products)
    products, (grad_kv,) = pack_products(
        [
            (inner, in_keep, in_got, 2, in_slot, [(0, 0, 3 * part), (width, 3 * part, part)]),
            (outer, out_keep, out_got, 2, out_slot, [(0, 0, part), (width, part, part)]),
        ],
        width,
        n_wide,
        [],
        5,
        share_chore(grad_kv, n_wide),
    )
    grad_kv = grad_kv.reshape(keys, 2 * columns)
    middle = Reduction([inner, outer], products)
    mark = feed.step([products[0][0]])
    products = spatial_products(
        q_pack, o_pack, h_all, h_flip, q_keep, q_got, grad_y1_list, dy_flip, a_keep, a_got, frames_here, n_wide, [mark], 6
    )
    spatial = Reduction([q_pack, o_pack], products)
    mark = middle.step([products[0][0]])
    mark = feed.step([mark])
    mark = spatial.step([mark])
    mark = middle.step([mark])
    mark = feed.step([mark])
    mark = spatial.step([mark])
    mark = middle.step([mark])
    mark = spatial.step([mark])
    while feed.bits != [pack.first for pack in feed.packs]:
        feed.step()
        middle.step()
        spatial.step()
    grad_fc1, grad_fc2 = feed.finish()
    grad_tqkv, grad_cq, grad_to, grad_co = middle.finish()
    grad_sqkv, grad_so = spatial.finish()

    grad_ckv = dot_tn(context_cols, grad_kv).reshape(-1, 2, columns)
    grad_context = dot_nn(grad_kv, ckv_rows)
    sides = grad_context.reshape(keys, n_tp, width // n_tp)
    relative = [
        lax.dynamic_index_in_dim(sides, (tp_at + k) % n_tp, 1, keepdims=False) for k in range(n_tp)
    ]
    grad_context = tp_sum(relative).astype(BF)
    grad_text = dot_tn(caption_cols, grad_context)

    frame_sums = jnp.concatenate([frame_sums, grad_gate], axis=1)
    here_sum = lax.dot_general(hot_here, frame_sums, (((0,), (0,)), ((), ())), precision=HIGH)
    grad_mod = jnp.concatenate([here_sum, mod_sum], axis=1).reshape(clip_count, n_tp, -1)
    relative = [
        lax.dynamic_index_in_dim(grad_mod, (tp_at + k) % n_tp, 1, keepdims=False) for k in range(n_tp)
    ]
    grad_mod = tp_sum(relative, F32).reshape(clip_count, n_wide, -1).transpose(1, 0, 2)
    grad_mod = jnp.sum(swap_wide(grad_mod), axis=0)
    grad_w_mod = lax.dot_general(
        silu_embed.astype(F32), grad_mod, (((0,), (0,)), ((), ())), precision=HIGH
    )

    return (
        block_out,
        grad_tokens.reshape(tokens.shape),
        grad_w_mod,
        jnp.sum(grad_mod, axis=0),
        grad_text,
        grad_sqkv.transpose(1, 0, 2),
        grad_so.T,
        grad_tqkv.transpose(1, 0, 2),
        grad_to.T,
        grad_cq,
        grad_ckv,
        grad_co.T,
        grad_fc1,
        grad_fc2.T,
    )


def solution(mesh):
    placed = (
        P("wide", "tp", None),
        P("wide", "tp", None),
        P("wide", None),
        P(),
        P(),
        P(),
        P(None, "tp"),
        P("tp"),
        P(None, "tp"),
        P(None, None, "tp"),
        P("tp", None),
        P(None, None, "tp"),
        P("tp", None),
        P(None, "tp"),
        P(None, None, "tp"),
        P("tp", None),
        P(None, "tp"),
        P("tp", None),
    )
    return jax.shard_map(
        on_device,
        mesh=mesh,
        in_specs=placed,
        out_specs=(
            P("wide", "tp", None),
            P("wide", "tp", None),
            P(None, ("tp", "wide")),
            P(("tp", "wide")),
            P("wide", "tp"),
            P("wide", None, "tp"),
            P("tp", "wide"),
            P("wide", None, "tp"),
            P("tp", "wide"),
            P("wide", "tp"),
            P("wide", None, "tp"),
            P("tp", "wide"),
            P("wide", "tp"),
            P("tp", "wide"),
        ),
        check_vma=False,
    )
```

```python
import functools
import math

import jax
import jax.numpy as jnp
import numpy as np
from jax import lax
from jax.experimental import pallas as pl
from jax.experimental.pallas import tpu as pltpu
from jax.sharding import PartitionSpec as P

HD = 72
LTXT = 120
EPS = 1e-06
NEGATIVE = -1e30
HIGH = lax.Precision.HIGHEST
BF = jnp.bfloat16
F32 = jnp.float32
LANES = 128
FACTOR = HD ** (-0.5)
VMEM = pltpu.VMEM
MB = 1 << 20


def dot_nn(left, right):
    return lax.dot_general(left, right, (((1,), (0,)), ((), ())), preferred_element_type=F32)


def dot_nt(left, right):
    return lax.dot_general(left, right, (((1,), (1,)), ((), ())), preferred_element_type=F32)


def dot_tn(left, right):
    return lax.dot_general(left, right, (((0,), (0,)), ((), ())), preferred_element_type=F32)


def norm_of(rows):
    average = jnp.mean(rows, axis=-1, keepdims=True)
    centred = rows - average
    inverse = lax.rsqrt(jnp.mean(centred * centred, axis=-1, keepdims=True) + EPS)
    return centred * inverse, inverse


def norm_back(grad_normed, normed, inverse):
    grad_mean = jnp.mean(grad_normed, axis=-1, keepdims=True)
    grad_cross = jnp.mean(grad_normed * normed, axis=-1, keepdims=True)
    return inverse * (grad_normed - grad_mean - normed * grad_cross)


def window(head, columns):
    low = HD * head
    start = low // LANES * LANES
    stop = min(-(-(low + HD) // LANES) * LANES, columns)
    at = lax.broadcasted_iota(jnp.int32, (1, stop - start), 1) + start
    own = jnp.where((at >= low) & (at < low + HD), 1.0, 0.0).astype(BF)
    return start, stop, own


class Tiles:
    def __init__(self, write, columns, scale=None):
        self.write, self.columns, self.scale, self.open = write, columns, scale, {}

    def add(self, start, stop, value):
        for low in range(start, stop, LANES):
            part = value[:, low - start : min(low + LANES, stop) - start]
            self.open[low] = self.open[low] + part if low in self.open else part

    def flush(self, below):
        for low in sorted(self.open):
            if low + LANES <= below or below >= self.columns:
                part = self.open.pop(low)
                if self.scale is not None:
                    part = part * self.scale
                self.write(low, min(low + LANES, self.columns), part)


def attend(query, key, value, bias, heads, columns, keep_probs, write, between=None):
    out = Tiles(write, columns)
    for head in range(heads):
        start, stop, own = window(head, columns)
        scores = dot_nt(query(start, stop) * own, key(start, stop)) * FACTOR
        if bias is not None:
            scores = scores + bias
        scores = jnp.exp(scores - jnp.max(scores, axis=-1, keepdims=True))
        probs = (scores * (1.0 / jnp.sum(scores, axis=-1, keepdims=True))).astype(BF)
        keep_probs(head, probs)
        out.add(start, stop, dot_nn(probs, value(start, stop) * own))
        out.flush(HD * (head + 1))
        if between is not None and head == heads // 2:
            between()


def attend_back(query, key, value, grad_out, probs_of, heads, columns, write_q, write_k, write_v):
    grad_q = Tiles(write_q, columns, FACTOR)
    grad_k = Tiles(write_k, columns, FACTOR)
    grad_v = Tiles(write_v, columns)
    for head in range(heads):
        start, stop, own = window(head, columns)
        probs = probs_of(head)
        grad_own = grad_out(start, stop) * own
        grad_probs = dot_nt(grad_own, value(start, stop))
        wide_probs = probs.astype(F32)
        grad_scores = wide_probs * grad_probs
        row = jnp.sum(grad_scores, axis=-1, keepdims=True)
        grad_scores = (grad_scores - wide_probs * row).astype(BF)
        grad_q.add(start, stop, dot_nn(grad_scores, key(start, stop) * own))
        grad_k.add(start, stop, dot_tn(grad_scores, query(start, stop) * own))
        grad_v.add(start, stop, dot_tn(probs, grad_own))
        for tiles in (grad_q, grad_k, grad_v):
            tiles.flush(HD * (head + 1))


class Moves:
    def __init__(self, sems):
        self.sems, self.used = sems, 0

    def start(self, source, target):
        copy = pltpu.make_async_copy(source, target, self.sems.at[self.used])
        self.used += 1
        copy.start()
        return copy


def any_spec():
    return pl.BlockSpec(memory_space=pl.ANY)


def vmem_spec():
    return pl.BlockSpec(memory_space=VMEM)


def call(kernel, outs, ins, in_any, out_any, scratch, after=(), limit=56, **params):
    given, extra = len(ins), len(after)

    def ordered(*refs):
        kernel(*refs[:given], *refs[given + extra :])

    return pl.pallas_call(
        ordered,
        out_shape=tuple(outs),
        in_specs=[any_spec() if flag else vmem_spec() for flag in in_any] + [any_spec()] * extra,
        out_specs=tuple(any_spec() if flag else vmem_spec() for flag in out_any),
        scratch_shapes=scratch,
        compiler_params=pltpu.CompilerParams(vmem_limit_bytes=limit * MB, **params),
        cost_estimate=pl.CostEstimate(flops=1, bytes_accessed=1, transcendentals=0),
    )(*ins, *after)


def whole_tiles(columns):
    return -(-columns // LANES) * LANES


def like(shape, dtype=BF):
    return jax.ShapeDtypeStruct(shape, dtype)


def greet(more=()):
    barrier = pltpu.get_barrier_semaphore()
    size = lax.axis_size("wide")
    me = lax.axis_index("wide")

    def signal(k, carry):
        pl.semaphore_signal(
            barrier,
            inc=1,
            device_id={"wide": lax.rem(me + k, size)},
            device_id_type=pl.DeviceIdType.MESH,
        )
        return carry

    lax.fori_loop(1, size, signal, 0)
    for place in more:
        pl.semaphore_signal(barrier, inc=1, device_id=place, device_id_type=pl.DeviceIdType.MESH)
    pl.semaphore_wait(barrier, size - 1 + len(more))


class Swap:
    def __init__(self, send, recv, send_sem, recv_sem, shared=False):
        self.send, self.recv, self.shared = send, recv, shared
        self.send_sem, self.recv_sem = send_sem, recv_sem

    def source(self, at):
        return self.send if self.shared else self.send.at[at]

    def copy(self, k, source, target, peer):
        return pltpu.make_async_remote_copy(
            src_ref=self.source(source),
            dst_ref=self.recv.at[target],
            send_sem=self.send_sem.at[k],
            recv_sem=self.recv_sem.at[k],
            device_id={"wide": peer},
            device_id_type=pl.DeviceIdType.MESH,
        )

    def start(self):
        size, me = lax.axis_size("wide"), lax.axis_index("wide")

        def step(k, carry):
            peer = lax.rem(me + k, size)
            self.copy(k, peer, me, peer).start()
            return carry

        lax.fori_loop(1, size, step, 0)
        self.recv[me] = self.send[...] if self.shared else self.send[me]

    def finish(self):
        size, me = lax.axis_size("wide"), lax.axis_index("wide")

        def arrive(k, carry):
            peer = lax.rem(me + size - k, size)
            self.copy(k, peer, peer, peer).wait_recv()
            return carry

        def leave(k, carry):
            peer = lax.rem(me + k, size)
            self.copy(k, peer, me, peer).wait_send()
            return carry

        lax.fori_loop(1, size, arrive, 0)
        lax.fori_loop(1, size, leave, 0)


def wide_bits():
    return lax.axis_size("wide").bit_length() - 1


def mirrored(at):
    bits = wide_bits()
    return sum(((at >> bit) & 1) << (bits - 1 - bit) for bit in range(bits))


def bit_of(bit):
    return lax.rem(lax.div(lax.axis_index("wide"), 1 << bit), 2)


def partner(bit):
    return lax.axis_index("wide") + (1 - 2 * bit_of(bit)) * (1 << bit)


def greet_devices(places):
    barrier = pltpu.get_barrier_semaphore()
    for place in places:
        pl.semaphore_signal(barrier, inc=1, device_id=place, device_id_type=pl.DeviceIdType.MESH)
    pl.semaphore_wait(barrier, len(places))


def pair_places():
    return [{"wide": partner(bit)} for bit in range(wide_bits())]


def core_places():
    size, me = lax.axis_size("tp"), lax.axis_index("tp")
    return [{"tp": lax.rem(me + k, size)} for k in range(1, size)]


class Doubling:
    def __init__(self, levels, send_sem, recv_sem):
        self.levels, self.send_sem, self.recv_sem = levels, send_sem, recv_sem
        self.bit = wide_bits()
        self.copy = None

    def start(self):
        self.send()

    def send(self):
        bit = self.bit - 1
        have = self.levels[self.bit]
        half = have.shape[0]
        mine = bit_of(bit)
        there = self.levels[bit].at[pl.ds(mine * half, half)]
        self.copy = pltpu.make_async_remote_copy(
            src_ref=have,
            dst_ref=there,
            send_sem=self.send_sem.at[bit],
            recv_sem=self.recv_sem.at[bit],
            device_id={"wide": partner(bit)},
            device_id_type=pl.DeviceIdType.MESH,
        )
        self.copy.start()
        self.levels[bit][pl.ds(mine * half, half)] = have[...]

    def advance(self):
        if self.bit == 0:
            return
        self.copy.wait()
        self.bit -= 1
        if self.bit:
            self.send()

    def finish(self, out):
        while self.bit:
            self.advance()
        for at in range(self.levels[0].shape[0]):
            out[at] = self.levels[0][mirrored(at)]


class Halving:
    def __init__(self, levels, landing, send_sem, recv_sem):
        self.levels, self.landing = levels, landing
        self.send_sem, self.recv_sem = send_sem, recv_sem
        self.bit = 0

    def start(self):
        self.send()

    def send(self):
        bit = self.bit
        half = self.landing[bit].shape[0]
        other = 1 - bit_of(bit)
        self.copy = pltpu.make_async_remote_copy(
            src_ref=self.levels[bit].at[pl.ds(other * half, half)],
            dst_ref=self.landing[bit],
            send_sem=self.send_sem.at[bit],
            recv_sem=self.recv_sem.at[bit],
            device_id={"wide": partner(bit)},
            device_id_type=pl.DeviceIdType.MESH,
        )
        self.copy.start()

    def advance(self):
        bit = self.bit
        if bit == wide_bits():
            return
        half = self.landing[bit].shape[0]
        self.copy.wait()
        own = self.levels[bit][pl.ds(bit_of(bit) * half, half)]
        self.levels[bit + 1][...] = (own.astype(F32) + self.landing[bit][...].astype(F32)).astype(BF)
        self.bit += 1
        if self.bit < wide_bits():
            self.send()

    def finish(self, out):
        while self.bit < wide_bits():
            self.advance()
        out[...] = self.levels[-1][0]


def level_scratch(size, block):
    bits = size.bit_length() - 1
    return [VMEM((size >> s,) + block, BF) for s in range(bits + 1)]


class CoreCopies:
    def __init__(self, send_sem, recv_sem):
        self.send_sem, self.recv_sem, self.used = send_sem, recv_sem, 0

    def start(self, source, target, place):
        copy = pltpu.make_async_remote_copy(
            src_ref=source,
            dst_ref=target,
            send_sem=self.send_sem.at[self.used],
            recv_sem=self.recv_sem.at[self.used],
            device_id=place,
            device_id_type=pl.DeviceIdType.MESH,
        )
        copy.start()
        self.used += 1
        return copy


class PairCopies:
    def __init__(self, send_sem, recv_sem):
        self.send_sem, self.recv_sem, self.copies = send_sem, recv_sem, []

    def start(self, source, target, bit):
        at = len(self.copies)
        copy = pltpu.make_async_remote_copy(
            src_ref=source,
            dst_ref=target,
            send_sem=self.send_sem.at[at],
            recv_sem=self.recv_sem.at[at],
            device_id={"wide": partner(bit)},
            device_id_type=pl.DeviceIdType.MESH,
        )
        copy.start()
        self.copies.append(copy)

    def finish(self):
        for copy in self.copies:
            copy.wait()


def swap_sems(size, count):
    return [pltpu.SemaphoreType.DMA((size,))] * (2 * count)


def spatial_forward(tokens_list, mod_here, sqkv_rows, w_so, frames_here, keyval_part, o_first):
    n_tp = len(tokens_list)
    rows, width = tokens_list[0].shape
    columns = w_so.shape[0]
    patch_part = rows // frames_here
    per_frame = n_tp * patch_part
    count = n_tp * rows
    heads = columns // HD
    size = lax.axis_size("wide")
    bits = wide_bits()

    def kernel(*refs):
        token_refs = refs[:n_tp]
        mod_ref, qkv_hbm, so_hbm, kv_ref = refs[n_tp : n_tp + 4]
        at = n_tp + 4
        h_ref, h_own, qkv_out, probs_out, a_keep, a_give, y_ref = refs[at : at + 7]
        y_others = refs[at + 7 : at + 6 + n_tp]
        at += 6 + n_tp
        kv_out = refs[at]
        weight_qkv, weight_o, qkv_ref, probs_ref, attn_ref, sems, *levels = refs[at + 1 :]
        *levels, send_sem, recv_sem = levels
        greet_devices(pair_places())
        share = Doubling(levels, send_sem, recv_sem)
        levels[bits][0] = kv_ref[...]
        share.start()
        moves = Moves(sems)
        weights = [moves.start(qkv_hbm.at[i], weight_qkv.at[i]) for i in range(3)]
        weight_out = moves.start(so_hbm, weight_o)
        for frame in range(frames_here):
            shift = mod_ref[frame : frame + 1, 0:width]
            scale = 1.0 + mod_ref[frame : frame + 1, width : 2 * width]
            for r in range(n_tp):
                part = token_refs[r][frame * patch_part : (frame + 1) * patch_part, :]
                normed, unused = norm_of(part.astype(F32))
                at = frame * per_frame + r * patch_part
                value = (normed * scale + shift).astype(BF)
                h_ref[at : at + patch_part, :] = value
                if r == 0:
                    h_own[frame * patch_part : (frame + 1) * patch_part, :] = value
        outgoing = []
        for i in range(3):
            weights[i].wait()
            qkv_ref[i] = dot_nt(h_ref[...], weight_qkv[i]).astype(BF)
        share.advance()
        outgoing.append(moves.start(qkv_ref, qkv_out))
        for frame in range(frames_here):
            at = slice(frame * per_frame, (frame + 1) * per_frame)

            def keep_probs(head, probs, frame=frame):
                probs_ref[frame * heads + head] = probs

            def write(low, high, part, at=at):
                attn_ref[at, low:high] = part.astype(BF)

            attend(
                lambda low, high, at=at: qkv_ref[0, at, low:high],
                lambda low, high, at=at: qkv_ref[1, at, low:high],
                lambda low, high, at=at: qkv_ref[2, at, low:high],
                None,
                heads,
                columns,
                keep_probs,
                write,
                share.advance,
            )
            share.advance()
        outgoing.append(moves.start(probs_ref, probs_out))
        mine = bit_of(o_first)
        first, second = attn_ref[:, : columns // 2], attn_ref[:, columns // 2 :]
        part = columns // 2
        a_keep[:, 0:part] = jnp.where(mine == 0, first, second)
        a_give[:, 0:part] = jnp.where(mine == 0, second, first)
        for ref in (a_keep, a_give):
            if ref.shape[1] > part:
                ref[:, part:] = jnp.zeros((count, ref.shape[1] - part), BF)
        weight_out.wait()
        for frame in range(frames_here):
            at = frame * per_frame
            branch = dot_nn(attn_ref[at : at + per_frame, :], weight_o[...])
            here = slice(frame * patch_part, (frame + 1) * patch_part)
            y_ref[here, :] = branch[:patch_part]
            for r in range(1, n_tp):
                y_others[r - 1][here, :] = branch[r * patch_part : (r + 1) * patch_part].astype(BF)
        for copy in outgoing:
            copy.wait()
        share.finish(kv_out)

    outs = [
        like((count, width)),
        like((rows, width)),
        like((3, count, columns)),
        like((frames_here * heads, per_frame, per_frame)),
        like((count, whole_tiles(columns // 2))),
        like((count, whole_tiles(columns // 2))),
        like((rows, width), F32),
    ] + [like((rows, width))] * (n_tp - 1)
    outs.append(like((size,) + keyval_part.shape))
    ins = list(tokens_list) + [mod_here, sqkv_rows, w_so, keyval_part]
    return call(
        kernel,
        outs,
        ins,
        [False] * (n_tp + 1) + [True, True, False],
        [False, False, True, True] + [False] * (n_tp + 3),
        [
            VMEM((3, columns, width), BF),
            VMEM((columns, width), BF),
            VMEM((3, count, columns), BF),
            VMEM((frames_here * heads, per_frame, per_frame), BF),
            VMEM((count, columns), BF),
            pltpu.SemaphoreType.DMA((6,)),
        ]
        + level_scratch(size, keyval_part.shape)
        + swap_sems(bits, 1),
        collective_id=1,
        has_side_effects=True,
    )


def stream_to_patches(tokens_rows, y_own, y_others, mod_here, frames_here):
    size = lax.axis_size("wide")
    rows, width = tokens_rows.shape
    patch_part = rows // frames_here
    patch_here = patch_part // size
    block = frames_here * patch_here
    others = len(y_others)

    def kernel(*refs):
        token_ref, y_ref, mod_ref = refs[0], refs[1], refs[2 + others]
        out_ref, total_ref = refs[3 + others : 5 + others]
        send, recv, send_sem, recv_sem = refs[5 + others :]
        greet()
        for frame in range(frames_here):
            at = slice(frame * patch_part, (frame + 1) * patch_part)
            branch = y_ref[at, :]
            for other in refs[2 : 2 + others]:
                branch = branch + other[at, :].astype(F32)
            total_ref[at, :] = branch
            gate = mod_ref[frame : frame + 1, 2 * width : 3 * width]
            stream = token_ref[at, :].astype(F32) + gate * branch
            for owner in range(size):
                send[owner, frame * patch_here : (frame + 1) * patch_here, :] = stream[
                    owner * patch_here : (owner + 1) * patch_here
                ].astype(BF)
        exchange = Swap(send, recv, send_sem, recv_sem)
        exchange.start()
        exchange.finish()
        out_ref[...] = recv[...]

    ins = [tokens_rows, y_own] + list(y_others) + [mod_here]
    return call(
        kernel,
        [like((size, block, width)), like((rows, width), F32)],
        ins,
        [False] * len(ins),
        [False, False],
        [VMEM((size, block, width), BF)] * 2 + swap_sems(size, 1),
        collective_id=2,
        has_side_effects=True,
    )


def grads_to_frames(grad_blocks, y_one, mod_here, frames_here, members):
    size, block, width = grad_blocks.shape
    rows = y_one.shape[0]
    patch_part = rows // frames_here
    patch_here = patch_part // size
    n_tp = lax.axis_size("tp")
    others = n_tp - 1
    number = len(members)
    every, most = members[0][1].shape[0], max(member[0].across for member in members)
    token_rows = every // n_tp
    head = members[0][3].shape[1]

    def kernel(*refs):
        grad_ref, y_ref, mod_ref = refs[:3]
        operands = [refs[3 + 4 * p : 7 + 4 * p] for p in range(number)]
        at = 3 + 4 * number
        stream_ref, branch_ref, gate_ref = refs[at : at + 3]
        outs = [refs[at + 3 + 2 * p : at + 5 + 2 * p] for p in range(number)]
        at += 3 + 2 * number
        recv, exchange_send, exchange_recv, models, heads, total, sems, send_sem, recv_sem = refs[at:]
        greet(core_places())
        exchange = Swap(grad_ref, recv, exchange_send, exchange_recv)
        exchange.start()
        core = CoreCopies(send_sem, recv_sem)
        moves = Moves(sems)
        flights, loads = [], []
        for p, (model, got, keep, other) in enumerate(operands):
            flights.append(
                [
                    core.start(got, models.at[2 * p + 1, pl.ds((n_tp - 1 - k) * token_rows, token_rows), :], place)
                    for k, place in enumerate(core_places())
                ]
            )
            loads.append(
                [
                    moves.start(model, models.at[2 * p]),
                    moves.start(keep, heads.at[2 * p]),
                    moves.start(got, models.at[2 * p + 1, pl.ds(0, token_rows), :]),
                    moves.start(other, heads.at[2 * p + 1]),
                ]
            )
        for p, member in enumerate(members):
            across = member[0].across
            for copy in loads[p]:
                copy.wait()
            total[:, 0:across] = dot_tn(models[2 * p], heads[2 * p, :, 0:across])
            for copy in flights[p]:
                copy.wait()
            total[:, 0:across] += dot_tn(models[2 * p + 1], heads[2 * p + 1, :, 0:across])
            scatter_rows(total, outs[p][0], outs[p][1], member[0], size)
        exchange.finish()
        for owner in range(size):
            part = recv[owner].astype(F32)
            for frame in range(frames_here):
                at = frame * patch_part + owner * patch_here
                stream_ref[at : at + patch_here, :] = part[
                    frame * patch_here : (frame + 1) * patch_here
                ]
        for frame in range(frames_here):
            at = slice(frame * patch_part, (frame + 1) * patch_part)
            stream = stream_ref[at, :]
            gate_ref[frame : frame + 1, :] = jnp.sum(stream * y_ref[at, :], axis=0, keepdims=True)
            branch_ref[at, :] = (stream * mod_ref[frame : frame + 1, 2 * width : 3 * width]).astype(BF)

    ins = [grad_blocks, y_one, mod_here] + [array for member in members for array in member[1:5]]
    halves = [
        like((size // 2, width // size, member[0].across)) for member in members for unused in range(2)
    ]
    out = call(
        kernel,
        [like((rows, width), F32), like((rows, width)), like((frames_here, width), F32)] + halves,
        ins,
        [False] * 3 + [True] * (4 * number),
        [False] * (3 + 2 * number),
        [VMEM((size, block, width), BF)]
        + swap_sems(size, 1)
        + [
            VMEM((2 * number, every, width), BF),
            VMEM((2 * number, every, head), BF),
            VMEM((width, most), F32),
            pltpu.SemaphoreType.DMA((4 * number,)),
            pltpu.SemaphoreType.DMA((number * others,)),
            pltpu.SemaphoreType.DMA((number * others,)),
        ],
        collective_id=3,
        has_side_effects=True,
    )
    return out[:3], [out[3 + 2 * p : 5 + 2 * p] for p in range(number)]


def fill_rows(moves, sources, target):
    step = sources[0].shape[0]
    return [moves.start(ref, target.at[pl.ds(r * step, step), :]) for r, ref in enumerate(sources)]


def middle_forward(stream, row_codes, key_codes, blocks, keyval_list, tqkv_list, to_list, cq_list, co_list, out_first):
    n_tp = len(tqkv_list)
    count, width = stream.shape
    keys = keyval_list[0].shape[0]
    columns = to_list[0].shape[0]
    heads = width // HD
    part = columns // 2
    out_slot = whole_tiles(2 * part)

    def kernel(*refs):
        stream_ref, row_ref, key_ref = refs[:3]
        block_refs = refs[3 : 3 + len(blocks)]
        at = 3 + len(blocks)
        groups = []
        for unused in range(5):
            groups.append(refs[at : at + n_tp])
            at += n_tp
        keyvals, tqkvs, tos, cqs, cos = groups
        h2_out, qkv_out, p2_out, inv2_ref, h3_out, q3_out, p3_out, inv3_ref, x_ref, kv_ref, a_keep, a_give = refs[at : at + 12]
        block_outs = refs[at + 12 : at + 12 + len(blocks)]
        w_qkv, w_o, w_q, w_c, h2, qkv, p2, a2, h3, q3, p3, a3, sems, *swap = refs[at + 12 + len(blocks) :]
        greet()
        exchanges = [
            Swap(ref, swap[3 * i], swap[3 * i + 1], swap[3 * i + 2]) for i, ref in enumerate(block_refs)
        ]
        for exchange in exchanges:
            exchange.start()
        moves = Moves(sems)
        qkv_in = [
            [
                moves.start(tqkvs[r].at[i], w_qkv.at[i, pl.ds(r * columns, columns), :])
                for r in range(n_tp)
            ]
            for i in range(3)
        ]
        o_in = fill_rows(moves, tos, w_o)
        q_in = fill_rows(moves, cqs, w_q)
        c_in = fill_rows(moves, cos, w_c)
        outgoing = []
        for i in range(2):
            for r in range(n_tp):
                kv_ref[i, :, r * columns : (r + 1) * columns] = keyvals[r][
                    :, i * columns : (i + 1) * columns
                ]
        stream_one = stream_ref[...].astype(F32)
        normed, inverse = norm_of(stream_one)
        inv2_ref[...] = jnp.broadcast_to(inverse, inv2_ref.shape)
        h2[...] = normed.astype(BF)
        outgoing.append(moves.start(h2, h2_out))
        for i in range(3):
            for copy in qkv_in[i]:
                copy.wait()
            qkv[i] = dot_nt(h2[...], w_qkv[i]).astype(BF)
        outgoing.append(moves.start(qkv, qkv_out))

        def keep_two(head, probs):
            p2[head] = probs

        def write_two(low, high, part):
            a2[:, low:high] = part.astype(BF)

        attend(
            lambda low, high: qkv[0, :, low:high],
            lambda low, high: qkv[1, :, low:high],
            lambda low, high: qkv[2, :, low:high],
            jnp.where(row_ref[:, 0:1] == key_ref[0:1, 0:count], 0.0, NEGATIVE),
            heads,
            width,
            keep_two,
            write_two,
        )
        outgoing.append(moves.start(p2, p2_out))
        for copy in o_in:
            copy.wait()
        x_ref[...] = stream_one + dot_nn(a2[...], w_o[...])
        normed, inverse = norm_of(x_ref[...])
        inv3_ref[...] = jnp.broadcast_to(inverse, inv3_ref.shape)
        h3[...] = normed.astype(BF)
        outgoing.append(moves.start(h3, h3_out))
        for copy in q_in:
            copy.wait()
        q3[...] = dot_nt(h3[...], w_q[...]).astype(BF)
        outgoing.append(moves.start(q3, q3_out))

        def keep_three(head, probs):
            p3[head] = probs

        def write_three(low, high, part):
            a3[:, low:high] = part.astype(BF)

        attend(
            lambda low, high: q3[:, low:high],
            lambda low, high: kv_ref[0, :, low:high],
            lambda low, high: kv_ref[1, :, low:high],
            jnp.where(row_ref[:, 1:2] == key_ref[1:2, 0:keys], 0.0, NEGATIVE),
            heads,
            width,
            keep_three,
            write_three,
        )
        outgoing.append(moves.start(p3, p3_out))
        mine = bit_of(out_first)
        for r in range(n_tp):
            for i, ref in enumerate((a2, a3)):
                low = r * out_slot + i * part
                first = ref[:, r * columns : r * columns + part]
                second = ref[:, r * columns + part : (r + 1) * columns]
                a_keep[:, low : low + part] = jnp.where(mine == 0, first, second)
                a_give[:, low : low + part] = jnp.where(mine == 0, second, first)
            for ref in (a_keep, a_give):
                if out_slot > 2 * part:
                    spare = jnp.zeros((count, out_slot - 2 * part), BF)
                    ref[:, r * out_slot + 2 * part : (r + 1) * out_slot] = spare
        for copy in c_in:
            copy.wait()
        x_ref[...] = x_ref[...] + dot_nn(a3[...], w_c[...])
        for copy in outgoing:
            copy.wait()
        for exchange, out in zip(exchanges, block_outs):
            exchange.finish()
            out[...] = exchange.recv[...]

    square = (count, width)
    outs = [
        like(square),
        like((3,) + square),
        like((heads, count, count)),
        like((count, LANES), F32),
        like(square),
        like(square),
        like((heads, count, keys)),
        like((count, LANES), F32),
        like(square, F32),
        like((2, keys, width)),
        like((count, n_tp * out_slot)),
        like((count, n_tp * out_slot)),
    ] + [like(array.shape) for array in blocks]
    kept = [square, (3,) + square, (heads, count, count), square, square, square, (heads, count, keys), square]
    ins = [stream, row_codes, key_codes, *blocks, *keyval_list, *tqkv_list, *to_list, *cq_list, *co_list]
    full = n_tp * columns
    return call(
        kernel,
        outs,
        ins,
        [False] * (3 + len(blocks) + n_tp) + [True] * (4 * n_tp),
        [True, True, True, False, True, True, True, False, False, False, False, False] + [False] * len(blocks),
        [VMEM((3, full, width), BF)]
        + [VMEM((full, width), BF)] * 3
        + [VMEM(shape, BF) for shape in kept]
        + [pltpu.SemaphoreType.DMA((6 * n_tp + 8,))]
        + [
            kind
            for array in blocks
            for kind in (VMEM(array.shape, BF), *swap_sems(array.shape[0], 1))
        ],
        collective_id=6,
        has_side_effects=True,
    )


def feed_forward(stream, grad_out, mod_rows, hot_rows, w_fc1, w_fc2, firsts, given):
    n_tp = lax.axis_size("tp")
    others = n_tp - 1
    count, width = stream.shape
    every = n_tp * count
    hidden = w_fc1.shape[1]
    half = hidden // 2
    padded = whole_tiles(half)
    clips = hot_rows.shape[1]
    pieces = 2 if half % LANES == 0 else 1

    def kernel(*refs):
        stream_ref, grad_ref, mod_ref, hot_ref, fc1_hbm, fc2_hbm = refs[:6]
        given_refs, refs = refs[6 : 6 + len(given)], refs[:6] + refs[6 + len(given) :]
        out_ref, h_all, up_keep, up_give, dy_all, down_keep, down_give, g_ref, mod_sum = refs[6:15]
        h_own, dy_own, h_got, dy_got = refs[15:19]
        given_got, refs = refs[19 : 19 + len(given)], refs[19 + len(given) :]
        w1, w2, h_land, total_y, total_h, send_y, send_h, land_y, land_h, sems, send_sem, recv_sem = refs[:12]
        moves = Moves(sems)
        loads = []
        for piece in range(pieces):
            cols = pl.ds(piece * (hidden // pieces), hidden // pieces)
            loads.append(
                (
                    moves.start(fc1_hbm.at[:, cols], w1.at[:, cols]),
                    moves.start(fc2_hbm.at[cols, :], w2.at[cols, :]),
                )
            )
        greet_devices(core_places() + pair_places())
        core = CoreCopies(send_sem, recv_sem)
        pairs = PairCopies(*refs[12:])
        for (unused, first), ref, target in zip(given, given_refs, given_got):
            pairs.start(ref, target, first)
        bit = [bit_of(first) for first in firsts]
        own = slice(0, count)
        gate = mod_ref[:, 2 * width :].astype(F32)
        dy_own[...] = (gate * grad_ref[...].astype(F32)).astype(BF)
        flights = [core.start(dy_own, h_land.at[n_tp - 2 - k], place) for k, place in enumerate(core_places())]
        pairs.start(dy_own, dy_got, firsts[1])
        shift = mod_ref[:, 0:width].astype(F32)
        scale = 1.0 + mod_ref[:, width : 2 * width].astype(F32)
        normed, inverse = norm_of(stream_ref[...])
        h_own[...] = (normed * scale + shift).astype(BF)
        flights += [
            core.start(h_own, h_land.at[others + n_tp - 2 - k], place) for k, place in enumerate(core_places())
        ]
        pairs.start(h_own, h_got, firsts[0])
        h_all[own, :] = h_own[...]
        dy_all[own, :] = dy_own[...]
        for pack in (up_keep, up_give, down_keep, down_give):
            if padded > half:
                pack[:, half:] = jnp.zeros((every, padded - half), BF)
        back = []
        for part in range(2):
            if part < pieces:
                for copy in loads[part]:
                    copy.wait()
            hid = slice(part * half, (part + 1) * half)
            for r in range(n_tp) if part == 0 else [*range(1, n_tp), 0]:
                at = slice(r * count, (r + 1) * count)
                if part == 0 and r == 1:
                    for copy in flights:
                        copy.wait()
                    for k in range(others):
                        there = slice((k + 1) * count, (k + 2) * count)
                        dy_all[there, :] = h_land[k]
                        h_all[there, :] = h_land[others + k]
                upper = dot_nn(h_all[at, :], w1[:, hid])
                square = upper * upper
                tanh = jnp.tanh(upper * (0.7978845608028654 + 0.035677408136300125 * square))
                rise = 0.5 + 0.5 * tanh
                active = (upper * rise).astype(BF)
                slope = rise + (0.5 * upper) * (1.0 - tanh * tanh) * (
                    0.7978845608028654 + 0.10703222440890037 * square
                )
                grad_upper = (dot_nt(dy_all[at, :], w2[hid, :]) * slope).astype(BF)
                for keep, give, mine, value in (
                    (up_keep, up_give, bit[0], grad_upper),
                    (down_keep, down_give, bit[1], active),
                ):

                    @pl.when(mine == part)
                    def _():
                        keep[at, 0:half] = value

                    @pl.when(mine != part)
                    def _():
                        give[at, 0:half] = value

                y_term = dot_nn(active, w2[hid, :])
                h_term = dot_nt(grad_upper, w1[:, hid])
                if part == 0:
                    total_y[at, :] = y_term
                    total_h[at, :] = h_term
                elif r == 0:
                    total_y[at, :] += y_term
                    total_h[at, :] += h_term
                else:
                    send_y[r - 1] = (total_y[at, :] + y_term).astype(BF)
                    send_h[r - 1] = (total_h[at, :] + h_term).astype(BF)
                    place = core_places()[r - 1]
                    back.append(core.start(send_y.at[r - 1], land_y.at[r - 1], place))
                    back.append(core.start(send_h.at[r - 1], land_h.at[r - 1], place))
        for copy in back:
            copy.wait()
        branch, grad_h = total_y[own, :], total_h[own, :]
        for k in range(others):
            branch = branch + land_y[k].astype(F32)
            grad_h = grad_h + land_h[k].astype(F32)
        gate = mod_ref[:, 2 * width :].astype(F32)
        out_ref[...] = (stream_ref[...] + gate * branch).astype(BF)
        grad = grad_ref[...].astype(F32)
        hot = hot_ref[...]
        mod_sum[:, 2 * width :] = dot_tn(hot, (grad * branch).astype(BF))
        mod_sum[:, 0:width] = dot_tn(hot, grad_h.astype(BF))
        normed, inverse = norm_of(stream_ref[...])
        mod_sum[:, width : 2 * width] = dot_tn(hot, (grad_h * normed).astype(BF))
        scale = 1.0 + mod_ref[:, width : 2 * width].astype(F32)
        g_ref[...] = grad + norm_back(grad_h * scale, normed, inverse)
        pairs.finish()

    side = like((every, padded))
    ins = [stream, grad_out, mod_rows, hot_rows, w_fc1, w_fc2] + [array for array, unused in given]
    n_pairs = 2 + len(given)
    square = (count, width)
    return call(
        kernel,
        [
            like(square),
            like((every, width)),
            side,
            side,
            like((every, width)),
            side,
            side,
            like(square, F32),
            like((clips, 3 * width), F32),
            like(square),
            like(square),
            like(square),
            like(square),
        ]
        + [like(array.shape) for array, unused in given],
        ins,
        [False] * 4 + [True] * (2 + len(given)),
        [False] * 11 + [True] * n_pairs,
        [
            VMEM((width, hidden), BF),
            VMEM((hidden, width), BF),
            VMEM((2 * others,) + square, BF),
            VMEM((every, width), F32),
            VMEM((every, width), F32),
            VMEM((others,) + square, BF),
            VMEM((others,) + square, BF),
            VMEM((others,) + square, BF),
            VMEM((others,) + square, BF),
            pltpu.SemaphoreType.DMA((4,)),
            pltpu.SemaphoreType.DMA((4 * others,)),
            pltpu.SemaphoreType.DMA((4 * others,)),
            pltpu.SemaphoreType.DMA((n_pairs,)),
            pltpu.SemaphoreType.DMA((n_pairs,)),
        ],
        collective_id=5,
        has_side_effects=True,
    )


def middle_backward(grad, kept, keyval, out_blocks, texts, tqkv_list, to_list, cq_list, co_list, in_first, given):
    n_tp = len(tqkv_list)
    h2, qkv, p2, inv2, h3, q3, p3, inv3 = kept
    count, width = grad.shape
    keys = keyval.shape[1]
    columns = to_list[0].shape[0]
    part = columns // 2
    heads = width // HD
    full = n_tp * columns
    in_slot = whole_tiles(4 * part)

    def kernel(*refs):
        grad_ref, inv2_ref, inv3_ref, h2_ref, h3_ref, block_ref, text_ref = refs[:7]
        qkv_hbm, p2_hbm, q3_hbm, p3_hbm, kv_hbm = refs[7:12]
        given_refs = refs[12 : 12 + len(given)]
        at = 12 + len(given)
        groups = []
        for unused in range(4):
            groups.append(refs[at : at + n_tp])
            at += n_tp
        tqkvs, tos, cqs, cos = groups
        in_keep, in_give, dy2_ref, dy3_ref, stream_ref, block_out, text_out = refs[at : at + 7]
        given_got = refs[at + 7 : at + 7 + len(given)]
        at += 2 + len(given)
        kv_outs = refs[at + 5 : at + 5 + n_tp]
        (
            w_qkv, w_o, w_q, w_c, qkv_ref, p2_ref, q3_ref, p3_ref, kv_ref,
            grad_attn, d_q, d_k, d_v, total, sems, recv, send_sem, recv_sem, text_recv, text_sem, text_recv_sem, pair_send, pair_recv,
        ) = refs[at + 5 + n_tp :]
        greet()
        exchange = Swap(block_ref, recv, send_sem, recv_sem)
        pairs = PairCopies(pair_send, pair_recv)
        for (unused, first), ref, target in zip(given, given_refs, given_got):
            pairs.start(ref, target, first)
        exchange.start()
        text_exchange = Swap(text_ref, text_recv, text_sem, text_recv_sem)
        text_exchange.start()
        moves = Moves(sems)
        c_in = fill_rows(moves, cos, w_c)
        kv_in = moves.start(kv_hbm, kv_ref)
        p3_in = moves.start(p3_hbm, p3_ref)
        q3_in = moves.start(q3_hbm, q3_ref)
        q_in = fill_rows(moves, cqs, w_q)
        o_in = fill_rows(moves, tos, w_o)
        qkv_load = moves.start(qkv_hbm, qkv_ref)
        p2_in = moves.start(p2_hbm, p2_ref)
        qkv_in = [
            [
                moves.start(tqkvs[r].at[i], w_qkv.at[i, pl.ds(r * columns, columns), :])
                for r in range(n_tp)
            ]
            for i in range(3)
        ]
        bit = bit_of(in_first)

        def split(value, r, mine, keep, give, low):
            first = value[:, r * columns : r * columns + part]
            second = value[:, r * columns + part : (r + 1) * columns]
            keep[:, low : low + part] = jnp.where(mine == 0, first, second)
            give[:, low : low + part] = jnp.where(mine == 0, second, first)

        def into(ref, upto):
            def write(low, high, value):
                ref[0:upto, low:high] = value.astype(BF)

            return write

        if in_slot > 4 * part:
            for pack in (in_keep, in_give):
                for r in range(n_tp):
                    spare = jnp.zeros((count, in_slot - 4 * part), BF)
                    pack[:, r * in_slot + 4 * part : (r + 1) * in_slot] = spare
        grad_y = grad_ref[...].astype(BF)
        dy3_ref[...] = grad_y
        for copy in c_in:
            copy.wait()
        grad_attn[...] = dot_nt(grad_y, w_c[...]).astype(BF)
        for copy in (kv_in, p3_in, q3_in):
            copy.wait()
        attend_back(
            lambda low, high: q3_ref[:, low:high],
            lambda low, high: kv_ref[0, :, low:high],
            lambda low, high: kv_ref[1, :, low:high],
            lambda low, high: grad_attn[:, low:high],
            lambda head: p3_ref[head],
            heads,
            width,
            into(d_q, count),
            into(d_k, keys),
            into(d_v, keys),
        )
        for r in range(n_tp):
            kv_outs[r][:, 0:columns] = d_k[0:keys, r * columns : (r + 1) * columns]
            kv_outs[r][:, columns:] = d_v[0:keys, r * columns : (r + 1) * columns]
            split(d_q[...], r, bit, in_keep, in_give, r * in_slot + 3 * part)
        for copy in q_in:
            copy.wait()
        grad_h = dot_nn(d_q[...], w_q[...])
        total[...] = grad_ref[...] + norm_back(grad_h, h3_ref[...].astype(F32), inv3_ref[:, 0:1])

        grad_y = total[...].astype(BF)
        dy2_ref[...] = grad_y
        for copy in o_in:
            copy.wait()
        grad_attn[...] = dot_nt(grad_y, w_o[...]).astype(BF)
        for copy in (qkv_load, p2_in):
            copy.wait()
        attend_back(
            lambda low, high: qkv_ref[0, :, low:high],
            lambda low, high: qkv_ref[1, :, low:high],
            lambda low, high: qkv_ref[2, :, low:high],
            lambda low, high: grad_attn[:, low:high],
            lambda head: p2_ref[head],
            heads,
            width,
            into(d_q, count),
            into(d_k, count),
            into(d_v, count),
        )
        for i, ref in enumerate((d_q, d_k, d_v)):
            for r in range(n_tp):
                split(ref[0:count, :], r, bit, in_keep, in_give, r * in_slot + i * part)
            for copy in qkv_in[i]:
                copy.wait()
            term = dot_nn(ref[0:count, :], w_qkv[i])
            grad_h = term if i == 0 else grad_h + term
        stream_ref[...] = (
            total[...] + norm_back(grad_h, h2_ref[...].astype(F32), inv2_ref[:, 0:1])
        ).astype(BF)
        pairs.finish()
        exchange.finish()
        block_out[...] = recv[...]
        text_exchange.finish()
        text_out[...] = text_recv[...]

    square = (count, width)
    in_pack = like((count, n_tp * in_slot))
    ins = [grad, inv2, inv3, h2, h3, out_blocks, texts, qkv, p2, q3, p3, keyval]
    ins = ins + [array for array, unused in given]
    ins = ins + [*tqkv_list, *to_list, *cq_list, *co_list]
    square_keys = (keys, width)
    return call(
        kernel,
        [in_pack, in_pack, like(square), like(square), like(square), like(out_blocks.shape), like(texts.shape)]
        + [like(array.shape) for array, unused in given]
        + [like((keys, 2 * columns))] * n_tp,
        ins,
        [False] * 7 + [True] * (5 + len(given) + 4 * n_tp),
        [False] * 7 + [True] * len(given) + [False] * n_tp,
        [VMEM((3, full, width), BF)]
        + [VMEM((full, width), BF)] * 3
        + [
            VMEM((3,) + square, BF),
            VMEM((heads, count, count), BF),
            VMEM(square, BF),
            VMEM((heads, count, keys), BF),
            VMEM((2,) + square_keys, BF),
            VMEM(square, BF),
            VMEM(square, BF),
            VMEM((max(count, keys), width), BF),
            VMEM((max(count, keys), width), BF),
            VMEM(square, F32),
            pltpu.SemaphoreType.DMA((6 * n_tp + 7,)),
            VMEM(out_blocks.shape, BF),
        ]
        + swap_sems(out_blocks.shape[0], 1)
        + [VMEM(texts.shape, BF)]
        + swap_sems(out_blocks.shape[0], 1)
        + swap_sems(len(given), 1),
        collective_id=7,
        has_side_effects=True,
    )


def spatial_backward(grad_y_list, probs, qkv, sqkv_rows, w_so, frames_here, given):
    n_tp = len(grad_y_list)
    rows, width = grad_y_list[0].shape
    columns = w_so.shape[0]
    part = columns // 2
    patch_part = rows // frames_here
    per_frame = n_tp * patch_part
    count = n_tp * rows
    heads = columns // HD
    side = whole_tiles(3 * part)

    def kernel(*refs):
        grads = refs[:n_tp]
        probs_hbm, qkv_hbm, wqkv_hbm, so_hbm = refs[n_tp : n_tp + 4]
        given_refs, refs = refs[n_tp + 4 : n_tp + 4 + len(given)], refs[: n_tp + 4] + refs[n_tp + 4 + len(given) :]
        keep, give, own_ref = refs[n_tp + 4 : n_tp + 7]
        others = refs[n_tp + 7 : 2 * n_tp + 6]
        grad_y = refs[2 * n_tp + 6]
        given_got, refs = refs[2 * n_tp + 7 : 2 * n_tp + 7 + len(given)], refs[2 * n_tp + 7 + len(given) :]
        w_qkv, w_o, qkv_ref, probs_ref, grad_attn, d_all, sems, pair_send, pair_recv = refs
        greet_devices(pair_places())
        pairs = PairCopies(pair_send, pair_recv)
        for (unused, first), ref, target in zip(given, given_refs, given_got):
            pairs.start(ref, target, first)
        if side > 3 * part:
            for ref in (keep, give):
                ref[:, 3 * part :] = jnp.zeros((count, side - 3 * part), BF)
        moves = Moves(sems)
        o_in = moves.start(so_hbm, w_o)
        qkv_in = moves.start(qkv_hbm, qkv_ref)
        probs_in = moves.start(probs_hbm, probs_ref)
        weight_in = moves.start(wqkv_hbm, w_qkv)
        for frame in range(frames_here):
            for r in range(n_tp):
                at = frame * per_frame + r * patch_part
                grad_y[at : at + patch_part, :] = grads[r][
                    frame * patch_part : (frame + 1) * patch_part, :
                ]
        o_in.wait()
        grad_attn[...] = dot_nt(grad_y[...], w_o[...]).astype(BF)
        qkv_in.wait()
        probs_in.wait()
        for frame in range(frames_here):
            at = slice(frame * per_frame, (frame + 1) * per_frame)

            def into(i, at=at):
                def write(low, high, value):
                    d_all[i, at, low:high] = value.astype(BF)

                return write

            attend_back(
                lambda low, high, at=at: qkv_ref[0, at, low:high],
                lambda low, high, at=at: qkv_ref[1, at, low:high],
                lambda low, high, at=at: qkv_ref[2, at, low:high],
                lambda low, high, at=at: grad_attn[at, low:high],
                lambda head, frame=frame: probs_ref[frame * heads + head],
                heads,
                columns,
                into(0),
                into(1),
                into(2),
            )
        mine = lax.rem(lax.axis_index("wide"), 2)
        weight_in.wait()
        for i in range(3):
            value = d_all[i]
            first, second = value[:, :part], value[:, part:]
            keep[:, i * part : (i + 1) * part] = jnp.where(mine == 0, first, second)
            give[:, i * part : (i + 1) * part] = jnp.where(mine == 0, second, first)
        for frame in range(frames_here):
            at = slice(frame * per_frame, (frame + 1) * per_frame)
            grad_h = dot_nn(d_all[0, at, :], w_qkv[0])
            for i in (1, 2):
                grad_h = grad_h + dot_nn(d_all[i, at, :], w_qkv[i])
            here = slice(frame * patch_part, (frame + 1) * patch_part)
            own_ref[here, :] = grad_h[:patch_part]
            for r in range(1, n_tp):
                others[r - 1][here, :] = grad_h[r * patch_part : (r + 1) * patch_part].astype(BF)
        pairs.finish()

    ins = [*grad_y_list, probs, qkv, sqkv_rows, w_so] + [array for array, unused in given]
    return call(
        kernel,
        [like((count, side))] * 2
        + [like((rows, width), F32)]
        + [like((rows, width))] * (n_tp - 1)
        + [like((count, width))]
        + [like(array.shape) for array, unused in given],
        ins,
        [False] * n_tp + [True] * (4 + len(given)),
        [False] * (n_tp + 3) + [True] * len(given),
        [
            VMEM((3, columns, width), BF),
            VMEM((columns, width), BF),
            VMEM((3, count, columns), BF),
            VMEM(probs.shape, BF),
            VMEM((count, columns), BF),
            VMEM((3, count, columns), BF),
            pltpu.SemaphoreType.DMA((4,)),
        ]
        + swap_sems(len(given), 1),
        collective_id=8,
        has_side_effects=True,
    )


def tokens_gradient(tokens_rows, grad, grad_h_own, grad_h_others, mod_here, frames_here, after):
    rows, width = tokens_rows.shape
    patch_part = rows // frames_here
    others = len(grad_h_others)

    def kernel(*refs):
        token_ref, grad_ref, own_ref = refs[:3]
        mod_ref, out_ref, sum_ref = refs[3 + others :]
        for frame in range(frames_here):
            at = slice(frame * patch_part, (frame + 1) * patch_part)
            grad_h = own_ref[at, :]
            for other in refs[3 : 3 + others]:
                grad_h = grad_h + other[at, :].astype(F32)
            normed, inverse = norm_of(token_ref[at, :].astype(F32))
            sum_ref[frame : frame + 1, 0:width] = jnp.sum(grad_h, axis=0, keepdims=True)
            sum_ref[frame : frame + 1, width:] = jnp.sum(grad_h * normed, axis=0, keepdims=True)
            scale = 1.0 + mod_ref[frame : frame + 1, width : 2 * width]
            out_ref[at, :] = (grad_ref[at, :] + norm_back(grad_h * scale, normed, inverse)).astype(BF)

    ins = [tokens_rows, grad, grad_h_own, *grad_h_others, mod_here]
    return call(
        kernel,
        [like((rows, width)), like((frames_here, 2 * width), F32)],
        ins,
        [False] * len(ins),
        [False] * 2,
        [],
        after,
    )


def flip(operand, mask):
    size = lax.axis_size("wide")
    return lax.ppermute(operand, "wide", [(s, s ^ mask) for s in range(size)])


def tp_from(operand, shift):
    size = lax.axis_size("tp")
    return lax.ppermute(operand, "tp", [(s, (s - shift) % size) for s in range(size)])


def tp_to(operand, shift):
    size = lax.axis_size("tp")
    return lax.ppermute(operand, "tp", [(s, (s + shift) % size) for s in range(size)])


def tp_gather(operand):
    return [operand] + [tp_from(operand, k) for k in range(1, lax.axis_size("tp"))]


class Pack:
    def __init__(self, first, order, layout):
        self.first, self.layout = first, layout
        self.order = order + [bit for bit in range(wide_bits()) if bit != first and bit not in order]
        self.across = sum(groups * cols for groups, cols in layout)


def scatter_rows(total, keep, give, pack, size):
    block = keep.shape[1]
    across = pack.across
    mine = bit_of(pack.order[0])
    inner = pack.order[1:] + [pack.first]
    for at in range(size // 2):
        parts = []
        for value in range(2):
            place = value << pack.order[0]
            for depth, bit in enumerate(inner):
                place |= ((at >> (len(inner) - 1 - depth)) & 1) << bit
            parts.append(total[place * block : (place + 1) * block, 0:across].astype(BF))
        keep[at] = jnp.where(mine == 0, parts[0], parts[1])
        give[at] = jnp.where(mine == 0, parts[1], parts[0])


class Flow:
    def __init__(self, pack, keep, give, lands, send_sem, recv_sem, outs):
        self.pack, self.keep, self.give, self.lands = pack, keep, give, lands
        self.send_sem, self.recv_sem, self.outs = send_sem, recv_sem, outs
        self.bits = pack.order + [pack.first]
        self.level, self.copy, self.placed = 0, None, False

    def send(self):
        if self.copy is not None or self.placed:
            return
        land = self.lands[self.level]
        bit = self.bits[self.level]
        self.copy = pltpu.make_async_remote_copy(
            src_ref=self.give.at[pl.ds(0, land.shape[0])],
            dst_ref=land,
            send_sem=self.send_sem.at[self.level],
            recv_sem=self.recv_sem.at[self.level],
            device_id={"wide": partner(bit)},
            device_id_type=pl.DeviceIdType.MESH,
        )
        self.copy.start()

    def wait(self):
        if self.placed:
            return
        self.send()
        self.copy.wait()
        self.copy = None
        land = self.lands[self.level]
        self.level += 1
        if self.level == len(self.bits):
            self.place(land)
            return
        half = land.shape[0] // 2
        mine = bit_of(self.bits[self.level])
        for at in range(half):
            here, there = mine * half + at, (1 - mine) * half + at
            own = (self.keep[here].astype(F32) + land[here].astype(F32)).astype(BF)
            other = (self.keep[there].astype(F32) + land[there].astype(F32)).astype(BF)
            self.give[at] = other
            if half == 1:
                self.keep[at] = own
            else:
                land[here] = own
        if half > 1:
            for at in range(half):
                self.keep[at] = land[mine * half + at]

    def go(self):
        self.wait()
        self.send()

    def place(self, land):
        self.placed = True
        mine = bit_of(self.pack.first)
        own, other = self.keep[0].astype(F32), land[0].astype(F32)
        sides = [jnp.where(mine == 0, own, other), jnp.where(mine == 0, other, own)]
        low = 0
        for out, (groups, cols) in zip(self.outs, self.pack.layout):
            for g in range(groups):
                for side in range(2):
                    value = sides[side][:, low + g * cols : low + (g + 1) * cols]
                    if groups == 1:
                        out[:, side * cols : (side + 1) * cols] = value
                    else:
                        out[g, :, side * cols : (side + 1) * cols] = value
            low += groups * cols


def reduce_all(ready_packs, rows_packs, slot_packs, kv_parts, mod_blocks, embed, texts, text_cols, ckv_rows, schedule, after, extra_rows=0):
    n_tp, size = lax.axis_size("tp"), lax.axis_size("wide")
    bits = wide_bits()
    packs = [member[0] for member in (*ready_packs, *rows_packs, *slot_packs)]
    n_ready, n_rows, n_slots = len(ready_packs), len(rows_packs), len(slot_packs)
    rows, width = rows_packs[0][2].shape
    count = n_tp * rows
    block = width // size
    others = n_tp - 1
    most = max(whole_tiles(member[0].across) for member in rows_packs)
    token_rows = slot_packs[0][3].shape[0]
    models = len(slot_packs[0][1])
    slot_width = max(member[3].shape[1] for member in slot_packs)
    keys, columns = kv_parts[0].shape[0] * kv_parts[0].shape[1], kv_parts[0].shape[2]
    context_cols = width // size
    owned = width // n_tp

    row_ins = [array for member in rows_packs for array in member[1:5]]
    slot_ins = [array for member in slot_packs for array in (*member[1], *member[2], *member[3:5])]
    ready_ins = [array for member in ready_packs for array in member[1:]]
    ins = ready_ins + row_ins + slot_ins + [ckv_rows, texts, mod_blocks, embed] + list(kv_parts)
    in_any = [True] * (len(ready_ins) + len(row_ins) + len(slot_ins) + 1) + [False] * 3 + [True] * len(kv_parts)
    result = []
    for pack in packs:
        for groups, cols in pack.layout:
            result.append(like((block, 2 * cols) if groups == 1 else (groups, block, 2 * cols), F32))
    landing = [like((rows, width))] * (n_rows * others)
    for member in slot_packs:
        landing += [like((token_rows, width))] * (2 * models * others)
        landing += [like(member[3].shape)] * (2 * others)
    pairs = [p for p, member in enumerate(rows_packs) if member[6]]
    landing += [like(rows_packs[p][4].shape) for p in pairs]
    spare = mod_blocks.shape[1]
    kv_block_rows = kv_parts[0].shape[1]
    clips = embed.shape[0]
    mod_row = kv_block_rows if extra_rows else kv_block_rows - spare
    mod_cols = 6 * width // (n_tp * size)
    outs = result + [like((context_cols, columns), F32), like((owned, text_cols), F32)]
    outs += [like((mod_cols, width), F32), like((1, mod_cols), F32)] + landing
    out_any = [False] * (len(result) + 4) + [True] * len(landing)
    scratch = [VMEM((count, width), BF)] * 2 + [VMEM((count, most), BF)] * 2
    scratch += [VMEM((token_rows, width), BF)] * (2 * n_tp * models)
    scratch += [VMEM((token_rows, slot_width), BF)] * (2 * n_tp)
    scratch += [VMEM((width, max(pack.across for pack in packs)), F32)]
    for pack in packs:
        shape = (block, pack.across)
        scratch += [VMEM((size // 2,) + shape, BF)] * 2
        scratch += [VMEM((size >> (s + 1),) + shape, BF) for s in range(bits)]
        scratch += [pltpu.SemaphoreType.DMA((bits,))] * 2
    n_core = others * (n_rows + 2 * (models + 1) * n_slots + 2)
    n_moves = n_rows * 3 + sum(member[5] * n_tp for member in rows_packs) + 2 * n_tp * n_slots * (models + 1) + 1 + 2 * n_ready + n_tp
    kv_block = kv_parts[0].shape[1:]
    sum_block = (kv_block[0] + extra_rows, kv_block[1])
    kv_scratch = level_scratch(size, sum_block) + level_scratch(size, sum_block)[1:] + level_scratch(size, kv_block)
    scratch += [pltpu.SemaphoreType.DMA((n_core,))] * 2 + [pltpu.SemaphoreType.DMA((n_moves,))]
    scratch += [VMEM(kv_parts[0].shape, BF)] + kv_scratch + [pltpu.SemaphoreType.DMA((bits,))] * 4
    scratch += [VMEM((keys, columns), BF), VMEM((columns, width), BF), VMEM((2 * others, keys, owned), BF)]
    scratch += [VMEM((keys, owned), F32), VMEM((2 * others, 8, whole_tiles(clips * mod_cols)), F32)]
    scratch += [pltpu.SemaphoreType.DMA((max(len(pairs), 1),))] * 2

    def kernel(*refs):
        refs = list(refs)

        def take(number):
            taken = refs[:number]
            del refs[:number]
            return taken

        ready_refs = [take(2) for unused in range(n_ready)]
        row_refs = [take(4) for unused in range(n_rows)]
        slot_refs = [[take(models), take(models), take(2)] for unused in range(n_slots)]
        ckv_ref, text_ref, mod_ref, embed_ref = take(4)
        kv_refs = take(len(kv_parts))
        results = [take(len(pack.layout)) for pack in packs]
        grad_ckv, grad_text, grad_mod, grad_bias = take(4)
        row_land = [take(others) for unused in range(n_rows)]
        slot_land = [
            [[take(models) for unused in range(2)] for unused2 in range(others)]
            + [[take(others) for unused in range(2)]]
            for unused3 in range(n_slots)
        ]
        pair_land = dict(zip(pairs, take(len(pairs))))
        own_model, got_model, own_head, got_head = take(4)
        model_stages = [take(models) for unused in range(2 * n_tp)]
        stages = take(2 * n_tp)
        (total,) = take(1)
        flows = []
        for pack, result_refs in zip(packs, results):
            keep, give = take(2)
            lands = take(bits)
            flows.append(Flow(pack, keep, give, lands, *take(2), result_refs))
        send_sem, recv_sem, move_sem, kv_stage = take(4)
        halving_levels, halving_lands, doubling_levels = take(bits + 1), take(bits), take(bits + 1)
        kv_sems = take(4)
        kv_all, ckv, exchange, text_own, mod_exchange, pair_send, pair_recv = take(7)

        greet_devices(core_places() + pair_places())
        moves = Moves(move_sem)
        core = CoreCopies(send_sem, recv_sem)
        for i, ref in enumerate(kv_refs):
            moves.start(ref, kv_stage).wait()
            for at in range(size):
                value = kv_stage[at].astype(F32)
                level = halving_levels[0].at[mirrored(at)]
                if i == 0:
                    if extra_rows:
                        value = jnp.concatenate([value, jnp.zeros((extra_rows, kv_block[1]), F32)], axis=0)
                    row = lax.broadcasted_iota(jnp.int32, sum_block, 0)
                    for j in range(spare):
                        value = jnp.where(row == mod_row + j, mod_ref[at, j : j + 1, :], value)
                    level[...] = value.astype(BF)
                else:
                    own = level[0 : kv_block[0], :].astype(F32)
                    level[0 : kv_block[0], :] = (own + value).astype(BF)
        ready_loads = [
            (moves.start(give, flows[p].give), moves.start(keep, flows[p].keep))
            for p, (keep, give) in enumerate(ready_refs)
        ]
        halving = Halving(halving_levels, halving_lands, *kv_sems[:2])
        halving.start()
        doubling = Doubling(doubling_levels, *kv_sems[2:])

        pair_flights = {}
        for i, p in enumerate(pairs):
            copy = pltpu.make_async_remote_copy(
                src_ref=row_refs[p][3],
                dst_ref=pair_land[p],
                send_sem=pair_send.at[i],
                recv_sem=pair_recv.at[i],
                device_id={"wide": partner(rows_packs[p][0].first)},
                device_id_type=pl.DeviceIdType.MESH,
            )
            copy.start()
            pair_flights[p] = copy
        row_flights, slot_flights = {}, {}

        def core_rows(p):
            row_flights[p] = [
                core.start(row_refs[p][1], row_land[p][n_tp - 2 - k], place)
                for k, place in enumerate(core_places())
            ]

        def core_slots(p):
            slot = slot_packs[p][5]
            flights = []
            for k, place in enumerate(core_places()):
                for side in range(2):
                    for ref, to in zip(slot_refs[p][side], slot_land[p][k][side]):
                        flights.append(core.start(ref, to, place))
                    ref, to = slot_refs[p][2][side], slot_land[p][others][side][k]
                    cols = pl.ds((k + 1) * slot, slot)
                    flights.append(core.start(ref.at[:, cols], to.at[:, cols], place))
            slot_flights[p] = flights

        ckv_in = moves.start(ckv_ref, ckv)
        loads = {}

        def load_rows(p):
            model, got, keep, other = row_refs[p]
            frames = rows_packs[p][5]
            step = rows // frames
            cols = pl.ds(0, keep.shape[1])
            loads[p] = [moves.start(model, own_model), moves.start(keep, own_head.at[:, cols])]
            if p in pair_flights:
                pair_flights[p].wait()
                other = pair_land[p]
            loads[p].append(moves.start(other, got_head.at[:, cols]))
            for frame in range(frames):
                target = got_model.at[pl.ds(frame * n_tp * step, step), :]
                loads[p].append(moves.start(got.at[pl.ds(frame * step, step), :], target))

        def rows_product(p):
            frames = rows_packs[p][5]
            step = rows // frames
            across = rows_packs[p][0].across
            for copy in loads[p][:2]:
                copy.wait()
            total[:, 0:across] = dot_tn(own_model[...], own_head[:, 0:across])
            for copy in row_flights[p]:
                copy.wait()
            rest = loads[p][2:]
            for frame in range(frames):
                for k in range(others):
                    target = got_model.at[pl.ds((frame * n_tp + k + 1) * step, step), :]
                    rest.append(moves.start(row_land[p][k].at[pl.ds(frame * step, step), :], target))
            for copy in rest:
                copy.wait()
            total[:, 0:across] += dot_tn(got_model[...], got_head[:, 0:across])
            flow = flows[n_ready + p]
            scatter_rows(total, flow.keep, flow.give, rows_packs[p][0], size)

        def stage(p, side, k):
            wide = slot_packs[p][3].shape[1]
            at = 2 * k + side
            if k == 0:
                model_refs, head = slot_refs[p][side], slot_refs[p][2][side]
            else:
                model_refs, head = slot_land[p][k - 1][side], slot_land[p][others][side][k - 1]
            found = [moves.start(ref, to) for ref, to in zip(model_refs, model_stages[at])]
            return found + [moves.start(head, stages[at].at[:, pl.ds(0, wide)])]

        def load_slots(p):
            loads[n_rows + p] = stage(p, 0, 0) + stage(p, 1, 0)

        def slots_product(p):
            pack, unused, unused2, unused3, unused4, slot, weights = slot_packs[p]

            def add(k):
                low = 0
                for model, column, cols in weights:
                    at = k * slot + column
                    terms = [
                        dot_tn(model_stages[2 * k + side][model][...], stages[2 * k + side][:, at : at + cols])
                        for side in range(2)
                    ]
                    if k == 0:
                        total[:, low : low + cols] = terms[0] + terms[1]
                    else:
                        total[:, low : low + cols] += terms[0] + terms[1]
                    low += cols

            for copy in loads[n_rows + p]:
                copy.wait()
            add(0)
            for copy in slot_flights[p]:
                copy.wait()
            rest = [copy for k in range(1, n_tp) for side in range(2) for copy in stage(p, side, k)]
            for copy in rest:
                copy.wait()
            for k in range(1, n_tp):
                add(k)
            flow = flows[n_ready + n_rows + p]
            scatter_rows(total, flow.keep, flow.give, pack, size)

        def caption():
            if halving.bit < bits:
                halving.advance()
                if halving.bit == bits:
                    doubling_levels[bits][0] = halving_levels[bits][0, 0 : kv_block[0], :]
                    doubling.start()
            elif doubling.bit:
                doubling.advance()

        text_flights = []

        def context():
            while doubling.bit:
                caption()
            for at in range(size):
                kv_all[at * kv_block[0] : (at + 1) * kv_block[0], :] = doubling_levels[0][mirrored(at)]
            grad_ckv[...] = dot_tn(text_ref[:, text_cols : text_cols + context_cols], kv_all[...])
            ckv_in.wait()
            grad = dot_nn(kv_all[...], ckv[...])
            here = lax.axis_index("tp")

            def part(owner):
                chosen = grad[:, 0:owned]
                for other in range(1, n_tp):
                    chosen = jnp.where(owner == other, grad[:, other * owned : (other + 1) * owned], chosen)
                return chosen

            for k, place in enumerate(core_places()):
                exchange[k] = part(lax.rem(here + k + 1, n_tp)).astype(BF)
                text_flights.append(core.start(exchange.at[k], exchange.at[others + k], place))
            text_own[...] = part(here)

        def text():
            grad = text_own[...]
            for k, copy in enumerate(text_flights):
                copy.wait()
                grad = grad + exchange[others + k].astype(F32)
            grad_text[...] = dot_tn(grad.astype(BF), text_ref[:, 0:text_cols])

        mod_flights = []
        flat = clips * mod_cols

        def modulation_part(owner):
            rows_here = halving_levels[bits][0].astype(F32)[mod_row : mod_row + spare, :]
            row = jnp.concatenate([rows_here[i : i + 1] for i in range(spare)], axis=1)
            chosen = row[:, 0:flat]
            for other in range(1, n_tp):
                chosen = jnp.where(owner == other, row[:, other * flat : (other + 1) * flat], chosen)
            return chosen

        def modulation_send():
            here = lax.axis_index("tp")
            for k, place in enumerate(core_places()):
                part = modulation_part(lax.rem(here + k + 1, n_tp))
                mod_exchange[k, :, 0:flat] = jnp.broadcast_to(part, (8, flat))
                if mod_exchange.shape[2] > flat:
                    mod_exchange[k, :, flat:] = jnp.zeros((8, mod_exchange.shape[2] - flat), F32)
                mod_flights.append(core.start(mod_exchange.at[k], mod_exchange.at[others + k], place))

        def modulation():
            total_row = modulation_part(lax.axis_index("tp"))
            for k, copy in enumerate(mod_flights):
                copy.wait()
                total_row = total_row + mod_exchange[others + k, 0:1, 0:flat]
            sums = jnp.concatenate(
                [total_row[:, c * mod_cols : (c + 1) * mod_cols] for c in range(clips)], axis=0
            )
            grad_bias[...] = jnp.sum(sums, axis=0, keepdims=True)
            grad_mod[...] = dot_tn(sums.astype(BF), embed_ref[...])

        for what, p in schedule:
            row, slot = p - n_ready, p - n_ready - n_rows
            if what == "core":
                core_rows(row) if slot < 0 else core_slots(slot)
            elif what == "load":
                load_rows(row) if slot < 0 else load_slots(slot)
            elif what == "product":
                if row < 0:
                    for copy in ready_loads[p]:
                        copy.wait()
                elif slot < 0:
                    rows_product(row)
                else:
                    slots_product(slot)
            elif what == "send":
                flows[p].send()
            elif what == "wait":
                flows[p].wait()
            elif what == "go":
                flows[p].go()
            elif what == "caption":
                caption()
            elif what == "context":
                context()
                modulation_send()
            elif what == "modulation":
                modulation()
            else:
                text()
        while not all(flow.placed for flow in flows):
            for flow in flows:
                flow.go()

    out = call(
        kernel,
        outs,
        ins,
        in_any,
        out_any,
        scratch,
        after,
        limit=63,
        collective_id=4,
        has_side_effects=True,
    )
    return out[: len(result)], *out[len(result) : len(result) + 4]


def tp_sum(parts, dtype=BF):
    total = parts[0].astype(F32)
    for k in range(1, lax.axis_size("tp")):
        total = total + tp_to(parts[k].astype(dtype), k).astype(F32)
    return total


def tp_ordered(relative):
    size = lax.axis_size("tp")
    start = (size - lax.axis_index("tp")) % size
    return lax.dynamic_slice_in_dim(jnp.stack(relative + relative), start, size, axis=0)


def swap_wide(blocks):
    return lax.all_to_all(blocks, "wide", split_axis=0, concat_axis=0, tiled=True)


def on_device(
    tokens,
    cotangent,
    caption,
    caption_len,
    clip_id,
    timestep,
    w_mod,
    b_mod,
    w_text,
    w_sqkv,
    w_so,
    w_tqkv,
    w_to,
    w_cq,
    w_ckv,
    w_co,
    w_fc1,
    w_fc2,
):
    n_tp = lax.axis_size("tp")
    n_wide = lax.axis_size("wide")
    frames_here, patch_part, width = tokens.shape
    columns = w_so.shape[0]
    part = columns // 2
    half = w_fc1.shape[1] // 2
    clip_count = timestep.shape[0]
    frames = clip_id.shape[0]
    patch_here = patch_part // n_wide
    rows = frames_here * patch_part
    block = frames_here * patch_here
    count = frames * patch_here
    wide_at = lax.axis_index("wide")
    tp_at = lax.axis_index("tp")

    tokens_rows = tokens.reshape(rows, width)
    tokens_list = tp_gather(tokens_rows)
    sqkv_rows = w_sqkv.transpose(1, 2, 0)
    tqkv_list = tp_gather(w_tqkv.transpose(1, 2, 0))
    to_list = tp_gather(w_to)
    cq_list = tp_gather(w_cq.T)
    co_list = tp_gather(w_co)

    half_width = width // 2
    frequencies = jnp.exp(-math.log(10000.0) * jnp.arange(half_width).astype(F32) / half_width)
    angles = timestep.astype(F32)[:, None] * frequencies[None, :]
    embedding = jnp.concatenate([jnp.cos(angles), jnp.sin(angles)], axis=1)
    silu_embed = jax.nn.silu(embedding).astype(BF)
    mod_part = (dot_nn(silu_embed, w_mod) + b_mod.astype(F32)).astype(BF)
    modulation = tp_ordered(tp_gather(mod_part)).transpose(1, 0, 2).reshape(clip_count, -1)
    clip_hot = clip_id[:, None] == jnp.arange(clip_count)[None, :]
    hot_here = lax.dynamic_slice_in_dim(
        clip_hot.astype(F32), wide_at * frames_here, frames_here
    )
    mod_here = dot_nn(hot_here.astype(BF), modulation[:, : 3 * width])
    clip_rows = jnp.broadcast_to(clip_id[:, None], (frames, patch_here)).reshape(count)
    hot_rows = (clip_rows[:, None] == jnp.arange(clip_count)[None, :]).astype(BF)
    mod_rows = dot_nn(hot_rows, modulation[:, 3 * width :]).astype(BF)

    caption_rows = caption.shape[0]
    spare_rows = -(-clip_count * 6 * width // (n_wide * 2 * columns))
    block_rows = -(-caption_rows // 16) * 16
    extra_rows = 0 if caption_rows + spare_rows <= block_rows else -(-spare_rows // 16) * 16
    keys = n_wide * block_rows
    padded = jnp.pad(caption, ((0, block_rows - caption_rows), (0, 0)))
    context_part = dot_nt(padded, w_text.T).astype(BF)
    context = tp_ordered(tp_gather(context_part)).transpose(1, 0, 2).reshape(block_rows, width)
    ckv_rows = w_ckv.transpose(1, 2, 0).reshape(2 * columns, width)
    keyval_part = dot_nt(context, ckv_rows).astype(BF)
    text_cols = caption.shape[1] // n_wide
    context_cols = width // n_wide
    spare = -(text_cols + context_cols) % LANES
    texts = jnp.concatenate(
        [
            padded.reshape(block_rows, n_wide, text_cols),
            context.reshape(block_rows, n_wide, context_cols),
            jnp.zeros((block_rows, n_wide, spare), BF),
        ],
        axis=2,
    ).transpose(1, 0, 2)

    row_two = clip_rows * patch_here + np.arange(count, dtype=np.int32) % patch_here
    key_at = np.arange(keys)
    key_row = key_at // block_rows * caption_rows + key_at % block_rows
    key_real = jnp.asarray(key_at % block_rows < caption_rows)[None, :]
    key_clip = (key_row // LTXT).astype(np.int32)[None, :]
    key_in = (key_row % LTXT).astype(np.int32)[None, :]
    key_three = jnp.full((1, keys), -1, jnp.int32)
    for clip in range(clip_count):
        seen = key_real & (key_clip == clip) & (key_in < caption_len[clip])
        key_three = jnp.where(seen, clip, key_three)
    row_codes = jnp.stack([row_two, clip_rows], axis=1)
    longest = max(count, keys)
    key_codes = jnp.concatenate(
        [jnp.pad(row_two[None, :], ((0, 0), (0, longest - count))), jnp.pad(key_three, ((0, 0), (0, longest - keys)))]
    )

    grad_blocks = cotangent.reshape(frames_here, n_wide, patch_here, width).transpose(1, 0, 2, 3)
    grad_blocks = grad_blocks.reshape(n_wide, block, width)

    up = Pack(0, [1, 3, 2], [(1, half)])
    down = Pack(1, [2, 0, 3], [(1, half)])
    inner = Pack(2, [0, 1, 3], [(3, part), (1, part)])
    outer = Pack(0, [3, 1, 2], [(1, part), (1, part)])
    q_pack = Pack(0, [1, 2, 3], [(3, part)])
    o_pack = Pack(1, [0, 2, 3], [(1, part)])

    h_all, h_own, qkv_one, probs_one, a_keep, a_give, y_own, *others = spatial_forward(
        tokens_list, mod_here, sqkv_rows, w_so, frames_here, keyval_part, o_pack.first
    )
    y_others, keyval = others[: n_tp - 1], others[n_tp - 1]
    keyval_list = tp_gather(keyval.reshape(keys, 2 * columns))
    y_others = [tp_to(other, k + 1) for k, other in enumerate(y_others)]
    h_flip = flip(h_own, 1)
    a_got = flip(a_give, 1 << o_pack.first)
    stream, y_one = stream_to_patches(tokens_rows, y_own, y_others, mod_here, frames_here)
    *kept, stream, keyval_full, t_keep, t_give, grad_out = middle_forward(
        stream.reshape(count, width), row_codes, key_codes, [grad_blocks], keyval_list, tqkv_list, to_list, cq_list, co_list, outer.first
    )
    grad_out = grad_out.reshape(count, width)
    h2, h3 = kept[0], kept[4]
    (
        block_out,
        h4_all,
        up_keep,
        up_give,
        dy4_all,
        down_keep,
        down_give,
        grad,
        mod_sum,
        unused,
        unused,
        h4_got,
        dy4_got,
        h2_got,
        h3_got,
        t_got,
    ) = feed_forward(
        stream,
        grad_out,
        mod_rows,
        hot_rows,
        w_fc1,
        w_fc2,
        [up.first, down.first],
        [(h2, inner.first), (h3, inner.first), (t_give, outer.first)],
    )

    in_keep, in_give, dy2, dy3, grad, block_out, texts, up_got, down_got, *grad_kv = middle_backward(
        grad,
        kept,
        keyval_full,
        block_out.reshape(n_wide, block, width),
        texts,
        tqkv_list,
        to_list,
        cq_list,
        co_list,
        inner.first,
        [(up_give, up.first), (down_give, down.first)],
    )
    block_out = block_out.reshape(n_wide, frames_here, patch_here, width).transpose(1, 0, 2, 3)
    block_out = block_out.reshape(frames_here, patch_part, width)
    (grad_stream, grad_y1, grad_gate), (up_halves, down_halves) = grads_to_frames(
        grad.reshape(n_wide, block, width),
        y_one,
        mod_here,
        frames_here,
        [(up, h4_all, h4_got, up_keep, up_got), (down, dy4_all, dy4_got, down_keep, down_got)],
    )
    grad_y1_list = tp_gather(grad_y1)
    given = [(in_give, inner.first), (dy2, outer.first), (dy3, outer.first), (grad_y1, o_pack.first)]
    q_keep, q_give, grad_h_own, *grad_h_others, dy_all, in_got, dy2_got, dy3_got, dy_got = spatial_backward(
        grad_y1_list, probs_one, qkv_one, sqkv_rows, w_so, frames_here, given
    )
    grad_h_others = [tp_to(other, k + 1) for k, other in enumerate(grad_h_others)]
    grad_tokens, frame_sums = tokens_gradient(
        tokens_rows, grad_stream, grad_h_own, grad_h_others, mod_here, frames_here, []
    )
    frame_sums = jnp.concatenate([frame_sums, grad_gate], axis=1)
    here_sum = lax.dot_general(hot_here, frame_sums, (((0,), (0,)), ((), ())), precision=HIGH)
    grad_mod = jnp.concatenate([here_sum, mod_sum], axis=1).reshape(clip_count, n_tp, n_wide, -1)
    mod_blocks = grad_mod.transpose(2, 1, 0, 3).reshape(n_wide, -1)
    mod_blocks = jnp.pad(mod_blocks, ((0, 0), (0, spare_rows * 2 * columns - mod_blocks.shape[1])))
    mod_blocks = mod_blocks.reshape(n_wide, spare_rows, 2 * columns)
    kv_parts = [grad_kv[0].reshape(n_wide, block_rows, -1)]
    kv_parts += [tp_to(grad_kv[k], k).reshape(n_wide, block_rows, -1) for k in range(1, n_tp)]
    schedule = [
        ("core", 5), ("core", 3), ("load", 5), ("load", 3), ("product", 0), ("send", 0),
        ("product", 1), ("send", 1), ("product", 5), ("core", 4), ("load", 4), ("send", 5),
        ("product", 3), ("core", 2), ("send", 3), ("product", 4), ("wait", 3), ("send", 4),
        ("caption", 0), ("wait", 0), ("load", 2), ("product", 2), ("send", 2), ("send", 0),
        ("wait", 5), ("send", 5), ("caption", 0), ("wait", 1), ("send", 1), ("send", 3),
        ("wait", 5), ("caption", 0), ("wait", 4), ("send", 4), ("wait", 3), ("send", 5),
        ("caption", 0), ("wait", 0), ("send", 3), ("send", 0), ("wait", 5), ("send", 5),
        ("caption", 0), ("wait", 1), ("send", 1), ("wait", 2), ("caption", 0), ("wait", 5),
        ("wait", 3), ("send", 3), ("caption", 0), ("wait", 3), ("send", 2), ("wait", 4),
        ("caption", 0), ("wait", 0), ("send", 0), ("wait", 0), ("send", 4), ("context", 0),
        ("wait", 1), ("send", 1), ("text", 0), ("wait", 1), ("modulation", 0), ("wait", 2),
        ("send", 2), ("wait", 4), ("send", 4), ("wait", 2), ("send", 2), ("wait", 4),
        ("wait", 2),
    ]
    gradients, grad_ckv, grad_text, grad_w_mod, grad_b_mod = reduce_all(
        [(up, *up_halves), (down, *down_halves)],
        [
            (q_pack, h_all, h_flip, q_keep, q_give, frames_here, True),
            (o_pack, dy_all, dy_got, a_keep, a_got, frames_here, False),
        ],
        [
            (
                inner,
                [h2, h3],
                [h2_got, h3_got],
                in_keep,
                in_got,
                whole_tiles(4 * part),
                [(0, 0, 3 * part), (1, 3 * part, part)],
            ),
            (
                outer,
                [dy2, dy3],
                [dy2_got, dy3_got],
                t_keep,
                t_got,
                whole_tiles(2 * part),
                [(0, 0, part), (1, part, part)],
            ),
        ],
        kv_parts,
        mod_blocks,
        silu_embed,
        texts.reshape(keys, -1),
        text_cols,
        ckv_rows,
        schedule,
        [grad_tokens],
        extra_rows,
    )
    grad_fc1, grad_fc2, grad_sqkv, grad_so, grad_tqkv, grad_cq, grad_to, grad_co = gradients
    grad_ckv = grad_ckv.reshape(-1, 2, columns)
    grad_text = grad_text.T

    return (
        block_out,
        grad_tokens.reshape(tokens.shape),
        grad_w_mod.T,
        grad_b_mod.reshape(-1),
        grad_text,
        grad_sqkv.transpose(1, 0, 2),
        grad_so.T,
        grad_tqkv.transpose(1, 0, 2),
        grad_to.T,
        grad_cq,
        grad_ckv,
        grad_co.T,
        grad_fc1,
        grad_fc2.T,
    )


def solution(mesh):
    placed = (
        P("wide", "tp", None),
        P("wide", "tp", None),
        P("wide", None),
        P(),
        P(),
        P(),
        P(None, "tp"),
        P("tp"),
        P(None, "tp"),
        P(None, None, "tp"),
        P("tp", None),
        P(None, None, "tp"),
        P("tp", None),
        P(None, "tp"),
        P(None, None, "tp"),
        P("tp", None),
        P(None, "tp"),
        P("tp", None),
    )
    return jax.shard_map(
        on_device,
        mesh=mesh,
        in_specs=placed,
        out_specs=(
            P("wide", "tp", None),
            P("wide", "tp", None),
            P(None, ("tp", "wide")),
            P(("tp", "wide")),
            P("wide", "tp"),
            P("wide", None, "tp"),
            P("tp", "wide"),
            P("wide", None, "tp"),
            P("tp", "wide"),
            P("wide", "tp"),
            P("wide", None, "tp"),
            P("tp", "wide"),
            P("wide", "tp"),
            P("tp", "wide"),
        ),
        check_vma=False,
    )
```

```python
import functools
import math

import jax
import jax.numpy as jnp
import numpy as np
from jax import lax
from jax.experimental import pallas as pl
from jax.experimental.pallas import tpu as pltpu
from jax.sharding import PartitionSpec as P

HD = 72
LTXT = 120
EPS = 1e-06
NEGATIVE = -1e30
HIGH = lax.Precision.HIGHEST
BF = jnp.bfloat16
F32 = jnp.float32
LANES = 128
FACTOR = HD ** (-0.5)
VMEM = pltpu.VMEM
MB = 1 << 20


def dot_nn(left, right):
    return lax.dot_general(left, right, (((1,), (0,)), ((), ())), preferred_element_type=F32)


def dot_nt(left, right):
    return lax.dot_general(left, right, (((1,), (1,)), ((), ())), preferred_element_type=F32)


def dot_tn(left, right):
    return lax.dot_general(left, right, (((0,), (0,)), ((), ())), preferred_element_type=F32)


def norm_of(rows):
    average = jnp.mean(rows, axis=-1, keepdims=True)
    centred = rows - average
    inverse = lax.rsqrt(jnp.mean(centred * centred, axis=-1, keepdims=True) + EPS)
    return centred * inverse, inverse


def norm_back(grad_normed, normed, inverse):
    grad_mean = jnp.mean(grad_normed, axis=-1, keepdims=True)
    grad_cross = jnp.mean(grad_normed * normed, axis=-1, keepdims=True)
    return inverse * (grad_normed - grad_mean - normed * grad_cross)


def window(head, columns):
    low = HD * head
    start = low // LANES * LANES
    stop = min(-(-(low + HD) // LANES) * LANES, columns)
    at = lax.broadcasted_iota(jnp.int32, (1, stop - start), 1) + start
    own = jnp.where((at >= low) & (at < low + HD), 1.0, 0.0).astype(BF)
    return start, stop, own


class Tiles:
    def __init__(self, write, columns, scale=None):
        self.write, self.columns, self.scale, self.open = write, columns, scale, {}

    def add(self, start, stop, value):
        for low in range(start, stop, LANES):
            part = value[:, low - start : min(low + LANES, stop) - start]
            self.open[low] = self.open[low] + part if low in self.open else part

    def flush(self, below):
        for low in sorted(self.open):
            if low + LANES <= below or below >= self.columns:
                part = self.open.pop(low)
                if self.scale is not None:
                    part = part * self.scale
                self.write(low, min(low + LANES, self.columns), part)


def attend(query, key, value, bias, heads, columns, keep_probs, write, between=None):
    out = Tiles(write, columns)
    for head in range(heads):
        start, stop, own = window(head, columns)
        scores = dot_nt(query(start, stop) * own, key(start, stop)) * FACTOR
        if bias is not None:
            scores = scores + bias
        scores = jnp.exp(scores - jnp.max(scores, axis=-1, keepdims=True))
        probs = (scores * (1.0 / jnp.sum(scores, axis=-1, keepdims=True))).astype(BF)
        keep_probs(head, probs)
        out.add(start, stop, dot_nn(probs, value(start, stop) * own))
        out.flush(HD * (head + 1))
        if between is not None and head == heads // 2:
            between()


def attend_back(query, key, value, grad_out, probs_of, heads, columns, write_q, write_k, write_v):
    grad_q = Tiles(write_q, columns, FACTOR)
    grad_k = Tiles(write_k, columns, FACTOR)
    grad_v = Tiles(write_v, columns)
    for head in range(heads):
        start, stop, own = window(head, columns)
        probs = probs_of(head)
        grad_own = grad_out(start, stop) * own
        grad_probs = dot_nt(grad_own, value(start, stop))
        wide_probs = probs.astype(F32)
        grad_scores = wide_probs * grad_probs
        row = jnp.sum(grad_scores, axis=-1, keepdims=True)
        grad_scores = (grad_scores - wide_probs * row).astype(BF)
        grad_q.add(start, stop, dot_nn(grad_scores, key(start, stop) * own))
        grad_k.add(start, stop, dot_tn(grad_scores, query(start, stop) * own))
        grad_v.add(start, stop, dot_tn(probs, grad_own))
        for tiles in (grad_q, grad_k, grad_v):
            tiles.flush(HD * (head + 1))


class Moves:
    def __init__(self, sems):
        self.sems, self.used = sems, 0

    def start(self, source, target):
        copy = pltpu.make_async_copy(source, target, self.sems.at[self.used])
        self.used += 1
        copy.start()
        return copy


def any_spec():
    return pl.BlockSpec(memory_space=pl.ANY)


def vmem_spec():
    return pl.BlockSpec(memory_space=VMEM)


def call(kernel, outs, ins, in_any, out_any, scratch, after=(), limit=56, **params):
    given, extra = len(ins), len(after)

    def ordered(*refs):
        kernel(*refs[:given], *refs[given + extra :])

    return pl.pallas_call(
        ordered,
        out_shape=tuple(outs),
        in_specs=[any_spec() if flag else vmem_spec() for flag in in_any] + [any_spec()] * extra,
        out_specs=tuple(any_spec() if flag else vmem_spec() for flag in out_any),
        scratch_shapes=scratch,
        compiler_params=pltpu.CompilerParams(vmem_limit_bytes=limit * MB, **params),
        cost_estimate=pl.CostEstimate(flops=1, bytes_accessed=1, transcendentals=0),
    )(*ins, *after)


def whole_tiles(columns):
    return -(-columns // LANES) * LANES


def like(shape, dtype=BF):
    return jax.ShapeDtypeStruct(shape, dtype)


def greet(more=()):
    barrier = pltpu.get_barrier_semaphore()
    size = lax.axis_size("wide")
    me = lax.axis_index("wide")

    def signal(k, carry):
        pl.semaphore_signal(
            barrier,
            inc=1,
            device_id={"wide": lax.rem(me + k, size)},
            device_id_type=pl.DeviceIdType.MESH,
        )
        return carry

    lax.fori_loop(1, size, signal, 0)
    for place in more:
        pl.semaphore_signal(barrier, inc=1, device_id=place, device_id_type=pl.DeviceIdType.MESH)
    pl.semaphore_wait(barrier, size - 1 + len(more))


class Swap:
    def __init__(self, send, recv, send_sem, recv_sem, shared=False):
        self.send, self.recv, self.shared = send, recv, shared
        self.send_sem, self.recv_sem = send_sem, recv_sem

    def source(self, at):
        return self.send if self.shared else self.send.at[at]

    def copy(self, k, source, target, peer):
        return pltpu.make_async_remote_copy(
            src_ref=self.source(source),
            dst_ref=self.recv.at[target],
            send_sem=self.send_sem.at[k],
            recv_sem=self.recv_sem.at[k],
            device_id={"wide": peer},
            device_id_type=pl.DeviceIdType.MESH,
        )

    def start(self):
        size, me = lax.axis_size("wide"), lax.axis_index("wide")

        def step(k, carry):
            peer = lax.rem(me + k, size)
            self.copy(k, peer, me, peer).start()
            return carry

        lax.fori_loop(1, size, step, 0)
        self.recv[me] = self.send[...] if self.shared else self.send[me]

    def finish(self):
        size, me = lax.axis_size("wide"), lax.axis_index("wide")

        def arrive(k, carry):
            peer = lax.rem(me + size - k, size)
            self.copy(k, peer, peer, peer).wait_recv()
            return carry

        def leave(k, carry):
            peer = lax.rem(me + k, size)
            self.copy(k, peer, me, peer).wait_send()
            return carry

        lax.fori_loop(1, size, arrive, 0)
        lax.fori_loop(1, size, leave, 0)


def wide_bits():
    return lax.axis_size("wide").bit_length() - 1


def mirrored(at):
    bits = wide_bits()
    return sum(((at >> bit) & 1) << (bits - 1 - bit) for bit in range(bits))


def bit_of(bit):
    return lax.rem(lax.div(lax.axis_index("wide"), 1 << bit), 2)


def partner(bit):
    return lax.axis_index("wide") + (1 - 2 * bit_of(bit)) * (1 << bit)


def greet_devices(places):
    barrier = pltpu.get_barrier_semaphore()
    for place in places:
        pl.semaphore_signal(barrier, inc=1, device_id=place, device_id_type=pl.DeviceIdType.MESH)
    pl.semaphore_wait(barrier, len(places))


def pair_places():
    return [{"wide": partner(bit)} for bit in range(wide_bits())]


def core_places():
    size, me = lax.axis_size("tp"), lax.axis_index("tp")
    return [{"tp": lax.rem(me + k, size)} for k in range(1, size)]


class Doubling:
    def __init__(self, levels, send_sem, recv_sem):
        self.levels, self.send_sem, self.recv_sem = levels, send_sem, recv_sem
        self.bit = wide_bits()
        self.copy = None

    def start(self):
        self.send()

    def send(self):
        bit = self.bit - 1
        have = self.levels[self.bit]
        half = have.shape[0]
        mine = bit_of(bit)
        there = self.levels[bit].at[pl.ds(mine * half, half)]
        self.copy = pltpu.make_async_remote_copy(
            src_ref=have,
            dst_ref=there,
            send_sem=self.send_sem.at[bit],
            recv_sem=self.recv_sem.at[bit],
            device_id={"wide": partner(bit)},
            device_id_type=pl.DeviceIdType.MESH,
        )
        self.copy.start()
        self.levels[bit][pl.ds(mine * half, half)] = have[...]

    def advance(self):
        if self.bit == 0:
            return
        self.copy.wait()
        self.bit -= 1
        if self.bit:
            self.send()

    def finish(self, out):
        while self.bit:
            self.advance()
        for at in range(self.levels[0].shape[0]):
            out[at] = self.levels[0][mirrored(at)]


class Halving:
    def __init__(self, levels, landing, send_sem, recv_sem):
        self.levels, self.landing = levels, landing
        self.send_sem, self.recv_sem = send_sem, recv_sem
        self.bit = 0

    def start(self):
        self.send()

    def send(self):
        bit = self.bit
        half = self.landing[bit].shape[0]
        other = 1 - bit_of(bit)
        self.copy = pltpu.make_async_remote_copy(
            src_ref=self.levels[bit].at[pl.ds(other * half, half)],
            dst_ref=self.landing[bit],
            send_sem=self.send_sem.at[bit],
            recv_sem=self.recv_sem.at[bit],
            device_id={"wide": partner(bit)},
            device_id_type=pl.DeviceIdType.MESH,
        )
        self.copy.start()

    def advance(self):
        bit = self.bit
        if bit == wide_bits():
            return
        half = self.landing[bit].shape[0]
        self.copy.wait()
        own = self.levels[bit][pl.ds(bit_of(bit) * half, half)]
        self.levels[bit + 1][...] = (own.astype(F32) + self.landing[bit][...].astype(F32)).astype(BF)
        self.bit += 1
        if self.bit < wide_bits():
            self.send()

    def finish(self, out):
        while self.bit < wide_bits():
            self.advance()
        out[...] = self.levels[-1][0]


def level_scratch(size, block):
    bits = size.bit_length() - 1
    return [VMEM((size >> s,) + block, BF) for s in range(bits + 1)]


class CoreCopies:
    def __init__(self, send_sem, recv_sem):
        self.send_sem, self.recv_sem, self.used = send_sem, recv_sem, 0

    def start(self, source, target, place):
        copy = pltpu.make_async_remote_copy(
            src_ref=source,
            dst_ref=target,
            send_sem=self.send_sem.at[self.used],
            recv_sem=self.recv_sem.at[self.used],
            device_id=place,
            device_id_type=pl.DeviceIdType.MESH,
        )
        copy.start()
        self.used += 1
        return copy


class PairCopies:
    def __init__(self, send_sem, recv_sem):
        self.send_sem, self.recv_sem, self.copies = send_sem, recv_sem, []

    def start(self, source, target, bit):
        at = len(self.copies)
        copy = pltpu.make_async_remote_copy(
            src_ref=source,
            dst_ref=target,
            send_sem=self.send_sem.at[at],
            recv_sem=self.recv_sem.at[at],
            device_id={"wide": partner(bit)},
            device_id_type=pl.DeviceIdType.MESH,
        )
        copy.start()
        self.copies.append(copy)

    def finish(self):
        for copy in self.copies:
            copy.wait()


def swap_sems(size, count):
    return [pltpu.SemaphoreType.DMA((size,))] * (2 * count)


def spatial_forward(tokens_list, mod_here, sqkv_rows, w_so, frames_here, keyval_part, o_first):
    n_tp = len(tokens_list)
    rows, width = tokens_list[0].shape
    columns = w_so.shape[0]
    patch_part = rows // frames_here
    per_frame = n_tp * patch_part
    count = n_tp * rows
    heads = columns // HD
    size = lax.axis_size("wide")
    bits = wide_bits()

    def kernel(*refs):
        token_refs = refs[:n_tp]
        mod_ref, qkv_hbm, so_hbm, kv_ref = refs[n_tp : n_tp + 4]
        at = n_tp + 4
        h_ref, h_own, qkv_out, probs_out, a_keep, a_give, y_ref = refs[at : at + 7]
        y_others = refs[at + 7 : at + 6 + n_tp]
        at += 6 + n_tp
        kv_out = refs[at]
        weight_qkv, weight_o, qkv_ref, probs_ref, attn_ref, sems, *levels = refs[at + 1 :]
        *levels, send_sem, recv_sem = levels
        greet_devices(pair_places())
        share = Doubling(levels, send_sem, recv_sem)
        levels[bits][0] = kv_ref[...]
        share.start()
        moves = Moves(sems)
        weights = [moves.start(qkv_hbm.at[i], weight_qkv.at[i]) for i in range(3)]
        weight_out = moves.start(so_hbm, weight_o)
        for frame in range(frames_here):
            shift = mod_ref[frame : frame + 1, 0:width]
            scale = 1.0 + mod_ref[frame : frame + 1, width : 2 * width]
            for r in range(n_tp):
                part = token_refs[r][frame * patch_part : (frame + 1) * patch_part, :]
                normed, unused = norm_of(part.astype(F32))
                at = frame * per_frame + r * patch_part
                value = (normed * scale + shift).astype(BF)
                h_ref[at : at + patch_part, :] = value
                if r == 0:
                    h_own[frame * patch_part : (frame + 1) * patch_part, :] = value
        outgoing = []
        for i in range(3):
            weights[i].wait()
            qkv_ref[i] = dot_nt(h_ref[...], weight_qkv[i]).astype(BF)
        share.advance()
        outgoing.append(moves.start(qkv_ref, qkv_out))
        for frame in range(frames_here):
            at = slice(frame * per_frame, (frame + 1) * per_frame)

            def keep_probs(head, probs, frame=frame):
                probs_ref[frame * heads + head] = probs

            def write(low, high, part, at=at):
                attn_ref[at, low:high] = part.astype(BF)

            attend(
                lambda low, high, at=at: qkv_ref[0, at, low:high],
                lambda low, high, at=at: qkv_ref[1, at, low:high],
                lambda low, high, at=at: qkv_ref[2, at, low:high],
                None,
                heads,
                columns,
                keep_probs,
                write,
                share.advance,
            )
            share.advance()
        outgoing.append(moves.start(probs_ref, probs_out))
        mine = bit_of(o_first)
        first, second = attn_ref[:, : columns // 2], attn_ref[:, columns // 2 :]
        part = columns // 2
        a_keep[:, 0:part] = jnp.where(mine == 0, first, second)
        a_give[:, 0:part] = jnp.where(mine == 0, second, first)
        for ref in (a_keep, a_give):
            if ref.shape[1] > part:
                ref[:, part:] = jnp.zeros((count, ref.shape[1] - part), BF)
        weight_out.wait()
        for frame in range(frames_here):
            at = frame * per_frame
            branch = dot_nn(attn_ref[at : at + per_frame, :], weight_o[...])
            here = slice(frame * patch_part, (frame + 1) * patch_part)
            y_ref[here, :] = branch[:patch_part]
            for r in range(1, n_tp):
                y_others[r - 1][here, :] = branch[r * patch_part : (r + 1) * patch_part].astype(BF)
        for copy in outgoing:
            copy.wait()
        share.finish(kv_out)

    outs = [
        like((count, width)),
        like((rows, width)),
        like((3, count, columns)),
        like((frames_here * heads, per_frame, per_frame)),
        like((count, whole_tiles(columns // 2))),
        like((count, whole_tiles(columns // 2))),
        like((rows, width), F32),
    ] + [like((rows, width))] * (n_tp - 1)
    outs.append(like((size,) + keyval_part.shape))
    ins = list(tokens_list) + [mod_here, sqkv_rows, w_so, keyval_part]
    return call(
        kernel,
        outs,
        ins,
        [False] * (n_tp + 1) + [True, True, False],
        [False, False, True, True] + [False] * (n_tp + 3),
        [
            VMEM((3, columns, width), BF),
            VMEM((columns, width), BF),
            VMEM((3, count, columns), BF),
            VMEM((frames_here * heads, per_frame, per_frame), BF),
            VMEM((count, columns), BF),
            pltpu.SemaphoreType.DMA((6,)),
        ]
        + level_scratch(size, keyval_part.shape)
        + swap_sems(bits, 1),
        collective_id=1,
        has_side_effects=True,
    )


def stream_to_patches(tokens_rows, y_own, y_others, mod_here, frames_here):
    size = lax.axis_size("wide")
    rows, width = tokens_rows.shape
    patch_part = rows // frames_here
    patch_here = patch_part // size
    block = frames_here * patch_here
    others = len(y_others)

    def kernel(*refs):
        token_ref, y_ref, mod_ref = refs[0], refs[1], refs[2 + others]
        out_ref, total_ref = refs[3 + others : 5 + others]
        send, recv, send_sem, recv_sem = refs[5 + others :]
        greet()
        for frame in range(frames_here):
            at = slice(frame * patch_part, (frame + 1) * patch_part)
            branch = y_ref[at, :]
            for other in refs[2 : 2 + others]:
                branch = branch + other[at, :].astype(F32)
            total_ref[at, :] = branch
            gate = mod_ref[frame : frame + 1, 2 * width : 3 * width]
            stream = token_ref[at, :].astype(F32) + gate * branch
            for owner in range(size):
                send[owner, frame * patch_here : (frame + 1) * patch_here, :] = stream[
                    owner * patch_here : (owner + 1) * patch_here
                ].astype(BF)
        exchange = Swap(send, recv, send_sem, recv_sem)
        exchange.start()
        exchange.finish()
        out_ref[...] = recv[...]

    ins = [tokens_rows, y_own] + list(y_others) + [mod_here]
    return call(
        kernel,
        [like((size, block, width)), like((rows, width), F32)],
        ins,
        [False] * len(ins),
        [False, False],
        [VMEM((size, block, width), BF)] * 2 + swap_sems(size, 1),
        collective_id=2,
        has_side_effects=True,
    )


def grads_to_frames(grad_blocks, y_one, mod_here, frames_here, members):
    size, block, width = grad_blocks.shape
    rows = y_one.shape[0]
    patch_part = rows // frames_here
    patch_here = patch_part // size
    n_tp = lax.axis_size("tp")
    others = n_tp - 1
    number = len(members)
    every, most = members[0][1].shape[0], max(member[0].across for member in members)
    token_rows = every // n_tp
    head = members[0][3].shape[1]

    def kernel(*refs):
        grad_ref, y_ref, mod_ref = refs[:3]
        operands = [refs[3 + 4 * p : 7 + 4 * p] for p in range(number)]
        at = 3 + 4 * number
        stream_ref, branch_ref, gate_ref = refs[at : at + 3]
        outs = [refs[at + 3 + 2 * p : at + 5 + 2 * p] for p in range(number)]
        at += 3 + 2 * number
        recv, exchange_send, exchange_recv, models, heads, total, sems, send_sem, recv_sem = refs[at:]
        greet(core_places())
        exchange = Swap(grad_ref, recv, exchange_send, exchange_recv)
        exchange.start()
        core = CoreCopies(send_sem, recv_sem)
        moves = Moves(sems)
        flights, loads = [], []
        for p, (model, got, keep, other) in enumerate(operands):
            flights.append(
                [
                    core.start(got, models.at[2 * p + 1, pl.ds((n_tp - 1 - k) * token_rows, token_rows), :], place)
                    for k, place in enumerate(core_places())
                ]
            )
            loads.append(
                [
                    moves.start(model, models.at[2 * p]),
                    moves.start(keep, heads.at[2 * p]),
                    moves.start(got, models.at[2 * p + 1, pl.ds(0, token_rows), :]),
                    moves.start(other, heads.at[2 * p + 1]),
                ]
            )
        for p, member in enumerate(members):
            across = member[0].across
            for copy in loads[p]:
                copy.wait()
            total[:, 0:across] = dot_tn(models[2 * p], heads[2 * p, :, 0:across])
            for copy in flights[p]:
                copy.wait()
            total[:, 0:across] += dot_tn(models[2 * p + 1], heads[2 * p + 1, :, 0:across])
            scatter_rows(total, outs[p][0], outs[p][1], member[0], size)
        exchange.finish()
        for owner in range(size):
            part = recv[owner].astype(F32)
            for frame in range(frames_here):
                at = frame * patch_part + owner * patch_here
                stream_ref[at : at + patch_here, :] = part[
                    frame * patch_here : (frame + 1) * patch_here
                ]
        for frame in range(frames_here):
            at = slice(frame * patch_part, (frame + 1) * patch_part)
            stream = stream_ref[at, :]
            gate_ref[frame : frame + 1, :] = jnp.sum(stream * y_ref[at, :], axis=0, keepdims=True)
            branch_ref[at, :] = (stream * mod_ref[frame : frame + 1, 2 * width : 3 * width]).astype(BF)

    ins = [grad_blocks, y_one, mod_here] + [array for member in members for array in member[1:5]]
    halves = [
        like((size // 2, width // size, member[0].across)) for member in members for unused in range(2)
    ]
    out = call(
        kernel,
        [like((rows, width), F32), like((rows, width)), like((frames_here, width), F32)] + halves,
        ins,
        [False] * 3 + [True] * (4 * number),
        [False] * (3 + 2 * number),
        [VMEM((size, block, width), BF)]
        + swap_sems(size, 1)
        + [
            VMEM((2 * number, every, width), BF),
            VMEM((2 * number, every, head), BF),
            VMEM((width, most), F32),
            pltpu.SemaphoreType.DMA((4 * number,)),
            pltpu.SemaphoreType.DMA((number * others,)),
            pltpu.SemaphoreType.DMA((number * others,)),
        ],
        collective_id=3,
        has_side_effects=True,
    )
    return out[:3], [out[3 + 2 * p : 5 + 2 * p] for p in range(number)]


def fill_rows(moves, sources, target):
    step = sources[0].shape[0]
    return [moves.start(ref, target.at[pl.ds(r * step, step), :]) for r, ref in enumerate(sources)]


def middle_forward(stream, row_codes, key_codes, blocks, keyval_list, tqkv_list, to_list, cq_list, co_list, out_first, given):
    n_tp = len(tqkv_list)
    count, width = stream.shape
    keys = keyval_list[0].shape[0]
    columns = to_list[0].shape[0]
    heads = width // HD
    part = columns // 2
    out_slot = whole_tiles(2 * part)

    def kernel(*refs):
        stream_ref, row_ref, key_ref = refs[:3]
        block_refs = refs[3 : 3 + len(blocks)]
        at = 3 + len(blocks)
        groups = []
        for unused in range(5):
            groups.append(refs[at : at + n_tp])
            at += n_tp
        keyvals, tqkvs, tos, cqs, cos = groups
        given_refs = refs[at : at + len(given)]
        at += len(given)
        h2_out, qkv_out, p2_out, inv2_ref, h3_out, q3_out, p3_out, inv3_ref, x_ref, kv_ref, a_keep, a_give = refs[at : at + 12]
        block_outs = refs[at + 12 : at + 12 + len(blocks)]
        at += 12 + len(blocks)
        given_got = refs[at : at + len(given)]
        w_qkv, w_o, w_q, w_c, h2, qkv, p2, a2, h3, q3, p3, a3, sems, *swap = refs[at + len(given) :]
        greet()
        pairs = PairCopies(*swap[-2:])
        for (unused, first), ref, target in zip(given, given_refs, given_got):
            pairs.start(ref, target, first)
        exchanges = [
            Swap(ref, swap[3 * i], swap[3 * i + 1], swap[3 * i + 2]) for i, ref in enumerate(block_refs)
        ]
        for exchange in exchanges:
            exchange.start()
        moves = Moves(sems)
        qkv_in = [
            [
                moves.start(tqkvs[r].at[i], w_qkv.at[i, pl.ds(r * columns, columns), :])
                for r in range(n_tp)
            ]
            for i in range(3)
        ]
        o_in = fill_rows(moves, tos, w_o)
        q_in = fill_rows(moves, cqs, w_q)
        c_in = fill_rows(moves, cos, w_c)
        outgoing = []
        for i in range(2):
            for r in range(n_tp):
                kv_ref[i, :, r * columns : (r + 1) * columns] = keyvals[r][
                    :, i * columns : (i + 1) * columns
                ]
        stream_one = stream_ref[...].astype(F32)
        normed, inverse = norm_of(stream_one)
        inv2_ref[...] = jnp.broadcast_to(inverse, inv2_ref.shape)
        h2[...] = normed.astype(BF)
        outgoing.append(moves.start(h2, h2_out))
        for i in range(3):
            for copy in qkv_in[i]:
                copy.wait()
            qkv[i] = dot_nt(h2[...], w_qkv[i]).astype(BF)
        outgoing.append(moves.start(qkv, qkv_out))

        def keep_two(head, probs):
            p2[head] = probs

        def write_two(low, high, part):
            a2[:, low:high] = part.astype(BF)

        attend(
            lambda low, high: qkv[0, :, low:high],
            lambda low, high: qkv[1, :, low:high],
            lambda low, high: qkv[2, :, low:high],
            jnp.where(row_ref[:, 0:1] == key_ref[0:1, 0:count], 0.0, NEGATIVE),
            heads,
            width,
            keep_two,
            write_two,
        )
        outgoing.append(moves.start(p2, p2_out))
        for copy in o_in:
            copy.wait()
        x_ref[...] = stream_one + dot_nn(a2[...], w_o[...])
        normed, inverse = norm_of(x_ref[...])
        inv3_ref[...] = jnp.broadcast_to(inverse, inv3_ref.shape)
        h3[...] = normed.astype(BF)
        outgoing.append(moves.start(h3, h3_out))
        for copy in q_in:
            copy.wait()
        q3[...] = dot_nt(h3[...], w_q[...]).astype(BF)
        outgoing.append(moves.start(q3, q3_out))

        def keep_three(head, probs):
            p3[head] = probs

        def write_three(low, high, part):
            a3[:, low:high] = part.astype(BF)

        attend(
            lambda low, high: q3[:, low:high],
            lambda low, high: kv_ref[0, :, low:high],
            lambda low, high: kv_ref[1, :, low:high],
            jnp.where(row_ref[:, 1:2] == key_ref[1:2, 0:keys], 0.0, NEGATIVE),
            heads,
            width,
            keep_three,
            write_three,
        )
        outgoing.append(moves.start(p3, p3_out))
        mine = bit_of(out_first)
        for r in range(n_tp):
            for i, ref in enumerate((a2, a3)):
                low = r * out_slot + i * part
                first = ref[:, r * columns : r * columns + part]
                second = ref[:, r * columns + part : (r + 1) * columns]
                a_keep[:, low : low + part] = jnp.where(mine == 0, first, second)
                a_give[:, low : low + part] = jnp.where(mine == 0, second, first)
            for ref in (a_keep, a_give):
                if out_slot > 2 * part:
                    spare = jnp.zeros((count, out_slot - 2 * part), BF)
                    ref[:, r * out_slot + 2 * part : (r + 1) * out_slot] = spare
        for copy in c_in:
            copy.wait()
        x_ref[...] = x_ref[...] + dot_nn(a3[...], w_c[...])
        for copy in outgoing:
            copy.wait()
        for exchange, out in zip(exchanges, block_outs):
            exchange.finish()
            out[...] = exchange.recv[...]
        pairs.finish()

    square = (count, width)
    outs = [
        like(square),
        like((3,) + square),
        like((heads, count, count)),
        like((count, LANES), F32),
        like(square),
        like(square),
        like((heads, count, keys)),
        like((count, LANES), F32),
        like(square, F32),
        like((2, keys, width)),
        like((count, n_tp * out_slot)),
        like((count, n_tp * out_slot)),
    ] + [like(array.shape) for array in blocks]
    outs += [like(array.shape) for array, unused in given]
    kept = [square, (3,) + square, (heads, count, count), square, square, square, (heads, count, keys), square]
    ins = [stream, row_codes, key_codes, *blocks, *keyval_list, *tqkv_list, *to_list, *cq_list, *co_list]
    ins += [array for array, unused in given]
    full = n_tp * columns
    return call(
        kernel,
        outs,
        ins,
        [False] * (3 + len(blocks) + n_tp) + [True] * (4 * n_tp + len(given)),
        [True, True, True, False, True, True, True, False, False, False, False, False] + [False] * len(blocks) + [True] * len(given),
        [VMEM((3, full, width), BF)]
        + [VMEM((full, width), BF)] * 3
        + [VMEM(shape, BF) for shape in kept]
        + [pltpu.SemaphoreType.DMA((6 * n_tp + 8,))]
        + [
            kind
            for array in blocks
            for kind in (VMEM(array.shape, BF), *swap_sems(array.shape[0], 1))
        ]
        + swap_sems(len(given), 1),
        collective_id=6,
        has_side_effects=True,
    )


def feed_forward(stream, grad_out, mod_rows, hot_rows, w_fc1, w_fc2, firsts, given):
    n_tp = lax.axis_size("tp")
    others = n_tp - 1
    count, width = stream.shape
    every = n_tp * count
    hidden = w_fc1.shape[1]
    half = hidden // 2
    padded = whole_tiles(half)
    clips = hot_rows.shape[1]
    pieces = 2 if half % LANES == 0 else 1

    def kernel(*refs):
        stream_ref, grad_ref, mod_ref, hot_ref, fc1_hbm, fc2_hbm = refs[:6]
        given_refs, refs = refs[6 : 6 + len(given)], refs[:6] + refs[6 + len(given) :]
        out_ref, h_all, up_keep, up_give, dy_all, down_keep, down_give, g_ref, mod_sum = refs[6:15]
        h_own, dy_own, h_got, dy_got = refs[15:19]
        given_got, refs = refs[19 : 19 + len(given)], refs[19 + len(given) :]
        w1, w2, h_land, total_y, total_h, send_y, send_h, land_y, land_h, sems, send_sem, recv_sem = refs[:12]
        moves = Moves(sems)
        loads = []
        for piece in range(pieces):
            cols = pl.ds(piece * (hidden // pieces), hidden // pieces)
            loads.append(
                (
                    moves.start(fc1_hbm.at[:, cols], w1.at[:, cols]),
                    moves.start(fc2_hbm.at[cols, :], w2.at[cols, :]),
                )
            )
        greet_devices(core_places() + pair_places())
        core = CoreCopies(send_sem, recv_sem)
        pairs = PairCopies(*refs[12:])
        for (unused, first), ref, target in zip(given, given_refs, given_got):
            pairs.start(ref, target, first)
        bit = [bit_of(first) for first in firsts]
        own = slice(0, count)
        gate = mod_ref[:, 2 * width :].astype(F32)
        dy_own[...] = (gate * grad_ref[...].astype(F32)).astype(BF)
        flights = [core.start(dy_own, h_land.at[n_tp - 2 - k], place) for k, place in enumerate(core_places())]
        pairs.start(dy_own, dy_got, firsts[1])
        shift = mod_ref[:, 0:width].astype(F32)
        scale = 1.0 + mod_ref[:, width : 2 * width].astype(F32)
        normed, inverse = norm_of(stream_ref[...])
        h_own[...] = (normed * scale + shift).astype(BF)
        flights += [
            core.start(h_own, h_land.at[others + n_tp - 2 - k], place) for k, place in enumerate(core_places())
        ]
        pairs.start(h_own, h_got, firsts[0])
        h_all[own, :] = h_own[...]
        dy_all[own, :] = dy_own[...]
        for pack in (up_keep, up_give, down_keep, down_give):
            if padded > half:
                pack[:, half:] = jnp.zeros((every, padded - half), BF)
        back = []
        for part in range(2):
            if part < pieces:
                for copy in loads[part]:
                    copy.wait()
            hid = slice(part * half, (part + 1) * half)
            for r in range(n_tp) if part == 0 else [*range(1, n_tp), 0]:
                at = slice(r * count, (r + 1) * count)
                if part == 0 and r == 1:
                    for copy in flights:
                        copy.wait()
                    for k in range(others):
                        there = slice((k + 1) * count, (k + 2) * count)
                        dy_all[there, :] = h_land[k]
                        h_all[there, :] = h_land[others + k]
                upper = dot_nn(h_all[at, :], w1[:, hid])
                square = upper * upper
                tanh = jnp.tanh(upper * (0.7978845608028654 + 0.035677408136300125 * square))
                rise = 0.5 + 0.5 * tanh
                active = (upper * rise).astype(BF)
                slope = rise + (0.5 * upper) * (1.0 - tanh * tanh) * (
                    0.7978845608028654 + 0.10703222440890037 * square
                )
                grad_upper = (dot_nt(dy_all[at, :], w2[hid, :]) * slope).astype(BF)
                for keep, give, mine, value in (
                    (up_keep, up_give, bit[0], grad_upper),
                    (down_keep, down_give, bit[1], active),
                ):

                    @pl.when(mine == part)
                    def _():
                        keep[at, 0:half] = value

                    @pl.when(mine != part)
                    def _():
                        give[at, 0:half] = value

                y_term = dot_nn(active, w2[hid, :])
                h_term = dot_nt(grad_upper, w1[:, hid])
                if part == 0:
                    total_y[at, :] = y_term
                    total_h[at, :] = h_term
                elif r == 0:
                    total_y[at, :] += y_term
                    total_h[at, :] += h_term
                else:
                    send_y[r - 1] = (total_y[at, :] + y_term).astype(BF)
                    send_h[r - 1] = (total_h[at, :] + h_term).astype(BF)
                    place = core_places()[r - 1]
                    back.append(core.start(send_y.at[r - 1], land_y.at[r - 1], place))
                    back.append(core.start(send_h.at[r - 1], land_h.at[r - 1], place))
        for copy in back:
            copy.wait()
        branch, grad_h = total_y[own, :], total_h[own, :]
        for k in range(others):
            branch = branch + land_y[k].astype(F32)
            grad_h = grad_h + land_h[k].astype(F32)
        gate = mod_ref[:, 2 * width :].astype(F32)
        out_ref[...] = (stream_ref[...] + gate * branch).astype(BF)
        grad = grad_ref[...].astype(F32)
        hot = hot_ref[...]
        mod_sum[:, 2 * width :] = dot_tn(hot, (grad * branch).astype(BF))
        mod_sum[:, 0:width] = dot_tn(hot, grad_h.astype(BF))
        normed, inverse = norm_of(stream_ref[...])
        mod_sum[:, width : 2 * width] = dot_tn(hot, (grad_h * normed).astype(BF))
        scale = 1.0 + mod_ref[:, width : 2 * width].astype(F32)
        g_ref[...] = grad + norm_back(grad_h * scale, normed, inverse)
        pairs.finish()

    side = like((every, padded))
    ins = [stream, grad_out, mod_rows, hot_rows, w_fc1, w_fc2] + [array for array, unused in given]
    n_pairs = 2 + len(given)
    square = (count, width)
    return call(
        kernel,
        [
            like(square),
            like((every, width)),
            side,
            side,
            like((every, width)),
            side,
            side,
            like(square, F32),
            like((clips, 3 * width), F32),
            like(square),
            like(square),
            like(square),
            like(square),
        ]
        + [like(array.shape) for array, unused in given],
        ins,
        [False] * 4 + [True] * (2 + len(given)),
        [False] * 11 + [True] * n_pairs,
        [
            VMEM((width, hidden), BF),
            VMEM((hidden, width), BF),
            VMEM((2 * others,) + square, BF),
            VMEM((every, width), F32),
            VMEM((every, width), F32),
            VMEM((others,) + square, BF),
            VMEM((others,) + square, BF),
            VMEM((others,) + square, BF),
            VMEM((others,) + square, BF),
            pltpu.SemaphoreType.DMA((4,)),
            pltpu.SemaphoreType.DMA((4 * others,)),
            pltpu.SemaphoreType.DMA((4 * others,)),
            pltpu.SemaphoreType.DMA((n_pairs,)),
            pltpu.SemaphoreType.DMA((n_pairs,)),
        ],
        collective_id=5,
        has_side_effects=True,
    )


def middle_backward(grad, kept, keyval, out_blocks, texts, tqkv_list, to_list, cq_list, co_list, in_first, given):
    n_tp = len(tqkv_list)
    h2, qkv, p2, inv2, h3, q3, p3, inv3 = kept
    count, width = grad.shape
    keys = keyval.shape[1]
    columns = to_list[0].shape[0]
    part = columns // 2
    heads = width // HD
    full = n_tp * columns
    in_slot = whole_tiles(4 * part)

    def kernel(*refs):
        grad_ref, inv2_ref, inv3_ref, h2_ref, h3_ref, block_ref, text_ref = refs[:7]
        qkv_hbm, p2_hbm, q3_hbm, p3_hbm, kv_hbm = refs[7:12]
        given_refs = refs[12 : 12 + len(given)]
        at = 12 + len(given)
        groups = []
        for unused in range(4):
            groups.append(refs[at : at + n_tp])
            at += n_tp
        tqkvs, tos, cqs, cos = groups
        in_keep, in_give, dy2_ref, dy3_ref, stream_ref, block_out, text_out = refs[at : at + 7]
        given_got = refs[at + 7 : at + 7 + len(given)]
        at += 2 + len(given)
        kv_outs = refs[at + 5 : at + 5 + n_tp]
        (
            w_qkv, w_o, w_q, w_c, qkv_ref, p2_ref, q3_ref, p3_ref, kv_ref,
            grad_attn, d_q, d_k, d_v, total, sems, recv, send_sem, recv_sem, text_recv, text_sem, text_recv_sem, pair_send, pair_recv,
        ) = refs[at + 5 + n_tp :]
        greet()
        exchange = Swap(block_ref, recv, send_sem, recv_sem)
        pairs = PairCopies(pair_send, pair_recv)
        for (unused, first), ref, target in zip(given, given_refs, given_got):
            pairs.start(ref, target, first)
        exchange.start()
        text_exchange = Swap(text_ref, text_recv, text_sem, text_recv_sem)
        text_exchange.start()
        moves = Moves(sems)
        c_in = fill_rows(moves, cos, w_c)
        kv_in = moves.start(kv_hbm, kv_ref)
        p3_in = moves.start(p3_hbm, p3_ref)
        q3_in = moves.start(q3_hbm, q3_ref)
        q_in = fill_rows(moves, cqs, w_q)
        o_in = fill_rows(moves, tos, w_o)
        qkv_load = moves.start(qkv_hbm, qkv_ref)
        p2_in = moves.start(p2_hbm, p2_ref)
        qkv_in = [
            [
                moves.start(tqkvs[r].at[i], w_qkv.at[i, pl.ds(r * columns, columns), :])
                for r in range(n_tp)
            ]
            for i in range(3)
        ]
        bit = bit_of(in_first)

        def split(value, r, mine, keep, give, low):
            first = value[:, r * columns : r * columns + part]
            second = value[:, r * columns + part : (r + 1) * columns]
            keep[:, low : low + part] = jnp.where(mine == 0, first, second)
            give[:, low : low + part] = jnp.where(mine == 0, second, first)

        def into(ref, upto):
            def write(low, high, value):
                ref[0:upto, low:high] = value.astype(BF)

            return write

        if in_slot > 4 * part:
            for pack in (in_keep, in_give):
                for r in range(n_tp):
                    spare = jnp.zeros((count, in_slot - 4 * part), BF)
                    pack[:, r * in_slot + 4 * part : (r + 1) * in_slot] = spare
        grad_y = grad_ref[...].astype(BF)
        dy3_ref[...] = grad_y
        for copy in c_in:
            copy.wait()
        grad_attn[...] = dot_nt(grad_y, w_c[...]).astype(BF)
        for copy in (kv_in, p3_in, q3_in):
            copy.wait()
        attend_back(
            lambda low, high: q3_ref[:, low:high],
            lambda low, high: kv_ref[0, :, low:high],
            lambda low, high: kv_ref[1, :, low:high],
            lambda low, high: grad_attn[:, low:high],
            lambda head: p3_ref[head],
            heads,
            width,
            into(d_q, count),
            into(d_k, keys),
            into(d_v, keys),
        )
        for r in range(n_tp):
            kv_outs[r][:, 0:columns] = d_k[0:keys, r * columns : (r + 1) * columns]
            kv_outs[r][:, columns:] = d_v[0:keys, r * columns : (r + 1) * columns]
            split(d_q[...], r, bit, in_keep, in_give, r * in_slot + 3 * part)
        for copy in q_in:
            copy.wait()
        grad_h = dot_nn(d_q[...], w_q[...])
        total[...] = grad_ref[...] + norm_back(grad_h, h3_ref[...].astype(F32), inv3_ref[:, 0:1])

        grad_y = total[...].astype(BF)
        dy2_ref[...] = grad_y
        for copy in o_in:
            copy.wait()
        grad_attn[...] = dot_nt(grad_y, w_o[...]).astype(BF)
        for copy in (qkv_load, p2_in):
            copy.wait()
        attend_back(
            lambda low, high: qkv_ref[0, :, low:high],
            lambda low, high: qkv_ref[1, :, low:high],
            lambda low, high: qkv_ref[2, :, low:high],
            lambda low, high: grad_attn[:, low:high],
            lambda head: p2_ref[head],
            heads,
            width,
            into(d_q, count),
            into(d_k, count),
            into(d_v, count),
        )
        for i, ref in enumerate((d_q, d_k, d_v)):
            for r in range(n_tp):
                split(ref[0:count, :], r, bit, in_keep, in_give, r * in_slot + i * part)
            for copy in qkv_in[i]:
                copy.wait()
            term = dot_nn(ref[0:count, :], w_qkv[i])
            grad_h = term if i == 0 else grad_h + term
        stream_ref[...] = (
            total[...] + norm_back(grad_h, h2_ref[...].astype(F32), inv2_ref[:, 0:1])
        ).astype(BF)
        pairs.finish()
        exchange.finish()
        block_out[...] = recv[...]
        text_exchange.finish()
        text_out[...] = text_recv[...]

    square = (count, width)
    in_pack = like((count, n_tp * in_slot))
    ins = [grad, inv2, inv3, h2, h3, out_blocks, texts, qkv, p2, q3, p3, keyval]
    ins = ins + [array for array, unused in given]
    ins = ins + [*tqkv_list, *to_list, *cq_list, *co_list]
    square_keys = (keys, width)
    return call(
        kernel,
        [in_pack, in_pack, like(square), like(square), like(square), like(out_blocks.shape), like(texts.shape)]
        + [like(array.shape) for array, unused in given]
        + [like((keys, 2 * columns))] * n_tp,
        ins,
        [False] * 7 + [True] * (5 + len(given) + 4 * n_tp),
        [False] * 7 + [True] * len(given) + [False] * n_tp,
        [VMEM((3, full, width), BF)]
        + [VMEM((full, width), BF)] * 3
        + [
            VMEM((3,) + square, BF),
            VMEM((heads, count, count), BF),
            VMEM(square, BF),
            VMEM((heads, count, keys), BF),
            VMEM((2,) + square_keys, BF),
            VMEM(square, BF),
            VMEM(square, BF),
            VMEM((max(count, keys), width), BF),
            VMEM((max(count, keys), width), BF),
            VMEM(square, F32),
            pltpu.SemaphoreType.DMA((6 * n_tp + 7,)),
            VMEM(out_blocks.shape, BF),
        ]
        + swap_sems(out_blocks.shape[0], 1)
        + [VMEM(texts.shape, BF)]
        + swap_sems(out_blocks.shape[0], 1)
        + swap_sems(len(given), 1),
        collective_id=7,
        has_side_effects=True,
    )


def spatial_backward(grad_y_list, probs, qkv, sqkv_rows, w_so, frames_here, given, q_first):
    n_tp = len(grad_y_list)
    rows, width = grad_y_list[0].shape
    columns = w_so.shape[0]
    part = columns // 2
    patch_part = rows // frames_here
    per_frame = n_tp * patch_part
    count = n_tp * rows
    heads = columns // HD
    side = whole_tiles(3 * part)

    def kernel(*refs):
        grads = refs[:n_tp]
        probs_hbm, qkv_hbm, wqkv_hbm, so_hbm = refs[n_tp : n_tp + 4]
        given_refs, refs = refs[n_tp + 4 : n_tp + 4 + len(given)], refs[: n_tp + 4] + refs[n_tp + 4 + len(given) :]
        keep, give, own_ref = refs[n_tp + 4 : n_tp + 7]
        others = refs[n_tp + 7 : 2 * n_tp + 6]
        grad_y = refs[2 * n_tp + 6]
        given_got, refs = refs[2 * n_tp + 7 : 2 * n_tp + 8 + len(given)], refs[2 * n_tp + 8 + len(given) :]
        w_qkv, w_o, qkv_ref, probs_ref, grad_attn, d_all, sems, pair_send, pair_recv = refs
        greet_devices(pair_places())
        pairs = PairCopies(pair_send, pair_recv)
        for (unused, first), ref, target in zip(given, given_refs, given_got):
            pairs.start(ref, target, first)
        if side > 3 * part:
            for ref in (keep, give):
                ref[:, 3 * part :] = jnp.zeros((count, side - 3 * part), BF)
        moves = Moves(sems)
        o_in = moves.start(so_hbm, w_o)
        qkv_in = moves.start(qkv_hbm, qkv_ref)
        probs_in = moves.start(probs_hbm, probs_ref)
        weight_in = moves.start(wqkv_hbm, w_qkv)
        for frame in range(frames_here):
            for r in range(n_tp):
                at = frame * per_frame + r * patch_part
                grad_y[at : at + patch_part, :] = grads[r][
                    frame * patch_part : (frame + 1) * patch_part, :
                ]
        o_in.wait()
        grad_attn[...] = dot_nt(grad_y[...], w_o[...]).astype(BF)
        qkv_in.wait()
        probs_in.wait()
        for frame in range(frames_here):
            at = slice(frame * per_frame, (frame + 1) * per_frame)

            def into(i, at=at):
                def write(low, high, value):
                    d_all[i, at, low:high] = value.astype(BF)

                return write

            attend_back(
                lambda low, high, at=at: qkv_ref[0, at, low:high],
                lambda low, high, at=at: qkv_ref[1, at, low:high],
                lambda low, high, at=at: qkv_ref[2, at, low:high],
                lambda low, high, at=at: grad_attn[at, low:high],
                lambda head, frame=frame: probs_ref[frame * heads + head],
                heads,
                columns,
                into(0),
                into(1),
                into(2),
            )
        mine = bit_of(q_first)
        for i in range(3):
            value = d_all[i]
            first, second = value[:, :part], value[:, part:]
            keep[:, i * part : (i + 1) * part] = jnp.where(mine == 0, first, second)
            give[:, i * part : (i + 1) * part] = jnp.where(mine == 0, second, first)
        pairs.start(give, given_got[-1], q_first)
        weight_in.wait()
        for frame in range(frames_here):
            at = slice(frame * per_frame, (frame + 1) * per_frame)
            grad_h = dot_nn(d_all[0, at, :], w_qkv[0])
            for i in (1, 2):
                grad_h = grad_h + dot_nn(d_all[i, at, :], w_qkv[i])
            here = slice(frame * patch_part, (frame + 1) * patch_part)
            own_ref[here, :] = grad_h[:patch_part]
            for r in range(1, n_tp):
                others[r - 1][here, :] = grad_h[r * patch_part : (r + 1) * patch_part].astype(BF)
        pairs.finish()

    ins = [*grad_y_list, probs, qkv, sqkv_rows, w_so] + [array for array, unused in given]
    return call(
        kernel,
        [like((count, side))] * 2
        + [like((rows, width), F32)]
        + [like((rows, width))] * (n_tp - 1)
        + [like((count, width))]
        + [like(array.shape) for array, unused in given]
        + [like((count, side))],
        ins,
        [False] * n_tp + [True] * (4 + len(given)),
        [False] * (n_tp + 3) + [True] * (len(given) + 1),
        [
            VMEM((3, columns, width), BF),
            VMEM((columns, width), BF),
            VMEM((3, count, columns), BF),
            VMEM(probs.shape, BF),
            VMEM((count, columns), BF),
            VMEM((3, count, columns), BF),
            pltpu.SemaphoreType.DMA((4,)),
        ]
        + swap_sems(len(given) + 1, 1),
        collective_id=8,
        has_side_effects=True,
    )


def tokens_gradient(tokens_rows, grad, grad_h_own, grad_h_others, mod_here, frames_here, after):
    rows, width = tokens_rows.shape
    patch_part = rows // frames_here
    others = len(grad_h_others)

    def kernel(*refs):
        token_ref, grad_ref, own_ref = refs[:3]
        mod_ref, out_ref, sum_ref = refs[3 + others :]
        for frame in range(frames_here):
            at = slice(frame * patch_part, (frame + 1) * patch_part)
            grad_h = own_ref[at, :]
            for other in refs[3 : 3 + others]:
                grad_h = grad_h + other[at, :].astype(F32)
            normed, inverse = norm_of(token_ref[at, :].astype(F32))
            sum_ref[frame : frame + 1, 0:width] = jnp.sum(grad_h, axis=0, keepdims=True)
            sum_ref[frame : frame + 1, width:] = jnp.sum(grad_h * normed, axis=0, keepdims=True)
            scale = 1.0 + mod_ref[frame : frame + 1, width : 2 * width]
            out_ref[at, :] = (grad_ref[at, :] + norm_back(grad_h * scale, normed, inverse)).astype(BF)

    ins = [tokens_rows, grad, grad_h_own, *grad_h_others, mod_here]
    return call(
        kernel,
        [like((rows, width)), like((frames_here, 2 * width), F32)],
        ins,
        [False] * len(ins),
        [False] * 2,
        [],
        after,
    )


def flip(operand, mask):
    size = lax.axis_size("wide")
    return lax.ppermute(operand, "wide", [(s, s ^ mask) for s in range(size)])


def tp_from(operand, shift):
    size = lax.axis_size("tp")
    return lax.ppermute(operand, "tp", [(s, (s - shift) % size) for s in range(size)])


def tp_to(operand, shift):
    size = lax.axis_size("tp")
    return lax.ppermute(operand, "tp", [(s, (s + shift) % size) for s in range(size)])


def tp_gather(operand):
    return [operand] + [tp_from(operand, k) for k in range(1, lax.axis_size("tp"))]


class Pack:
    def __init__(self, first, order, layout):
        self.first, self.layout = first, layout
        self.order = order + [bit for bit in range(wide_bits()) if bit != first and bit not in order]
        self.across = sum(groups * cols for groups, cols in layout)


def scatter_rows(total, keep, give, pack, size):
    block = keep.shape[1]
    across = pack.across
    mine = bit_of(pack.order[0])
    inner = pack.order[1:] + [pack.first]
    for at in range(size // 2):
        parts = []
        for value in range(2):
            place = value << pack.order[0]
            for depth, bit in enumerate(inner):
                place |= ((at >> (len(inner) - 1 - depth)) & 1) << bit
            parts.append(total[place * block : (place + 1) * block, 0:across].astype(BF))
        keep[at] = jnp.where(mine == 0, parts[0], parts[1])
        give[at] = jnp.where(mine == 0, parts[1], parts[0])


class Flow:
    def __init__(self, pack, keep, give, lands, send_sem, recv_sem, outs):
        self.pack, self.keep, self.give, self.lands = pack, keep, give, lands
        self.send_sem, self.recv_sem, self.outs = send_sem, recv_sem, outs
        self.bits = pack.order + [pack.first]
        self.level, self.behind, self.base = 0, 0, 0
        self.first, self.second, self.placed = None, None, False

    def region(self, level, part):
        number = self.lands[level].shape[0]
        if number == 1:
            return 0, 1
        half = number // 2
        mine = bit_of(self.bits[level + 1])
        return (mine if part else 1 - mine) * half, half

    def start(self, part):
        level = self.level
        low, number = self.region(level, part)
        if level == 0:
            source = self.give.at[pl.ds(low, number)]
        else:
            shift = self.region(level - 1, 0)[0]
            source = self.lands[level - 1].at[pl.ds(shift + low, number)]
        copy = pltpu.make_async_remote_copy(
            src_ref=source,
            dst_ref=self.lands[level].at[pl.ds(low, number)],
            send_sem=self.send_sem.at[2 * level + part],
            recv_sem=self.recv_sem.at[2 * level + part],
            device_id={"wide": partner(self.bits[level])},
            device_id_type=pl.DeviceIdType.MESH,
        )
        copy.start()
        return copy

    def send(self):
        if self.first is None and not self.placed:
            self.first = self.start(0)

    def wait(self):
        if self.placed:
            return
        self.part()
        self.send()
        self.first.wait()
        level = self.level
        land = self.lands[level]
        if land.shape[0] == 1:
            self.place(land)
            return
        self.second = self.start(1)
        low, number = self.region(level, 0)
        for i in range(number):
            own = self.keep[self.base + low + i].astype(F32)
            land[low + i] = (own + land[low + i].astype(F32)).astype(BF)
        self.level, self.first = level + 1, None

    def part(self):
        if self.second is None:
            return
        self.second.wait()
        self.second = None
        low, number = self.region(self.behind, 1)
        land = self.lands[self.behind]
        for i in range(number):
            own = self.keep[self.base + low + i].astype(F32)
            self.keep[self.base + low + i] = (own + land[low + i].astype(F32)).astype(BF)
        self.base = self.base + low
        self.behind += 1

    def go(self):
        self.wait()
        self.send()

    def place(self, land):
        self.placed = True
        mine = bit_of(self.pack.first)
        own, other = self.keep[self.base].astype(F32), land[0].astype(F32)
        sides = [jnp.where(mine == 0, own, other), jnp.where(mine == 0, other, own)]
        low = 0
        for out, (groups, cols) in zip(self.outs, self.pack.layout):
            for g in range(groups):
                for side in range(2):
                    value = sides[side][:, low + g * cols : low + (g + 1) * cols]
                    if groups == 1:
                        out[:, side * cols : (side + 1) * cols] = value
                    else:
                        out[g, :, side * cols : (side + 1) * cols] = value
            low += groups * cols


def reduce_all(ready_packs, rows_packs, slot_packs, kv_parts, mod_blocks, embed, texts, text_cols, ckv_rows, schedule, after, extra_rows=0):
    n_tp, size = lax.axis_size("tp"), lax.axis_size("wide")
    bits = wide_bits()
    packs = [member[0] for member in (*ready_packs, *rows_packs, *slot_packs)]
    n_ready, n_rows, n_slots = len(ready_packs), len(rows_packs), len(slot_packs)
    rows, width = rows_packs[0][2].shape
    count = n_tp * rows
    block = width // size
    others = n_tp - 1
    most = max(whole_tiles(member[0].across) for member in rows_packs)
    token_rows = slot_packs[0][3].shape[0]
    models = len(slot_packs[0][1])
    slot_width = max(member[3].shape[1] for member in slot_packs)
    keys, columns = kv_parts[0].shape[0] * kv_parts[0].shape[1], kv_parts[0].shape[2]
    context_cols = width // size
    owned = width // n_tp

    row_ins = [array for member in rows_packs for array in member[1:5]]
    slot_ins = [array for member in slot_packs for array in (*member[1], *member[2], *member[3:5])]
    ready_ins = [array for member in ready_packs for array in member[1:]]
    ins = ready_ins + row_ins + slot_ins + [ckv_rows, texts, mod_blocks, embed] + list(kv_parts)
    in_any = [True] * (len(ready_ins) + len(row_ins) + len(slot_ins) + 1) + [False] * 3 + [True] * len(kv_parts)
    result = []
    for pack in packs:
        for groups, cols in pack.layout:
            result.append(like((block, 2 * cols) if groups == 1 else (groups, block, 2 * cols), F32))
    landing = [like((rows, width))] * (n_rows * others)
    for member in slot_packs:
        landing += [like((token_rows, width))] * (2 * models * others)
        landing += [like(member[3].shape)] * (2 * others)
    pairs = [p for p, member in enumerate(rows_packs) if member[6]]
    landing += [like(rows_packs[p][4].shape) for p in pairs]
    spare = mod_blocks.shape[1]
    kv_block_rows = kv_parts[0].shape[1]
    clips = embed.shape[0]
    mod_row = kv_block_rows if extra_rows else kv_block_rows - spare
    mod_cols = 6 * width // (n_tp * size)
    outs = result + [like((context_cols, columns), F32), like((owned, text_cols), F32)]
    outs += [like((mod_cols, width), F32), like((1, mod_cols), F32)] + landing
    out_any = [False] * (len(result) + 4) + [True] * len(landing)
    scratch = [VMEM((count, width), BF)] * 2 + [VMEM((count, most), BF)] * 2
    scratch += [VMEM((token_rows, width), BF)] * (2 * n_tp * models)
    scratch += [VMEM((token_rows, slot_width), BF)] * (2 * n_tp)
    scratch += [VMEM((width, max(pack.across for pack in packs)), F32)]
    for pack in packs:
        shape = (block, pack.across)
        scratch += [VMEM((size // 2,) + shape, BF)] * 2
        scratch += [VMEM((size >> (s + 1),) + shape, BF) for s in range(bits)]
        scratch += [pltpu.SemaphoreType.DMA((2 * bits,))] * 2
    n_core = others * (n_rows + 2 * (models + 1) * n_slots + 2)
    n_moves = n_rows * 3 + sum(member[5] * n_tp for member in rows_packs) + 2 * n_tp * n_slots * (models + 1) + 1 + 2 * n_ready + n_tp
    kv_block = kv_parts[0].shape[1:]
    sum_block = (kv_block[0] + extra_rows, kv_block[1])
    kv_scratch = level_scratch(size, sum_block) + level_scratch(size, sum_block)[1:] + level_scratch(size, kv_block)
    scratch += [pltpu.SemaphoreType.DMA((n_core,))] * 2 + [pltpu.SemaphoreType.DMA((n_moves,))]
    scratch += [VMEM(kv_parts[0].shape, BF)] + kv_scratch + [pltpu.SemaphoreType.DMA((bits,))] * 4
    scratch += [VMEM((keys, columns), BF), VMEM((columns, width), BF), VMEM((2 * others, keys, owned), BF)]
    scratch += [VMEM((keys, owned), F32), VMEM((2 * others, 8, whole_tiles(clips * mod_cols)), F32)]
    scratch += [pltpu.SemaphoreType.DMA((max(len(pairs), 1),))] * 2

    def kernel(*refs):
        refs = list(refs)

        def take(number):
            taken = refs[:number]
            del refs[:number]
            return taken

        ready_refs = [take(2) for unused in range(n_ready)]
        row_refs = [take(4) for unused in range(n_rows)]
        slot_refs = [[take(models), take(models), take(2)] for unused in range(n_slots)]
        ckv_ref, text_ref, mod_ref, embed_ref = take(4)
        kv_refs = take(len(kv_parts))
        results = [take(len(pack.layout)) for pack in packs]
        grad_ckv, grad_text, grad_mod, grad_bias = take(4)
        row_land = [take(others) for unused in range(n_rows)]
        slot_land = [
            [[take(models) for unused in range(2)] for unused2 in range(others)]
            + [[take(others) for unused in range(2)]]
            for unused3 in range(n_slots)
        ]
        pair_land = dict(zip(pairs, take(len(pairs))))
        own_model, got_model, own_head, got_head = take(4)
        model_stages = [take(models) for unused in range(2 * n_tp)]
        stages = take(2 * n_tp)
        (total,) = take(1)
        flows = []
        for pack, result_refs in zip(packs, results):
            keep, give = take(2)
            lands = take(bits)
            flows.append(Flow(pack, keep, give, lands, *take(2), result_refs))
        send_sem, recv_sem, move_sem, kv_stage = take(4)
        halving_levels, halving_lands, doubling_levels = take(bits + 1), take(bits), take(bits + 1)
        kv_sems = take(4)
        kv_all, ckv, exchange, text_own, mod_exchange, pair_send, pair_recv = take(7)

        greet_devices(core_places() + pair_places())
        moves = Moves(move_sem)
        core = CoreCopies(send_sem, recv_sem)
        for i, ref in enumerate(kv_refs):
            moves.start(ref, kv_stage).wait()
            for at in range(size):
                value = kv_stage[at].astype(F32)
                level = halving_levels[0].at[mirrored(at)]
                if i == 0:
                    if extra_rows:
                        value = jnp.concatenate([value, jnp.zeros((extra_rows, kv_block[1]), F32)], axis=0)
                    row = lax.broadcasted_iota(jnp.int32, sum_block, 0)
                    for j in range(spare):
                        value = jnp.where(row == mod_row + j, mod_ref[at, j : j + 1, :], value)
                    level[...] = value.astype(BF)
                else:
                    own = level[0 : kv_block[0], :].astype(F32)
                    level[0 : kv_block[0], :] = (own + value).astype(BF)
        ready_loads = [
            (moves.start(give, flows[p].give), moves.start(keep, flows[p].keep))
            for p, (keep, give) in enumerate(ready_refs)
        ]
        halving = Halving(halving_levels, halving_lands, *kv_sems[:2])
        halving.start()
        doubling = Doubling(doubling_levels, *kv_sems[2:])

        pair_flights = {}
        for i, p in enumerate(pairs):
            copy = pltpu.make_async_remote_copy(
                src_ref=row_refs[p][3],
                dst_ref=pair_land[p],
                send_sem=pair_send.at[i],
                recv_sem=pair_recv.at[i],
                device_id={"wide": partner(rows_packs[p][0].first)},
                device_id_type=pl.DeviceIdType.MESH,
            )
            copy.start()
            pair_flights[p] = copy
        row_flights, slot_flights = {}, {}

        def core_rows(p):
            row_flights[p] = [
                core.start(row_refs[p][1], row_land[p][n_tp - 2 - k], place)
                for k, place in enumerate(core_places())
            ]

        def core_slots(p):
            slot = slot_packs[p][5]
            flights = []
            for k, place in enumerate(core_places()):
                for side in range(2):
                    for ref, to in zip(slot_refs[p][side], slot_land[p][k][side]):
                        flights.append(core.start(ref, to, place))
                    ref, to = slot_refs[p][2][side], slot_land[p][others][side][k]
                    cols = pl.ds((k + 1) * slot, slot)
                    flights.append(core.start(ref.at[:, cols], to.at[:, cols], place))
            slot_flights[p] = flights

        ckv_in = moves.start(ckv_ref, ckv)
        loads = {}

        def load_rows(p):
            model, got, keep, other = row_refs[p]
            frames = rows_packs[p][5]
            step = rows // frames
            cols = pl.ds(0, keep.shape[1])
            loads[p] = [moves.start(model, own_model), moves.start(keep, own_head.at[:, cols])]
            if p in pair_flights:
                pair_flights[p].wait()
                other = pair_land[p]
            loads[p].append(moves.start(other, got_head.at[:, cols]))
            for frame in range(frames):
                target = got_model.at[pl.ds(frame * n_tp * step, step), :]
                loads[p].append(moves.start(got.at[pl.ds(frame * step, step), :], target))

        def rows_product(p):
            frames = rows_packs[p][5]
            step = rows // frames
            across = rows_packs[p][0].across
            for copy in loads[p][:2]:
                copy.wait()
            total[:, 0:across] = dot_tn(own_model[...], own_head[:, 0:across])
            for copy in row_flights[p]:
                copy.wait()
            rest = loads[p][2:]
            for frame in range(frames):
                for k in range(others):
                    target = got_model.at[pl.ds((frame * n_tp + k + 1) * step, step), :]
                    rest.append(moves.start(row_land[p][k].at[pl.ds(frame * step, step), :], target))
            for copy in rest:
                copy.wait()
            total[:, 0:across] += dot_tn(got_model[...], got_head[:, 0:across])
            flow = flows[n_ready + p]
            scatter_rows(total, flow.keep, flow.give, rows_packs[p][0], size)

        def stage(p, side, k):
            wide = slot_packs[p][3].shape[1]
            at = 2 * k + side
            if k == 0:
                model_refs, head = slot_refs[p][side], slot_refs[p][2][side]
            else:
                model_refs, head = slot_land[p][k - 1][side], slot_land[p][others][side][k - 1]
            found = [moves.start(ref, to) for ref, to in zip(model_refs, model_stages[at])]
            return found + [moves.start(head, stages[at].at[:, pl.ds(0, wide)])]

        def load_slots(p):
            loads[n_rows + p] = stage(p, 0, 0) + stage(p, 1, 0)

        def slots_product(p):
            pack, unused, unused2, unused3, unused4, slot, weights = slot_packs[p]

            def add(k):
                low = 0
                for model, column, cols in weights:
                    at = k * slot + column
                    terms = [
                        dot_tn(model_stages[2 * k + side][model][...], stages[2 * k + side][:, at : at + cols])
                        for side in range(2)
                    ]
                    if k == 0:
                        total[:, low : low + cols] = terms[0] + terms[1]
                    else:
                        total[:, low : low + cols] += terms[0] + terms[1]
                    low += cols

            for copy in loads[n_rows + p]:
                copy.wait()
            add(0)
            for copy in slot_flights[p]:
                copy.wait()
            rest = [copy for k in range(1, n_tp) for side in range(2) for copy in stage(p, side, k)]
            for copy in rest:
                copy.wait()
            for k in range(1, n_tp):
                add(k)
            flow = flows[n_ready + n_rows + p]
            scatter_rows(total, flow.keep, flow.give, pack, size)

        def caption():
            if halving.bit < bits:
                halving.advance()
                if halving.bit == bits:
                    doubling_levels[bits][0] = halving_levels[bits][0, 0 : kv_block[0], :]
                    doubling.start()
            elif doubling.bit:
                doubling.advance()

        text_flights = []

        def context():
            while doubling.bit:
                caption()
            for at in range(size):
                kv_all[at * kv_block[0] : (at + 1) * kv_block[0], :] = doubling_levels[0][mirrored(at)]
            grad_ckv[...] = dot_tn(text_ref[:, text_cols : text_cols + context_cols], kv_all[...])
            ckv_in.wait()
            grad = dot_nn(kv_all[...], ckv[...])
            here = lax.axis_index("tp")

            def part(owner):
                chosen = grad[:, 0:owned]
                for other in range(1, n_tp):
                    chosen = jnp.where(owner == other, grad[:, other * owned : (other + 1) * owned], chosen)
                return chosen

            for k, place in enumerate(core_places()):
                exchange[k] = part(lax.rem(here + k + 1, n_tp)).astype(BF)
                text_flights.append(core.start(exchange.at[k], exchange.at[others + k], place))
            text_own[...] = part(here)

        def text():
            grad = text_own[...]
            for k, copy in enumerate(text_flights):
                copy.wait()
                grad = grad + exchange[others + k].astype(F32)
            grad_text[...] = dot_tn(grad.astype(BF), text_ref[:, 0:text_cols])

        mod_flights = []
        flat = clips * mod_cols

        def modulation_part(owner):
            rows_here = halving_levels[bits][0].astype(F32)[mod_row : mod_row + spare, :]
            row = jnp.concatenate([rows_here[i : i + 1] for i in range(spare)], axis=1)
            chosen = row[:, 0:flat]
            for other in range(1, n_tp):
                chosen = jnp.where(owner == other, row[:, other * flat : (other + 1) * flat], chosen)
            return chosen

        def modulation_send():
            here = lax.axis_index("tp")
            for k, place in enumerate(core_places()):
                part = modulation_part(lax.rem(here + k + 1, n_tp))
                mod_exchange[k, :, 0:flat] = jnp.broadcast_to(part, (8, flat))
                if mod_exchange.shape[2] > flat:
                    mod_exchange[k, :, flat:] = jnp.zeros((8, mod_exchange.shape[2] - flat), F32)
                mod_flights.append(core.start(mod_exchange.at[k], mod_exchange.at[others + k], place))

        def modulation():
            total_row = modulation_part(lax.axis_index("tp"))
            for k, copy in enumerate(mod_flights):
                copy.wait()
                total_row = total_row + mod_exchange[others + k, 0:1, 0:flat]
            sums = jnp.concatenate(
                [total_row[:, c * mod_cols : (c + 1) * mod_cols] for c in range(clips)], axis=0
            )
            grad_bias[...] = jnp.sum(sums, axis=0, keepdims=True)
            grad_mod[...] = dot_tn(sums.astype(BF), embed_ref[...])

        for what, p in schedule:
            row, slot = p - n_ready, p - n_ready - n_rows
            if what == "core":
                core_rows(row) if slot < 0 else core_slots(slot)
            elif what == "load":
                load_rows(row) if slot < 0 else load_slots(slot)
            elif what == "product":
                if row < 0:
                    for copy in ready_loads[p]:
                        copy.wait()
                elif slot < 0:
                    rows_product(row)
                else:
                    slots_product(slot)
            elif what == "send":
                flows[p].send()
            elif what == "wait":
                flows[p].wait()
            elif what == "part":
                flows[p].part()
            elif what == "go":
                flows[p].go()
            elif what == "caption":
                caption()
            elif what == "context":
                context()
                modulation_send()
            elif what == "modulation":
                modulation()
            else:
                text()
        while not all(flow.placed for flow in flows):
            for flow in flows:
                flow.go()

    out = call(
        kernel,
        outs,
        ins,
        in_any,
        out_any,
        scratch,
        after,
        limit=63,
        collective_id=4,
        has_side_effects=True,
    )
    return out[: len(result)], *out[len(result) : len(result) + 4]


def tp_sum(parts, dtype=BF):
    total = parts[0].astype(F32)
    for k in range(1, lax.axis_size("tp")):
        total = total + tp_to(parts[k].astype(dtype), k).astype(F32)
    return total


def tp_ordered(relative):
    size = lax.axis_size("tp")
    start = (size - lax.axis_index("tp")) % size
    return lax.dynamic_slice_in_dim(jnp.stack(relative + relative), start, size, axis=0)


def swap_wide(blocks):
    return lax.all_to_all(blocks, "wide", split_axis=0, concat_axis=0, tiled=True)


def on_device(
    tokens,
    cotangent,
    caption,
    caption_len,
    clip_id,
    timestep,
    w_mod,
    b_mod,
    w_text,
    w_sqkv,
    w_so,
    w_tqkv,
    w_to,
    w_cq,
    w_ckv,
    w_co,
    w_fc1,
    w_fc2,
):
    n_tp = lax.axis_size("tp")
    n_wide = lax.axis_size("wide")
    frames_here, patch_part, width = tokens.shape
    columns = w_so.shape[0]
    part = columns // 2
    half = w_fc1.shape[1] // 2
    clip_count = timestep.shape[0]
    frames = clip_id.shape[0]
    patch_here = patch_part // n_wide
    rows = frames_here * patch_part
    block = frames_here * patch_here
    count = frames * patch_here
    wide_at = lax.axis_index("wide")
    tp_at = lax.axis_index("tp")

    tokens_rows = tokens.reshape(rows, width)
    tokens_list = tp_gather(tokens_rows)
    sqkv_rows = w_sqkv.transpose(1, 2, 0)
    tqkv_list = tp_gather(w_tqkv.transpose(1, 2, 0))
    to_list = tp_gather(w_to)
    cq_list = tp_gather(w_cq.T)
    co_list = tp_gather(w_co)

    half_width = width // 2
    frequencies = jnp.exp(-math.log(10000.0) * jnp.arange(half_width).astype(F32) / half_width)
    angles = timestep.astype(F32)[:, None] * frequencies[None, :]
    embedding = jnp.concatenate([jnp.cos(angles), jnp.sin(angles)], axis=1)
    silu_embed = jax.nn.silu(embedding).astype(BF)
    mod_part = (dot_nn(silu_embed, w_mod) + b_mod.astype(F32)).astype(BF)
    modulation = tp_ordered(tp_gather(mod_part)).transpose(1, 0, 2).reshape(clip_count, -1)
    clip_hot = clip_id[:, None] == jnp.arange(clip_count)[None, :]
    hot_here = lax.dynamic_slice_in_dim(
        clip_hot.astype(F32), wide_at * frames_here, frames_here
    )
    mod_here = dot_nn(hot_here.astype(BF), modulation[:, : 3 * width])
    clip_rows = jnp.broadcast_to(clip_id[:, None], (frames, patch_here)).reshape(count)
    hot_rows = (clip_rows[:, None] == jnp.arange(clip_count)[None, :]).astype(BF)
    mod_rows = dot_nn(hot_rows, modulation[:, 3 * width :]).astype(BF)

    caption_rows = caption.shape[0]
    spare_rows = -(-clip_count * 6 * width // (n_wide * 2 * columns))
    block_rows = -(-caption_rows // 16) * 16
    extra_rows = 0 if caption_rows + spare_rows <= block_rows else -(-spare_rows // 16) * 16
    keys = n_wide * block_rows
    padded = jnp.pad(caption, ((0, block_rows - caption_rows), (0, 0)))
    context_part = dot_nt(padded, w_text.T).astype(BF)
    context = tp_ordered(tp_gather(context_part)).transpose(1, 0, 2).reshape(block_rows, width)
    ckv_rows = w_ckv.transpose(1, 2, 0).reshape(2 * columns, width)
    keyval_part = dot_nt(context, ckv_rows).astype(BF)
    text_cols = caption.shape[1] // n_wide
    context_cols = width // n_wide
    spare = -(text_cols + context_cols) % LANES
    texts = jnp.concatenate(
        [
            padded.reshape(block_rows, n_wide, text_cols),
            context.reshape(block_rows, n_wide, context_cols),
            jnp.zeros((block_rows, n_wide, spare), BF),
        ],
        axis=2,
    ).transpose(1, 0, 2)

    row_two = clip_rows * patch_here + np.arange(count, dtype=np.int32) % patch_here
    key_at = np.arange(keys)
    key_row = key_at // block_rows * caption_rows + key_at % block_rows
    key_real = jnp.asarray(key_at % block_rows < caption_rows)[None, :]
    key_clip = (key_row // LTXT).astype(np.int32)[None, :]
    key_in = (key_row % LTXT).astype(np.int32)[None, :]
    key_three = jnp.full((1, keys), -1, jnp.int32)
    for clip in range(clip_count):
        seen = key_real & (key_clip == clip) & (key_in < caption_len[clip])
        key_three = jnp.where(seen, clip, key_three)
    row_codes = jnp.stack([row_two, clip_rows], axis=1)
    longest = max(count, keys)
    key_codes = jnp.concatenate(
        [jnp.pad(row_two[None, :], ((0, 0), (0, longest - count))), jnp.pad(key_three, ((0, 0), (0, longest - keys)))]
    )

    grad_blocks = cotangent.reshape(frames_here, n_wide, patch_here, width).transpose(1, 0, 2, 3)
    grad_blocks = grad_blocks.reshape(n_wide, block, width)

    up = Pack(0, [1, 3, 2], [(1, half)])
    down = Pack(1, [0, 2, 3], [(1, half)])
    inner = Pack(2, [0, 1, 3], [(3, part), (1, part)])
    outer = Pack(1, [2, 0, 3], [(1, part), (1, part)])
    q_pack = Pack(0, [1, 2, 3], [(3, part)])
    o_pack = Pack(0, [2, 1, 3], [(1, part)])

    h_all, h_own, qkv_one, probs_one, a_keep, a_give, y_own, *others = spatial_forward(
        tokens_list, mod_here, sqkv_rows, w_so, frames_here, keyval_part, o_pack.first
    )
    y_others, keyval = others[: n_tp - 1], others[n_tp - 1]
    keyval_list = tp_gather(keyval.reshape(keys, 2 * columns))
    y_others = [tp_to(other, k + 1) for k, other in enumerate(y_others)]
    stream, y_one = stream_to_patches(tokens_rows, y_own, y_others, mod_here, frames_here)
    *kept, stream, keyval_full, t_keep, t_give, grad_out, a_got = middle_forward(
        stream.reshape(count, width), row_codes, key_codes, [grad_blocks], keyval_list, tqkv_list, to_list, cq_list, co_list, outer.first,
        [(a_give, o_pack.first)],
    )
    grad_out = grad_out.reshape(count, width)
    h2, h3 = kept[0], kept[4]
    (
        block_out,
        h4_all,
        up_keep,
        up_give,
        dy4_all,
        down_keep,
        down_give,
        grad,
        mod_sum,
        unused,
        unused,
        h4_got,
        dy4_got,
        h2_got,
        h3_got,
        t_got,
        h_flip,
    ) = feed_forward(
        stream,
        grad_out,
        mod_rows,
        hot_rows,
        w_fc1,
        w_fc2,
        [up.first, down.first],
        [(h2, inner.first), (h3, inner.first), (t_give, outer.first), (h_own, q_pack.first)],
    )

    in_keep, in_give, dy2, dy3, grad, block_out, texts, up_got, down_got, *grad_kv = middle_backward(
        grad,
        kept,
        keyval_full,
        block_out.reshape(n_wide, block, width),
        texts,
        tqkv_list,
        to_list,
        cq_list,
        co_list,
        inner.first,
        [(up_give, up.first), (down_give, down.first)],
    )
    block_out = block_out.reshape(n_wide, frames_here, patch_here, width).transpose(1, 0, 2, 3)
    block_out = block_out.reshape(frames_here, patch_part, width)
    (grad_stream, grad_y1, grad_gate), (up_halves, down_halves) = grads_to_frames(
        grad.reshape(n_wide, block, width),
        y_one,
        mod_here,
        frames_here,
        [(up, h4_all, h4_got, up_keep, up_got), (down, dy4_all, dy4_got, down_keep, down_got)],
    )
    grad_y1_list = tp_gather(grad_y1)
    given = [(in_give, inner.first), (dy2, outer.first), (dy3, outer.first), (grad_y1, o_pack.first)]
    q_keep, q_give, grad_h_own, *grad_h_others, dy_all, in_got, dy2_got, dy3_got, dy_got, q_got = spatial_backward(
        grad_y1_list, probs_one, qkv_one, sqkv_rows, w_so, frames_here, given, q_pack.first
    )
    grad_h_others = [tp_to(other, k + 1) for k, other in enumerate(grad_h_others)]
    grad_tokens, frame_sums = tokens_gradient(
        tokens_rows, grad_stream, grad_h_own, grad_h_others, mod_here, frames_here, []
    )
    frame_sums = jnp.concatenate([frame_sums, grad_gate], axis=1)
    here_sum = lax.dot_general(hot_here, frame_sums, (((0,), (0,)), ((), ())), precision=HIGH)
    grad_mod = jnp.concatenate([here_sum, mod_sum], axis=1).reshape(clip_count, n_tp, n_wide, -1)
    mod_blocks = grad_mod.transpose(2, 1, 0, 3).reshape(n_wide, -1)
    mod_blocks = jnp.pad(mod_blocks, ((0, 0), (0, spare_rows * 2 * columns - mod_blocks.shape[1])))
    mod_blocks = mod_blocks.reshape(n_wide, spare_rows, 2 * columns)
    kv_parts = [grad_kv[0].reshape(n_wide, block_rows, -1)]
    kv_parts += [tp_to(grad_kv[k], k).reshape(n_wide, block_rows, -1) for k in range(1, n_tp)]
    schedule = [
        ("core", 3), ("core", 5), ("load", 3), ("load", 5), ("product", 0), ("send", 0),
        ("product", 1), ("send", 1), ("product", 3), ("core", 2), ("load", 2), ("send", 3),
        ("product", 5), ("core", 4), ("load", 4), ("send", 5), ("product", 2), ("send", 2),
        ("wait", 3), ("send", 3), ("product", 4), ("send", 4), ("caption", 0), ("wait", 5),
        ("send", 5), ("part", 3), ("wait", 0), ("send", 0), ("wait", 3), ("send", 3),
        ("wait", 1), ("send", 1), ("part", 3), ("wait", 3), ("send", 3), ("caption", 0),
        ("part", 3), ("wait", 3), ("part", 5), ("wait", 5), ("send", 5), ("wait", 2),
        ("send", 2), ("caption", 0), ("caption", 0), ("part", 5), ("wait", 5), ("send", 5),
        ("caption", 0), ("part", 0), ("wait", 0), ("send", 0), ("wait", 4), ("send", 4),
        ("part", 1), ("part", 5), ("wait", 5), ("part", 2), ("wait", 2), ("send", 2),
        ("wait", 1), ("send", 1), ("caption", 0), ("caption", 0), ("part", 4), ("wait", 4),
        ("send", 4), ("caption", 0), ("context", 0), ("part", 4), ("part", 0), ("text", 0),
        ("modulation", 0), ("part", 2), ("wait", 2), ("send", 2), ("wait", 0), ("send", 0),
        ("wait", 4), ("send", 4), ("part", 1), ("wait", 1), ("send", 1), ("part", 2),
        ("wait", 2), ("part", 0), ("wait", 0), ("part", 4), ("wait", 4), ("part", 1),
        ("wait", 1),
    ]
    gradients, grad_ckv, grad_text, grad_w_mod, grad_b_mod = reduce_all(
        [(up, *up_halves), (down, *down_halves)],
        [
            (q_pack, h_all, h_flip, q_keep, q_got, frames_here, False),
            (o_pack, dy_all, dy_got, a_keep, a_got, frames_here, False),
        ],
        [
            (
                inner,
                [h2, h3],
                [h2_got, h3_got],
                in_keep,
                in_got,
                whole_tiles(4 * part),
                [(0, 0, 3 * part), (1, 3 * part, part)],
            ),
            (
                outer,
                [dy2, dy3],
                [dy2_got, dy3_got],
                t_keep,
                t_got,
                whole_tiles(2 * part),
                [(0, 0, part), (1, part, part)],
            ),
        ],
        kv_parts,
        mod_blocks,
        silu_embed,
        texts.reshape(keys, -1),
        text_cols,
        ckv_rows,
        schedule,
        [grad_tokens],
        extra_rows,
    )
    grad_fc1, grad_fc2, grad_sqkv, grad_so, grad_tqkv, grad_cq, grad_to, grad_co = gradients
    grad_ckv = grad_ckv.reshape(-1, 2, columns)
    grad_text = grad_text.T

    return (
        block_out,
        grad_tokens.reshape(tokens.shape),
        grad_w_mod.T,
        grad_b_mod.reshape(-1),
        grad_text,
        grad_sqkv.transpose(1, 0, 2),
        grad_so.T,
        grad_tqkv.transpose(1, 0, 2),
        grad_to.T,
        grad_cq,
        grad_ckv,
        grad_co.T,
        grad_fc1,
        grad_fc2.T,
    )


def solution(mesh):
    placed = (
        P("wide", "tp", None),
        P("wide", "tp", None),
        P("wide", None),
        P(),
        P(),
        P(),
        P(None, "tp"),
        P("tp"),
        P(None, "tp"),
        P(None, None, "tp"),
        P("tp", None),
        P(None, None, "tp"),
        P("tp", None),
        P(None, "tp"),
        P(None, None, "tp"),
        P("tp", None),
        P(None, "tp"),
        P("tp", None),
    )
    return jax.shard_map(
        on_device,
        mesh=mesh,
        in_specs=placed,
        out_specs=(
            P("wide", "tp", None),
            P("wide", "tp", None),
            P(None, ("tp", "wide")),
            P(("tp", "wide")),
            P("wide", "tp"),
            P("wide", None, "tp"),
            P("tp", "wide"),
            P("wide", None, "tp"),
            P("tp", "wide"),
            P("wide", "tp"),
            P("wide", None, "tp"),
            P("tp", "wide"),
            P("wide", "tp"),
            P("tp", "wide"),
        ),
        check_vma=False,
    )
```

```python
import functools
import math

import jax
import jax.numpy as jnp
import numpy as np
from jax import lax
from jax.experimental import pallas as pl
from jax.experimental.pallas import tpu as pltpu
from jax.sharding import PartitionSpec as P

HD = 72
LTXT = 120
EPS = 1e-06
NEGATIVE = -1e30
HIGH = lax.Precision.HIGHEST
BF = jnp.bfloat16
F32 = jnp.float32
LANES = 128
FACTOR = HD ** (-0.5)
VMEM = pltpu.VMEM
MB = 1 << 20


def dot_nn(left, right):
    return lax.dot_general(left, right, (((1,), (0,)), ((), ())), preferred_element_type=F32)


def dot_nt(left, right):
    return lax.dot_general(left, right, (((1,), (1,)), ((), ())), preferred_element_type=F32)


def dot_tn(left, right):
    return lax.dot_general(left, right, (((0,), (0,)), ((), ())), preferred_element_type=F32)


def norm_of(rows):
    average = jnp.mean(rows, axis=-1, keepdims=True)
    centred = rows - average
    inverse = lax.rsqrt(jnp.mean(centred * centred, axis=-1, keepdims=True) + EPS)
    return centred * inverse, inverse


def norm_back(grad_normed, normed, inverse):
    grad_mean = jnp.mean(grad_normed, axis=-1, keepdims=True)
    grad_cross = jnp.mean(grad_normed * normed, axis=-1, keepdims=True)
    return inverse * (grad_normed - grad_mean - normed * grad_cross)


def window(head, columns):
    low = HD * head
    start = low // LANES * LANES
    stop = min(-(-(low + HD) // LANES) * LANES, columns)
    at = lax.broadcasted_iota(jnp.int32, (1, stop - start), 1) + start
    own = jnp.where((at >= low) & (at < low + HD), 1.0, 0.0).astype(BF)
    return start, stop, own


class Tiles:
    def __init__(self, write, columns, scale=None):
        self.write, self.columns, self.scale, self.open = write, columns, scale, {}

    def add(self, start, stop, value):
        for low in range(start, stop, LANES):
            part = value[:, low - start : min(low + LANES, stop) - start]
            self.open[low] = self.open[low] + part if low in self.open else part

    def flush(self, below):
        for low in sorted(self.open):
            if low + LANES <= below or below >= self.columns:
                part = self.open.pop(low)
                if self.scale is not None:
                    part = part * self.scale
                self.write(low, min(low + LANES, self.columns), part)


def attend(query, key, value, bias, heads, columns, keep_probs, write, between=None):
    out = Tiles(write, columns)
    for head in range(heads):
        start, stop, own = window(head, columns)
        scores = dot_nt(query(start, stop) * own, key(start, stop)) * FACTOR
        if bias is not None:
            scores = scores + bias
        scores = jnp.exp(scores - jnp.max(scores, axis=-1, keepdims=True))
        probs = (scores * (1.0 / jnp.sum(scores, axis=-1, keepdims=True))).astype(BF)
        keep_probs(head, probs)
        out.add(start, stop, dot_nn(probs, value(start, stop) * own))
        out.flush(HD * (head + 1))
        if between is not None and head == heads // 2:
            between()


def attend_back(query, key, value, grad_out, probs_of, heads, columns, write_q, write_k, write_v):
    grad_q = Tiles(write_q, columns, FACTOR)
    grad_k = Tiles(write_k, columns, FACTOR)
    grad_v = Tiles(write_v, columns)
    for head in range(heads):
        start, stop, own = window(head, columns)
        probs = probs_of(head)
        grad_own = grad_out(start, stop) * own
        grad_probs = dot_nt(grad_own, value(start, stop))
        wide_probs = probs.astype(F32)
        grad_scores = wide_probs * grad_probs
        row = jnp.sum(grad_scores, axis=-1, keepdims=True)
        grad_scores = (grad_scores - wide_probs * row).astype(BF)
        grad_q.add(start, stop, dot_nn(grad_scores, key(start, stop) * own))
        grad_k.add(start, stop, dot_tn(grad_scores, query(start, stop) * own))
        grad_v.add(start, stop, dot_tn(probs, grad_own))
        for tiles in (grad_q, grad_k, grad_v):
            tiles.flush(HD * (head + 1))


class Moves:
    def __init__(self, sems):
        self.sems, self.used = sems, 0

    def start(self, source, target):
        copy = pltpu.make_async_copy(source, target, self.sems.at[self.used])
        self.used += 1
        copy.start()
        return copy


def any_spec():
    return pl.BlockSpec(memory_space=pl.ANY)


def vmem_spec():
    return pl.BlockSpec(memory_space=VMEM)


def call(kernel, outs, ins, in_any, out_any, scratch, after=(), limit=56, **params):
    given, extra = len(ins), len(after)

    def ordered(*refs):
        kernel(*refs[:given], *refs[given + extra :])

    return pl.pallas_call(
        ordered,
        out_shape=tuple(outs),
        in_specs=[any_spec() if flag else vmem_spec() for flag in in_any] + [any_spec()] * extra,
        out_specs=tuple(any_spec() if flag else vmem_spec() for flag in out_any),
        scratch_shapes=scratch,
        compiler_params=pltpu.CompilerParams(vmem_limit_bytes=limit * MB, **params),
        cost_estimate=pl.CostEstimate(flops=1, bytes_accessed=1, transcendentals=0),
    )(*ins, *after)


def whole_tiles(columns):
    return -(-columns // LANES) * LANES


def like(shape, dtype=BF):
    return jax.ShapeDtypeStruct(shape, dtype)


def greet(more=()):
    barrier = pltpu.get_barrier_semaphore()
    size = lax.axis_size("wide")
    me = lax.axis_index("wide")

    def signal(k, carry):
        pl.semaphore_signal(
            barrier,
            inc=1,
            device_id={"wide": lax.rem(me + k, size)},
            device_id_type=pl.DeviceIdType.MESH,
        )
        return carry

    lax.fori_loop(1, size, signal, 0)
    for place in more:
        pl.semaphore_signal(barrier, inc=1, device_id=place, device_id_type=pl.DeviceIdType.MESH)
    pl.semaphore_wait(barrier, size - 1 + len(more))


class Swap:
    def __init__(self, send, recv, send_sem, recv_sem, shared=False):
        self.send, self.recv, self.shared = send, recv, shared
        self.send_sem, self.recv_sem = send_sem, recv_sem

    def source(self, at):
        return self.send if self.shared else self.send.at[at]

    def copy(self, k, source, target, peer):
        return pltpu.make_async_remote_copy(
            src_ref=self.source(source),
            dst_ref=self.recv.at[target],
            send_sem=self.send_sem.at[k],
            recv_sem=self.recv_sem.at[k],
            device_id={"wide": peer},
            device_id_type=pl.DeviceIdType.MESH,
        )

    def start(self):
        size, me = lax.axis_size("wide"), lax.axis_index("wide")

        def step(k, carry):
            peer = lax.rem(me + k, size)
            self.copy(k, peer, me, peer).start()
            return carry

        lax.fori_loop(1, size, step, 0)
        self.recv[me] = self.send[...] if self.shared else self.send[me]

    def finish(self):
        size, me = lax.axis_size("wide"), lax.axis_index("wide")

        def arrive(k, carry):
            peer = lax.rem(me + size - k, size)
            self.copy(k, peer, peer, peer).wait_recv()
            return carry

        def leave(k, carry):
            peer = lax.rem(me + k, size)
            self.copy(k, peer, me, peer).wait_send()
            return carry

        lax.fori_loop(1, size, arrive, 0)
        lax.fori_loop(1, size, leave, 0)


def wide_bits():
    return lax.axis_size("wide").bit_length() - 1


def mirrored(at):
    bits = wide_bits()
    return sum(((at >> bit) & 1) << (bits - 1 - bit) for bit in range(bits))


def bit_of(bit):
    return lax.rem(lax.div(lax.axis_index("wide"), 1 << bit), 2)


def partner(bit):
    return lax.axis_index("wide") + (1 - 2 * bit_of(bit)) * (1 << bit)


def greet_devices(places):
    barrier = pltpu.get_barrier_semaphore()
    for place in places:
        pl.semaphore_signal(barrier, inc=1, device_id=place, device_id_type=pl.DeviceIdType.MESH)
    pl.semaphore_wait(barrier, len(places))


def pair_places():
    return [{"wide": partner(bit)} for bit in range(wide_bits())]


def core_places():
    size, me = lax.axis_size("tp"), lax.axis_index("tp")
    return [{"tp": lax.rem(me + k, size)} for k in range(1, size)]


class Doubling:
    def __init__(self, levels, send_sem, recv_sem):
        self.levels, self.send_sem, self.recv_sem = levels, send_sem, recv_sem
        self.bit = wide_bits()
        self.copy = None

    def start(self):
        self.send()

    def send(self):
        bit = self.bit - 1
        have = self.levels[self.bit]
        half = have.shape[0]
        mine = bit_of(bit)
        there = self.levels[bit].at[pl.ds(mine * half, half)]
        self.copy = pltpu.make_async_remote_copy(
            src_ref=have,
            dst_ref=there,
            send_sem=self.send_sem.at[bit],
            recv_sem=self.recv_sem.at[bit],
            device_id={"wide": partner(bit)},
            device_id_type=pl.DeviceIdType.MESH,
        )
        self.copy.start()
        self.levels[bit][pl.ds(mine * half, half)] = have[...]

    def advance(self):
        if self.bit == 0:
            return
        self.copy.wait()
        self.bit -= 1
        if self.bit:
            self.send()

    def finish(self, out):
        while self.bit:
            self.advance()
        for at in range(self.levels[0].shape[0]):
            out[at] = self.levels[0][mirrored(at)]


class Halving:
    def __init__(self, levels, landing, send_sem, recv_sem):
        self.levels, self.landing = levels, landing
        self.send_sem, self.recv_sem = send_sem, recv_sem
        self.bit = 0

    def start(self):
        self.send()

    def send(self):
        bit = self.bit
        half = self.landing[bit].shape[0]
        other = 1 - bit_of(bit)
        self.copy = pltpu.make_async_remote_copy(
            src_ref=self.levels[bit].at[pl.ds(other * half, half)],
            dst_ref=self.landing[bit],
            send_sem=self.send_sem.at[bit],
            recv_sem=self.recv_sem.at[bit],
            device_id={"wide": partner(bit)},
            device_id_type=pl.DeviceIdType.MESH,
        )
        self.copy.start()

    def advance(self):
        bit = self.bit
        if bit == wide_bits():
            return
        half = self.landing[bit].shape[0]
        self.copy.wait()
        own = self.levels[bit][pl.ds(bit_of(bit) * half, half)]
        self.levels[bit + 1][...] = (own.astype(F32) + self.landing[bit][...].astype(F32)).astype(BF)
        self.bit += 1
        if self.bit < wide_bits():
            self.send()

    def finish(self, out):
        while self.bit < wide_bits():
            self.advance()
        out[...] = self.levels[-1][0]


def level_scratch(size, block):
    bits = size.bit_length() - 1
    return [VMEM((size >> s,) + block, BF) for s in range(bits + 1)]


class CoreCopies:
    def __init__(self, send_sem, recv_sem):
        self.send_sem, self.recv_sem, self.used = send_sem, recv_sem, 0

    def start(self, source, target, place):
        copy = pltpu.make_async_remote_copy(
            src_ref=source,
            dst_ref=target,
            send_sem=self.send_sem.at[self.used],
            recv_sem=self.recv_sem.at[self.used],
            device_id=place,
            device_id_type=pl.DeviceIdType.MESH,
        )
        copy.start()
        self.used += 1
        return copy


class PairCopies:
    def __init__(self, send_sem, recv_sem):
        self.send_sem, self.recv_sem, self.copies = send_sem, recv_sem, []

    def start(self, source, target, bit):
        at = len(self.copies)
        copy = pltpu.make_async_remote_copy(
            src_ref=source,
            dst_ref=target,
            send_sem=self.send_sem.at[at],
            recv_sem=self.recv_sem.at[at],
            device_id={"wide": partner(bit)},
            device_id_type=pl.DeviceIdType.MESH,
        )
        copy.start()
        self.copies.append(copy)

    def finish(self):
        for copy in self.copies:
            copy.wait()


def swap_sems(size, count):
    return [pltpu.SemaphoreType.DMA((size,))] * (2 * count)


def spatial_forward(tokens_list, mod_here, sqkv_rows, w_so, frames_here, keyval_part, o_first):
    n_tp = len(tokens_list)
    rows, width = tokens_list[0].shape
    columns = w_so.shape[0]
    patch_part = rows // frames_here
    per_frame = n_tp * patch_part
    count = n_tp * rows
    heads = columns // HD
    size = lax.axis_size("wide")
    bits = wide_bits()

    def kernel(*refs):
        token_refs = refs[:n_tp]
        mod_ref, qkv_hbm, so_hbm, kv_ref = refs[n_tp : n_tp + 4]
        at = n_tp + 4
        h_ref, h_own, qkv_out, probs_out, a_keep, a_give, y_ref = refs[at : at + 7]
        y_others = refs[at + 7 : at + 6 + n_tp]
        at += 6 + n_tp
        kv_out = refs[at]
        weight_qkv, weight_o, qkv_ref, probs_ref, attn_ref, sems, *levels = refs[at + 1 :]
        *levels, send_sem, recv_sem = levels
        greet_devices(pair_places())
        share = Doubling(levels, send_sem, recv_sem)
        levels[bits][0] = kv_ref[...]
        share.start()
        moves = Moves(sems)
        weights = [moves.start(qkv_hbm.at[i], weight_qkv.at[i]) for i in range(3)]
        weight_out = moves.start(so_hbm, weight_o)
        for frame in range(frames_here):
            shift = mod_ref[frame : frame + 1, 0:width]
            scale = 1.0 + mod_ref[frame : frame + 1, width : 2 * width]
            for r in range(n_tp):
                part = token_refs[r][frame * patch_part : (frame + 1) * patch_part, :]
                normed, unused = norm_of(part.astype(F32))
                at = frame * per_frame + r * patch_part
                value = (normed * scale + shift).astype(BF)
                h_ref[at : at + patch_part, :] = value
                if r == 0:
                    h_own[frame * patch_part : (frame + 1) * patch_part, :] = value
        outgoing = []
        share.advance()
        for i in range(3):
            weights[i].wait()
            qkv_ref[i] = dot_nt(h_ref[...], weight_qkv[i]).astype(BF)
            if i == 1:
                share.advance()
        outgoing.append(moves.start(qkv_ref, qkv_out))
        for frame in range(frames_here):
            at = slice(frame * per_frame, (frame + 1) * per_frame)

            def keep_probs(head, probs, frame=frame):
                probs_ref[frame * heads + head] = probs

            def write(low, high, part, at=at):
                attn_ref[at, low:high] = part.astype(BF)

            attend(
                lambda low, high, at=at: qkv_ref[0, at, low:high],
                lambda low, high, at=at: qkv_ref[1, at, low:high],
                lambda low, high, at=at: qkv_ref[2, at, low:high],
                None,
                heads,
                columns,
                keep_probs,
                write,
                share.advance if frame == 0 else None,
            )
        outgoing.append(moves.start(probs_ref, probs_out))
        mine = bit_of(o_first)
        first, second = attn_ref[:, : columns // 2], attn_ref[:, columns // 2 :]
        part = columns // 2
        a_keep[:, 0:part] = jnp.where(mine == 0, first, second)
        a_give[:, 0:part] = jnp.where(mine == 0, second, first)
        for ref in (a_keep, a_give):
            if ref.shape[1] > part:
                ref[:, part:] = jnp.zeros((count, ref.shape[1] - part), BF)
        weight_out.wait()
        for frame in range(frames_here):
            at = frame * per_frame
            branch = dot_nn(attn_ref[at : at + per_frame, :], weight_o[...])
            here = slice(frame * patch_part, (frame + 1) * patch_part)
            y_ref[here, :] = branch[:patch_part]
            for r in range(1, n_tp):
                y_others[r - 1][here, :] = branch[r * patch_part : (r + 1) * patch_part].astype(BF)
        for copy in outgoing:
            copy.wait()
        share.finish(kv_out)

    outs = [
        like((count, width)),
        like((rows, width)),
        like((3, count, columns)),
        like((frames_here * heads, per_frame, per_frame)),
        like((count, whole_tiles(columns // 2))),
        like((count, whole_tiles(columns // 2))),
        like((rows, width), F32),
    ] + [like((rows, width))] * (n_tp - 1)
    outs.append(like((size,) + keyval_part.shape))
    ins = list(tokens_list) + [mod_here, sqkv_rows, w_so, keyval_part]
    return call(
        kernel,
        outs,
        ins,
        [False] * (n_tp + 1) + [True, True, False],
        [False, False, True, True] + [False] * (n_tp + 3),
        [
            VMEM((3, columns, width), BF),
            VMEM((columns, width), BF),
            VMEM((3, count, columns), BF),
            VMEM((frames_here * heads, per_frame, per_frame), BF),
            VMEM((count, columns), BF),
            pltpu.SemaphoreType.DMA((6,)),
        ]
        + level_scratch(size, keyval_part.shape)
        + swap_sems(bits, 1),
        collective_id=1,
        has_side_effects=True,
    )


def stream_to_patches(tokens_rows, y_own, y_others, mod_here, frames_here):
    size = lax.axis_size("wide")
    rows, width = tokens_rows.shape
    patch_part = rows // frames_here
    patch_here = patch_part // size
    block = frames_here * patch_here
    others = len(y_others)

    def kernel(*refs):
        token_ref, y_ref, mod_ref = refs[0], refs[1], refs[2 + others]
        out_ref, total_ref = refs[3 + others : 5 + others]
        send, recv, send_sem, recv_sem = refs[5 + others :]
        greet()
        for frame in range(frames_here):
            at = slice(frame * patch_part, (frame + 1) * patch_part)
            branch = y_ref[at, :]
            for other in refs[2 : 2 + others]:
                branch = branch + other[at, :].astype(F32)
            total_ref[at, :] = branch
            gate = mod_ref[frame : frame + 1, 2 * width : 3 * width]
            stream = token_ref[at, :].astype(F32) + gate * branch
            for owner in range(size):
                send[owner, frame * patch_here : (frame + 1) * patch_here, :] = stream[
                    owner * patch_here : (owner + 1) * patch_here
                ].astype(BF)
        exchange = Swap(send, recv, send_sem, recv_sem)
        exchange.start()
        exchange.finish()
        out_ref[...] = recv[...]

    ins = [tokens_rows, y_own] + list(y_others) + [mod_here]
    return call(
        kernel,
        [like((size, block, width)), like((rows, width), F32)],
        ins,
        [False] * len(ins),
        [False, False],
        [VMEM((size, block, width), BF)] * 2 + swap_sems(size, 1),
        collective_id=2,
        has_side_effects=True,
    )


def grads_to_frames(grad_blocks, y_one, mod_here, frames_here, members):
    size, block, width = grad_blocks.shape
    rows = y_one.shape[0]
    patch_part = rows // frames_here
    patch_here = patch_part // size
    n_tp = lax.axis_size("tp")
    others = n_tp - 1
    number = len(members)
    every, most = members[0][1].shape[0], max(member[0].across for member in members)
    token_rows = every // n_tp
    head = members[0][3].shape[1]

    def kernel(*refs):
        grad_ref, y_ref, mod_ref = refs[:3]
        operands = [refs[3 + 4 * p : 7 + 4 * p] for p in range(number)]
        at = 3 + 4 * number
        stream_ref, branch_ref, gate_ref = refs[at : at + 3]
        outs = [refs[at + 3 + 2 * p : at + 5 + 2 * p] for p in range(number)]
        at += 3 + 2 * number
        recv, exchange_send, exchange_recv, models, heads, total, sems, send_sem, recv_sem = refs[at:]
        greet(core_places())
        exchange = Swap(grad_ref, recv, exchange_send, exchange_recv)
        exchange.start()
        core = CoreCopies(send_sem, recv_sem)
        moves = Moves(sems)
        flights, loads = [], []
        for p, (model, got, keep, other) in enumerate(operands):
            flights.append(
                [
                    core.start(got, models.at[2 * p + 1, pl.ds((n_tp - 1 - k) * token_rows, token_rows), :], place)
                    for k, place in enumerate(core_places())
                ]
            )
            loads.append(
                [
                    moves.start(model, models.at[2 * p]),
                    moves.start(keep, heads.at[2 * p]),
                    moves.start(got, models.at[2 * p + 1, pl.ds(0, token_rows), :]),
                    moves.start(other, heads.at[2 * p + 1]),
                ]
            )
        for p, member in enumerate(members):
            across = member[0].across
            for copy in loads[p]:
                copy.wait()
            total[:, 0:across] = dot_tn(models[2 * p], heads[2 * p, :, 0:across])
            for copy in flights[p]:
                copy.wait()
            total[:, 0:across] += dot_tn(models[2 * p + 1], heads[2 * p + 1, :, 0:across])
            scatter_rows(total, outs[p][0], outs[p][1], member[0], size)
        exchange.finish()
        for owner in range(size):
            part = recv[owner].astype(F32)
            for frame in range(frames_here):
                at = frame * patch_part + owner * patch_here
                stream_ref[at : at + patch_here, :] = part[
                    frame * patch_here : (frame + 1) * patch_here
                ]
        for frame in range(frames_here):
            at = slice(frame * patch_part, (frame + 1) * patch_part)
            stream = stream_ref[at, :]
            gate_ref[frame : frame + 1, :] = jnp.sum(stream * y_ref[at, :], axis=0, keepdims=True)
            branch_ref[at, :] = (stream * mod_ref[frame : frame + 1, 2 * width : 3 * width]).astype(BF)

    ins = [grad_blocks, y_one, mod_here] + [array for member in members for array in member[1:5]]
    halves = [
        like((size // 2, width // size, member[0].across)) for member in members for unused in range(2)
    ]
    out = call(
        kernel,
        [like((rows, width), F32), like((rows, width)), like((frames_here, width), F32)] + halves,
        ins,
        [False] * 3 + [True] * (4 * number),
        [False] * (3 + 2 * number),
        [VMEM((size, block, width), BF)]
        + swap_sems(size, 1)
        + [
            VMEM((2 * number, every, width), BF),
            VMEM((2 * number, every, head), BF),
            VMEM((width, most), F32),
            pltpu.SemaphoreType.DMA((4 * number,)),
            pltpu.SemaphoreType.DMA((number * others,)),
            pltpu.SemaphoreType.DMA((number * others,)),
        ],
        collective_id=3,
        has_side_effects=True,
    )
    return out[:3], [out[3 + 2 * p : 5 + 2 * p] for p in range(number)]


def fill_rows(moves, sources, target):
    step = sources[0].shape[0]
    return [moves.start(ref, target.at[pl.ds(r * step, step), :]) for r, ref in enumerate(sources)]


def middle_forward(stream, row_codes, key_codes, blocks, keyval_list, tqkv_list, to_list, cq_list, co_list, out_first, given):
    n_tp = len(tqkv_list)
    count, width = stream.shape
    keys = keyval_list[0].shape[0]
    columns = to_list[0].shape[0]
    heads = width // HD
    part = columns // 2
    out_slot = whole_tiles(2 * part)

    def kernel(*refs):
        stream_ref, row_ref, key_ref = refs[:3]
        block_refs = refs[3 : 3 + len(blocks)]
        at = 3 + len(blocks)
        groups = []
        for unused in range(5):
            groups.append(refs[at : at + n_tp])
            at += n_tp
        keyvals, tqkvs, tos, cqs, cos = groups
        given_refs = refs[at : at + len(given)]
        at += len(given)
        h2_out, qkv_out, p2_out, inv2_ref, h3_out, q3_out, p3_out, inv3_ref, x_ref, kv_ref, a_keep, a_give = refs[at : at + 12]
        block_outs = refs[at + 12 : at + 12 + len(blocks)]
        at += 12 + len(blocks)
        given_got = refs[at : at + len(given)]
        w_qkv, w_o, w_q, w_c, h2, qkv, p2, a2, h3, q3, p3, a3, sems, *swap = refs[at + len(given) :]
        greet()
        pairs = PairCopies(*swap[-2:])
        for (unused, first), ref, target in zip(given, given_refs, given_got):
            pairs.start(ref, target, first)
        exchanges = [
            Swap(ref, swap[3 * i], swap[3 * i + 1], swap[3 * i + 2]) for i, ref in enumerate(block_refs)
        ]
        for exchange in exchanges:
            exchange.start()
        moves = Moves(sems)
        qkv_in = [
            [
                moves.start(tqkvs[r].at[i], w_qkv.at[i, pl.ds(r * columns, columns), :])
                for r in range(n_tp)
            ]
            for i in range(3)
        ]
        o_in = fill_rows(moves, tos, w_o)
        q_in = fill_rows(moves, cqs, w_q)
        c_in = fill_rows(moves, cos, w_c)
        outgoing = []
        for i in range(2):
            for r in range(n_tp):
                kv_ref[i, :, r * columns : (r + 1) * columns] = keyvals[r][
                    :, i * columns : (i + 1) * columns
                ]
        stream_one = stream_ref[...].astype(F32)
        normed, inverse = norm_of(stream_one)
        inv2_ref[...] = jnp.broadcast_to(inverse, inv2_ref.shape)
        h2[...] = normed.astype(BF)
        outgoing.append(moves.start(h2, h2_out))
        for i in range(3):
            for copy in qkv_in[i]:
                copy.wait()
            qkv[i] = dot_nt(h2[...], w_qkv[i]).astype(BF)
        outgoing.append(moves.start(qkv, qkv_out))

        def keep_two(head, probs):
            p2[head] = probs

        def write_two(low, high, part):
            a2[:, low:high] = part.astype(BF)

        attend(
            lambda low, high: qkv[0, :, low:high],
            lambda low, high: qkv[1, :, low:high],
            lambda low, high: qkv[2, :, low:high],
            jnp.where(row_ref[:, 0:1] == key_ref[0:1, 0:count], 0.0, NEGATIVE),
            heads,
            width,
            keep_two,
            write_two,
        )
        outgoing.append(moves.start(p2, p2_out))
        for copy in o_in:
            copy.wait()
        x_ref[...] = stream_one + dot_nn(a2[...], w_o[...])
        normed, inverse = norm_of(x_ref[...])
        inv3_ref[...] = jnp.broadcast_to(inverse, inv3_ref.shape)
        h3[...] = normed.astype(BF)
        outgoing.append(moves.start(h3, h3_out))
        for copy in q_in:
            copy.wait()
        q3[...] = dot_nt(h3[...], w_q[...]).astype(BF)
        outgoing.append(moves.start(q3, q3_out))

        def keep_three(head, probs):
            p3[head] = probs

        def write_three(low, high, part):
            a3[:, low:high] = part.astype(BF)

        attend(
            lambda low, high: q3[:, low:high],
            lambda low, high: kv_ref[0, :, low:high],
            lambda low, high: kv_ref[1, :, low:high],
            jnp.where(row_ref[:, 1:2] == key_ref[1:2, 0:keys], 0.0, NEGATIVE),
            heads,
            width,
            keep_three,
            write_three,
        )
        outgoing.append(moves.start(p3, p3_out))
        mine = bit_of(out_first)
        for r in range(n_tp):
            for i, ref in enumerate((a2, a3)):
                low = r * out_slot + i * part
                first = ref[:, r * columns : r * columns + part]
                second = ref[:, r * columns + part : (r + 1) * columns]
                a_keep[:, low : low + part] = jnp.where(mine == 0, first, second)
                a_give[:, low : low + part] = jnp.where(mine == 0, second, first)
            for ref in (a_keep, a_give):
                if out_slot > 2 * part:
                    spare = jnp.zeros((count, out_slot - 2 * part), BF)
                    ref[:, r * out_slot + 2 * part : (r + 1) * out_slot] = spare
        for copy in c_in:
            copy.wait()
        x_ref[...] = x_ref[...] + dot_nn(a3[...], w_c[...])
        for copy in outgoing:
            copy.wait()
        for exchange, out in zip(exchanges, block_outs):
            exchange.finish()
            out[...] = exchange.recv[...]
        pairs.finish()

    square = (count, width)
    outs = [
        like(square),
        like((3,) + square),
        like((heads, count, count)),
        like((count, LANES), F32),
        like(square),
        like(square),
        like((heads, count, keys)),
        like((count, LANES), F32),
        like(square, F32),
        like((2, keys, width)),
        like((count, n_tp * out_slot)),
        like((count, n_tp * out_slot)),
    ] + [like(array.shape) for array in blocks]
    outs += [like(array.shape) for array, unused in given]
    kept = [square, (3,) + square, (heads, count, count), square, square, square, (heads, count, keys), square]
    ins = [stream, row_codes, key_codes, *blocks, *keyval_list, *tqkv_list, *to_list, *cq_list, *co_list]
    ins += [array for array, unused in given]
    full = n_tp * columns
    return call(
        kernel,
        outs,
        ins,
        [False] * (3 + len(blocks) + n_tp) + [True] * (4 * n_tp + len(given)),
        [True, True, True, False, True, True, True, False, False, False, False, False] + [False] * len(blocks) + [True] * len(given),
        [VMEM((3, full, width), BF)]
        + [VMEM((full, width), BF)] * 3
        + [VMEM(shape, BF) for shape in kept]
        + [pltpu.SemaphoreType.DMA((6 * n_tp + 8,))]
        + [
            kind
            for array in blocks
            for kind in (VMEM(array.shape, BF), *swap_sems(array.shape[0], 1))
        ]
        + swap_sems(len(given), 1),
        collective_id=6,
        has_side_effects=True,
    )


def feed_forward(stream, grad_out, mod_rows, hot_rows, w_fc1, w_fc2, firsts, given):
    n_tp = lax.axis_size("tp")
    others = n_tp - 1
    count, width = stream.shape
    every = n_tp * count
    hidden = w_fc1.shape[1]
    half = hidden // 2
    padded = whole_tiles(half)
    clips = hot_rows.shape[1]
    pieces = 2 if half % LANES == 0 else 1

    def kernel(*refs):
        stream_ref, grad_ref, mod_ref, hot_ref, fc1_hbm, fc2_hbm = refs[:6]
        given_refs, refs = refs[6 : 6 + len(given)], refs[:6] + refs[6 + len(given) :]
        out_ref, h_all, up_keep, up_give, dy_all, down_keep, down_give, g_ref, mod_sum = refs[6:15]
        h_own, dy_own, h_got, dy_got = refs[15:19]
        given_got, refs = refs[19 : 19 + len(given)], refs[19 + len(given) :]
        w1, w2, h_land, total_y, total_h, send_y, send_h, land_y, land_h, sems, send_sem, recv_sem = refs[:12]
        moves = Moves(sems)
        loads = []
        for piece in range(pieces):
            cols = pl.ds(piece * (hidden // pieces), hidden // pieces)
            loads.append(
                (
                    moves.start(fc1_hbm.at[:, cols], w1.at[:, cols]),
                    moves.start(fc2_hbm.at[cols, :], w2.at[cols, :]),
                )
            )
        greet_devices(core_places() + pair_places())
        core = CoreCopies(send_sem, recv_sem)
        pairs = PairCopies(*refs[12:])
        for (unused, first), ref, target in zip(given, given_refs, given_got):
            pairs.start(ref, target, first)
        bit = [bit_of(first) for first in firsts]
        own = slice(0, count)
        gate = mod_ref[:, 2 * width :].astype(F32)
        dy_own[...] = (gate * grad_ref[...].astype(F32)).astype(BF)
        flights = [core.start(dy_own, h_land.at[n_tp - 2 - k], place) for k, place in enumerate(core_places())]
        pairs.start(dy_own, dy_got, firsts[1])
        shift = mod_ref[:, 0:width].astype(F32)
        scale = 1.0 + mod_ref[:, width : 2 * width].astype(F32)
        normed, inverse = norm_of(stream_ref[...])
        h_own[...] = (normed * scale + shift).astype(BF)
        flights += [
            core.start(h_own, h_land.at[others + n_tp - 2 - k], place) for k, place in enumerate(core_places())
        ]
        pairs.start(h_own, h_got, firsts[0])
        h_all[own, :] = h_own[...]
        dy_all[own, :] = dy_own[...]
        for pack in (up_keep, up_give, down_keep, down_give):
            if padded > half:
                pack[:, half:] = jnp.zeros((every, padded - half), BF)
        back = []
        for part in range(2):
            if part < pieces:
                for copy in loads[part]:
                    copy.wait()
            hid = slice(part * half, (part + 1) * half)
            for r in range(n_tp) if part == 0 else [*range(1, n_tp), 0]:
                at = slice(r * count, (r + 1) * count)
                if part == 0 and r == 1:
                    for copy in flights:
                        copy.wait()
                    for k in range(others):
                        there = slice((k + 1) * count, (k + 2) * count)
                        dy_all[there, :] = h_land[k]
                        h_all[there, :] = h_land[others + k]
                upper = dot_nn(h_all[at, :], w1[:, hid])
                square = upper * upper
                tanh = jnp.tanh(upper * (0.7978845608028654 + 0.035677408136300125 * square))
                rise = 0.5 + 0.5 * tanh
                active = (upper * rise).astype(BF)
                slope = rise + (0.5 * upper) * (1.0 - tanh * tanh) * (
                    0.7978845608028654 + 0.10703222440890037 * square
                )
                grad_upper = (dot_nt(dy_all[at, :], w2[hid, :]) * slope).astype(BF)
                for keep, give, mine, value in (
                    (up_keep, up_give, bit[0], grad_upper),
                    (down_keep, down_give, bit[1], active),
                ):

                    @pl.when(mine == part)
                    def _():
                        keep[at, 0:half] = value

                    @pl.when(mine != part)
                    def _():
                        give[at, 0:half] = value

                y_term = dot_nn(active, w2[hid, :])
                h_term = dot_nt(grad_upper, w1[:, hid])
                if part == 0:
                    total_y[at, :] = y_term
                    total_h[at, :] = h_term
                elif r == 0:
                    total_y[at, :] += y_term
                    total_h[at, :] += h_term
                else:
                    send_y[r - 1] = (total_y[at, :] + y_term).astype(BF)
                    send_h[r - 1] = (total_h[at, :] + h_term).astype(BF)
                    place = core_places()[r - 1]
                    back.append(core.start(send_y.at[r - 1], land_y.at[r - 1], place))
                    back.append(core.start(send_h.at[r - 1], land_h.at[r - 1], place))
        for copy in back:
            copy.wait()
        branch, grad_h = total_y[own, :], total_h[own, :]
        for k in range(others):
            branch = branch + land_y[k].astype(F32)
            grad_h = grad_h + land_h[k].astype(F32)
        gate = mod_ref[:, 2 * width :].astype(F32)
        out_ref[...] = (stream_ref[...] + gate * branch).astype(BF)
        grad = grad_ref[...].astype(F32)
        hot = hot_ref[...]
        mod_sum[:, 2 * width :] = dot_tn(hot, (grad * branch).astype(BF))
        mod_sum[:, 0:width] = dot_tn(hot, grad_h.astype(BF))
        normed, inverse = norm_of(stream_ref[...])
        mod_sum[:, width : 2 * width] = dot_tn(hot, (grad_h * normed).astype(BF))
        scale = 1.0 + mod_ref[:, width : 2 * width].astype(F32)
        g_ref[...] = grad + norm_back(grad_h * scale, normed, inverse)
        pairs.finish()

    side = like((every, padded))
    ins = [stream, grad_out, mod_rows, hot_rows, w_fc1, w_fc2] + [array for array, unused in given]
    n_pairs = 2 + len(given)
    square = (count, width)
    return call(
        kernel,
        [
            like(square),
            like((every, width)),
            side,
            side,
            like((every, width)),
            side,
            side,
            like(square, F32),
            like((clips, 3 * width), F32),
            like(square),
            like(square),
            like(square),
            like(square),
        ]
        + [like(array.shape) for array, unused in given],
        ins,
        [False] * 4 + [True] * (2 + len(given)),
        [False] * 11 + [True] * n_pairs,
        [
            VMEM((width, hidden), BF),
            VMEM((hidden, width), BF),
            VMEM((2 * others,) + square, BF),
            VMEM((every, width), F32),
            VMEM((every, width), F32),
            VMEM((others,) + square, BF),
            VMEM((others,) + square, BF),
            VMEM((others,) + square, BF),
            VMEM((others,) + square, BF),
            pltpu.SemaphoreType.DMA((4,)),
            pltpu.SemaphoreType.DMA((4 * others,)),
            pltpu.SemaphoreType.DMA((4 * others,)),
            pltpu.SemaphoreType.DMA((n_pairs,)),
            pltpu.SemaphoreType.DMA((n_pairs,)),
        ],
        collective_id=5,
        has_side_effects=True,
    )


def middle_backward(grad, kept, keyval, out_blocks, texts, tqkv_list, to_list, cq_list, co_list, in_first, given):
    n_tp = len(tqkv_list)
    h2, qkv, p2, inv2, h3, q3, p3, inv3 = kept
    count, width = grad.shape
    keys = keyval.shape[1]
    columns = to_list[0].shape[0]
    part = columns // 2
    heads = width // HD
    full = n_tp * columns
    in_slot = whole_tiles(4 * part)

    def kernel(*refs):
        grad_ref, inv2_ref, inv3_ref, h2_ref, h3_ref, block_ref, text_ref = refs[:7]
        qkv_hbm, p2_hbm, q3_hbm, p3_hbm, kv_hbm = refs[7:12]
        given_refs = refs[12 : 12 + len(given)]
        at = 12 + len(given)
        groups = []
        for unused in range(4):
            groups.append(refs[at : at + n_tp])
            at += n_tp
        tqkvs, tos, cqs, cos = groups
        in_keep, in_give, dy2_ref, dy3_ref, stream_ref, block_out, text_out = refs[at : at + 7]
        given_got = refs[at + 7 : at + 7 + len(given)]
        at += 2 + len(given)
        kv_outs = refs[at + 5 : at + 5 + n_tp]
        (
            w_qkv, w_o, w_q, w_c, qkv_ref, p2_ref, q3_ref, p3_ref, kv_ref,
            grad_attn, d_q, d_k, d_v, total, sems, recv, send_sem, recv_sem, text_recv, text_sem, text_recv_sem, pair_send, pair_recv,
        ) = refs[at + 5 + n_tp :]
        greet()
        exchange = Swap(block_ref, recv, send_sem, recv_sem)
        pairs = PairCopies(pair_send, pair_recv)
        for (unused, first), ref, target in zip(given, given_refs, given_got):
            pairs.start(ref, target, first)
        exchange.start()
        text_exchange = Swap(text_ref, text_recv, text_sem, text_recv_sem)
        text_exchange.start()
        moves = Moves(sems)
        c_in = fill_rows(moves, cos, w_c)
        kv_in = moves.start(kv_hbm, kv_ref)
        p3_in = moves.start(p3_hbm, p3_ref)
        q3_in = moves.start(q3_hbm, q3_ref)
        q_in = fill_rows(moves, cqs, w_q)
        o_in = fill_rows(moves, tos, w_o)
        qkv_load = moves.start(qkv_hbm, qkv_ref)
        p2_in = moves.start(p2_hbm, p2_ref)
        qkv_in = [
            [
                moves.start(tqkvs[r].at[i], w_qkv.at[i, pl.ds(r * columns, columns), :])
                for r in range(n_tp)
            ]
            for i in range(3)
        ]
        bit = bit_of(in_first)

        def split(value, r, mine, keep, give, low):
            first = value[:, r * columns : r * columns + part]
            second = value[:, r * columns + part : (r + 1) * columns]
            keep[:, low : low + part] = jnp.where(mine == 0, first, second)
            give[:, low : low + part] = jnp.where(mine == 0, second, first)

        def into(ref, upto):
            def write(low, high, value):
                ref[0:upto, low:high] = value.astype(BF)

            return write

        if in_slot > 4 * part:
            for pack in (in_keep, in_give):
                for r in range(n_tp):
                    spare = jnp.zeros((count, in_slot - 4 * part), BF)
                    pack[:, r * in_slot + 4 * part : (r + 1) * in_slot] = spare
        grad_y = grad_ref[...].astype(BF)
        dy3_ref[...] = grad_y
        for copy in c_in:
            copy.wait()
        grad_attn[...] = dot_nt(grad_y, w_c[...]).astype(BF)
        for copy in (kv_in, p3_in, q3_in):
            copy.wait()
        attend_back(
            lambda low, high: q3_ref[:, low:high],
            lambda low, high: kv_ref[0, :, low:high],
            lambda low, high: kv_ref[1, :, low:high],
            lambda low, high: grad_attn[:, low:high],
            lambda head: p3_ref[head],
            heads,
            width,
            into(d_q, count),
            into(d_k, keys),
            into(d_v, keys),
        )
        for r in range(n_tp):
            kv_outs[r][:, 0:columns] = d_k[0:keys, r * columns : (r + 1) * columns]
            kv_outs[r][:, columns:] = d_v[0:keys, r * columns : (r + 1) * columns]
            split(d_q[...], r, bit, in_keep, in_give, r * in_slot + 3 * part)
        for copy in q_in:
            copy.wait()
        grad_h = dot_nn(d_q[...], w_q[...])
        total[...] = grad_ref[...] + norm_back(grad_h, h3_ref[...].astype(F32), inv3_ref[:, 0:1])

        grad_y = total[...].astype(BF)
        dy2_ref[...] = grad_y
        for copy in o_in:
            copy.wait()
        grad_attn[...] = dot_nt(grad_y, w_o[...]).astype(BF)
        for copy in (qkv_load, p2_in):
            copy.wait()
        attend_back(
            lambda low, high: qkv_ref[0, :, low:high],
            lambda low, high: qkv_ref[1, :, low:high],
            lambda low, high: qkv_ref[2, :, low:high],
            lambda low, high: grad_attn[:, low:high],
            lambda head: p2_ref[head],
            heads,
            width,
            into(d_q, count),
            into(d_k, count),
            into(d_v, count),
        )
        for i, ref in enumerate((d_q, d_k, d_v)):
            for r in range(n_tp):
                split(ref[0:count, :], r, bit, in_keep, in_give, r * in_slot + i * part)
            for copy in qkv_in[i]:
                copy.wait()
            term = dot_nn(ref[0:count, :], w_qkv[i])
            grad_h = term if i == 0 else grad_h + term
        stream_ref[...] = (
            total[...] + norm_back(grad_h, h2_ref[...].astype(F32), inv2_ref[:, 0:1])
        ).astype(BF)
        pairs.finish()
        exchange.finish()
        block_out[...] = recv[...]
        text_exchange.finish()
        text_out[...] = text_recv[...]

    square = (count, width)
    in_pack = like((count, n_tp * in_slot))
    ins = [grad, inv2, inv3, h2, h3, out_blocks, texts, qkv, p2, q3, p3, keyval]
    ins = ins + [array for array, unused in given]
    ins = ins + [*tqkv_list, *to_list, *cq_list, *co_list]
    square_keys = (keys, width)
    return call(
        kernel,
        [in_pack, in_pack, like(square), like(square), like(square), like(out_blocks.shape), like(texts.shape)]
        + [like(array.shape) for array, unused in given]
        + [like((keys, 2 * columns))] * n_tp,
        ins,
        [False] * 7 + [True] * (5 + len(given) + 4 * n_tp),
        [False] * 7 + [True] * len(given) + [False] * n_tp,
        [VMEM((3, full, width), BF)]
        + [VMEM((full, width), BF)] * 3
        + [
            VMEM((3,) + square, BF),
            VMEM((heads, count, count), BF),
            VMEM(square, BF),
            VMEM((heads, count, keys), BF),
            VMEM((2,) + square_keys, BF),
            VMEM(square, BF),
            VMEM(square, BF),
            VMEM((max(count, keys), width), BF),
            VMEM((max(count, keys), width), BF),
            VMEM(square, F32),
            pltpu.SemaphoreType.DMA((6 * n_tp + 7,)),
            VMEM(out_blocks.shape, BF),
        ]
        + swap_sems(out_blocks.shape[0], 1)
        + [VMEM(texts.shape, BF)]
        + swap_sems(out_blocks.shape[0], 1)
        + swap_sems(len(given), 1),
        collective_id=7,
        has_side_effects=True,
    )


def spatial_backward(grad_y_list, probs, qkv, sqkv_rows, w_so, frames_here, given, q_first):
    n_tp = len(grad_y_list)
    rows, width = grad_y_list[0].shape
    columns = w_so.shape[0]
    part = columns // 2
    patch_part = rows // frames_here
    per_frame = n_tp * patch_part
    count = n_tp * rows
    heads = columns // HD
    side = whole_tiles(3 * part)

    def kernel(*refs):
        grads = refs[:n_tp]
        probs_hbm, qkv_hbm, wqkv_hbm, so_hbm = refs[n_tp : n_tp + 4]
        given_refs, refs = refs[n_tp + 4 : n_tp + 4 + len(given)], refs[: n_tp + 4] + refs[n_tp + 4 + len(given) :]
        keep, give, own_ref = refs[n_tp + 4 : n_tp + 7]
        others = refs[n_tp + 7 : 2 * n_tp + 6]
        grad_y = refs[2 * n_tp + 6]
        given_got, refs = refs[2 * n_tp + 7 : 2 * n_tp + 8 + len(given)], refs[2 * n_tp + 8 + len(given) :]
        w_qkv, w_o, qkv_ref, probs_ref, grad_attn, d_all, sems, pair_send, pair_recv = refs
        greet_devices(pair_places())
        pairs = PairCopies(pair_send, pair_recv)
        for (unused, first), ref, target in zip(given, given_refs, given_got):
            pairs.start(ref, target, first)
        if side > 3 * part:
            for ref in (keep, give):
                ref[:, 3 * part :] = jnp.zeros((count, side - 3 * part), BF)
        moves = Moves(sems)
        o_in = moves.start(so_hbm, w_o)
        qkv_in = moves.start(qkv_hbm, qkv_ref)
        probs_in = moves.start(probs_hbm, probs_ref)
        weight_in = moves.start(wqkv_hbm, w_qkv)
        for frame in range(frames_here):
            for r in range(n_tp):
                at = frame * per_frame + r * patch_part
                grad_y[at : at + patch_part, :] = grads[r][
                    frame * patch_part : (frame + 1) * patch_part, :
                ]
        o_in.wait()
        grad_attn[...] = dot_nt(grad_y[...], w_o[...]).astype(BF)
        qkv_in.wait()
        probs_in.wait()
        for frame in range(frames_here):
            at = slice(frame * per_frame, (frame + 1) * per_frame)

            def into(i, at=at):
                def write(low, high, value):
                    d_all[i, at, low:high] = value.astype(BF)

                return write

            attend_back(
                lambda low, high, at=at: qkv_ref[0, at, low:high],
                lambda low, high, at=at: qkv_ref[1, at, low:high],
                lambda low, high, at=at: qkv_ref[2, at, low:high],
                lambda low, high, at=at: grad_attn[at, low:high],
                lambda head, frame=frame: probs_ref[frame * heads + head],
                heads,
                columns,
                into(0),
                into(1),
                into(2),
            )
        mine = bit_of(q_first)
        for i in range(3):
            value = d_all[i]
            first, second = value[:, :part], value[:, part:]
            keep[:, i * part : (i + 1) * part] = jnp.where(mine == 0, first, second)
            give[:, i * part : (i + 1) * part] = jnp.where(mine == 0, second, first)
        pairs.start(give, given_got[-1], q_first)
        weight_in.wait()
        for frame in range(frames_here):
            at = slice(frame * per_frame, (frame + 1) * per_frame)
            grad_h = dot_nn(d_all[0, at, :], w_qkv[0])
            for i in (1, 2):
                grad_h = grad_h + dot_nn(d_all[i, at, :], w_qkv[i])
            here = slice(frame * patch_part, (frame + 1) * patch_part)
            own_ref[here, :] = grad_h[:patch_part]
            for r in range(1, n_tp):
                others[r - 1][here, :] = grad_h[r * patch_part : (r + 1) * patch_part].astype(BF)
        pairs.finish()

    ins = [*grad_y_list, probs, qkv, sqkv_rows, w_so] + [array for array, unused in given]
    return call(
        kernel,
        [like((count, side))] * 2
        + [like((rows, width), F32)]
        + [like((rows, width))] * (n_tp - 1)
        + [like((count, width))]
        + [like(array.shape) for array, unused in given]
        + [like((count, side))],
        ins,
        [False] * n_tp + [True] * (4 + len(given)),
        [False] * (n_tp + 3) + [True] * (len(given) + 1),
        [
            VMEM((3, columns, width), BF),
            VMEM((columns, width), BF),
            VMEM((3, count, columns), BF),
            VMEM(probs.shape, BF),
            VMEM((count, columns), BF),
            VMEM((3, count, columns), BF),
            pltpu.SemaphoreType.DMA((4,)),
        ]
        + swap_sems(len(given) + 1, 1),
        collective_id=8,
        has_side_effects=True,
    )


def tokens_gradient(tokens_rows, grad, grad_h_own, grad_h_others, mod_here, frames_here, after):
    rows, width = tokens_rows.shape
    patch_part = rows // frames_here
    others = len(grad_h_others)

    def kernel(*refs):
        token_ref, grad_ref, own_ref = refs[:3]
        mod_ref, out_ref, sum_ref = refs[3 + others :]
        for frame in range(frames_here):
            at = slice(frame * patch_part, (frame + 1) * patch_part)
            grad_h = own_ref[at, :]
            for other in refs[3 : 3 + others]:
                grad_h = grad_h + other[at, :].astype(F32)
            normed, inverse = norm_of(token_ref[at, :].astype(F32))
            sum_ref[frame : frame + 1, 0:width] = jnp.sum(grad_h, axis=0, keepdims=True)
            sum_ref[frame : frame + 1, width:] = jnp.sum(grad_h * normed, axis=0, keepdims=True)
            scale = 1.0 + mod_ref[frame : frame + 1, width : 2 * width]
            out_ref[at, :] = (grad_ref[at, :] + norm_back(grad_h * scale, normed, inverse)).astype(BF)

    ins = [tokens_rows, grad, grad_h_own, *grad_h_others, mod_here]
    return call(
        kernel,
        [like((rows, width)), like((frames_here, 2 * width), F32)],
        ins,
        [False] * len(ins),
        [False] * 2,
        [],
        after,
    )


def flip(operand, mask):
    size = lax.axis_size("wide")
    return lax.ppermute(operand, "wide", [(s, s ^ mask) for s in range(size)])


def tp_from(operand, shift):
    size = lax.axis_size("tp")
    return lax.ppermute(operand, "tp", [(s, (s - shift) % size) for s in range(size)])


def tp_to(operand, shift):
    size = lax.axis_size("tp")
    return lax.ppermute(operand, "tp", [(s, (s + shift) % size) for s in range(size)])


def tp_gather(operand):
    return [operand] + [tp_from(operand, k) for k in range(1, lax.axis_size("tp"))]


class Pack:
    def __init__(self, first, order, layout):
        self.first, self.layout = first, layout
        self.order = order + [bit for bit in range(wide_bits()) if bit != first and bit not in order]
        self.across = sum(groups * cols for groups, cols in layout)


def scatter_rows(total, keep, give, pack, size):
    block = keep.shape[1]
    across = pack.across
    mine = bit_of(pack.order[0])
    inner = pack.order[1:] + [pack.first]
    for at in range(size // 2):
        parts = []
        for value in range(2):
            place = value << pack.order[0]
            for depth, bit in enumerate(inner):
                place |= ((at >> (len(inner) - 1 - depth)) & 1) << bit
            parts.append(total[place * block : (place + 1) * block, 0:across].astype(BF))
        keep[at] = jnp.where(mine == 0, parts[0], parts[1])
        give[at] = jnp.where(mine == 0, parts[1], parts[0])


class Flow:
    def __init__(self, pack, keep, give, lands, send_sem, recv_sem, outs):
        self.pack, self.keep, self.give, self.lands = pack, keep, give, lands
        self.send_sem, self.recv_sem, self.outs = send_sem, recv_sem, outs
        self.bits = pack.order + [pack.first]
        self.level, self.behind, self.base = 0, 0, 0
        self.first, self.second, self.placed = None, None, False

    def region(self, level, part):
        number = self.lands[level].shape[0]
        if number == 1:
            return 0, 1
        half = number // 2
        mine = bit_of(self.bits[level + 1])
        return (mine if part else 1 - mine) * half, half

    def start(self, part):
        level = self.level
        low, number = self.region(level, part)
        if level == 0:
            source = self.give.at[pl.ds(low, number)]
        else:
            shift = self.region(level - 1, 0)[0]
            source = self.lands[level - 1].at[pl.ds(shift + low, number)]
        copy = pltpu.make_async_remote_copy(
            src_ref=source,
            dst_ref=self.lands[level].at[pl.ds(low, number)],
            send_sem=self.send_sem.at[2 * level + part],
            recv_sem=self.recv_sem.at[2 * level + part],
            device_id={"wide": partner(self.bits[level])},
            device_id_type=pl.DeviceIdType.MESH,
        )
        copy.start()
        return copy

    def send(self):
        if self.first is None and not self.placed:
            self.first = self.start(0)

    def wait(self):
        if self.placed:
            return
        self.part()
        self.send()
        self.first.wait()
        level = self.level
        land = self.lands[level]
        if land.shape[0] == 1:
            self.place(land)
            return
        self.second = self.start(1)
        low, number = self.region(level, 0)
        for i in range(number):
            own = self.keep[self.base + low + i].astype(F32)
            land[low + i] = (own + land[low + i].astype(F32)).astype(BF)
        self.level, self.first = level + 1, None

    def part(self):
        if self.second is None:
            return
        self.second.wait()
        self.second = None
        low, number = self.region(self.behind, 1)
        land = self.lands[self.behind]
        for i in range(number):
            own = self.keep[self.base + low + i].astype(F32)
            self.keep[self.base + low + i] = (own + land[low + i].astype(F32)).astype(BF)
        self.base = self.base + low
        self.behind += 1

    def go(self):
        self.wait()
        self.send()

    def place(self, land):
        self.placed = True
        mine = bit_of(self.pack.first)
        own, other = self.keep[self.base].astype(F32), land[0].astype(F32)
        sides = [jnp.where(mine == 0, own, other), jnp.where(mine == 0, other, own)]
        low = 0
        for out, (groups, cols) in zip(self.outs, self.pack.layout):
            for g in range(groups):
                for side in range(2):
                    value = sides[side][:, low + g * cols : low + (g + 1) * cols]
                    if groups == 1:
                        out[:, side * cols : (side + 1) * cols] = value
                    else:
                        out[g, :, side * cols : (side + 1) * cols] = value
            low += groups * cols


def reduce_all(ready_packs, rows_packs, slot_packs, kv_parts, mod_blocks, embed, texts, text_cols, ckv_rows, schedule, after, extra_rows=0):
    n_tp, size = lax.axis_size("tp"), lax.axis_size("wide")
    bits = wide_bits()
    packs = [member[0] for member in (*ready_packs, *rows_packs, *slot_packs)]
    n_ready, n_rows, n_slots = len(ready_packs), len(rows_packs), len(slot_packs)
    rows, width = rows_packs[0][2].shape
    count = n_tp * rows
    block = width // size
    others = n_tp - 1
    most = max(whole_tiles(member[0].across) for member in rows_packs)
    token_rows = slot_packs[0][3].shape[0]
    models = len(slot_packs[0][1])
    slot_width = max(member[3].shape[1] for member in slot_packs)
    keys, columns = kv_parts[0].shape[0] * kv_parts[0].shape[1], kv_parts[0].shape[2]
    context_cols = width // size
    owned = width // n_tp

    row_ins = [array for member in rows_packs for array in member[1:5]]
    slot_ins = [array for member in slot_packs for array in (*member[1], *member[2], *member[3:5])]
    ready_ins = [array for member in ready_packs for array in member[1:]]
    ins = ready_ins + row_ins + slot_ins + [ckv_rows, texts, mod_blocks, embed] + list(kv_parts)
    in_any = [True] * (len(ready_ins) + len(row_ins) + len(slot_ins) + 1) + [False] * 3 + [True] * len(kv_parts)
    result = []
    for pack in packs:
        for groups, cols in pack.layout:
            result.append(like((block, 2 * cols) if groups == 1 else (groups, block, 2 * cols), F32))
    landing = [like((rows, width))] * (n_rows * others)
    for member in slot_packs:
        landing += [like((token_rows, width))] * (2 * models * others)
        landing += [like(member[3].shape)] * (2 * others)
    pairs = [p for p, member in enumerate(rows_packs) if member[6]]
    landing += [like(rows_packs[p][4].shape) for p in pairs]
    spare = mod_blocks.shape[1]
    kv_block_rows = kv_parts[0].shape[1]
    clips = embed.shape[0]
    mod_row = kv_block_rows if extra_rows else kv_block_rows - spare
    mod_cols = 6 * width // (n_tp * size)
    outs = result + [like((context_cols, columns), F32), like((owned, text_cols), F32)]
    outs += [like((mod_cols, width), F32), like((1, mod_cols), F32)] + landing
    out_any = [False] * (len(result) + 4) + [True] * len(landing)
    scratch = [VMEM((count, width), BF)] * 2 + [VMEM((count, most), BF)] * 2
    scratch += [VMEM((token_rows, width), BF)] * (2 * n_tp * models)
    scratch += [VMEM((token_rows, slot_width), BF)] * (2 * n_tp)
    scratch += [VMEM((width, max(pack.across for pack in packs)), F32)]
    for pack in packs:
        shape = (block, pack.across)
        scratch += [VMEM((size // 2,) + shape, BF)] * 2
        scratch += [VMEM((size >> (s + 1),) + shape, BF) for s in range(bits)]
        scratch += [pltpu.SemaphoreType.DMA((2 * bits,))] * 2
    n_core = others * (n_rows + 2 * (models + 1) * n_slots + 2)
    n_moves = n_rows * 3 + sum(member[5] * n_tp for member in rows_packs) + 2 * n_tp * n_slots * (models + 1) + 1 + 2 * n_ready + n_tp
    kv_block = kv_parts[0].shape[1:]
    sum_block = (kv_block[0] + extra_rows, kv_block[1])
    kv_scratch = level_scratch(size, sum_block) + level_scratch(size, sum_block)[1:] + level_scratch(size, kv_block)
    scratch += [pltpu.SemaphoreType.DMA((n_core,))] * 2 + [pltpu.SemaphoreType.DMA((n_moves,))]
    scratch += [VMEM(kv_parts[0].shape, BF)] + kv_scratch + [pltpu.SemaphoreType.DMA((bits,))] * 4
    scratch += [VMEM((keys, columns), BF), VMEM((columns, width), BF), VMEM((2 * others, keys, owned), BF)]
    scratch += [VMEM((keys, owned), F32), VMEM((2 * others, 8, whole_tiles(clips * mod_cols)), F32)]
    scratch += [pltpu.SemaphoreType.DMA((max(len(pairs), 1),))] * 2

    def kernel(*refs):
        refs = list(refs)

        def take(number):
            taken = refs[:number]
            del refs[:number]
            return taken

        ready_refs = [take(2) for unused in range(n_ready)]
        row_refs = [take(4) for unused in range(n_rows)]
        slot_refs = [[take(models), take(models), take(2)] for unused in range(n_slots)]
        ckv_ref, text_ref, mod_ref, embed_ref = take(4)
        kv_refs = take(len(kv_parts))
        results = [take(len(pack.layout)) for pack in packs]
        grad_ckv, grad_text, grad_mod, grad_bias = take(4)
        row_land = [take(others) for unused in range(n_rows)]
        slot_land = [
            [[take(models) for unused in range(2)] for unused2 in range(others)]
            + [[take(others) for unused in range(2)]]
            for unused3 in range(n_slots)
        ]
        pair_land = dict(zip(pairs, take(len(pairs))))
        own_model, got_model, own_head, got_head = take(4)
        model_stages = [take(models) for unused in range(2 * n_tp)]
        stages = take(2 * n_tp)
        (total,) = take(1)
        flows = []
        for pack, result_refs in zip(packs, results):
            keep, give = take(2)
            lands = take(bits)
            flows.append(Flow(pack, keep, give, lands, *take(2), result_refs))
        send_sem, recv_sem, move_sem, kv_stage = take(4)
        halving_levels, halving_lands, doubling_levels = take(bits + 1), take(bits), take(bits + 1)
        kv_sems = take(4)
        kv_all, ckv, exchange, text_own, mod_exchange, pair_send, pair_recv = take(7)

        greet_devices(core_places() + pair_places())
        moves = Moves(move_sem)
        core = CoreCopies(send_sem, recv_sem)
        for i, ref in enumerate(kv_refs):
            moves.start(ref, kv_stage).wait()
            for at in range(size):
                value = kv_stage[at].astype(F32)
                level = halving_levels[0].at[mirrored(at)]
                if i == 0:
                    if extra_rows:
                        value = jnp.concatenate([value, jnp.zeros((extra_rows, kv_block[1]), F32)], axis=0)
                    row = lax.broadcasted_iota(jnp.int32, sum_block, 0)
                    for j in range(spare):
                        value = jnp.where(row == mod_row + j, mod_ref[at, j : j + 1, :], value)
                    level[...] = value.astype(BF)
                else:
                    own = level[0 : kv_block[0], :].astype(F32)
                    level[0 : kv_block[0], :] = (own + value).astype(BF)
        ready_loads = [
            (moves.start(give, flows[p].give), moves.start(keep, flows[p].keep))
            for p, (keep, give) in enumerate(ready_refs)
        ]
        halving = Halving(halving_levels, halving_lands, *kv_sems[:2])
        halving.start()
        doubling = Doubling(doubling_levels, *kv_sems[2:])

        pair_flights = {}
        for i, p in enumerate(pairs):
            copy = pltpu.make_async_remote_copy(
                src_ref=row_refs[p][3],
                dst_ref=pair_land[p],
                send_sem=pair_send.at[i],
                recv_sem=pair_recv.at[i],
                device_id={"wide": partner(rows_packs[p][0].first)},
                device_id_type=pl.DeviceIdType.MESH,
            )
            copy.start()
            pair_flights[p] = copy
        row_flights, slot_flights = {}, {}

        def core_rows(p):
            row_flights[p] = [
                core.start(row_refs[p][1], row_land[p][n_tp - 2 - k], place)
                for k, place in enumerate(core_places())
            ]

        def core_slots(p):
            slot = slot_packs[p][5]
            flights = []
            for k, place in enumerate(core_places()):
                for side in range(2):
                    for ref, to in zip(slot_refs[p][side], slot_land[p][k][side]):
                        flights.append(core.start(ref, to, place))
                    ref, to = slot_refs[p][2][side], slot_land[p][others][side][k]
                    cols = pl.ds((k + 1) * slot, slot)
                    flights.append(core.start(ref.at[:, cols], to.at[:, cols], place))
            slot_flights[p] = flights

        ckv_in = moves.start(ckv_ref, ckv)
        loads = {}

        def load_rows(p):
            model, got, keep, other = row_refs[p]
            frames = rows_packs[p][5]
            step = rows // frames
            cols = pl.ds(0, keep.shape[1])
            loads[p] = [moves.start(model, own_model), moves.start(keep, own_head.at[:, cols])]
            if p in pair_flights:
                pair_flights[p].wait()
                other = pair_land[p]
            loads[p].append(moves.start(other, got_head.at[:, cols]))
            for frame in range(frames):
                target = got_model.at[pl.ds(frame * n_tp * step, step), :]
                loads[p].append(moves.start(got.at[pl.ds(frame * step, step), :], target))

        def rows_product(p):
            frames = rows_packs[p][5]
            step = rows // frames
            across = rows_packs[p][0].across
            for copy in loads[p][:2]:
                copy.wait()
            total[:, 0:across] = dot_tn(own_model[...], own_head[:, 0:across])
            for copy in row_flights[p]:
                copy.wait()
            rest = loads[p][2:]
            for frame in range(frames):
                for k in range(others):
                    target = got_model.at[pl.ds((frame * n_tp + k + 1) * step, step), :]
                    rest.append(moves.start(row_land[p][k].at[pl.ds(frame * step, step), :], target))
            for copy in rest:
                copy.wait()
            total[:, 0:across] += dot_tn(got_model[...], got_head[:, 0:across])
            flow = flows[n_ready + p]
            scatter_rows(total, flow.keep, flow.give, rows_packs[p][0], size)

        def stage(p, side, k):
            wide = slot_packs[p][3].shape[1]
            at = 2 * k + side
            if k == 0:
                model_refs, head = slot_refs[p][side], slot_refs[p][2][side]
            else:
                model_refs, head = slot_land[p][k - 1][side], slot_land[p][others][side][k - 1]
            found = [moves.start(ref, to) for ref, to in zip(model_refs, model_stages[at])]
            return found + [moves.start(head, stages[at].at[:, pl.ds(0, wide)])]

        def load_slots(p):
            loads[n_rows + p] = stage(p, 0, 0) + stage(p, 1, 0)

        def slots_product(p):
            pack, unused, unused2, unused3, unused4, slot, weights = slot_packs[p]

            def add(k):
                low = 0
                for model, column, cols in weights:
                    at = k * slot + column
                    terms = [
                        dot_tn(model_stages[2 * k + side][model][...], stages[2 * k + side][:, at : at + cols])
                        for side in range(2)
                    ]
                    if k == 0:
                        total[:, low : low + cols] = terms[0] + terms[1]
                    else:
                        total[:, low : low + cols] += terms[0] + terms[1]
                    low += cols

            for copy in loads[n_rows + p]:
                copy.wait()
            add(0)
            for copy in slot_flights[p]:
                copy.wait()
            rest = [copy for k in range(1, n_tp) for side in range(2) for copy in stage(p, side, k)]
            for copy in rest:
                copy.wait()
            for k in range(1, n_tp):
                add(k)
            flow = flows[n_ready + n_rows + p]
            scatter_rows(total, flow.keep, flow.give, pack, size)

        def caption():
            if halving.bit < bits:
                halving.advance()
                if halving.bit == bits:
                    doubling_levels[bits][0] = halving_levels[bits][0, 0 : kv_block[0], :]
                    doubling.start()
            elif doubling.bit:
                doubling.advance()

        text_flights = []

        def context():
            while doubling.bit:
                caption()
            for at in range(size):
                kv_all[at * kv_block[0] : (at + 1) * kv_block[0], :] = doubling_levels[0][mirrored(at)]
            grad_ckv[...] = dot_tn(text_ref[:, text_cols : text_cols + context_cols], kv_all[...])
            ckv_in.wait()
            grad = dot_nn(kv_all[...], ckv[...])
            here = lax.axis_index("tp")

            def part(owner):
                chosen = grad[:, 0:owned]
                for other in range(1, n_tp):
                    chosen = jnp.where(owner == other, grad[:, other * owned : (other + 1) * owned], chosen)
                return chosen

            for k, place in enumerate(core_places()):
                exchange[k] = part(lax.rem(here + k + 1, n_tp)).astype(BF)
                text_flights.append(core.start(exchange.at[k], exchange.at[others + k], place))
            text_own[...] = part(here)

        def text():
            grad = text_own[...]
            for k, copy in enumerate(text_flights):
                copy.wait()
                grad = grad + exchange[others + k].astype(F32)
            grad_text[...] = dot_tn(grad.astype(BF), text_ref[:, 0:text_cols])

        mod_flights = []
        flat = clips * mod_cols

        def modulation_part(owner):
            rows_here = halving_levels[bits][0].astype(F32)[mod_row : mod_row + spare, :]
            row = jnp.concatenate([rows_here[i : i + 1] for i in range(spare)], axis=1)
            chosen = row[:, 0:flat]
            for other in range(1, n_tp):
                chosen = jnp.where(owner == other, row[:, other * flat : (other + 1) * flat], chosen)
            return chosen

        def modulation_send():
            here = lax.axis_index("tp")
            for k, place in enumerate(core_places()):
                part = modulation_part(lax.rem(here + k + 1, n_tp))
                mod_exchange[k, :, 0:flat] = jnp.broadcast_to(part, (8, flat))
                if mod_exchange.shape[2] > flat:
                    mod_exchange[k, :, flat:] = jnp.zeros((8, mod_exchange.shape[2] - flat), F32)
                mod_flights.append(core.start(mod_exchange.at[k], mod_exchange.at[others + k], place))

        def modulation():
            total_row = modulation_part(lax.axis_index("tp"))
            for k, copy in enumerate(mod_flights):
                copy.wait()
                total_row = total_row + mod_exchange[others + k, 0:1, 0:flat]
            sums = jnp.concatenate(
                [total_row[:, c * mod_cols : (c + 1) * mod_cols] for c in range(clips)], axis=0
            )
            grad_bias[...] = jnp.sum(sums, axis=0, keepdims=True)
            grad_mod[...] = dot_tn(sums.astype(BF), embed_ref[...])

        for what, p in schedule:
            row, slot = p - n_ready, p - n_ready - n_rows
            if what == "core":
                core_rows(row) if slot < 0 else core_slots(slot)
            elif what == "load":
                load_rows(row) if slot < 0 else load_slots(slot)
            elif what == "product":
                if row < 0:
                    for copy in ready_loads[p]:
                        copy.wait()
                elif slot < 0:
                    rows_product(row)
                else:
                    slots_product(slot)
            elif what == "send":
                flows[p].send()
            elif what == "wait":
                flows[p].wait()
            elif what == "part":
                flows[p].part()
            elif what == "go":
                flows[p].go()
            elif what == "caption":
                caption()
            elif what == "context":
                context()
                modulation_send()
            elif what == "modulation":
                modulation()
            else:
                text()
        while not all(flow.placed for flow in flows):
            for flow in flows:
                flow.go()

    out = call(
        kernel,
        outs,
        ins,
        in_any,
        out_any,
        scratch,
        after,
        limit=63,
        collective_id=4,
        has_side_effects=True,
    )
    return out[: len(result)], *out[len(result) : len(result) + 4]


def tp_sum(parts, dtype=BF):
    total = parts[0].astype(F32)
    for k in range(1, lax.axis_size("tp")):
        total = total + tp_to(parts[k].astype(dtype), k).astype(F32)
    return total


def tp_ordered(relative):
    size = lax.axis_size("tp")
    start = (size - lax.axis_index("tp")) % size
    return lax.dynamic_slice_in_dim(jnp.stack(relative + relative), start, size, axis=0)


def swap_wide(blocks):
    return lax.all_to_all(blocks, "wide", split_axis=0, concat_axis=0, tiled=True)


def on_device(
    tokens,
    cotangent,
    caption,
    caption_len,
    clip_id,
    timestep,
    w_mod,
    b_mod,
    w_text,
    w_sqkv,
    w_so,
    w_tqkv,
    w_to,
    w_cq,
    w_ckv,
    w_co,
    w_fc1,
    w_fc2,
):
    n_tp = lax.axis_size("tp")
    n_wide = lax.axis_size("wide")
    frames_here, patch_part, width = tokens.shape
    columns = w_so.shape[0]
    part = columns // 2
    half = w_fc1.shape[1] // 2
    clip_count = timestep.shape[0]
    frames = clip_id.shape[0]
    patch_here = patch_part // n_wide
    rows = frames_here * patch_part
    block = frames_here * patch_here
    count = frames * patch_here
    wide_at = lax.axis_index("wide")
    tp_at = lax.axis_index("tp")

    tokens_rows = tokens.reshape(rows, width)
    tokens_list = tp_gather(tokens_rows)
    sqkv_rows = w_sqkv.transpose(1, 2, 0)
    tqkv_list = tp_gather(w_tqkv.transpose(1, 2, 0))
    to_list = tp_gather(w_to)
    cq_list = tp_gather(w_cq.T)
    co_list = tp_gather(w_co)

    half_width = width // 2
    frequencies = jnp.exp(-math.log(10000.0) * jnp.arange(half_width).astype(F32) / half_width)
    angles = timestep.astype(F32)[:, None] * frequencies[None, :]
    embedding = jnp.concatenate([jnp.cos(angles), jnp.sin(angles)], axis=1)
    silu_embed = jax.nn.silu(embedding).astype(BF)
    mod_part = (dot_nn(silu_embed, w_mod) + b_mod.astype(F32)).astype(BF)
    modulation = tp_ordered(tp_gather(mod_part)).transpose(1, 0, 2).reshape(clip_count, -1)
    clip_hot = clip_id[:, None] == jnp.arange(clip_count)[None, :]
    hot_here = lax.dynamic_slice_in_dim(
        clip_hot.astype(F32), wide_at * frames_here, frames_here
    )
    mod_here = dot_nn(hot_here.astype(BF), modulation[:, : 3 * width])
    clip_rows = jnp.broadcast_to(clip_id[:, None], (frames, patch_here)).reshape(count)
    hot_rows = (clip_rows[:, None] == jnp.arange(clip_count)[None, :]).astype(BF)
    mod_rows = dot_nn(hot_rows, modulation[:, 3 * width :]).astype(BF)

    caption_rows = caption.shape[0]
    spare_rows = -(-clip_count * 6 * width // (n_wide * 2 * columns))
    block_rows = -(-caption_rows // 16) * 16
    extra_rows = 0 if caption_rows + spare_rows <= block_rows else -(-spare_rows // 16) * 16
    keys = n_wide * block_rows
    padded = jnp.pad(caption, ((0, block_rows - caption_rows), (0, 0)))
    context_part = dot_nt(padded, w_text.T).astype(BF)
    context = tp_ordered(tp_gather(context_part)).transpose(1, 0, 2).reshape(block_rows, width)
    ckv_rows = w_ckv.transpose(1, 2, 0).reshape(2 * columns, width)
    keyval_part = dot_nt(context, ckv_rows).astype(BF)
    text_cols = caption.shape[1] // n_wide
    context_cols = width // n_wide
    spare = -(text_cols + context_cols) % LANES
    texts = jnp.concatenate(
        [
            padded.reshape(block_rows, n_wide, text_cols),
            context.reshape(block_rows, n_wide, context_cols),
            jnp.zeros((block_rows, n_wide, spare), BF),
        ],
        axis=2,
    ).transpose(1, 0, 2)

    row_two = clip_rows * patch_here + np.arange(count, dtype=np.int32) % patch_here
    key_at = np.arange(keys)
    key_row = key_at // block_rows * caption_rows + key_at % block_rows
    key_real = jnp.asarray(key_at % block_rows < caption_rows)[None, :]
    key_clip = (key_row // LTXT).astype(np.int32)[None, :]
    key_in = (key_row % LTXT).astype(np.int32)[None, :]
    key_three = jnp.full((1, keys), -1, jnp.int32)
    for clip in range(clip_count):
        seen = key_real & (key_clip == clip) & (key_in < caption_len[clip])
        key_three = jnp.where(seen, clip, key_three)
    row_codes = jnp.stack([row_two, clip_rows], axis=1)
    longest = max(count, keys)
    key_codes = jnp.concatenate(
        [jnp.pad(row_two[None, :], ((0, 0), (0, longest - count))), jnp.pad(key_three, ((0, 0), (0, longest - keys)))]
    )

    grad_blocks = cotangent.reshape(frames_here, n_wide, patch_here, width).transpose(1, 0, 2, 3)
    grad_blocks = grad_blocks.reshape(n_wide, block, width)

    up = Pack(0, [1, 3, 2], [(1, half)])
    down = Pack(1, [0, 2, 3], [(1, half)])
    inner = Pack(2, [0, 1, 3], [(3, part), (1, part)])
    outer = Pack(1, [2, 0, 3], [(1, part), (1, part)])
    q_pack = Pack(0, [1, 2, 3], [(3, part)])
    o_pack = Pack(0, [2, 1, 3], [(1, part)])

    h_all, h_own, qkv_one, probs_one, a_keep, a_give, y_own, *others = spatial_forward(
        tokens_list, mod_here, sqkv_rows, w_so, frames_here, keyval_part, o_pack.first
    )
    y_others, keyval = others[: n_tp - 1], others[n_tp - 1]
    keyval_list = tp_gather(keyval.reshape(keys, 2 * columns))
    y_others = [tp_to(other, k + 1) for k, other in enumerate(y_others)]
    stream, y_one = stream_to_patches(tokens_rows, y_own, y_others, mod_here, frames_here)
    *kept, stream, keyval_full, t_keep, t_give, grad_out, a_got = middle_forward(
        stream.reshape(count, width), row_codes, key_codes, [grad_blocks], keyval_list, tqkv_list, to_list, cq_list, co_list, outer.first,
        [(a_give, o_pack.first)],
    )
    grad_out = grad_out.reshape(count, width)
    h2, h3 = kept[0], kept[4]
    (
        block_out,
        h4_all,
        up_keep,
        up_give,
        dy4_all,
        down_keep,
        down_give,
        grad,
        mod_sum,
        unused,
        unused,
        h4_got,
        dy4_got,
        h2_got,
        h3_got,
        t_got,
        h_flip,
    ) = feed_forward(
        stream,
        grad_out,
        mod_rows,
        hot_rows,
        w_fc1,
        w_fc2,
        [up.first, down.first],
        [(h2, inner.first), (h3, inner.first), (t_give, outer.first), (h_own, q_pack.first)],
    )

    in_keep, in_give, dy2, dy3, grad, block_out, texts, up_got, down_got, *grad_kv = middle_backward(
        grad,
        kept,
        keyval_full,
        block_out.reshape(n_wide, block, width),
        texts,
        tqkv_list,
        to_list,
        cq_list,
        co_list,
        inner.first,
        [(up_give, up.first), (down_give, down.first)],
    )
    block_out = block_out.reshape(n_wide, frames_here, patch_here, width).transpose(1, 0, 2, 3)
    block_out = block_out.reshape(frames_here, patch_part, width)
    (grad_stream, grad_y1, grad_gate), (up_halves, down_halves) = grads_to_frames(
        grad.reshape(n_wide, block, width),
        y_one,
        mod_here,
        frames_here,
        [(up, h4_all, h4_got, up_keep, up_got), (down, dy4_all, dy4_got, down_keep, down_got)],
    )
    grad_y1_list = tp_gather(grad_y1)
    given = [(in_give, inner.first), (dy2, outer.first), (dy3, outer.first), (grad_y1, o_pack.first)]
    q_keep, q_give, grad_h_own, *grad_h_others, dy_all, in_got, dy2_got, dy3_got, dy_got, q_got = spatial_backward(
        grad_y1_list, probs_one, qkv_one, sqkv_rows, w_so, frames_here, given, q_pack.first
    )
    grad_h_others = [tp_to(other, k + 1) for k, other in enumerate(grad_h_others)]
    grad_tokens, frame_sums = tokens_gradient(
        tokens_rows, grad_stream, grad_h_own, grad_h_others, mod_here, frames_here, []
    )
    frame_sums = jnp.concatenate([frame_sums, grad_gate], axis=1)
    here_sum = lax.dot_general(hot_here, frame_sums, (((0,), (0,)), ((), ())), precision=HIGH)
    grad_mod = jnp.concatenate([here_sum, mod_sum], axis=1).reshape(clip_count, n_tp, n_wide, -1)
    mod_blocks = grad_mod.transpose(2, 1, 0, 3).reshape(n_wide, -1)
    mod_blocks = jnp.pad(mod_blocks, ((0, 0), (0, spare_rows * 2 * columns - mod_blocks.shape[1])))
    mod_blocks = mod_blocks.reshape(n_wide, spare_rows, 2 * columns)
    kv_parts = [grad_kv[0].reshape(n_wide, block_rows, -1)]
    kv_parts += [tp_to(grad_kv[k], k).reshape(n_wide, block_rows, -1) for k in range(1, n_tp)]
    schedule = [
        ("core", 3), ("core", 5), ("load", 3), ("load", 5), ("product", 0), ("send", 0),
        ("product", 1), ("send", 1), ("product", 3), ("core", 2), ("load", 2), ("send", 3),
        ("product", 5), ("core", 4), ("load", 4), ("send", 5), ("product", 2), ("send", 2),
        ("wait", 3), ("send", 3), ("product", 4), ("send", 4), ("caption", 0), ("wait", 5),
        ("send", 5), ("part", 3), ("wait", 0), ("send", 0), ("wait", 3), ("send", 3),
        ("wait", 1), ("send", 1), ("part", 3), ("wait", 3), ("send", 3), ("caption", 0),
        ("part", 3), ("wait", 3), ("part", 5), ("wait", 5), ("send", 5), ("wait", 2),
        ("send", 2), ("caption", 0), ("caption", 0), ("part", 5), ("wait", 5), ("send", 5),
        ("caption", 0), ("part", 0), ("wait", 0), ("send", 0), ("wait", 4), ("send", 4),
        ("part", 1), ("part", 5), ("wait", 5), ("part", 2), ("wait", 2), ("send", 2),
        ("wait", 1), ("send", 1), ("caption", 0), ("caption", 0), ("part", 4), ("wait", 4),
        ("send", 4), ("caption", 0), ("context", 0), ("part", 4), ("part", 0), ("text", 0),
        ("modulation", 0), ("part", 2), ("wait", 2), ("send", 2), ("wait", 0), ("send", 0),
        ("wait", 4), ("send", 4), ("part", 1), ("wait", 1), ("send", 1), ("part", 2),
        ("wait", 2), ("part", 0), ("wait", 0), ("part", 4), ("wait", 4), ("part", 1),
        ("wait", 1),
    ]
    gradients, grad_ckv, grad_text, grad_w_mod, grad_b_mod = reduce_all(
        [(up, *up_halves), (down, *down_halves)],
        [
            (q_pack, h_all, h_flip, q_keep, q_got, frames_here, False),
            (o_pack, dy_all, dy_got, a_keep, a_got, frames_here, False),
        ],
        [
            (
                inner,
                [h2, h3],
                [h2_got, h3_got],
                in_keep,
                in_got,
                whole_tiles(4 * part),
                [(0, 0, 3 * part), (1, 3 * part, part)],
            ),
            (
                outer,
                [dy2, dy3],
                [dy2_got, dy3_got],
                t_keep,
                t_got,
                whole_tiles(2 * part),
                [(0, 0, part), (1, part, part)],
            ),
        ],
        kv_parts,
        mod_blocks,
        silu_embed,
        texts.reshape(keys, -1),
        text_cols,
        ckv_rows,
        schedule,
        [grad_tokens],
        extra_rows,
    )
    grad_fc1, grad_fc2, grad_sqkv, grad_so, grad_tqkv, grad_cq, grad_to, grad_co = gradients
    grad_ckv = grad_ckv.reshape(-1, 2, columns)
    grad_text = grad_text.T

    return (
        block_out,
        grad_tokens.reshape(tokens.shape),
        grad_w_mod.T,
        grad_b_mod.reshape(-1),
        grad_text,
        grad_sqkv.transpose(1, 0, 2),
        grad_so.T,
        grad_tqkv.transpose(1, 0, 2),
        grad_to.T,
        grad_cq,
        grad_ckv,
        grad_co.T,
        grad_fc1,
        grad_fc2.T,
    )


def solution(mesh):
    placed = (
        P("wide", "tp", None),
        P("wide", "tp", None),
        P("wide", None),
        P(),
        P(),
        P(),
        P(None, "tp"),
        P("tp"),
        P(None, "tp"),
        P(None, None, "tp"),
        P("tp", None),
        P(None, None, "tp"),
        P("tp", None),
        P(None, "tp"),
        P(None, None, "tp"),
        P("tp", None),
        P(None, "tp"),
        P("tp", None),
    )
    return jax.shard_map(
        on_device,
        mesh=mesh,
        in_specs=placed,
        out_specs=(
            P("wide", "tp", None),
            P("wide", "tp", None),
            P(None, ("tp", "wide")),
            P(("tp", "wide")),
            P("wide", "tp"),
            P("wide", None, "tp"),
            P("tp", "wide"),
            P("wide", None, "tp"),
            P("tp", "wide"),
            P("wide", "tp"),
            P("wide", None, "tp"),
            P("tp", "wide"),
            P("wide", "tp"),
            P("tp", "wide"),
        ),
        check_vma=False,
    )
```

```python
import functools
import math

import jax
import jax.numpy as jnp
import numpy as np
from jax import lax
from jax.experimental import pallas as pl
from jax.experimental.pallas import tpu as pltpu
from jax.sharding import PartitionSpec as P

HD = 72
LTXT = 120
EPS = 1e-06
NEGATIVE = -1e30
HIGH = lax.Precision.HIGHEST
BF = jnp.bfloat16
F32 = jnp.float32
LANES = 128
FACTOR = HD ** (-0.5)
VMEM = pltpu.VMEM
MB = 1 << 20


def dot_nn(left, right):
    return lax.dot_general(left, right, (((1,), (0,)), ((), ())), preferred_element_type=F32)


def dot_nt(left, right):
    return lax.dot_general(left, right, (((1,), (1,)), ((), ())), preferred_element_type=F32)


def dot_tn(left, right):
    return lax.dot_general(left, right, (((0,), (0,)), ((), ())), preferred_element_type=F32)


def norm_of(rows):
    average = jnp.mean(rows, axis=-1, keepdims=True)
    centred = rows - average
    inverse = lax.rsqrt(jnp.mean(centred * centred, axis=-1, keepdims=True) + EPS)
    return centred * inverse, inverse


def norm_back(grad_normed, normed, inverse):
    grad_mean = jnp.mean(grad_normed, axis=-1, keepdims=True)
    grad_cross = jnp.mean(grad_normed * normed, axis=-1, keepdims=True)
    return inverse * (grad_normed - grad_mean - normed * grad_cross)


def window(head, columns):
    low = HD * head
    start = low // LANES * LANES
    stop = min(-(-(low + HD) // LANES) * LANES, columns)
    at = lax.broadcasted_iota(jnp.int32, (1, stop - start), 1) + start
    own = jnp.where((at >= low) & (at < low + HD), 1.0, 0.0).astype(BF)
    return start, stop, own


class Tiles:
    def __init__(self, write, columns, scale=None):
        self.write, self.columns, self.scale, self.open = write, columns, scale, {}

    def add(self, start, stop, value):
        for low in range(start, stop, LANES):
            part = value[:, low - start : min(low + LANES, stop) - start]
            self.open[low] = self.open[low] + part if low in self.open else part

    def flush(self, below):
        for low in sorted(self.open):
            if low + LANES <= below or below >= self.columns:
                part = self.open.pop(low)
                if self.scale is not None:
                    part = part * self.scale
                self.write(low, min(low + LANES, self.columns), part)


def attend(query, key, value, bias, heads, columns, keep_probs, write, between=None):
    out = Tiles(write, columns)
    for head in range(heads):
        start, stop, own = window(head, columns)
        scores = dot_nt(query(start, stop) * own, key(start, stop)) * FACTOR
        if bias is not None:
            scores = scores + bias
        scores = jnp.exp(scores - jnp.max(scores, axis=-1, keepdims=True))
        probs = (scores * (1.0 / jnp.sum(scores, axis=-1, keepdims=True))).astype(BF)
        keep_probs(head, probs)
        out.add(start, stop, dot_nn(probs, value(start, stop) * own))
        out.flush(HD * (head + 1))
        if between is not None and head == heads // 2:
            between()


def attend_back(query, key, value, grad_out, probs_of, heads, columns, write_q, write_k, write_v):
    grad_q = Tiles(write_q, columns, FACTOR)
    grad_k = Tiles(write_k, columns, FACTOR)
    grad_v = Tiles(write_v, columns)
    for head in range(heads):
        start, stop, own = window(head, columns)
        probs = probs_of(head)
        grad_own = grad_out(start, stop) * own
        grad_probs = dot_nt(grad_own, value(start, stop))
        wide_probs = probs.astype(F32)
        grad_scores = wide_probs * grad_probs
        row = jnp.sum(grad_scores, axis=-1, keepdims=True)
        grad_scores = (grad_scores - wide_probs * row).astype(BF)
        grad_q.add(start, stop, dot_nn(grad_scores, key(start, stop) * own))
        grad_k.add(start, stop, dot_tn(grad_scores, query(start, stop) * own))
        grad_v.add(start, stop, dot_tn(probs, grad_own))
        for tiles in (grad_q, grad_k, grad_v):
            tiles.flush(HD * (head + 1))


class Moves:
    def __init__(self, sems):
        self.sems, self.used = sems, 0

    def start(self, source, target):
        copy = pltpu.make_async_copy(source, target, self.sems.at[self.used])
        self.used += 1
        copy.start()
        return copy


def any_spec():
    return pl.BlockSpec(memory_space=pl.ANY)


def vmem_spec():
    return pl.BlockSpec(memory_space=VMEM)


def call(kernel, outs, ins, in_any, out_any, scratch, after=(), limit=56, **params):
    given, extra = len(ins), len(after)

    def ordered(*refs):
        kernel(*refs[:given], *refs[given + extra :])

    return pl.pallas_call(
        ordered,
        out_shape=tuple(outs),
        in_specs=[any_spec() if flag else vmem_spec() for flag in in_any] + [any_spec()] * extra,
        out_specs=tuple(any_spec() if flag else vmem_spec() for flag in out_any),
        scratch_shapes=scratch,
        compiler_params=pltpu.CompilerParams(vmem_limit_bytes=limit * MB, **params),
        cost_estimate=pl.CostEstimate(flops=1, bytes_accessed=1, transcendentals=0),
    )(*ins, *after)


def whole_tiles(columns):
    return -(-columns // LANES) * LANES


def like(shape, dtype=BF):
    return jax.ShapeDtypeStruct(shape, dtype)


def greet(more=()):
    barrier = pltpu.get_barrier_semaphore()
    size = lax.axis_size("wide")
    me = lax.axis_index("wide")

    def signal(k, carry):
        pl.semaphore_signal(
            barrier,
            inc=1,
            device_id={"wide": lax.rem(me + k, size)},
            device_id_type=pl.DeviceIdType.MESH,
        )
        return carry

    lax.fori_loop(1, size, signal, 0)
    for place in more:
        pl.semaphore_signal(barrier, inc=1, device_id=place, device_id_type=pl.DeviceIdType.MESH)
    pl.semaphore_wait(barrier, size - 1 + len(more))


class Swap:
    def __init__(self, send, recv, send_sem, recv_sem, shared=False):
        self.send, self.recv, self.shared = send, recv, shared
        self.send_sem, self.recv_sem = send_sem, recv_sem

    def source(self, at):
        return self.send if self.shared else self.send.at[at]

    def copy(self, k, source, target, peer):
        return pltpu.make_async_remote_copy(
            src_ref=self.source(source),
            dst_ref=self.recv.at[target],
            send_sem=self.send_sem.at[k],
            recv_sem=self.recv_sem.at[k],
            device_id={"wide": peer},
            device_id_type=pl.DeviceIdType.MESH,
        )

    def start(self):
        size, me = lax.axis_size("wide"), lax.axis_index("wide")

        def step(k, carry):
            peer = lax.rem(me + k, size)
            self.copy(k, peer, me, peer).start()
            return carry

        lax.fori_loop(1, size, step, 0)
        self.recv[me] = self.send[...] if self.shared else self.send[me]

    def finish(self):
        size, me = lax.axis_size("wide"), lax.axis_index("wide")

        def arrive(k, carry):
            peer = lax.rem(me + size - k, size)
            self.copy(k, peer, peer, peer).wait_recv()
            return carry

        def leave(k, carry):
            peer = lax.rem(me + k, size)
            self.copy(k, peer, me, peer).wait_send()
            return carry

        lax.fori_loop(1, size, arrive, 0)
        lax.fori_loop(1, size, leave, 0)


def wide_bits():
    return lax.axis_size("wide").bit_length() - 1


def mirrored(at):
    bits = wide_bits()
    return sum(((at >> bit) & 1) << (bits - 1 - bit) for bit in range(bits))


def bit_of(bit):
    return lax.rem(lax.div(lax.axis_index("wide"), 1 << bit), 2)


def partner(bit):
    return lax.axis_index("wide") + (1 - 2 * bit_of(bit)) * (1 << bit)


def greet_devices(places):
    barrier = pltpu.get_barrier_semaphore()
    for place in places:
        pl.semaphore_signal(barrier, inc=1, device_id=place, device_id_type=pl.DeviceIdType.MESH)
    pl.semaphore_wait(barrier, len(places))


def pair_places():
    return [{"wide": partner(bit)} for bit in range(wide_bits())]


def core_places():
    size, me = lax.axis_size("tp"), lax.axis_index("tp")
    return [{"tp": lax.rem(me + k, size)} for k in range(1, size)]


class Doubling:
    def __init__(self, levels, send_sem, recv_sem):
        self.levels, self.send_sem, self.recv_sem = levels, send_sem, recv_sem
        self.bit = wide_bits()
        self.copy = None

    def start(self):
        self.send()

    def send(self):
        bit = self.bit - 1
        have = self.levels[self.bit]
        half = have.shape[0]
        mine = bit_of(bit)
        there = self.levels[bit].at[pl.ds(mine * half, half)]
        self.copy = pltpu.make_async_remote_copy(
            src_ref=have,
            dst_ref=there,
            send_sem=self.send_sem.at[bit],
            recv_sem=self.recv_sem.at[bit],
            device_id={"wide": partner(bit)},
            device_id_type=pl.DeviceIdType.MESH,
        )
        self.copy.start()
        self.levels[bit][pl.ds(mine * half, half)] = have[...]

    def advance(self):
        if self.bit == 0:
            return
        self.copy.wait()
        self.bit -= 1
        if self.bit:
            self.send()

    def finish(self, out):
        while self.bit:
            self.advance()
        for at in range(self.levels[0].shape[0]):
            out[at] = self.levels[0][mirrored(at)]


class Halving:
    def __init__(self, levels, landing, send_sem, recv_sem):
        self.levels, self.landing = levels, landing
        self.send_sem, self.recv_sem = send_sem, recv_sem
        self.bit = 0

    def start(self):
        self.send()

    def send(self):
        bit = self.bit
        half = self.landing[bit].shape[0]
        other = 1 - bit_of(bit)
        self.copy = pltpu.make_async_remote_copy(
            src_ref=self.levels[bit].at[pl.ds(other * half, half)],
            dst_ref=self.landing[bit],
            send_sem=self.send_sem.at[bit],
            recv_sem=self.recv_sem.at[bit],
            device_id={"wide": partner(bit)},
            device_id_type=pl.DeviceIdType.MESH,
        )
        self.copy.start()

    def advance(self):
        bit = self.bit
        if bit == wide_bits():
            return
        half = self.landing[bit].shape[0]
        self.copy.wait()
        own = self.levels[bit][pl.ds(bit_of(bit) * half, half)]
        self.levels[bit + 1][...] = (own.astype(F32) + self.landing[bit][...].astype(F32)).astype(BF)
        self.bit += 1
        if self.bit < wide_bits():
            self.send()

    def finish(self, out):
        while self.bit < wide_bits():
            self.advance()
        out[...] = self.levels[-1][0]


def level_scratch(size, block):
    bits = size.bit_length() - 1
    return [VMEM((size >> s,) + block, BF) for s in range(bits + 1)]


class CoreCopies:
    def __init__(self, send_sem, recv_sem):
        self.send_sem, self.recv_sem, self.used = send_sem, recv_sem, 0

    def start(self, source, target, place):
        copy = pltpu.make_async_remote_copy(
            src_ref=source,
            dst_ref=target,
            send_sem=self.send_sem.at[self.used],
            recv_sem=self.recv_sem.at[self.used],
            device_id=place,
            device_id_type=pl.DeviceIdType.MESH,
        )
        copy.start()
        self.used += 1
        return copy


class PairCopies:
    def __init__(self, send_sem, recv_sem):
        self.send_sem, self.recv_sem, self.copies = send_sem, recv_sem, []

    def start(self, source, target, bit):
        at = len(self.copies)
        copy = pltpu.make_async_remote_copy(
            src_ref=source,
            dst_ref=target,
            send_sem=self.send_sem.at[at],
            recv_sem=self.recv_sem.at[at],
            device_id={"wide": partner(bit)},
            device_id_type=pl.DeviceIdType.MESH,
        )
        copy.start()
        self.copies.append(copy)

    def finish(self):
        for copy in self.copies:
            copy.wait()


def swap_sems(size, count):
    return [pltpu.SemaphoreType.DMA((size,))] * (2 * count)


def spatial_forward(tokens_list, mod_here, sqkv_rows, w_so, frames_here, keyval_part, o_first):
    n_tp = len(tokens_list)
    rows, width = tokens_list[0].shape
    columns = w_so.shape[0]
    patch_part = rows // frames_here
    per_frame = n_tp * patch_part
    count = n_tp * rows
    heads = columns // HD
    size = lax.axis_size("wide")
    bits = wide_bits()

    def kernel(*refs):
        token_refs = refs[:n_tp]
        mod_ref, qkv_hbm, so_hbm, kv_ref = refs[n_tp : n_tp + 4]
        at = n_tp + 4
        h_ref, h_own, qkv_out, probs_out, a_keep, a_give, y_ref = refs[at : at + 7]
        y_others = refs[at + 7 : at + 6 + n_tp]
        at += 6 + n_tp
        kv_out = refs[at]
        weight_qkv, weight_o, qkv_ref, probs_ref, attn_ref, sems, *levels = refs[at + 1 :]
        *levels, send_sem, recv_sem = levels
        greet_devices(pair_places())
        share = Doubling(levels, send_sem, recv_sem)
        levels[bits][0] = kv_ref[...]
        share.start()
        moves = Moves(sems)
        weights = [moves.start(qkv_hbm.at[i], weight_qkv.at[i]) for i in range(3)]
        weight_out = moves.start(so_hbm, weight_o)
        for frame in range(frames_here):
            shift = mod_ref[frame : frame + 1, 0:width]
            scale = 1.0 + mod_ref[frame : frame + 1, width : 2 * width]
            for r in range(n_tp):
                part = token_refs[r][frame * patch_part : (frame + 1) * patch_part, :]
                normed, unused = norm_of(part.astype(F32))
                at = frame * per_frame + r * patch_part
                value = (normed * scale + shift).astype(BF)
                h_ref[at : at + patch_part, :] = value
                if r == 0:
                    h_own[frame * patch_part : (frame + 1) * patch_part, :] = value
        outgoing = []
        share.advance()
        for i in range(3):
            weights[i].wait()
            qkv_ref[i] = dot_nt(h_ref[...], weight_qkv[i]).astype(BF)
            if i == 1:
                share.advance()
        outgoing.append(moves.start(qkv_ref, qkv_out))
        for frame in range(frames_here):
            at = slice(frame * per_frame, (frame + 1) * per_frame)

            def keep_probs(head, probs, frame=frame):
                probs_ref[frame * heads + head] = probs

            def write(low, high, part, at=at):
                attn_ref[at, low:high] = part.astype(BF)

            attend(
                lambda low, high, at=at: qkv_ref[0, at, low:high],
                lambda low, high, at=at: qkv_ref[1, at, low:high],
                lambda low, high, at=at: qkv_ref[2, at, low:high],
                None,
                heads,
                columns,
                keep_probs,
                write,
                share.advance if frame == 0 else None,
            )
        outgoing.append(moves.start(probs_ref, probs_out))
        mine = bit_of(o_first)
        first, second = attn_ref[:, : columns // 2], attn_ref[:, columns // 2 :]
        part = columns // 2
        a_keep[:, 0:part] = jnp.where(mine == 0, first, second)
        a_give[:, 0:part] = jnp.where(mine == 0, second, first)
        for ref in (a_keep, a_give):
            if ref.shape[1] > part:
                ref[:, part:] = jnp.zeros((count, ref.shape[1] - part), BF)
        weight_out.wait()
        for frame in range(frames_here):
            at = frame * per_frame
            branch = dot_nn(attn_ref[at : at + per_frame, :], weight_o[...])
            here = slice(frame * patch_part, (frame + 1) * patch_part)
            y_ref[here, :] = branch[:patch_part]
            for r in range(1, n_tp):
                y_others[r - 1][here, :] = branch[r * patch_part : (r + 1) * patch_part].astype(BF)
        for copy in outgoing:
            copy.wait()
        share.finish(kv_out)

    outs = [
        like((count, width)),
        like((rows, width)),
        like((3, count, columns)),
        like((frames_here * heads, per_frame, per_frame)),
        like((count, whole_tiles(columns // 2))),
        like((count, whole_tiles(columns // 2))),
        like((rows, width), F32),
    ] + [like((rows, width))] * (n_tp - 1)
    outs.append(like((size,) + keyval_part.shape))
    ins = list(tokens_list) + [mod_here, sqkv_rows, w_so, keyval_part]
    return call(
        kernel,
        outs,
        ins,
        [False] * (n_tp + 1) + [True, True, False],
        [False, False, True, True] + [False] * (n_tp + 3),
        [
            VMEM((3, columns, width), BF),
            VMEM((columns, width), BF),
            VMEM((3, count, columns), BF),
            VMEM((frames_here * heads, per_frame, per_frame), BF),
            VMEM((count, columns), BF),
            pltpu.SemaphoreType.DMA((6,)),
        ]
        + level_scratch(size, keyval_part.shape)
        + swap_sems(bits, 1),
        collective_id=1,
        has_side_effects=True,
    )


def stream_to_patches(tokens_rows, y_own, y_others, mod_here, frames_here):
    size = lax.axis_size("wide")
    rows, width = tokens_rows.shape
    patch_part = rows // frames_here
    patch_here = patch_part // size
    block = frames_here * patch_here
    others = len(y_others)

    def kernel(*refs):
        token_ref, y_ref, mod_ref = refs[0], refs[1], refs[2 + others]
        out_ref, total_ref = refs[3 + others : 5 + others]
        send, recv, send_sem, recv_sem = refs[5 + others :]
        greet()
        for frame in range(frames_here):
            at = slice(frame * patch_part, (frame + 1) * patch_part)
            branch = y_ref[at, :]
            for other in refs[2 : 2 + others]:
                branch = branch + other[at, :].astype(F32)
            total_ref[at, :] = branch
            gate = mod_ref[frame : frame + 1, 2 * width : 3 * width]
            stream = token_ref[at, :].astype(F32) + gate * branch
            for owner in range(size):
                send[owner, frame * patch_here : (frame + 1) * patch_here, :] = stream[
                    owner * patch_here : (owner + 1) * patch_here
                ].astype(BF)
        exchange = Swap(send, recv, send_sem, recv_sem)
        exchange.start()
        exchange.finish()
        out_ref[...] = recv[...]

    ins = [tokens_rows, y_own] + list(y_others) + [mod_here]
    return call(
        kernel,
        [like((size, block, width)), like((rows, width), F32)],
        ins,
        [False] * len(ins),
        [False, False],
        [VMEM((size, block, width), BF)] * 2 + swap_sems(size, 1),
        collective_id=2,
        has_side_effects=True,
    )


def grads_to_frames(grad_blocks, y_one, mod_here, frames_here, members):
    size, block, width = grad_blocks.shape
    rows = y_one.shape[0]
    patch_part = rows // frames_here
    patch_here = patch_part // size
    n_tp = lax.axis_size("tp")
    others = n_tp - 1
    number = len(members)
    every, most = members[0][1].shape[0], max(member[0].across for member in members)
    token_rows = every // n_tp
    head = members[0][3].shape[1]

    def kernel(*refs):
        grad_ref, y_ref, mod_ref = refs[:3]
        operands = [refs[3 + 4 * p : 7 + 4 * p] for p in range(number)]
        at = 3 + 4 * number
        stream_ref, branch_ref, gate_ref = refs[at : at + 3]
        outs = [refs[at + 3 + 2 * p : at + 5 + 2 * p] for p in range(number)]
        at += 3 + 2 * number
        recv, exchange_send, exchange_recv, models, heads, total, sems, send_sem, recv_sem = refs[at:]
        greet(core_places())
        exchange = Swap(grad_ref, recv, exchange_send, exchange_recv)
        exchange.start()
        core = CoreCopies(send_sem, recv_sem)
        moves = Moves(sems)
        flights, loads = [], []
        for p, (model, got, keep, other) in enumerate(operands):
            flights.append(
                [
                    core.start(got, models.at[2 * p + 1, pl.ds((n_tp - 1 - k) * token_rows, token_rows), :], place)
                    for k, place in enumerate(core_places())
                ]
            )
            loads.append(
                [
                    moves.start(model, models.at[2 * p]),
                    moves.start(keep, heads.at[2 * p]),
                    moves.start(got, models.at[2 * p + 1, pl.ds(0, token_rows), :]),
                    moves.start(other, heads.at[2 * p + 1]),
                ]
            )
        for p, member in enumerate(members):
            across = member[0].across
            for copy in loads[p]:
                copy.wait()
            total[:, 0:across] = dot_tn(models[2 * p], heads[2 * p, :, 0:across])
            for copy in flights[p]:
                copy.wait()
            total[:, 0:across] += dot_tn(models[2 * p + 1], heads[2 * p + 1, :, 0:across])
            scatter_rows(total, outs[p][0], outs[p][1], member[0], size)
        exchange.finish()
        for owner in range(size):
            part = recv[owner].astype(F32)
            for frame in range(frames_here):
                at = frame * patch_part + owner * patch_here
                stream_ref[at : at + patch_here, :] = part[
                    frame * patch_here : (frame + 1) * patch_here
                ]
        for frame in range(frames_here):
            at = slice(frame * patch_part, (frame + 1) * patch_part)
            stream = stream_ref[at, :]
            gate_ref[frame : frame + 1, :] = jnp.sum(stream * y_ref[at, :], axis=0, keepdims=True)
            branch_ref[at, :] = (stream * mod_ref[frame : frame + 1, 2 * width : 3 * width]).astype(BF)

    ins = [grad_blocks, y_one, mod_here] + [array for member in members for array in member[1:5]]
    halves = [
        like((size // 2, width // size, member[0].across)) for member in members for unused in range(2)
    ]
    out = call(
        kernel,
        [like((rows, width), F32), like((rows, width)), like((frames_here, width), F32)] + halves,
        ins,
        [False] * 3 + [True] * (4 * number),
        [False] * (3 + 2 * number),
        [VMEM((size, block, width), BF)]
        + swap_sems(size, 1)
        + [
            VMEM((2 * number, every, width), BF),
            VMEM((2 * number, every, head), BF),
            VMEM((width, most), F32),
            pltpu.SemaphoreType.DMA((4 * number,)),
            pltpu.SemaphoreType.DMA((number * others,)),
            pltpu.SemaphoreType.DMA((number * others,)),
        ],
        collective_id=3,
        has_side_effects=True,
    )
    return out[:3], [out[3 + 2 * p : 5 + 2 * p] for p in range(number)]


def fill_rows(moves, sources, target):
    step = sources[0].shape[0]
    return [moves.start(ref, target.at[pl.ds(r * step, step), :]) for r, ref in enumerate(sources)]


def middle_forward(stream, row_codes, key_codes, blocks, keyval_list, tqkv_list, to_list, cq_list, co_list, out_first, given):
    n_tp = len(tqkv_list)
    count, width = stream.shape
    keys = keyval_list[0].shape[0]
    columns = to_list[0].shape[0]
    heads = width // HD
    part = columns // 2
    out_slot = whole_tiles(2 * part)

    def kernel(*refs):
        stream_ref, row_ref, key_ref = refs[:3]
        block_refs = refs[3 : 3 + len(blocks)]
        at = 3 + len(blocks)
        groups = []
        for unused in range(5):
            groups.append(refs[at : at + n_tp])
            at += n_tp
        keyvals, tqkvs, tos, cqs, cos = groups
        given_refs = refs[at : at + len(given)]
        at += len(given)
        h2_out, qkv_out, p2_out, inv2_ref, h3_out, q3_out, p3_out, inv3_ref, x_ref, kv_ref, a_keep, a_give = refs[at : at + 12]
        block_outs = refs[at + 12 : at + 12 + len(blocks)]
        at += 12 + len(blocks)
        given_got = refs[at : at + len(given)]
        w_qkv, w_o, w_q, w_c, h2, qkv, p2, a2, h3, q3, p3, a3, sems, *swap = refs[at + len(given) :]
        greet()
        pairs = PairCopies(*swap[-2:])
        for (unused, first), ref, target in zip(given, given_refs, given_got):
            pairs.start(ref, target, first)
        exchanges = [
            Swap(ref, swap[3 * i], swap[3 * i + 1], swap[3 * i + 2]) for i, ref in enumerate(block_refs)
        ]
        for exchange in exchanges:
            exchange.start()
        moves = Moves(sems)
        qkv_in = [
            [
                moves.start(tqkvs[r].at[i], w_qkv.at[i, pl.ds(r * columns, columns), :])
                for r in range(n_tp)
            ]
            for i in range(3)
        ]
        o_in = fill_rows(moves, tos, w_o)
        q_in = fill_rows(moves, cqs, w_q)
        c_in = fill_rows(moves, cos, w_c)
        outgoing = []
        for i in range(2):
            for r in range(n_tp):
                kv_ref[i, :, r * columns : (r + 1) * columns] = keyvals[r][
                    :, i * columns : (i + 1) * columns
                ]
        stream_one = stream_ref[...].astype(F32)
        normed, inverse = norm_of(stream_one)
        inv2_ref[...] = jnp.broadcast_to(inverse, inv2_ref.shape)
        h2[...] = normed.astype(BF)
        outgoing.append(moves.start(h2, h2_out))
        for i in range(3):
            for copy in qkv_in[i]:
                copy.wait()
            qkv[i] = dot_nt(h2[...], w_qkv[i]).astype(BF)
        outgoing.append(moves.start(qkv, qkv_out))

        def keep_two(head, probs):
            p2[head] = probs

        def write_two(low, high, part):
            a2[:, low:high] = part.astype(BF)

        attend(
            lambda low, high: qkv[0, :, low:high],
            lambda low, high: qkv[1, :, low:high],
            lambda low, high: qkv[2, :, low:high],
            jnp.where(row_ref[:, 0:1] == key_ref[0:1, 0:count], 0.0, NEGATIVE),
            heads,
            width,
            keep_two,
            write_two,
        )
        outgoing.append(moves.start(p2, p2_out))
        for copy in o_in:
            copy.wait()
        x_ref[...] = stream_one + dot_nn(a2[...], w_o[...])
        normed, inverse = norm_of(x_ref[...])
        inv3_ref[...] = jnp.broadcast_to(inverse, inv3_ref.shape)
        h3[...] = normed.astype(BF)
        outgoing.append(moves.start(h3, h3_out))
        for copy in q_in:
            copy.wait()
        q3[...] = dot_nt(h3[...], w_q[...]).astype(BF)
        outgoing.append(moves.start(q3, q3_out))

        def keep_three(head, probs):
            p3[head] = probs

        def write_three(low, high, part):
            a3[:, low:high] = part.astype(BF)

        attend(
            lambda low, high: q3[:, low:high],
            lambda low, high: kv_ref[0, :, low:high],
            lambda low, high: kv_ref[1, :, low:high],
            jnp.where(row_ref[:, 1:2] == key_ref[1:2, 0:keys], 0.0, NEGATIVE),
            heads,
            width,
            keep_three,
            write_three,
        )
        outgoing.append(moves.start(p3, p3_out))
        mine = bit_of(out_first)
        for r in range(n_tp):
            for i, ref in enumerate((a2, a3)):
                low = r * out_slot + i * part
                first = ref[:, r * columns : r * columns + part]
                second = ref[:, r * columns + part : (r + 1) * columns]
                a_keep[:, low : low + part] = jnp.where(mine == 0, first, second)
                a_give[:, low : low + part] = jnp.where(mine == 0, second, first)
            for ref in (a_keep, a_give):
                if out_slot > 2 * part:
                    spare = jnp.zeros((count, out_slot - 2 * part), BF)
                    ref[:, r * out_slot + 2 * part : (r + 1) * out_slot] = spare
        for copy in c_in:
            copy.wait()
        x_ref[...] = x_ref[...] + dot_nn(a3[...], w_c[...])
        for copy in outgoing:
            copy.wait()
        for exchange, out in zip(exchanges, block_outs):
            exchange.finish()
            out[...] = exchange.recv[...]
        pairs.finish()

    square = (count, width)
    outs = [
        like(square),
        like((3,) + square),
        like((heads, count, count)),
        like((count, LANES), F32),
        like(square),
        like(square),
        like((heads, count, keys)),
        like((count, LANES), F32),
        like(square, F32),
        like((2, keys, width)),
        like((count, n_tp * out_slot)),
        like((count, n_tp * out_slot)),
    ] + [like(array.shape) for array in blocks]
    outs += [like(array.shape) for array, unused in given]
    kept = [square, (3,) + square, (heads, count, count), square, square, square, (heads, count, keys), square]
    ins = [stream, row_codes, key_codes, *blocks, *keyval_list, *tqkv_list, *to_list, *cq_list, *co_list]
    ins += [array for array, unused in given]
    full = n_tp * columns
    return call(
        kernel,
        outs,
        ins,
        [False] * (3 + len(blocks) + n_tp) + [True] * (4 * n_tp + len(given)),
        [True, True, True, False, True, True, True, False, False, False, False, False] + [False] * len(blocks) + [True] * len(given),
        [VMEM((3, full, width), BF)]
        + [VMEM((full, width), BF)] * 3
        + [VMEM(shape, BF) for shape in kept]
        + [pltpu.SemaphoreType.DMA((6 * n_tp + 8,))]
        + [
            kind
            for array in blocks
            for kind in (VMEM(array.shape, BF), *swap_sems(array.shape[0], 1))
        ]
        + swap_sems(len(given), 1),
        collective_id=6,
        has_side_effects=True,
    )


def feed_forward(stream, grad_out, mod_rows, hot_rows, w_fc1, w_fc2, firsts, given):
    n_tp = lax.axis_size("tp")
    others = n_tp - 1
    count, width = stream.shape
    every = n_tp * count
    hidden = w_fc1.shape[1]
    half = hidden // 2
    padded = whole_tiles(half)
    clips = hot_rows.shape[1]
    pieces = 2 if half % LANES == 0 else 1

    def kernel(*refs):
        stream_ref, grad_ref, mod_ref, hot_ref, fc1_hbm, fc2_hbm = refs[:6]
        given_refs, refs = refs[6 : 6 + len(given)], refs[:6] + refs[6 + len(given) :]
        out_ref, h_all, up_keep, up_give, dy_all, down_keep, down_give, g_ref, mod_sum = refs[6:15]
        h_own, dy_own, h_got, dy_got = refs[15:19]
        given_got, refs = refs[19 : 19 + len(given)], refs[19 + len(given) :]
        w1, w2, h_land, total_y, total_h, send_y, send_h, land_y, land_h, sems, send_sem, recv_sem = refs[:12]
        moves = Moves(sems)
        loads = []
        for piece in range(pieces):
            cols = pl.ds(piece * (hidden // pieces), hidden // pieces)
            loads.append(
                (
                    moves.start(fc1_hbm.at[:, cols], w1.at[:, cols]),
                    moves.start(fc2_hbm.at[cols, :], w2.at[cols, :]),
                )
            )
        greet_devices(core_places() + pair_places())
        core = CoreCopies(send_sem, recv_sem)
        pairs = PairCopies(*refs[12:])
        for (unused, first), ref, target in zip(given, given_refs, given_got):
            pairs.start(ref, target, first)
        bit = [bit_of(first) for first in firsts]
        own = slice(0, count)
        gate = mod_ref[:, 2 * width :].astype(F32)
        dy_own[...] = (gate * grad_ref[...].astype(F32)).astype(BF)
        flights = [core.start(dy_own, h_land.at[n_tp - 2 - k], place) for k, place in enumerate(core_places())]
        pairs.start(dy_own, dy_got, firsts[1])
        shift = mod_ref[:, 0:width].astype(F32)
        scale = 1.0 + mod_ref[:, width : 2 * width].astype(F32)
        normed, inverse = norm_of(stream_ref[...])
        h_own[...] = (normed * scale + shift).astype(BF)
        flights += [
            core.start(h_own, h_land.at[others + n_tp - 2 - k], place) for k, place in enumerate(core_places())
        ]
        pairs.start(h_own, h_got, firsts[0])
        h_all[own, :] = h_own[...]
        dy_all[own, :] = dy_own[...]
        for pack in (up_keep, up_give, down_keep, down_give):
            if padded > half:
                pack[:, half:] = jnp.zeros((every, padded - half), BF)
        back = []
        for part in range(2):
            if part < pieces:
                for copy in loads[part]:
                    copy.wait()
            hid = slice(part * half, (part + 1) * half)
            for r in range(n_tp) if part == 0 else [*range(1, n_tp), 0]:
                at = slice(r * count, (r + 1) * count)
                if part == 0 and r == 1:
                    for copy in flights:
                        copy.wait()
                    for k in range(others):
                        there = slice((k + 1) * count, (k + 2) * count)
                        dy_all[there, :] = h_land[k]
                        h_all[there, :] = h_land[others + k]
                upper = dot_nn(h_all[at, :], w1[:, hid])
                square = upper * upper
                tanh = jnp.tanh(upper * (0.7978845608028654 + 0.035677408136300125 * square))
                rise = 0.5 + 0.5 * tanh
                active = (upper * rise).astype(BF)
                slope = rise + (0.5 * upper) * (1.0 - tanh * tanh) * (
                    0.7978845608028654 + 0.10703222440890037 * square
                )
                grad_upper = (dot_nt(dy_all[at, :], w2[hid, :]) * slope).astype(BF)
                for keep, give, mine, value in (
                    (up_keep, up_give, bit[0], grad_upper),
                    (down_keep, down_give, bit[1], active),
                ):

                    @pl.when(mine == part)
                    def _():
                        keep[at, 0:half] = value

                    @pl.when(mine != part)
                    def _():
                        give[at, 0:half] = value

                y_term = dot_nn(active, w2[hid, :])
                h_term = dot_nt(grad_upper, w1[:, hid])
                if part == 0:
                    total_y[at, :] = y_term
                    total_h[at, :] = h_term
                elif r == 0:
                    total_y[at, :] += y_term
                    total_h[at, :] += h_term
                else:
                    send_y[r - 1] = (total_y[at, :] + y_term).astype(BF)
                    send_h[r - 1] = (total_h[at, :] + h_term).astype(BF)
                    place = core_places()[r - 1]
                    back.append(core.start(send_y.at[r - 1], land_y.at[r - 1], place))
                    back.append(core.start(send_h.at[r - 1], land_h.at[r - 1], place))
        for copy in back:
            copy.wait()
        branch, grad_h = total_y[own, :], total_h[own, :]
        for k in range(others):
            branch = branch + land_y[k].astype(F32)
            grad_h = grad_h + land_h[k].astype(F32)
        gate = mod_ref[:, 2 * width :].astype(F32)
        out_ref[...] = (stream_ref[...] + gate * branch).astype(BF)
        grad = grad_ref[...].astype(F32)
        hot = hot_ref[...]
        mod_sum[:, 2 * width :] = dot_tn(hot, (grad * branch).astype(BF))
        mod_sum[:, 0:width] = dot_tn(hot, grad_h.astype(BF))
        normed, inverse = norm_of(stream_ref[...])
        mod_sum[:, width : 2 * width] = dot_tn(hot, (grad_h * normed).astype(BF))
        scale = 1.0 + mod_ref[:, width : 2 * width].astype(F32)
        g_ref[...] = grad + norm_back(grad_h * scale, normed, inverse)
        pairs.finish()

    side = like((every, padded))
    ins = [stream, grad_out, mod_rows, hot_rows, w_fc1, w_fc2] + [array for array, unused in given]
    n_pairs = 2 + len(given)
    square = (count, width)
    return call(
        kernel,
        [
            like(square),
            like((every, width)),
            side,
            side,
            like((every, width)),
            side,
            side,
            like(square, F32),
            like((clips, 3 * width), F32),
            like(square),
            like(square),
            like(square),
            like(square),
        ]
        + [like(array.shape) for array, unused in given],
        ins,
        [False] * 4 + [True] * (2 + len(given)),
        [False] * 11 + [True] * n_pairs,
        [
            VMEM((width, hidden), BF),
            VMEM((hidden, width), BF),
            VMEM((2 * others,) + square, BF),
            VMEM((every, width), F32),
            VMEM((every, width), F32),
            VMEM((others,) + square, BF),
            VMEM((others,) + square, BF),
            VMEM((others,) + square, BF),
            VMEM((others,) + square, BF),
            pltpu.SemaphoreType.DMA((4,)),
            pltpu.SemaphoreType.DMA((4 * others,)),
            pltpu.SemaphoreType.DMA((4 * others,)),
            pltpu.SemaphoreType.DMA((n_pairs,)),
            pltpu.SemaphoreType.DMA((n_pairs,)),
        ],
        collective_id=5,
        has_side_effects=True,
    )


def middle_backward(grad, kept, keyval, out_blocks, texts, tqkv_list, to_list, cq_list, co_list, in_first, given):
    n_tp = len(tqkv_list)
    h2, qkv, p2, inv2, h3, q3, p3, inv3 = kept
    count, width = grad.shape
    keys = keyval.shape[1]
    columns = to_list[0].shape[0]
    part = columns // 2
    heads = width // HD
    full = n_tp * columns
    in_slot = whole_tiles(4 * part)

    def kernel(*refs):
        grad_ref, inv2_ref, inv3_ref, h2_ref, h3_ref, block_ref, text_ref = refs[:7]
        qkv_hbm, p2_hbm, q3_hbm, p3_hbm, kv_hbm = refs[7:12]
        given_refs = refs[12 : 12 + len(given)]
        at = 12 + len(given)
        groups = []
        for unused in range(4):
            groups.append(refs[at : at + n_tp])
            at += n_tp
        tqkvs, tos, cqs, cos = groups
        in_keep, in_give, dy2_ref, dy3_ref, stream_ref, block_out, text_out = refs[at : at + 7]
        given_got = refs[at + 7 : at + 7 + len(given)]
        at += 2 + len(given)
        kv_outs = refs[at + 5 : at + 5 + n_tp]
        (
            w_qkv, w_o, w_q, w_c, qkv_ref, p2_ref, q3_ref, p3_ref, kv_ref,
            grad_attn, d_q, d_k, d_v, total, sems, recv, send_sem, recv_sem, text_recv, text_sem, text_recv_sem, pair_send, pair_recv,
        ) = refs[at + 5 + n_tp :]
        greet()
        exchange = Swap(block_ref, recv, send_sem, recv_sem)
        pairs = PairCopies(pair_send, pair_recv)
        for (unused, first), ref, target in zip(given, given_refs, given_got):
            pairs.start(ref, target, first)
        exchange.start()
        text_exchange = Swap(text_ref, text_recv, text_sem, text_recv_sem)
        text_exchange.start()
        moves = Moves(sems)
        c_in = fill_rows(moves, cos, w_c)
        kv_in = moves.start(kv_hbm, kv_ref)
        p3_in = moves.start(p3_hbm, p3_ref)
        q3_in = moves.start(q3_hbm, q3_ref)
        q_in = fill_rows(moves, cqs, w_q)
        o_in = fill_rows(moves, tos, w_o)
        qkv_load = moves.start(qkv_hbm, qkv_ref)
        p2_in = moves.start(p2_hbm, p2_ref)
        qkv_in = [
            [
                moves.start(tqkvs[r].at[i], w_qkv.at[i, pl.ds(r * columns, columns), :])
                for r in range(n_tp)
            ]
            for i in range(3)
        ]
        bit = bit_of(in_first)

        def split(value, r, mine, keep, give, low):
            first = value[:, r * columns : r * columns + part]
            second = value[:, r * columns + part : (r + 1) * columns]
            keep[:, low : low + part] = jnp.where(mine == 0, first, second)
            give[:, low : low + part] = jnp.where(mine == 0, second, first)

        def into(ref, upto):
            def write(low, high, value):
                ref[0:upto, low:high] = value.astype(BF)

            return write

        if in_slot > 4 * part:
            for pack in (in_keep, in_give):
                for r in range(n_tp):
                    spare = jnp.zeros((count, in_slot - 4 * part), BF)
                    pack[:, r * in_slot + 4 * part : (r + 1) * in_slot] = spare
        grad_y = grad_ref[...].astype(BF)
        dy3_ref[...] = grad_y
        for copy in c_in:
            copy.wait()
        grad_attn[...] = dot_nt(grad_y, w_c[...]).astype(BF)
        for copy in (kv_in, p3_in, q3_in):
            copy.wait()
        attend_back(
            lambda low, high: q3_ref[:, low:high],
            lambda low, high: kv_ref[0, :, low:high],
            lambda low, high: kv_ref[1, :, low:high],
            lambda low, high: grad_attn[:, low:high],
            lambda head: p3_ref[head],
            heads,
            width,
            into(d_q, count),
            into(d_k, keys),
            into(d_v, keys),
        )
        for r in range(n_tp):
            kv_outs[r][:, 0:columns] = d_k[0:keys, r * columns : (r + 1) * columns]
            kv_outs[r][:, columns:] = d_v[0:keys, r * columns : (r + 1) * columns]
            split(d_q[...], r, bit, in_keep, in_give, r * in_slot + 3 * part)
        for copy in q_in:
            copy.wait()
        grad_h = dot_nn(d_q[...], w_q[...])
        total[...] = grad_ref[...] + norm_back(grad_h, h3_ref[...].astype(F32), inv3_ref[:, 0:1])

        grad_y = total[...].astype(BF)
        dy2_ref[...] = grad_y
        for copy in o_in:
            copy.wait()
        grad_attn[...] = dot_nt(grad_y, w_o[...]).astype(BF)
        for copy in (qkv_load, p2_in):
            copy.wait()
        attend_back(
            lambda low, high: qkv_ref[0, :, low:high],
            lambda low, high: qkv_ref[1, :, low:high],
            lambda low, high: qkv_ref[2, :, low:high],
            lambda low, high: grad_attn[:, low:high],
            lambda head: p2_ref[head],
            heads,
            width,
            into(d_q, count),
            into(d_k, count),
            into(d_v, count),
        )
        for i, ref in enumerate((d_q, d_k, d_v)):
            for r in range(n_tp):
                split(ref[0:count, :], r, bit, in_keep, in_give, r * in_slot + i * part)
            for copy in qkv_in[i]:
                copy.wait()
            term = dot_nn(ref[0:count, :], w_qkv[i])
            grad_h = term if i == 0 else grad_h + term
        stream_ref[...] = (
            total[...] + norm_back(grad_h, h2_ref[...].astype(F32), inv2_ref[:, 0:1])
        ).astype(BF)
        pairs.finish()
        exchange.finish()
        block_out[...] = recv[...]
        text_exchange.finish()
        text_out[...] = text_recv[...]

    square = (count, width)
    in_pack = like((count, n_tp * in_slot))
    ins = [grad, inv2, inv3, h2, h3, out_blocks, texts, qkv, p2, q3, p3, keyval]
    ins = ins + [array for array, unused in given]
    ins = ins + [*tqkv_list, *to_list, *cq_list, *co_list]
    square_keys = (keys, width)
    return call(
        kernel,
        [in_pack, in_pack, like(square), like(square), like(square), like(out_blocks.shape), like(texts.shape)]
        + [like(array.shape) for array, unused in given]
        + [like((keys, 2 * columns))] * n_tp,
        ins,
        [False] * 7 + [True] * (5 + len(given) + 4 * n_tp),
        [False] * 7 + [True] * len(given) + [False] * n_tp,
        [VMEM((3, full, width), BF)]
        + [VMEM((full, width), BF)] * 3
        + [
            VMEM((3,) + square, BF),
            VMEM((heads, count, count), BF),
            VMEM(square, BF),
            VMEM((heads, count, keys), BF),
            VMEM((2,) + square_keys, BF),
            VMEM(square, BF),
            VMEM(square, BF),
            VMEM((max(count, keys), width), BF),
            VMEM((max(count, keys), width), BF),
            VMEM(square, F32),
            pltpu.SemaphoreType.DMA((6 * n_tp + 7,)),
            VMEM(out_blocks.shape, BF),
        ]
        + swap_sems(out_blocks.shape[0], 1)
        + [VMEM(texts.shape, BF)]
        + swap_sems(out_blocks.shape[0], 1)
        + swap_sems(len(given), 1),
        collective_id=7,
        has_side_effects=True,
    )


def spatial_backward(grad_y_list, probs, qkv, sqkv_rows, w_so, frames_here, given, q_first):
    n_tp = len(grad_y_list)
    rows, width = grad_y_list[0].shape
    columns = w_so.shape[0]
    part = columns // 2
    patch_part = rows // frames_here
    per_frame = n_tp * patch_part
    count = n_tp * rows
    heads = columns // HD
    side = whole_tiles(3 * part)

    def kernel(*refs):
        grads = refs[:n_tp]
        probs_hbm, qkv_hbm, wqkv_hbm, so_hbm = refs[n_tp : n_tp + 4]
        given_refs, refs = refs[n_tp + 4 : n_tp + 4 + len(given)], refs[: n_tp + 4] + refs[n_tp + 4 + len(given) :]
        keep, give, own_ref = refs[n_tp + 4 : n_tp + 7]
        others = refs[n_tp + 7 : 2 * n_tp + 6]
        grad_y = refs[2 * n_tp + 6]
        given_got, refs = refs[2 * n_tp + 7 : 2 * n_tp + 8 + len(given)], refs[2 * n_tp + 8 + len(given) :]
        w_qkv, w_o, qkv_ref, probs_ref, grad_attn, d_all, sems, pair_send, pair_recv = refs
        greet_devices(pair_places())
        pairs = PairCopies(pair_send, pair_recv)
        for (unused, first), ref, target in zip(given, given_refs, given_got):
            pairs.start(ref, target, first)
        if side > 3 * part:
            for ref in (keep, give):
                ref[:, 3 * part :] = jnp.zeros((count, side - 3 * part), BF)
        moves = Moves(sems)
        o_in = moves.start(so_hbm, w_o)
        qkv_in = moves.start(qkv_hbm, qkv_ref)
        probs_in = moves.start(probs_hbm, probs_ref)
        weight_in = moves.start(wqkv_hbm, w_qkv)
        for frame in range(frames_here):
            for r in range(n_tp):
                at = frame * per_frame + r * patch_part
                grad_y[at : at + patch_part, :] = grads[r][
                    frame * patch_part : (frame + 1) * patch_part, :
                ]
        o_in.wait()
        grad_attn[...] = dot_nt(grad_y[...], w_o[...]).astype(BF)
        qkv_in.wait()
        probs_in.wait()
        mine = bit_of(q_first)
        for frame in range(frames_here):
            at = slice(frame * per_frame, (frame + 1) * per_frame)

            def into(i, at=at):
                def write(low, high, value):
                    d_all[i, at, low:high] = value.astype(BF)

                return write

            attend_back(
                lambda low, high, at=at: qkv_ref[0, at, low:high],
                lambda low, high, at=at: qkv_ref[1, at, low:high],
                lambda low, high, at=at: qkv_ref[2, at, low:high],
                lambda low, high, at=at: grad_attn[at, low:high],
                lambda head, frame=frame: probs_ref[frame * heads + head],
                heads,
                columns,
                into(0),
                into(1),
                into(2),
            )
            for i in range(3):
                value = d_all[i, at, :]
                first, second = value[:, :part], value[:, part:]
                keep[at, i * part : (i + 1) * part] = jnp.where(mine == 0, first, second)
                give[at, i * part : (i + 1) * part] = jnp.where(mine == 0, second, first)
            done = pl.ds(frame * per_frame, per_frame)
            pairs.start(give.at[done, :], given_got[-1].at[done, :], q_first)
        weight_in.wait()
        for frame in range(frames_here):
            at = slice(frame * per_frame, (frame + 1) * per_frame)
            grad_h = dot_nn(d_all[0, at, :], w_qkv[0])
            for i in (1, 2):
                grad_h = grad_h + dot_nn(d_all[i, at, :], w_qkv[i])
            here = slice(frame * patch_part, (frame + 1) * patch_part)
            own_ref[here, :] = grad_h[:patch_part]
            for r in range(1, n_tp):
                others[r - 1][here, :] = grad_h[r * patch_part : (r + 1) * patch_part].astype(BF)
        pairs.finish()

    ins = [*grad_y_list, probs, qkv, sqkv_rows, w_so] + [array for array, unused in given]
    return call(
        kernel,
        [like((count, side))] * 2
        + [like((rows, width), F32)]
        + [like((rows, width))] * (n_tp - 1)
        + [like((count, width))]
        + [like(array.shape) for array, unused in given]
        + [like((count, side))],
        ins,
        [False] * n_tp + [True] * (4 + len(given)),
        [False] * (n_tp + 3) + [True] * (len(given) + 1),
        [
            VMEM((3, columns, width), BF),
            VMEM((columns, width), BF),
            VMEM((3, count, columns), BF),
            VMEM(probs.shape, BF),
            VMEM((count, columns), BF),
            VMEM((3, count, columns), BF),
            pltpu.SemaphoreType.DMA((4,)),
        ]
        + swap_sems(len(given) + frames_here, 1),
        collective_id=8,
        has_side_effects=True,
    )


def tokens_gradient(tokens_rows, grad, grad_h_own, grad_h_others, mod_here, frames_here, after):
    rows, width = tokens_rows.shape
    patch_part = rows // frames_here
    others = len(grad_h_others)

    def kernel(*refs):
        token_ref, grad_ref, own_ref = refs[:3]
        mod_ref, out_ref, sum_ref = refs[3 + others :]
        for frame in range(frames_here):
            at = slice(frame * patch_part, (frame + 1) * patch_part)
            grad_h = own_ref[at, :]
            for other in refs[3 : 3 + others]:
                grad_h = grad_h + other[at, :].astype(F32)
            normed, inverse = norm_of(token_ref[at, :].astype(F32))
            sum_ref[frame : frame + 1, 0:width] = jnp.sum(grad_h, axis=0, keepdims=True)
            sum_ref[frame : frame + 1, width:] = jnp.sum(grad_h * normed, axis=0, keepdims=True)
            scale = 1.0 + mod_ref[frame : frame + 1, width : 2 * width]
            out_ref[at, :] = (grad_ref[at, :] + norm_back(grad_h * scale, normed, inverse)).astype(BF)

    ins = [tokens_rows, grad, grad_h_own, *grad_h_others, mod_here]
    return call(
        kernel,
        [like((rows, width)), like((frames_here, 2 * width), F32)],
        ins,
        [False] * len(ins),
        [False] * 2,
        [],
        after,
    )


def flip(operand, mask):
    size = lax.axis_size("wide")
    return lax.ppermute(operand, "wide", [(s, s ^ mask) for s in range(size)])


def tp_from(operand, shift):
    size = lax.axis_size("tp")
    return lax.ppermute(operand, "tp", [(s, (s - shift) % size) for s in range(size)])


def tp_to(operand, shift):
    size = lax.axis_size("tp")
    return lax.ppermute(operand, "tp", [(s, (s + shift) % size) for s in range(size)])


def tp_gather(operand):
    return [operand] + [tp_from(operand, k) for k in range(1, lax.axis_size("tp"))]


class Pack:
    def __init__(self, first, order, layout):
        self.first, self.layout = first, layout
        self.order = order + [bit for bit in range(wide_bits()) if bit != first and bit not in order]
        self.across = sum(groups * cols for groups, cols in layout)


def scatter_rows(total, keep, give, pack, size):
    block = keep.shape[1]
    across = pack.across
    mine = bit_of(pack.order[0])
    inner = pack.order[1:] + [pack.first]
    for at in range(size // 2):
        parts = []
        for value in range(2):
            place = value << pack.order[0]
            for depth, bit in enumerate(inner):
                place |= ((at >> (len(inner) - 1 - depth)) & 1) << bit
            parts.append(total[place * block : (place + 1) * block, 0:across].astype(BF))
        keep[at] = jnp.where(mine == 0, parts[0], parts[1])
        give[at] = jnp.where(mine == 0, parts[1], parts[0])


class Flow:
    def __init__(self, pack, keep, give, lands, send_sem, recv_sem, outs):
        self.pack, self.keep, self.give, self.lands = pack, keep, give, lands
        self.send_sem, self.recv_sem, self.outs = send_sem, recv_sem, outs
        self.bits = pack.order + [pack.first]
        self.level, self.behind, self.base = 0, 0, 0
        self.first, self.second, self.placed = None, None, False

    def region(self, level, part):
        number = self.lands[level].shape[0]
        if number == 1:
            return 0, 1
        half = number // 2
        mine = bit_of(self.bits[level + 1])
        return (mine if part else 1 - mine) * half, half

    def start(self, part):
        level = self.level
        low, number = self.region(level, part)
        if level == 0:
            source = self.give.at[pl.ds(low, number)]
        else:
            shift = self.region(level - 1, 0)[0]
            source = self.lands[level - 1].at[pl.ds(shift + low, number)]
        copy = pltpu.make_async_remote_copy(
            src_ref=source,
            dst_ref=self.lands[level].at[pl.ds(low, number)],
            send_sem=self.send_sem.at[2 * level + part],
            recv_sem=self.recv_sem.at[2 * level + part],
            device_id={"wide": partner(self.bits[level])},
            device_id_type=pl.DeviceIdType.MESH,
        )
        copy.start()
        return copy

    def send(self):
        if self.first is None and not self.placed:
            self.first = self.start(0)

    def wait(self):
        if self.placed:
            return
        self.part()
        self.send()
        self.first.wait()
        level = self.level
        land = self.lands[level]
        if land.shape[0] == 1:
            self.place(land)
            return
        self.second = self.start(1)
        low, number = self.region(level, 0)
        for i in range(number):
            own = self.keep[self.base + low + i].astype(F32)
            land[low + i] = (own + land[low + i].astype(F32)).astype(BF)
        self.level, self.first = level + 1, None

    def part(self):
        if self.second is None:
            return
        self.second.wait()
        self.second = None
        low, number = self.region(self.behind, 1)
        land = self.lands[self.behind]
        for i in range(number):
            own = self.keep[self.base + low + i].astype(F32)
            self.keep[self.base + low + i] = (own + land[low + i].astype(F32)).astype(BF)
        self.base = self.base + low
        self.behind += 1

    def go(self):
        self.wait()
        self.send()

    def place(self, land):
        self.placed = True
        mine = bit_of(self.pack.first)
        own, other = self.keep[self.base].astype(F32), land[0].astype(F32)
        sides = [jnp.where(mine == 0, own, other), jnp.where(mine == 0, other, own)]
        low = 0
        for out, (groups, cols) in zip(self.outs, self.pack.layout):
            for g in range(groups):
                for side in range(2):
                    value = sides[side][:, low + g * cols : low + (g + 1) * cols]
                    if groups == 1:
                        out[:, side * cols : (side + 1) * cols] = value
                    else:
                        out[g, :, side * cols : (side + 1) * cols] = value
            low += groups * cols


def reduce_all(ready_packs, rows_packs, slot_packs, kv_parts, mod_blocks, embed, texts, text_cols, ckv_rows, schedule, after, extra_rows=0):
    n_tp, size = lax.axis_size("tp"), lax.axis_size("wide")
    bits = wide_bits()
    packs = [member[0] for member in (*ready_packs, *rows_packs, *slot_packs)]
    n_ready, n_rows, n_slots = len(ready_packs), len(rows_packs), len(slot_packs)
    rows, width = rows_packs[0][2].shape
    count = n_tp * rows
    block = width // size
    others = n_tp - 1
    most = max(whole_tiles(member[0].across) for member in rows_packs)
    token_rows = slot_packs[0][3].shape[0]
    models = len(slot_packs[0][1])
    slot_width = max(member[3].shape[1] for member in slot_packs)
    keys, columns = kv_parts[0].shape[0] * kv_parts[0].shape[1], kv_parts[0].shape[2]
    context_cols = width // size
    owned = width // n_tp

    row_ins = [array for member in rows_packs for array in member[1:5]]
    slot_ins = [array for member in slot_packs for array in (*member[1], *member[2], *member[3:5])]
    ready_ins = [array for member in ready_packs for array in member[1:]]
    ins = ready_ins + row_ins + slot_ins + [ckv_rows, texts, mod_blocks, embed] + list(kv_parts)
    in_any = [True] * (len(ready_ins) + len(row_ins) + len(slot_ins) + 1) + [False] * 3 + [True] * len(kv_parts)
    result = []
    for pack in packs:
        for groups, cols in pack.layout:
            result.append(like((block, 2 * cols) if groups == 1 else (groups, block, 2 * cols), F32))
    landing = [like((rows, width))] * (n_rows * others)
    for member in slot_packs:
        landing += [like((token_rows, width))] * (2 * models * others)
        landing += [like(member[3].shape)] * (2 * others)
    pairs = [p for p, member in enumerate(rows_packs) if member[6]]
    landing += [like(rows_packs[p][4].shape) for p in pairs]
    spare = mod_blocks.shape[1]
    kv_block_rows = kv_parts[0].shape[1]
    clips = embed.shape[0]
    mod_row = kv_block_rows if extra_rows else kv_block_rows - spare
    mod_cols = 6 * width // (n_tp * size)
    outs = result + [like((context_cols, columns), F32), like((owned, text_cols), F32)]
    outs += [like((mod_cols, width), F32), like((1, mod_cols), F32)] + landing
    out_any = [False] * (len(result) + 4) + [True] * len(landing)
    scratch = [VMEM((count, width), BF)] * 2 + [VMEM((count, most), BF)] * 2
    scratch += [VMEM((token_rows, width), BF)] * (2 * n_tp * models)
    scratch += [VMEM((token_rows, slot_width), BF)] * (2 * n_tp)
    scratch += [VMEM((width, max(pack.across for pack in packs)), F32)]
    for pack in packs:
        shape = (block, pack.across)
        scratch += [VMEM((size // 2,) + shape, BF)] * 2
        scratch += [VMEM((size >> (s + 1),) + shape, BF) for s in range(bits)]
        scratch += [pltpu.SemaphoreType.DMA((2 * bits,))] * 2
    n_core = others * (n_rows + 2 * (models + 1) * n_slots + 2)
    n_moves = n_rows * 3 + sum(member[5] * n_tp for member in rows_packs) + 2 * n_tp * n_slots * (models + 1) + 1 + 2 * n_ready + n_tp
    kv_block = kv_parts[0].shape[1:]
    sum_block = (kv_block[0] + extra_rows, kv_block[1])
    kv_scratch = level_scratch(size, sum_block) + level_scratch(size, sum_block)[1:] + level_scratch(size, kv_block)
    scratch += [pltpu.SemaphoreType.DMA((n_core,))] * 2 + [pltpu.SemaphoreType.DMA((n_moves,))]
    scratch += [VMEM(kv_parts[0].shape, BF)] + kv_scratch + [pltpu.SemaphoreType.DMA((bits,))] * 4
    scratch += [VMEM((keys, columns), BF), VMEM((columns, width), BF), VMEM((2 * others, keys, owned), BF)]
    scratch += [VMEM((keys, owned), F32), VMEM((2 * others, 8, whole_tiles(clips * mod_cols)), F32)]
    scratch += [pltpu.SemaphoreType.DMA((max(len(pairs), 1),))] * 2

    def kernel(*refs):
        refs = list(refs)

        def take(number):
            taken = refs[:number]
            del refs[:number]
            return taken

        ready_refs = [take(2) for unused in range(n_ready)]
        row_refs = [take(4) for unused in range(n_rows)]
        slot_refs = [[take(models), take(models), take(2)] for unused in range(n_slots)]
        ckv_ref, text_ref, mod_ref, embed_ref = take(4)
        kv_refs = take(len(kv_parts))
        results = [take(len(pack.layout)) for pack in packs]
        grad_ckv, grad_text, grad_mod, grad_bias = take(4)
        row_land = [take(others) for unused in range(n_rows)]
        slot_land = [
            [[take(models) for unused in range(2)] for unused2 in range(others)]
            + [[take(others) for unused in range(2)]]
            for unused3 in range(n_slots)
        ]
        pair_land = dict(zip(pairs, take(len(pairs))))
        own_model, got_model, own_head, got_head = take(4)
        model_stages = [take(models) for unused in range(2 * n_tp)]
        stages = take(2 * n_tp)
        (total,) = take(1)
        flows = []
        for pack, result_refs in zip(packs, results):
            keep, give = take(2)
            lands = take(bits)
            flows.append(Flow(pack, keep, give, lands, *take(2), result_refs))
        send_sem, recv_sem, move_sem, kv_stage = take(4)
        halving_levels, halving_lands, doubling_levels = take(bits + 1), take(bits), take(bits + 1)
        kv_sems = take(4)
        kv_all, ckv, exchange, text_own, mod_exchange, pair_send, pair_recv = take(7)

        greet_devices(core_places() + pair_places())
        moves = Moves(move_sem)
        core = CoreCopies(send_sem, recv_sem)
        for i, ref in enumerate(kv_refs):
            moves.start(ref, kv_stage).wait()
            for at in range(size):
                value = kv_stage[at].astype(F32)
                level = halving_levels[0].at[mirrored(at)]
                if i == 0:
                    if extra_rows:
                        value = jnp.concatenate([value, jnp.zeros((extra_rows, kv_block[1]), F32)], axis=0)
                    row = lax.broadcasted_iota(jnp.int32, sum_block, 0)
                    for j in range(spare):
                        value = jnp.where(row == mod_row + j, mod_ref[at, j : j + 1, :], value)
                    level[...] = value.astype(BF)
                else:
                    own = level[0 : kv_block[0], :].astype(F32)
                    level[0 : kv_block[0], :] = (own + value).astype(BF)
        ready_loads = [
            (moves.start(give, flows[p].give), moves.start(keep, flows[p].keep))
            for p, (keep, give) in enumerate(ready_refs)
        ]
        halving = Halving(halving_levels, halving_lands, *kv_sems[:2])
        halving.start()
        doubling = Doubling(doubling_levels, *kv_sems[2:])

        pair_flights = {}
        for i, p in enumerate(pairs):
            copy = pltpu.make_async_remote_copy(
                src_ref=row_refs[p][3],
                dst_ref=pair_land[p],
                send_sem=pair_send.at[i],
                recv_sem=pair_recv.at[i],
                device_id={"wide": partner(rows_packs[p][0].first)},
                device_id_type=pl.DeviceIdType.MESH,
            )
            copy.start()
            pair_flights[p] = copy
        row_flights, slot_flights = {}, {}

        def core_rows(p):
            row_flights[p] = [
                core.start(row_refs[p][1], row_land[p][n_tp - 2 - k], place)
                for k, place in enumerate(core_places())
            ]

        def core_slots(p):
            slot = slot_packs[p][5]
            flights = []
            for k, place in enumerate(core_places()):
                for side in range(2):
                    for ref, to in zip(slot_refs[p][side], slot_land[p][k][side]):
                        flights.append(core.start(ref, to, place))
                    ref, to = slot_refs[p][2][side], slot_land[p][others][side][k]
                    cols = pl.ds((k + 1) * slot, slot)
                    flights.append(core.start(ref.at[:, cols], to.at[:, cols], place))
            slot_flights[p] = flights

        ckv_in = moves.start(ckv_ref, ckv)
        loads = {}

        def load_rows(p):
            model, got, keep, other = row_refs[p]
            frames = rows_packs[p][5]
            step = rows // frames
            cols = pl.ds(0, keep.shape[1])
            loads[p] = [moves.start(model, own_model), moves.start(keep, own_head.at[:, cols])]
            if p in pair_flights:
                pair_flights[p].wait()
                other = pair_land[p]
            loads[p].append(moves.start(other, got_head.at[:, cols]))
            for frame in range(frames):
                target = got_model.at[pl.ds(frame * n_tp * step, step), :]
                loads[p].append(moves.start(got.at[pl.ds(frame * step, step), :], target))

        def rows_product(p):
            frames = rows_packs[p][5]
            step = rows // frames
            across = rows_packs[p][0].across
            for copy in loads[p][:2]:
                copy.wait()
            total[:, 0:across] = dot_tn(own_model[...], own_head[:, 0:across])
            for copy in row_flights[p]:
                copy.wait()
            rest = loads[p][2:]
            for frame in range(frames):
                for k in range(others):
                    target = got_model.at[pl.ds((frame * n_tp + k + 1) * step, step), :]
                    rest.append(moves.start(row_land[p][k].at[pl.ds(frame * step, step), :], target))
            for copy in rest:
                copy.wait()
            total[:, 0:across] += dot_tn(got_model[...], got_head[:, 0:across])
            flow = flows[n_ready + p]
            scatter_rows(total, flow.keep, flow.give, rows_packs[p][0], size)

        def stage(p, side, k):
            wide = slot_packs[p][3].shape[1]
            at = 2 * k + side
            if k == 0:
                model_refs, head = slot_refs[p][side], slot_refs[p][2][side]
            else:
                model_refs, head = slot_land[p][k - 1][side], slot_land[p][others][side][k - 1]
            found = [moves.start(ref, to) for ref, to in zip(model_refs, model_stages[at])]
            return found + [moves.start(head, stages[at].at[:, pl.ds(0, wide)])]

        def load_slots(p):
            loads[n_rows + p] = stage(p, 0, 0) + stage(p, 1, 0)

        def slots_product(p):
            pack, unused, unused2, unused3, unused4, slot, weights = slot_packs[p]

            def add(k):
                low = 0
                for model, column, cols in weights:
                    at = k * slot + column
                    terms = [
                        dot_tn(model_stages[2 * k + side][model][...], stages[2 * k + side][:, at : at + cols])
                        for side in range(2)
                    ]
                    if k == 0:
                        total[:, low : low + cols] = terms[0] + terms[1]
                    else:
                        total[:, low : low + cols] += terms[0] + terms[1]
                    low += cols

            for copy in loads[n_rows + p]:
                copy.wait()
            add(0)
            for copy in slot_flights[p]:
                copy.wait()
            rest = [copy for k in range(1, n_tp) for side in range(2) for copy in stage(p, side, k)]
            for copy in rest:
                copy.wait()
            for k in range(1, n_tp):
                add(k)
            flow = flows[n_ready + n_rows + p]
            scatter_rows(total, flow.keep, flow.give, pack, size)

        def caption():
            if halving.bit < bits:
                halving.advance()
                if halving.bit == bits:
                    doubling_levels[bits][0] = halving_levels[bits][0, 0 : kv_block[0], :]
                    doubling.start()
            elif doubling.bit:
                doubling.advance()

        text_flights = []

        def context():
            while doubling.bit:
                caption()
            for at in range(size):
                kv_all[at * kv_block[0] : (at + 1) * kv_block[0], :] = doubling_levels[0][mirrored(at)]
            grad_ckv[...] = dot_tn(text_ref[:, text_cols : text_cols + context_cols], kv_all[...])
            ckv_in.wait()
            grad = dot_nn(kv_all[...], ckv[...])
            here = lax.axis_index("tp")

            def part(owner):
                chosen = grad[:, 0:owned]
                for other in range(1, n_tp):
                    chosen = jnp.where(owner == other, grad[:, other * owned : (other + 1) * owned], chosen)
                return chosen

            for k, place in enumerate(core_places()):
                exchange[k] = part(lax.rem(here + k + 1, n_tp)).astype(BF)
                text_flights.append(core.start(exchange.at[k], exchange.at[others + k], place))
            text_own[...] = part(here)

        def text():
            grad = text_own[...]
            for k, copy in enumerate(text_flights):
                copy.wait()
                grad = grad + exchange[others + k].astype(F32)
            grad_text[...] = dot_tn(grad.astype(BF), text_ref[:, 0:text_cols])

        mod_flights = []
        flat = clips * mod_cols

        def modulation_part(owner):
            rows_here = halving_levels[bits][0].astype(F32)[mod_row : mod_row + spare, :]
            row = jnp.concatenate([rows_here[i : i + 1] for i in range(spare)], axis=1)
            chosen = row[:, 0:flat]
            for other in range(1, n_tp):
                chosen = jnp.where(owner == other, row[:, other * flat : (other + 1) * flat], chosen)
            return chosen

        def modulation_send():
            here = lax.axis_index("tp")
            for k, place in enumerate(core_places()):
                part = modulation_part(lax.rem(here + k + 1, n_tp))
                mod_exchange[k, :, 0:flat] = jnp.broadcast_to(part, (8, flat))
                if mod_exchange.shape[2] > flat:
                    mod_exchange[k, :, flat:] = jnp.zeros((8, mod_exchange.shape[2] - flat), F32)
                mod_flights.append(core.start(mod_exchange.at[k], mod_exchange.at[others + k], place))

        def modulation():
            total_row = modulation_part(lax.axis_index("tp"))
            for k, copy in enumerate(mod_flights):
                copy.wait()
                total_row = total_row + mod_exchange[others + k, 0:1, 0:flat]
            sums = jnp.concatenate(
                [total_row[:, c * mod_cols : (c + 1) * mod_cols] for c in range(clips)], axis=0
            )
            grad_bias[...] = jnp.sum(sums, axis=0, keepdims=True)
            grad_mod[...] = dot_tn(sums.astype(BF), embed_ref[...])

        for what, p in schedule:
            row, slot = p - n_ready, p - n_ready - n_rows
            if what == "core":
                core_rows(row) if slot < 0 else core_slots(slot)
            elif what == "load":
                load_rows(row) if slot < 0 else load_slots(slot)
            elif what == "product":
                if row < 0:
                    for copy in ready_loads[p]:
                        copy.wait()
                elif slot < 0:
                    rows_product(row)
                else:
                    slots_product(slot)
            elif what == "send":
                flows[p].send()
            elif what == "wait":
                flows[p].wait()
            elif what == "part":
                flows[p].part()
            elif what == "go":
                flows[p].go()
            elif what == "caption":
                caption()
            elif what == "context":
                context()
                modulation_send()
            elif what == "modulation":
                modulation()
            else:
                text()
        while not all(flow.placed for flow in flows):
            for flow in flows:
                flow.go()

    out = call(
        kernel,
        outs,
        ins,
        in_any,
        out_any,
        scratch,
        after,
        limit=63,
        collective_id=4,
        has_side_effects=True,
    )
    return out[: len(result)], *out[len(result) : len(result) + 4]


def tp_sum(parts, dtype=BF):
    total = parts[0].astype(F32)
    for k in range(1, lax.axis_size("tp")):
        total = total + tp_to(parts[k].astype(dtype), k).astype(F32)
    return total


def tp_ordered(relative):
    size = lax.axis_size("tp")
    start = (size - lax.axis_index("tp")) % size
    return lax.dynamic_slice_in_dim(jnp.stack(relative + relative), start, size, axis=0)


def swap_wide(blocks):
    return lax.all_to_all(blocks, "wide", split_axis=0, concat_axis=0, tiled=True)


def on_device(
    tokens,
    cotangent,
    caption,
    caption_len,
    clip_id,
    timestep,
    w_mod,
    b_mod,
    w_text,
    w_sqkv,
    w_so,
    w_tqkv,
    w_to,
    w_cq,
    w_ckv,
    w_co,
    w_fc1,
    w_fc2,
):
    n_tp = lax.axis_size("tp")
    n_wide = lax.axis_size("wide")
    frames_here, patch_part, width = tokens.shape
    columns = w_so.shape[0]
    part = columns // 2
    half = w_fc1.shape[1] // 2
    clip_count = timestep.shape[0]
    frames = clip_id.shape[0]
    patch_here = patch_part // n_wide
    rows = frames_here * patch_part
    block = frames_here * patch_here
    count = frames * patch_here
    wide_at = lax.axis_index("wide")
    tp_at = lax.axis_index("tp")

    tokens_rows = tokens.reshape(rows, width)
    tokens_list = tp_gather(tokens_rows)
    sqkv_rows = w_sqkv.transpose(1, 2, 0)
    tqkv_list = tp_gather(w_tqkv.transpose(1, 2, 0))
    to_list = tp_gather(w_to)
    cq_list = tp_gather(w_cq.T)
    co_list = tp_gather(w_co)

    half_width = width // 2
    frequencies = jnp.exp(-math.log(10000.0) * jnp.arange(half_width).astype(F32) / half_width)
    angles = timestep.astype(F32)[:, None] * frequencies[None, :]
    embedding = jnp.concatenate([jnp.cos(angles), jnp.sin(angles)], axis=1)
    silu_embed = jax.nn.silu(embedding).astype(BF)
    mod_part = (dot_nn(silu_embed, w_mod) + b_mod.astype(F32)).astype(BF)
    modulation = tp_ordered(tp_gather(mod_part)).transpose(1, 0, 2).reshape(clip_count, -1)
    clip_hot = clip_id[:, None] == jnp.arange(clip_count)[None, :]
    hot_here = lax.dynamic_slice_in_dim(
        clip_hot.astype(F32), wide_at * frames_here, frames_here
    )
    mod_here = dot_nn(hot_here.astype(BF), modulation[:, : 3 * width])
    clip_rows = jnp.broadcast_to(clip_id[:, None], (frames, patch_here)).reshape(count)
    hot_rows = (clip_rows[:, None] == jnp.arange(clip_count)[None, :]).astype(BF)
    mod_rows = dot_nn(hot_rows, modulation[:, 3 * width :]).astype(BF)

    caption_rows = caption.shape[0]
    spare_rows = -(-clip_count * 6 * width // (n_wide * 2 * columns))
    block_rows = -(-caption_rows // 16) * 16
    extra_rows = 0 if caption_rows + spare_rows <= block_rows else -(-spare_rows // 16) * 16
    keys = n_wide * block_rows
    padded = jnp.pad(caption, ((0, block_rows - caption_rows), (0, 0)))
    context_part = dot_nt(padded, w_text.T).astype(BF)
    context = tp_ordered(tp_gather(context_part)).transpose(1, 0, 2).reshape(block_rows, width)
    ckv_rows = w_ckv.transpose(1, 2, 0).reshape(2 * columns, width)
    keyval_part = dot_nt(context, ckv_rows).astype(BF)
    text_cols = caption.shape[1] // n_wide
    context_cols = width // n_wide
    spare = -(text_cols + context_cols) % LANES
    texts = jnp.concatenate(
        [
            padded.reshape(block_rows, n_wide, text_cols),
            context.reshape(block_rows, n_wide, context_cols),
            jnp.zeros((block_rows, n_wide, spare), BF),
        ],
        axis=2,
    ).transpose(1, 0, 2)

    row_two = clip_rows * patch_here + np.arange(count, dtype=np.int32) % patch_here
    key_at = np.arange(keys)
    key_row = key_at // block_rows * caption_rows + key_at % block_rows
    key_real = jnp.asarray(key_at % block_rows < caption_rows)[None, :]
    key_clip = (key_row // LTXT).astype(np.int32)[None, :]
    key_in = (key_row % LTXT).astype(np.int32)[None, :]
    key_three = jnp.full((1, keys), -1, jnp.int32)
    for clip in range(clip_count):
        seen = key_real & (key_clip == clip) & (key_in < caption_len[clip])
        key_three = jnp.where(seen, clip, key_three)
    row_codes = jnp.stack([row_two, clip_rows], axis=1)
    longest = max(count, keys)
    key_codes = jnp.concatenate(
        [jnp.pad(row_two[None, :], ((0, 0), (0, longest - count))), jnp.pad(key_three, ((0, 0), (0, longest - keys)))]
    )

    grad_blocks = cotangent.reshape(frames_here, n_wide, patch_here, width).transpose(1, 0, 2, 3)
    grad_blocks = grad_blocks.reshape(n_wide, block, width)

    up = Pack(0, [1, 3, 2], [(1, half)])
    down = Pack(1, [0, 2, 3], [(1, half)])
    inner = Pack(2, [0, 1, 3], [(3, part), (1, part)])
    outer = Pack(1, [2, 0, 3], [(1, part), (1, part)])
    q_pack = Pack(0, [1, 2, 3], [(3, part)])
    o_pack = Pack(0, [2, 1, 3], [(1, part)])

    h_all, h_own, qkv_one, probs_one, a_keep, a_give, y_own, *others = spatial_forward(
        tokens_list, mod_here, sqkv_rows, w_so, frames_here, keyval_part, o_pack.first
    )
    y_others, keyval = others[: n_tp - 1], others[n_tp - 1]
    keyval_list = tp_gather(keyval.reshape(keys, 2 * columns))
    y_others = [tp_to(other, k + 1) for k, other in enumerate(y_others)]
    stream, y_one = stream_to_patches(tokens_rows, y_own, y_others, mod_here, frames_here)
    *kept, stream, keyval_full, t_keep, t_give, grad_out, a_got = middle_forward(
        stream.reshape(count, width), row_codes, key_codes, [grad_blocks], keyval_list, tqkv_list, to_list, cq_list, co_list, outer.first,
        [(a_give, o_pack.first)],
    )
    grad_out = grad_out.reshape(count, width)
    h2, h3 = kept[0], kept[4]
    (
        block_out,
        h4_all,
        up_keep,
        up_give,
        dy4_all,
        down_keep,
        down_give,
        grad,
        mod_sum,
        unused,
        unused,
        h4_got,
        dy4_got,
        h2_got,
        h3_got,
        t_got,
        h_flip,
    ) = feed_forward(
        stream,
        grad_out,
        mod_rows,
        hot_rows,
        w_fc1,
        w_fc2,
        [up.first, down.first],
        [(h2, inner.first), (h3, inner.first), (t_give, outer.first), (h_own, q_pack.first)],
    )

    in_keep, in_give, dy2, dy3, grad, block_out, texts, up_got, down_got, *grad_kv = middle_backward(
        grad,
        kept,
        keyval_full,
        block_out.reshape(n_wide, block, width),
        texts,
        tqkv_list,
        to_list,
        cq_list,
        co_list,
        inner.first,
        [(up_give, up.first), (down_give, down.first)],
    )
    block_out = block_out.reshape(n_wide, frames_here, patch_here, width).transpose(1, 0, 2, 3)
    block_out = block_out.reshape(frames_here, patch_part, width)
    (grad_stream, grad_y1, grad_gate), (up_halves, down_halves) = grads_to_frames(
        grad.reshape(n_wide, block, width),
        y_one,
        mod_here,
        frames_here,
        [(up, h4_all, h4_got, up_keep, up_got), (down, dy4_all, dy4_got, down_keep, down_got)],
    )
    grad_y1_list = tp_gather(grad_y1)
    given = [(in_give, inner.first), (dy2, outer.first), (dy3, outer.first), (grad_y1, o_pack.first)]
    q_keep, q_give, grad_h_own, *grad_h_others, dy_all, in_got, dy2_got, dy3_got, dy_got, q_got = spatial_backward(
        grad_y1_list, probs_one, qkv_one, sqkv_rows, w_so, frames_here, given, q_pack.first
    )
    grad_h_others = [tp_to(other, k + 1) for k, other in enumerate(grad_h_others)]
    grad_tokens, frame_sums = tokens_gradient(
        tokens_rows, grad_stream, grad_h_own, grad_h_others, mod_here, frames_here, []
    )
    frame_sums = jnp.concatenate([frame_sums, grad_gate], axis=1)
    here_sum = lax.dot_general(hot_here, frame_sums, (((0,), (0,)), ((), ())), precision=HIGH)
    grad_mod = jnp.concatenate([here_sum, mod_sum], axis=1).reshape(clip_count, n_tp, n_wide, -1)
    mod_blocks = grad_mod.transpose(2, 1, 0, 3).reshape(n_wide, -1)
    mod_blocks = jnp.pad(mod_blocks, ((0, 0), (0, spare_rows * 2 * columns - mod_blocks.shape[1])))
    mod_blocks = mod_blocks.reshape(n_wide, spare_rows, 2 * columns)
    kv_parts = [grad_kv[0].reshape(n_wide, block_rows, -1)]
    kv_parts += [tp_to(grad_kv[k], k).reshape(n_wide, block_rows, -1) for k in range(1, n_tp)]
    schedule = [
        ("core", 3), ("core", 5), ("load", 3), ("load", 5), ("product", 0), ("send", 0),
        ("product", 1), ("send", 1), ("product", 3), ("core", 2), ("load", 2), ("send", 3),
        ("product", 5), ("core", 4), ("load", 4), ("send", 5), ("product", 2), ("send", 2),
        ("wait", 3), ("send", 3), ("product", 4), ("send", 4), ("caption", 0), ("wait", 5),
        ("send", 5), ("part", 3), ("wait", 0), ("send", 0), ("wait", 3), ("send", 3),
        ("wait", 1), ("send", 1), ("part", 3), ("wait", 3), ("send", 3), ("caption", 0),
        ("part", 3), ("wait", 3), ("part", 5), ("wait", 5), ("send", 5), ("wait", 2),
        ("send", 2), ("caption", 0), ("caption", 0), ("part", 5), ("wait", 5), ("send", 5),
        ("caption", 0), ("part", 0), ("wait", 0), ("send", 0), ("wait", 4), ("send", 4),
        ("part", 1), ("part", 5), ("wait", 5), ("part", 2), ("wait", 2), ("send", 2),
        ("wait", 1), ("send", 1), ("caption", 0), ("caption", 0), ("part", 4), ("wait", 4),
        ("send", 4), ("caption", 0), ("context", 0), ("part", 4), ("part", 0), ("text", 0),
        ("modulation", 0), ("part", 2), ("wait", 2), ("send", 2), ("wait", 0), ("send", 0),
        ("wait", 4), ("send", 4), ("part", 1), ("wait", 1), ("send", 1), ("part", 2),
        ("wait", 2), ("part", 0), ("wait", 0), ("part", 4), ("wait", 4), ("part", 1),
        ("wait", 1),
    ]
    gradients, grad_ckv, grad_text, grad_w_mod, grad_b_mod = reduce_all(
        [(up, *up_halves), (down, *down_halves)],
        [
            (q_pack, h_all, h_flip, q_keep, q_got, frames_here, False),
            (o_pack, dy_all, dy_got, a_keep, a_got, frames_here, False),
        ],
        [
            (
                inner,
                [h2, h3],
                [h2_got, h3_got],
                in_keep,
                in_got,
                whole_tiles(4 * part),
                [(0, 0, 3 * part), (1, 3 * part, part)],
            ),
            (
                outer,
                [dy2, dy3],
                [dy2_got, dy3_got],
                t_keep,
                t_got,
                whole_tiles(2 * part),
                [(0, 0, part), (1, part, part)],
            ),
        ],
        kv_parts,
        mod_blocks,
        silu_embed,
        texts.reshape(keys, -1),
        text_cols,
        ckv_rows,
        schedule,
        [grad_tokens],
        extra_rows,
    )
    grad_fc1, grad_fc2, grad_sqkv, grad_so, grad_tqkv, grad_cq, grad_to, grad_co = gradients
    grad_ckv = grad_ckv.reshape(-1, 2, columns)
    grad_text = grad_text.T

    return (
        block_out,
        grad_tokens.reshape(tokens.shape),
        grad_w_mod.T,
        grad_b_mod.reshape(-1),
        grad_text,
        grad_sqkv.transpose(1, 0, 2),
        grad_so.T,
        grad_tqkv.transpose(1, 0, 2),
        grad_to.T,
        grad_cq,
        grad_ckv,
        grad_co.T,
        grad_fc1,
        grad_fc2.T,
    )


def solution(mesh):
    placed = (
        P("wide", "tp", None),
        P("wide", "tp", None),
        P("wide", None),
        P(),
        P(),
        P(),
        P(None, "tp"),
        P("tp"),
        P(None, "tp"),
        P(None, None, "tp"),
        P("tp", None),
        P(None, None, "tp"),
        P("tp", None),
        P(None, "tp"),
        P(None, None, "tp"),
        P("tp", None),
        P(None, "tp"),
        P("tp", None),
    )
    return jax.shard_map(
        on_device,
        mesh=mesh,
        in_specs=placed,
        out_specs=(
            P("wide", "tp", None),
            P("wide", "tp", None),
            P(None, ("tp", "wide")),
            P(("tp", "wide")),
            P("wide", "tp"),
            P("wide", None, "tp"),
            P("tp", "wide"),
            P("wide", None, "tp"),
            P("tp", "wide"),
            P("wide", "tp"),
            P("wide", None, "tp"),
            P("tp", "wide"),
            P("wide", "tp"),
            P("tp", "wide"),
        ),
        check_vma=False,
    )
```
